32 devices in a mesh: ctx: 8 (over z, core), fsdp: 4 (over y, x).
Axes of the slice: x: 2, y: 2, z: 4, core: 2. Of those that a mesh axis runs over, the one named last changes fastest.
Arguments:
- hidden_in: bfloat16 [4, 3072, 1024], P('fsdp', 'ctx'), may hold values from -6 to 6
- w_qkv: bfloat16 [1024, 3072], P(None, 'fsdp'), may hold values from -0.25 to 0.25
- w_out: bfloat16 [1024, 1024], P(None, 'fsdp'), may hold values from -1 to 1
- w_in: bfloat16 [1024, 4096], P(None, 'fsdp'), may hold values from -0.1875 to 0.1875
- w_back: bfloat16 [4096, 1024], P(None, 'fsdp'), may hold values from -0.09375 to 0.09375
- vectors: float32 [8, 1024], replicated, may hold values from -1 to 1.5, as said below
- bias_in: float32 [4096], replicated, may hold values from -3 to 3
- cotangent: float32 [4, 3072, 1024], P('fsdp', 'ctx'), may hold values from -6 to 6
Outputs:
- layer_out: bfloat16 [4, 3072, 1024], P('fsdp', 'ctx')
- input_grad: float32 [4, 3072, 1024], P('fsdp', 'ctx')
- qkv_weight_grad: float32 [1024, 3072], P(('ctx', 'fsdp'))
- out_weight_grad: float32 [1024, 1024], P(('ctx', 'fsdp'))
- in_weight_grad: float32 [1024, 4096], P(('ctx', 'fsdp'))
- back_weight_grad: float32 [4096, 1024], P(None, ('ctx', 'fsdp'))
- vector_grad: float32 [8, 1024], P(None, ('ctx', 'fsdp'))
- in_bias_grad: float32 [4096], P(('ctx', 'fsdp'))
The draws below stay inside these ranges and needn't reach their ends.
Inputs may be any that keep to these rules, and one draw needn't show every extreme that they name: `vectors`: rows 3 and 6 (norm gains) lie within 0.5 to 1.5, the other rows within -1 to 1.
All inputs are finite; a program needn't handle non-finite values.
Results may differ from the reference program's by a relative error of at most 0.015.
The reference program's roundings to bfloat16 on the way count: a program that leaves them out, or rounds other values in their place, can miss the bound.
Values may be sent and summed in bfloat16 or wider, within the bound.
A program may use at most 384 MiB of HBM per device.

```python
import math
import jax
import jax.numpy as jnp
from jax import lax

D = 1024
HEADS = 16
HEAD = 64
FF = 4096
LENGTH = 3072
SEQS = 4


def draw_vectors(key, part):
    key = jax.random.fold_in(key, 11)
    first, second = jax.random.split(key)
    base = jnp.clip(jax.random.normal(first, (8, D), jnp.float32) * 0.3, -1.0, 1.0)
    gains = jax.random.uniform(second, (8, D), jnp.float32, 0.5, 1.5)
    rows = jnp.arange(8)[:, None]
    is_gain = (rows == 3) | (rows == 6)
    return jnp.where(is_gain, gains, base).astype(jnp.float32)


def steps_of(own_key, extent, pieces, smallest, top_value):
    def one(axis_at, blocks):
        steps = jax.random.uniform(jax.random.fold_in(jax.random.fold_in(own_key, 6), axis_at), (blocks,), jnp.float32, smallest / len(pieces), top_value / len(pieces))
        return jnp.repeat(jnp.exp(steps), extent[axis_at] // blocks).reshape((-1,) + (1,) * (len(extent) - axis_at - 1))

    level = one(*pieces[0])
    for cut in pieces[1:]:
        level = level * one(*cut)
    return level


def noise(rng, shape, scale, bound, cuts=(), held_as=jnp.bfloat16):
    values = jax.random.normal(rng, shape, jnp.float32) * scale
    if len(cuts) > 0:
        values = steps_of(rng, shape, cuts, -0.22, 0.18) * values
    return jnp.clip(values, min=-bound, max=bound).astype(held_as)


def setup_inputs(seed: int = 0) -> dict:
    splits = jax.random.split(jax.random.key(seed), 9)
    return {
        "hidden_in": noise(splits[0], (SEQS, LENGTH, D), 1.0, 6.0, ((0, 4), (1, 8))),
        "w_qkv": noise(splits[1], (D, 3 * D), (D // 2) ** -0.5, 0.25, ((1, 4),)),
        "w_out": noise(splits[2], (D, D), (D // 32) ** -0.5, 1.0, ((1, 4),)),
        "w_in": noise(splits[3], (D, FF), D ** -0.5, 0.1875, ((1, 4),)),
        "w_back": noise(splits[4], (FF, D), FF ** -0.5, 0.09375, ((1, 4),)),
        "vectors": draw_vectors(jax.random.fold_in(splits[8], 71), 0),
        "bias_in": noise(splits[6], (FF,), 0.5, 3.0, (), jnp.float32),
        "cotangent": noise(splits[7], (SEQS, LENGTH, D), 1.0, 6.0, ((0, 4), (1, 8)), jnp.float32),
    }


EPS = 1e-12
HI = lax.Precision.HIGHEST

@jax.custom_vjp
def low(v):
    return lax.optimization_barrier(v.astype(jnp.bfloat16)).astype(jnp.float32)

@jax.custom_vjp
def low_back(v):
    return v

def low_keep(v):
    return (low(v), None)

def low_pass(kept, grad):
    return (grad,)

def back_keep(v):
    return (v, None)

def back_low(kept, grad):
    return (low(grad),)
low.defvjp(low_keep, low_pass)
low_back.defvjp(back_keep, back_low)

def matmul(left, right):
    return jnp.dot(left, right, precision=HI)

def norm(resid, gain, shift):
    centre = resid - lax.optimization_barrier(jnp.mean(resid, axis=-1, keepdims=True))
    spread = lax.optimization_barrier(jnp.mean(centre * centre, axis=-1, keepdims=True))
    return centre * lax.rsqrt(spread + EPS) * gain + shift

def attention(query, keys, values):
    length = query.shape[0]
    block = min(512, length)
    scale = 1.0 / math.sqrt(HEAD)
    query4 = query.reshape(length // block, block, HEADS, HEAD)
    key3 = keys.reshape(length, HEADS, HEAD)
    value3 = values.reshape(length, HEADS, HEAD)

    def one_block(query_block):
        scores = low_back(scale * jnp.einsum('qhe,khe->hqk', query_block, key3, precision=HI))
        probs = jax.nn.softmax(scores, axis=-1)
        return jnp.einsum('hqk,khe->qhe', low(probs), value3, precision=HI)
    result = lax.map(jax.checkpoint(one_block), query4)
    return result.reshape(length, HEADS * HEAD)

def layer(tokens, w_qkv, w_out, w_in, w_back, vectors, bias_in):
    width = tokens.shape[1]
    qkv_bias = jnp.concatenate([vectors[0], jnp.zeros((width,), jnp.float32), vectors[1]])
    qkv = low(low_back(matmul(low(tokens), low(w_qkv))) + qkv_bias)
    qkv = low_back(qkv)
    attended = attention(qkv[:, :width], qkv[:, width:2 * width], qkv[:, 2 * width:])
    attended = low_back(low(attended))
    resid_one = tokens + low_back(matmul(attended, low(w_out))) + vectors[2]
    normed = norm(resid_one, vectors[3], vectors[4])
    pre = low_back(matmul(low(normed), low(w_in))) + bias_in
    act = low(jax.nn.gelu(pre, approximate=True))
    resid_two = normed + low_back(matmul(act, low(w_back))) + vectors[5]
    return norm(resid_two, vectors[6], vectors[7])

def reference(hidden_in, w_qkv, w_out, w_in, w_back, vectors, bias_in, cotangent):
    params = (w_qkv.astype(jnp.float32), w_out.astype(jnp.float32), w_in.astype(jnp.float32), w_back.astype(jnp.float32), vectors.astype(jnp.float32), bias_in.astype(jnp.float32))

    def one_seq(totals, pair):
        tokens, grad_out = pair
        result, pull = jax.vjp(layer, tokens.astype(jnp.float32), *params)
        grads = pull(grad_out.astype(jnp.float32))
        totals = tuple((a + b for a, b in zip(totals, grads[1:])))
        return (totals, (result.astype(jnp.bfloat16), grads[0]))
    init = tuple((jnp.zeros(p.shape, jnp.float32) for p in params))
    totals, (outputs, input_grads) = lax.scan(one_seq, init, (hidden_in, cotangent))
    return (outputs, input_grads, totals[0], totals[1], totals[2], totals[3], totals[4], totals[5])
```

```python
from functools import partial
import math

import jax
import jax.numpy as jnp
from jax import lax
from jax.experimental import pallas as pl
from jax.experimental.pallas import tpu as pltpu
from jax.sharding import PartitionSpec as P

HEADS = 16
HEAD = 64
EPS = 1e-12
F32 = jnp.float32
BF16 = jnp.bfloat16
NN = (((1,), (0,)), ((), ()))
NT = (((1,), (1,)), ((), ()))
TN = (((0,), (0,)), ((), ()))
VMEM_LIMIT = 50 * 1024 * 1024


def dot(left, right, dims):
    return lax.dot_general(left, right, dims, preferred_element_type=F32)


def one_head(block, head, heads):
    if heads == 1:
        return block
    lane = lax.broadcasted_iota(jnp.int32, block.shape, 1)
    return jnp.where(lane // HEAD == head, block, jnp.zeros_like(block))


def merge_heads(parts):
    if len(parts) == 1:
        return parts[0]
    lane = lax.broadcasted_iota(jnp.int32, parts[0].shape, 1)
    result = parts[0]
    for head in range(1, len(parts)):
        result = jnp.where(lane // HEAD == head, parts[head], result)
    return result


def attend_kernel(*refs, blocks, heads, q_rows, k_rows):
    ins, rest = refs[:blocks], refs[blocks:]
    outs, (full_ref, lse_ref, key_s, value_s) = rest[:blocks], rest[blocks:]
    rows = ins[0].shape[0]
    width = heads * HEAD
    length = rows * blocks
    for b in range(blocks):
        here = slice(b * rows, (b + 1) * rows)
        key_s[here, :] = ins[b][:, width : 2 * width]
        value_s[here, :] = ins[b][:, 2 * width : 3 * width]
    for b in range(blocks):

        def step(i, carry, b=b):
            local = pl.ds(pl.multiple_of(i * q_rows, q_rows), q_rows)
            where = pl.ds(pl.multiple_of(b * rows + i * q_rows, q_rows), q_rows)
            query = ins[b][local, 0:width] * BF16(HEAD**-0.5)
            outputs, sums = [], []
            for head in range(heads):
                masked = one_head(query, head, heads)
                scores = [
                    dot(masked, key_s[j : j + k_rows, :], NT) for j in range(0, length, k_rows)
                ]
                top = None
                for part in scores:
                    part_top = jnp.max(part, axis=1, keepdims=True)
                    top = part_top if top is None else jnp.maximum(top, part_top)
                total = acc = None
                for j, part in enumerate(scores):
                    probs = jnp.exp(part - top)
                    part_total = jnp.sum(probs, axis=1, keepdims=True)
                    value = value_s[j * k_rows : (j + 1) * k_rows, :]
                    part_acc = dot(probs.astype(BF16), value, NN)
                    total = part_total if total is None else total + part_total
                    acc = part_acc if acc is None else acc + part_acc
                outputs.append(acc / total)
                sums.append(jnp.broadcast_to(top + jnp.log(total), (q_rows, width)))
            result = merge_heads(outputs)
            full_ref[where, :] = result
            outs[b][local, :] = result.astype(BF16)
            lse_ref[where, :] = merge_heads(sums)
            return carry

        lax.fori_loop(0, rows // q_rows, step, 0)


def attend(qkv, heads):
    blocks = len(qkv)
    rows = qkv[0].shape[0]
    width = heads * HEAD
    length = rows * blocks
    out = [jax.ShapeDtypeStruct((rows, width), BF16)] * blocks
    out += [jax.ShapeDtypeStruct((length, width), F32)] * 2
    results = pl.pallas_call(
        partial(attend_kernel, blocks=blocks, heads=heads, q_rows=256, k_rows=512),
        out_shape=out,
        scratch_shapes=[pltpu.VMEM((length, width), BF16)] * 2,
        compiler_params=pltpu.CompilerParams(vmem_limit_bytes=VMEM_LIMIT),
        cost_estimate=pl.CostEstimate(
            flops=16 * length * length * width, bytes_accessed=10 * length * width,
            transcendentals=heads * length * length,
        ),
        name="attend",
    )(*qkv)
    return results[:blocks], results[blocks], results[blocks + 1]


def attend_back_kernel(*refs, blocks, heads, q_rows, k_rows):
    ins, grads, rest = refs[:blocks], refs[blocks : 2 * blocks], refs[2 * blocks :]
    full_ref, lse_ref, rest = rest[0], rest[1], rest[2:]
    outs, (lse_t, delta_t, gq_t, key_t) = rest[:blocks], rest[blocks:]
    rows = ins[0].shape[0]
    width = heads * HEAD
    scale = HEAD**-0.5
    chunk = 256
    for b in range(blocks):
        for i in range(0, rows, chunk):
            local = slice(i, i + chunk)
            where = slice(b * rows + i, b * rows + i + chunk)
            logs = lse_ref[where, :].T
            terms = (grads[b][local, :].astype(F32) * full_ref[where, :]).T
            for head in range(heads):
                first = head * HEAD
                lse_t[head : head + 1, where] = logs[first : first + 1]
                delta_t[head : head + 1, where] = jnp.sum(
                    terms[first : first + HEAD], axis=0, keepdims=True
                )
        key_t[:, b * rows : (b + 1) * rows] = ins[b][:, width : 2 * width].T
    gq_t[...] = jnp.zeros_like(gq_t)
    for b in range(blocks):

        def step(j, carry, b=b):
            local = pl.ds(pl.multiple_of(j * k_rows, k_rows), k_rows)
            where = pl.ds(pl.multiple_of(b * rows + j * k_rows, k_rows), k_rows)
            key = ins[b][local, width : 2 * width]
            value = ins[b][local, 2 * width : 3 * width]
            key_grads, value_grads = [], []
            for head in range(heads):
                feats = slice(head * HEAD, (head + 1) * HEAD)
                key_h = one_head(key, head, heads) * BF16(scale)
                value_h = one_head(value, head, heads)
                key_grad = value_grad = None
                for other in range(blocks):
                    for i in range(0, rows, q_rows):
                        here = slice(i, i + q_rows)
                        there = slice(other * rows + i, other * rows + i + q_rows)
                        query = ins[other][here, 0:width]
                        grad = grads[other][here, :]
                        scores = dot(key_h, query, NT)
                        probs = jnp.exp(scores - lse_t[head : head + 1, there])
                        grad_probs = dot(value_h, grad, NT)
                        grad_scores = probs * (grad_probs - delta_t[head : head + 1, there])
                        grad_scores = grad_scores.astype(BF16)
                        term = dot(probs.astype(BF16), grad, NN)
                        value_grad = term if value_grad is None else value_grad + term
                        term = dot(grad_scores, query, NN)
                        key_grad = term if key_grad is None else key_grad + term
                        gq_t[feats, there] += dot(key_t[feats, where], grad_scores, NN)
                key_grads.append(key_grad)
                value_grads.append(value_grad)
            outs[b][local, width : 2 * width] = (merge_heads(key_grads) * scale).astype(BF16)
            outs[b][local, 2 * width : 3 * width] = merge_heads(value_grads).astype(BF16)
            return carry

        lax.fori_loop(0, rows // k_rows, step, 0)
    for b in range(blocks):
        for i in range(0, rows, chunk):
            there = slice(b * rows + i, b * rows + i + chunk)
            outs[b][i : i + chunk, 0:width] = (gq_t[:, there].T * scale).astype(BF16)


def attend_back(qkv, grads, full, lse, heads):
    blocks = len(qkv)
    rows = qkv[0].shape[0]
    width = heads * HEAD
    length = rows * blocks
    return pl.pallas_call(
        partial(attend_back_kernel, blocks=blocks, heads=heads, q_rows=256, k_rows=rows),
        out_shape=[jax.ShapeDtypeStruct((rows, 3 * width), BF16)] * blocks,
        scratch_shapes=[
            pltpu.VMEM((8, length), F32),
            pltpu.VMEM((8, length), F32),
            pltpu.VMEM((width, length), F32),
            pltpu.VMEM((width, length), BF16),
        ],
        compiler_params=pltpu.CompilerParams(vmem_limit_bytes=VMEM_LIMIT),
        cost_estimate=pl.CostEstimate(
            flops=40 * length * length * width, bytes_accessed=20 * length * width,
            transcendentals=heads * length * length,
        ),
        name="attend_back",
    )(*qkv, *grads, full, lse)


def norm_fwd(resid, gain, shift):
    centre = resid - jnp.mean(resid, axis=-1, keepdims=True)
    spread = jnp.mean(centre * centre, axis=-1, keepdims=True)
    rstd = lax.rsqrt(spread + EPS)
    unit = centre * rstd
    return (unit * gain + shift, unit, rstd)


def norm_back(grad, unit, rstd, gain):
    scaled = grad * gain
    inner = (
        scaled
        - jnp.mean(scaled, axis=-1, keepdims=True)
        - unit * jnp.mean(scaled * unit, axis=-1, keepdims=True)
    )
    return (rstd * inner, jnp.sum(grad * unit, axis=0), jnp.sum(grad, axis=0))


def gelu_both(pre):
    slope = math.sqrt(2.0 / math.pi)
    square = pre * pre
    th = jnp.tanh(slope * (pre + 0.044715 * pre * square))
    half = 0.5 * (1.0 + th)
    grad = half + 0.5 * pre * (1.0 - th * th) * (slope * (1.0 + 3 * 0.044715 * square))
    return pre * half, grad


def on_device(x_in, w_qkv, w_out, w_in, w_back, vectors, bias_in, cot, *, n_ctx, n_f):
    ctx, fs = lax.axis_index("ctx"), lax.axis_index("fsdp")
    core, zed = ctx % 2, ctx // 2
    n_z = n_ctx // 2
    x_own = x_in[0]
    grad_out = cot[0]
    rows, width = x_own.shape
    hidden = w_back.shape[0]
    half_heads = HEADS // 2
    heads = half_heads // n_z
    wide = heads * HEAD

    def swap(v):
        return lax.ppermute(v, "ctx", [(i, i ^ 1) for i in range(n_ctx)])

    def over_z(v, m):
        return lax.ppermute(v, "ctx", [(i, i ^ (2 * m)) for i in range(n_ctx)])

    def over_f(v, m):
        return lax.ppermute(v, "fsdp", [(i, i ^ m) for i in range(n_f)])

    bits = [1 << b for b in range(n_f.bit_length() - 1)]

    def pair(v):
        return jnp.concatenate([v, swap(v)], axis=0)

    def pair_sum(partial_sum):
        return partial_sum[:rows] + swap(partial_sum[rows:])

    def place(pieces, index, axis):
        count = len(pieces)
        for bit in range(count.bit_length() - 1):
            flag = (index >> bit) & 1
            pieces = [jnp.where(flag, pieces[m ^ (1 << bit)], pieces[m]) for m in range(count)]
        return jnp.concatenate(pieces, axis=axis)

    def gather_cols(shard):
        half = shard.shape[0] // 2
        parts = []
        for piece, order in ((shard[:half], bits), (shard[half:], bits[1:] + bits[:1])):
            held = {0: piece}
            for bit in order:
                for m in list(held):
                    held[m ^ bit] = over_f(held[m], bit)
            parts.append(place([held[m] for m in range(n_f)], fs, 1))
        return jnp.concatenate(parts, axis=0)

    def after(value, *others):
        return lax.optimization_barrier((value,) + others)[0]

    half_in = width // 2
    mine = lax.dynamic_slice_in_dim(w_qkv, core * half_in, half_in, 0)
    all_cols = gather_cols(mine).reshape(half_in, 3, 2, width // 2)
    keep = lax.dynamic_index_in_dim(all_cols, core, 2, False)
    give = lax.dynamic_index_in_dim(all_cols, 1 - core, 2, False)
    got = swap(give)
    w_attn = place([keep, got], core, 0)
    w_attn = w_attn.reshape(width, 3, n_z, wide).transpose(0, 2, 1, 3).reshape(width, -1)

    ff_part = w_in.shape[1] // 2
    token = w_attn[0, 0]
    wo_mine = lax.dynamic_slice_in_dim(w_out, core * (width // 2), width // 2, 0)
    wo_half = gather_cols(after(wo_mine, got))
    wi_mine = lax.dynamic_slice_in_dim(w_in, core * ff_part, ff_part, 1)
    wi_half = gather_cols(after(wi_mine, wo_half))
    wb_mine = lax.dynamic_index_in_dim(
        w_back.reshape(n_f, 2, ff_part, w_back.shape[1]), core, 1, False
    ).reshape(n_f * ff_part, -1)
    wb_half = gather_cols(after(wb_mine, wi_half))

    x_two = pair(x_own)
    span = 3 * wide
    bias_q = vectors[0].reshape(2, n_z, 1, wide)
    bias_v = vectors[1].reshape(2, n_z, 1, wide)
    bias_qkv = jnp.concatenate([bias_q, jnp.zeros_like(bias_q), bias_v], axis=2)
    bias_qkv = lax.dynamic_index_in_dim(bias_qkv.reshape(2, n_z * span), core, 0, False)
    qkv = []
    for m in range(n_z):
        start = (zed ^ m) * span
        w_part = lax.dynamic_slice_in_dim(w_attn, start, span, 1)
        b_part = lax.dynamic_slice_in_dim(bias_qkv, start, span, 0)
        block = (dot(x_two, w_part, NN) + b_part).astype(BF16)
        qkv.append(block if m == 0 else over_z(block, m))
    att, att_full, lse = attend(qkv, heads)
    att = [att[m] if m == 0 else over_z(att[m], m) for m in range(n_z)]
    att_half = place(att, zed, 1)

    resid_one = (
        x_own.astype(F32) + pair_sum(dot(att_half, wo_half, NN)) + vectors[2]
    )
    normed, unit_one, rstd_one = norm_fwd(resid_one, vectors[3], vectors[4])
    h_two = pair(normed.astype(BF16))
    bias_half = lax.dynamic_index_in_dim(
        bias_in.reshape(n_f, 2, ff_part), core, 1, False
    ).reshape(-1)
    pre = dot(h_two, wi_half, NN) + bias_half
    act, slope = gelu_both(pre)
    act = act.astype(BF16)
    resid_two = normed + pair_sum(dot(act, wb_half, NN)) + vectors[5]
    result, unit_two, rstd_two = norm_fwd(resid_two, vectors[6], vectors[7])
    layer_out = result.astype(BF16)[None]
    grad_two, gain_two, shift_two = norm_back(grad_out, unit_two, rstd_two, vectors[6])
    g_two = pair(grad_two.astype(BF16))
    grad_pre = dot(g_two, wb_half, NT) * slope
    grad_pre_low = grad_pre.astype(BF16)
    grad_normed = grad_two + pair_sum(dot(grad_pre_low, wi_half, NT))
    grad_one, gain_one, shift_one = norm_back(grad_normed, unit_one, rstd_one, vectors[3])
    g_one = pair(grad_one.astype(BF16))
    grad_att = dot(g_one, wo_half, NT).astype(BF16)
    g_att = []
    for m in range(n_z):
        block = lax.dynamic_slice_in_dim(grad_att, (zed ^ m) * wide, wide, 1)
        g_att.append(block if m == 0 else over_z(block, m))

    def reduce_rows(partial_grad):
        cols = partial_grad.shape[1]
        low = width // (n_ctx * n_f)
        view = partial_grad.reshape((n_z, 2) + (2,) * len(bits) + (low, cols))
        done = []
        for side in range(2):
            now = view[:, side]
            order = bits if side == 0 else bits[1:] + bits[:1]
            left = list(reversed(bits))
            for bit in order:
                axis = 1 + left.index(bit)
                left.remove(bit)
                flag = (fs // bit) % 2
                stay = lax.dynamic_index_in_dim(now, flag, axis, False)
                go = lax.dynamic_index_in_dim(now, 1 - flag, axis, False)
                now = (stay.astype(F32) + over_f(go, bit).astype(F32)).astype(BF16)
            done.append(now)
        both = jnp.stack(done, axis=1)
        total = lax.dynamic_index_in_dim(both, zed, 0, False).astype(F32)
        for m in range(1, n_z):
            part = lax.dynamic_index_in_dim(both, zed ^ m, 0, False)
            total = total + over_z(part, m).astype(F32)
        stay = lax.dynamic_index_in_dim(total, core, 0, False)
        go = lax.dynamic_index_in_dim(total, 1 - core, 0, False)
        return stay, swap(go.astype(BF16)).astype(F32)

    def halves(stay, came, parts):
        low = stay.shape[0]
        first = jnp.where(core == 0, stay, came).reshape(low, parts, 1, -1)
        second = jnp.where(core == 0, came, stay).reshape(low, parts, 1, -1)
        return jnp.concatenate([first, second], axis=2).reshape(low, -1)

    ffn_grad = jnp.concatenate(
        [dot(h_two, grad_pre_low, TN).astype(BF16), dot(g_two, act, TN).astype(BF16)], axis=1
    )
    ffn_grad = after(ffn_grad, g_att[0])
    stay, came = reduce_rows(ffn_grad)
    n_half = hidden // 2
    in_weight_grad = halves(stay[:, :n_half], came[:, :n_half], n_f)
    back_weight_grad = halves(stay[:, n_half:], came[:, n_half:], n_f).T

    att_other = swap(att_half)
    att_other = jnp.concatenate([att_other[rows:], att_other[:rows]], axis=0)
    att_both = place([att_half, att_other], core, 1)
    out_cols = lax.dynamic_slice_in_dim(g_one, core * half_in, half_in, 1)
    out_grad = dot(att_both, out_cols, TN).astype(BF16)

    g_qkv = attend_back(qkv, g_att, att_full, lse, heads)
    g_qkv = [g_qkv[m] if m == 0 else over_z(g_qkv[m], m) for m in range(n_z)]
    g_qkv = place(g_qkv, zed, 1)
    grad_in = grad_one + pair_sum(dot(g_qkv, w_attn, NT))
    attn_grad = jnp.concatenate([dot(x_two, g_qkv, TN).astype(BF16), out_grad], axis=1)
    stay, came = reduce_rows(attn_grad)
    low = stay.shape[0]

    def heads_order(cols):
        return cols.reshape(low, n_z, 3, wide).transpose(0, 2, 1, 3).reshape(low, -1)

    cut = n_z * span
    qkv_weight_grad = halves(heads_order(stay[:, :cut]), heads_order(came[:, :cut]), 3)
    out_weight_grad = halves(stay[:, cut:], came[:, cut:], 1)

    def spread(half_row, parts):
        piece = half_row.reshape(parts, 1, -1)
        empty = jnp.zeros_like(piece)
        both = jnp.where(core == 0, jnp.concatenate([piece, empty], 1), jnp.concatenate([empty, piece], 1))
        return both.reshape(-1)

    sums = jnp.sum(g_qkv.astype(F32), axis=0).reshape(n_z, 3, wide)
    ratio = hidden // width
    early = jnp.stack(
        [
            jnp.sum(grad_one, axis=0),
            gain_one,
            shift_one,
            jnp.sum(grad_two, axis=0),
            gain_two,
            shift_two,
        ],
        axis=1,
    )
    bias_terms = spread(jnp.sum(grad_pre, axis=0), n_f).reshape(width, ratio)
    late = jnp.stack([spread(sums[:, 0], 1), spread(sums[:, 2], 1)], axis=1)
    table = jnp.concatenate([late, early, bias_terms], axis=1)
    table = jnp.pad(table, ((0, 0), (0, 128 - table.shape[1])))
    table = lax.psum_scatter(table, ("ctx", "fsdp"), scatter_dimension=0, tiled=True)
    vector_grad = table[:, :8].T
    in_bias_grad = table[:, 8 : 8 + ratio].reshape(-1)
    return (
        layer_out,
        grad_in[None],
        qkv_weight_grad,
        out_weight_grad,
        in_weight_grad,
        back_weight_grad,
        vector_grad,
        in_bias_grad,
    )


def solution(mesh):
    tokens = P("fsdp", "ctx", None)
    cols = P(None, "fsdp")
    shared = P(("ctx", "fsdp"), None)
    return jax.shard_map(
        partial(on_device, n_ctx=mesh.shape["ctx"], n_f=mesh.shape["fsdp"]),
        mesh=mesh,
        in_specs=(tokens, cols, cols, cols, cols, P(), P(), tokens),
        out_specs=(
            tokens,
            tokens,
            shared,
            shared,
            shared,
            P(None, ("ctx", "fsdp")),
            P(None, ("ctx", "fsdp")),
            P(("ctx", "fsdp")),
        ),
        check_vma=False,
    )
```

```python
from functools import partial
import math

import jax
import jax.numpy as jnp
from jax import lax
from jax.experimental import pallas as pl
from jax.experimental.pallas import tpu as pltpu
from jax.sharding import PartitionSpec as P

HEADS = 16
HEAD = 64
EPS = 1e-12
F32 = jnp.float32
BF16 = jnp.bfloat16
NN = (((1,), (0,)), ((), ()))
NT = (((1,), (1,)), ((), ()))
TN = (((0,), (0,)), ((), ()))
VMEM_LIMIT = 50 * 1024 * 1024
VMEM_MIDDLE = 56 * 1024 * 1024
MESH = pl.DeviceIdType.MESH


def dot(left, right, dims):
    return lax.dot_general(left, right, dims, preferred_element_type=F32)


def one_head(block, head, heads):
    if heads == 1:
        return block
    lane = lax.broadcasted_iota(jnp.int32, block.shape, 1)
    return jnp.where(lane // HEAD == head, block, jnp.zeros_like(block))


def merge_heads(parts):
    if len(parts) == 1:
        return parts[0]
    lane = lax.broadcasted_iota(jnp.int32, parts[0].shape, 1)
    result = parts[0]
    for head in range(1, len(parts)):
        result = jnp.where(lane // HEAD == head, parts[head], result)
    return result


def attend_kernel(*refs, blocks, heads, q_rows, k_rows):
    ins, rest = refs[:blocks], refs[blocks:]
    outs, (full_ref, lse_ref, key_s, value_s) = rest[:blocks], rest[blocks:]
    rows = ins[0].shape[0]
    width = heads * HEAD
    length = rows * blocks
    for b in range(blocks):
        here = slice(b * rows, (b + 1) * rows)
        key_s[here, :] = ins[b][:, width : 2 * width]
        value_s[here, :] = ins[b][:, 2 * width : 3 * width]
    for b in range(blocks):

        def step(i, carry, b=b):
            local = pl.ds(pl.multiple_of(i * q_rows, q_rows), q_rows)
            where = pl.ds(pl.multiple_of(b * rows + i * q_rows, q_rows), q_rows)
            query = ins[b][local, 0:width] * BF16(HEAD**-0.5)
            outputs, sums = [], []
            for head in range(heads):
                masked = one_head(query, head, heads)
                scores = [
                    dot(masked, key_s[j : j + k_rows, :], NT) for j in range(0, length, k_rows)
                ]
                top = None
                for part in scores:
                    part_top = jnp.max(part, axis=1, keepdims=True)
                    top = part_top if top is None else jnp.maximum(top, part_top)
                total = acc = None
                for j, part in enumerate(scores):
                    probs = jnp.exp(part - top)
                    part_total = jnp.sum(probs, axis=1, keepdims=True)
                    value = value_s[j * k_rows : (j + 1) * k_rows, :]
                    part_acc = dot(probs.astype(BF16), value, NN)
                    total = part_total if total is None else total + part_total
                    acc = part_acc if acc is None else acc + part_acc
                outputs.append(acc / total)
                sums.append(jnp.broadcast_to(top + jnp.log(total), (q_rows, width)))
            result = merge_heads(outputs)
            full_ref[where, :] = result
            outs[b][local, :] = result.astype(BF16)
            lse_ref[where, :] = merge_heads(sums)
            return carry

        lax.fori_loop(0, rows // q_rows, step, 0)


def attend(qkv, heads):
    blocks = len(qkv)
    rows = qkv[0].shape[0]
    width = heads * HEAD
    length = rows * blocks
    out = [jax.ShapeDtypeStruct((rows, width), BF16)] * blocks
    out += [jax.ShapeDtypeStruct((length, width), F32)] * 2
    results = pl.pallas_call(
        partial(attend_kernel, blocks=blocks, heads=heads, q_rows=256, k_rows=512),
        out_shape=out,
        scratch_shapes=[pltpu.VMEM((length, width), BF16)] * 2,
        compiler_params=pltpu.CompilerParams(vmem_limit_bytes=VMEM_LIMIT),
        cost_estimate=pl.CostEstimate(
            flops=16 * length * length * width, bytes_accessed=10 * length * width,
            transcendentals=heads * length * length,
        ),
        name="attend",
    )(*qkv)
    return results[:blocks], results[blocks], results[blocks + 1]


def attend_back_kernel(*refs, blocks, heads, q_rows, k_rows):
    ins, grads, rest = refs[:blocks], refs[blocks : 2 * blocks], refs[2 * blocks :]
    full_ref, lse_ref, rest = rest[0], rest[1], rest[2:]
    outs, (lse_t, delta_t, gq_t, key_t) = rest[:blocks], rest[blocks:]
    rows = ins[0].shape[0]
    width = heads * HEAD
    scale = HEAD**-0.5
    chunk = 256
    for b in range(blocks):
        for i in range(0, rows, chunk):
            local = slice(i, i + chunk)
            where = slice(b * rows + i, b * rows + i + chunk)
            logs = lse_ref[where, :].T
            terms = (grads[b][local, :].astype(F32) * full_ref[where, :]).T
            for head in range(heads):
                first = head * HEAD
                lse_t[head : head + 1, where] = logs[first : first + 1]
                delta_t[head : head + 1, where] = jnp.sum(
                    terms[first : first + HEAD], axis=0, keepdims=True
                )
        key_t[:, b * rows : (b + 1) * rows] = ins[b][:, width : 2 * width].T
    gq_t[...] = jnp.zeros_like(gq_t)
    for b in range(blocks):

        def step(j, carry, b=b):
            local = pl.ds(pl.multiple_of(j * k_rows, k_rows), k_rows)
            where = pl.ds(pl.multiple_of(b * rows + j * k_rows, k_rows), k_rows)
            key = ins[b][local, width : 2 * width]
            value = ins[b][local, 2 * width : 3 * width]
            key_grads, value_grads = [], []
            for head in range(heads):
                feats = slice(head * HEAD, (head + 1) * HEAD)
                key_h = one_head(key, head, heads) * BF16(scale)
                value_h = one_head(value, head, heads)
                key_grad = value_grad = None
                for other in range(blocks):
                    for i in range(0, rows, q_rows):
                        here = slice(i, i + q_rows)
                        there = slice(other * rows + i, other * rows + i + q_rows)
                        query = ins[other][here, 0:width]
                        grad = grads[other][here, :]
                        scores = dot(key_h, query, NT)
                        probs = jnp.exp(scores - lse_t[head : head + 1, there])
                        grad_probs = dot(value_h, grad, NT)
                        grad_scores = probs * (grad_probs - delta_t[head : head + 1, there])
                        grad_scores = grad_scores.astype(BF16)
                        term = dot(probs.astype(BF16), grad, NN)
                        value_grad = term if value_grad is None else value_grad + term
                        term = dot(grad_scores, query, NN)
                        key_grad = term if key_grad is None else key_grad + term
                        gq_t[feats, there] += dot(key_t[feats, where], grad_scores, NN)
                key_grads.append(key_grad)
                value_grads.append(value_grad)
            outs[b][local, width : 2 * width] = (merge_heads(key_grads) * scale).astype(BF16)
            outs[b][local, 2 * width : 3 * width] = merge_heads(value_grads).astype(BF16)
            return carry

        lax.fori_loop(0, rows // k_rows, step, 0)
    for b in range(blocks):
        for i in range(0, rows, chunk):
            there = slice(b * rows + i, b * rows + i + chunk)
            outs[b][i : i + chunk, 0:width] = (gq_t[:, there].T * scale).astype(BF16)


def attend_back(qkv, grads, full, lse, heads):
    blocks = len(qkv)
    rows = qkv[0].shape[0]
    width = heads * HEAD
    length = rows * blocks
    return pl.pallas_call(
        partial(attend_back_kernel, blocks=blocks, heads=heads, q_rows=256, k_rows=rows),
        out_shape=[jax.ShapeDtypeStruct((rows, 3 * width), BF16)] * blocks,
        scratch_shapes=[
            pltpu.VMEM((8, length), F32),
            pltpu.VMEM((8, length), F32),
            pltpu.VMEM((width, length), F32),
            pltpu.VMEM((width, length), BF16),
        ],
        compiler_params=pltpu.CompilerParams(vmem_limit_bytes=VMEM_LIMIT),
        cost_estimate=pl.CostEstimate(
            flops=40 * length * length * width, bytes_accessed=20 * length * width,
            transcendentals=heads * length * length,
        ),
        name="attend_back",
    )(*qkv, *grads, full, lse)


def gelu_both(pre):
    slope = math.sqrt(2.0 / math.pi)
    square = pre * pre
    th = jnp.tanh(slope * (pre + 0.044715 * pre * square))
    half = 0.5 * (1.0 + th)
    grad = half + 0.5 * pre * (1.0 - th * th) * (slope * (1.0 + 3 * 0.044715 * square))
    return pre * half, grad


def row_stats(value):
    return jnp.mean(value, axis=1, keepdims=True)


def mid_kernel(*refs, n_f, n_z, cfg):
    att_refs, refs = refs[:n_z], refs[n_z:]
    (x_ref, cot_ref, vec_ref, bias_ref), refs = refs[:4], refs[4:]
    wo_refs, refs = refs[: 2 * n_f], refs[2 * n_f :]
    wi_refs, refs = refs[: 2 * n_f], refs[2 * n_f :]
    wb_refs, refs = refs[: 2 * n_f], refs[2 * n_f :]
    (layer_ref, grad_one_ref, att_ref, h_ref, act_ref, g2_ref, gp_ref, g1_ref), refs = refs[:8], refs[8:]
    (sums_ref, bias_sum_ref), refs = refs[:2], refs[2:]
    ga_refs, refs = refs[:n_z], refs[n_z:]
    (wo_s, wi_s, wb_s, slope_s, normed_s, unit_s, acc_s, send_s, recv_s, rstd_s), refs = refs[:10], refs[10:]
    w_sem, send_sem, recv_sem = refs
    ctx, fs = lax.axis_index("ctx"), lax.axis_index("fsdp")
    core, zed = ctx % 2, ctx // 2
    partner = {"ctx": zed * 2 + (1 - core)}
    rows, width = x_ref.shape
    own, other = slice(0, rows), slice(rows, 2 * rows)
    wide = att_refs[0].shape[1]
    half_in = n_z * wide
    ff_half = wi_s.shape[1]
    step = cfg["step"]
    chunk = cfg["rows"]

    copies = []
    for pieces, target in ((wo_refs, wo_s), (wi_refs, wi_s), (wb_refs, wb_s)):
        group = []
        for side in range(2):
            for m in range(n_f):
                piece = pieces[side * n_f + m]
                p_rows, p_cols = piece.shape
                where = pl.ds(pl.multiple_of((fs ^ m) * p_cols, p_cols), p_cols)
                copy = pltpu.make_async_copy(
                    piece, target.at[pl.ds(side * p_rows, p_rows), where], w_sem.at[len(copies), side * n_f + m]
                )
                copy.start()
                group.append(copy)
        copies.append(group)
    barrier = pltpu.get_barrier_semaphore()
    pl.semaphore_signal(barrier, inc=1, device_id=partner, device_id_type=MESH)
    pl.semaphore_wait(barrier, 1)

    def exchange(n, src, dst):
        return pltpu.make_async_remote_copy(
            src_ref=src, dst_ref=dst, send_sem=send_sem.at[n], recv_sem=recv_sem.at[n],
            device_id=partner, device_id_type=MESH,
        )

    def over_cols(total, body):
        def run(i, carry):
            body(pl.ds(pl.multiple_of(i * step, step), step))
            return carry

        lax.fori_loop(0, total // step, run, 0)

    def over_rows(body):
        def run(i, carry):
            return body(pl.ds(pl.multiple_of(i * chunk, chunk), chunk), carry)

        zero = jnp.zeros((1, width), F32)
        return lax.fori_loop(0, rows // chunk, run, (zero, zero, zero))

    if wide % 128 == 0:
        for m in range(n_z):
            att_ref[:, pl.ds(pl.multiple_of((zed ^ m) * wide, wide), wide)] = att_refs[m][...]
    else:
        for m in range(0, n_z, 2):
            one, two = att_refs[m][...].astype(F32), att_refs[m + 1][...].astype(F32)
            odd = zed % 2 == 1
            block = jnp.concatenate([jnp.where(odd, two, one), jnp.where(odd, one, two)], axis=1)
            at = pl.ds(pl.multiple_of((zed // 2 ^ (m // 2)) * 2 * wide, 2 * wide), 2 * wide)
            att_ref[:, at] = block.astype(BF16)

    def wait_all(group):
        for copy in group:
            copy.wait()

    wait_all(copies[0])

    def out_other(cols):
        send_s[:, cols] = dot(att_ref[other, :], wo_s[:, cols], NN)

    over_cols(width, out_other)
    move = exchange(0, send_s, recv_s)
    move.start()

    def out_own(cols):
        part = dot(att_ref[own, :], wo_s[:, cols], NN)
        acc_s[:, cols] = part + x_ref[:, cols].astype(F32) + vec_ref[2:3, cols]

    over_cols(width, out_own)
    move.wait()

    def norm_one(r, carry):
        resid = acc_s[r, :] + recv_s[r, :]
        centre = resid - row_stats(resid)
        rstd = lax.rsqrt(row_stats(centre * centre) + EPS)
        unit = centre * rstd
        normed = unit * vec_ref[3:4, :] + vec_ref[4:5, :]
        unit_s[r, :] = unit
        rstd_s[r, :] = jnp.broadcast_to(rstd, (chunk, 128))
        normed_s[r, :] = normed
        h_ref[r, :] = normed.astype(BF16)
        return carry

    over_rows(norm_one)
    move = exchange(1, h_ref.at[own], h_ref.at[other])
    move.start()

    wait_all(copies[1])

    def up(where):
        def body(cols):
            pre = dot(h_ref[where, :], wi_s[:, cols], NN) + bias_ref[0:1, cols]
            act, slope = gelu_both(pre)
            act_ref[where, cols] = act.astype(BF16)
            slope_s[where, cols] = slope

        over_cols(ff_half, body)

    up(own)
    move.wait()
    up(other)
    wait_all(copies[2])

    def down_other(cols):
        send_s[:, cols] = dot(act_ref[other, :], wb_s[:, cols], NN)

    over_cols(width, down_other)
    move = exchange(2, send_s, recv_s)
    move.start()

    def down_own(cols):
        part = dot(act_ref[own, :], wb_s[:, cols], NN)
        acc_s[:, cols] = part + normed_s[:, cols] + vec_ref[5:6, cols]

    over_cols(width, down_own)
    move.wait()

    def norm_two(r, carry):
        resid = acc_s[r, :] + recv_s[r, :]
        centre = resid - row_stats(resid)
        rstd = lax.rsqrt(row_stats(centre * centre) + EPS)
        unit = centre * rstd
        gain = vec_ref[6:7, :]
        layer_ref[r, :] = (unit * gain + vec_ref[7:8, :]).astype(BF16)
        grad = cot_ref[r, :]
        scaled = grad * gain
        back = rstd * (scaled - row_stats(scaled) - unit * row_stats(scaled * unit))
        acc_s[r, :] = back
        g2_ref[r, :] = back.astype(BF16)
        sums = (back, grad * unit, grad)
        return tuple(c + jnp.sum(s, axis=0, keepdims=True) for c, s in zip(carry, sums))

    shift_two = over_rows(norm_two)
    move = exchange(3, g2_ref.at[own], g2_ref.at[other])
    move.start()
    for i, total in enumerate(shift_two):
        sums_ref[3 + i : 4 + i, :] = total

    def back_act(where, first):
        def body(cols):
            grad = dot(g2_ref[where, :], wb_s[cols, :], NT) * slope_s[where, cols]
            gp_ref[where, cols] = grad.astype(BF16)
            total = jnp.sum(grad, axis=0, keepdims=True)
            bias_sum_ref[0:1, cols] = total if first else bias_sum_ref[0:1, cols] + total

        over_cols(ff_half, body)

    back_act(own, True)
    move.wait()
    back_act(other, False)

    def back_other(cols):
        send_s[:, cols] = dot(gp_ref[other, :], wi_s[cols, :], NT)

    over_cols(width, back_other)
    move = exchange(4, send_s, recv_s)
    move.start()

    def back_own(cols):
        acc_s[:, cols] += dot(gp_ref[own, :], wi_s[cols, :], NT)

    over_cols(width, back_own)
    move.wait()

    def back_one(r, carry):
        grad = acc_s[r, :] + recv_s[r, :]
        unit = unit_s[r, :]
        rstd = rstd_s[r, 0:1]
        scaled = grad * vec_ref[3:4, :]
        back = rstd * (scaled - row_stats(scaled) - unit * row_stats(scaled * unit))
        grad_one_ref[r, :] = back
        g1_ref[r, :] = back.astype(BF16)
        sums = (back, grad * unit, grad)
        return tuple(c + jnp.sum(s, axis=0, keepdims=True) for c, s in zip(carry, sums))

    shift_one = over_rows(back_one)
    move = exchange(5, g1_ref.at[own], g1_ref.at[other])
    move.start()
    for i, total in enumerate(shift_one):
        sums_ref[i : 1 + i, :] = total
    sums_ref[6:8, :] = jnp.zeros((2, width), F32)

    for where in (own, other):
        if where is other:
            move.wait()
        for m in range(n_z):
            at = pl.ds(pl.multiple_of((zed ^ m) * wide, wide), wide)
            ga_refs[m][where, :] = dot(g1_ref[where, :], wo_s[at, :], NT).astype(BF16)


def middle(att, x_own, cot, vectors, bias_half, wo, wi, wb, n_f, n_z):
    rows, width = x_own.shape
    wide = att[0].shape[1]
    ff_half = bias_half.shape[0]
    half_in = n_z * wide
    sds = jax.ShapeDtypeStruct
    out_shape = [
        sds((rows, width), BF16),
        sds((rows, width), F32),
        sds((2 * rows, half_in), BF16),
        sds((2 * rows, width), BF16),
        sds((2 * rows, ff_half), BF16),
        sds((2 * rows, width), BF16),
        sds((2 * rows, ff_half), BF16),
        sds((2 * rows, width), BF16),
        sds((8, width), F32),
        sds((1, ff_half), F32),
    ] + [sds((2 * rows, wide), BF16)] * n_z
    in_vmem, anywhere = pl.BlockSpec(memory_space=pltpu.VMEM), pl.BlockSpec(memory_space=pl.ANY)
    cfg = {"step": 512, "rows": 64}
    results = pl.pallas_call(
        partial(mid_kernel, n_f=n_f, n_z=n_z, cfg=cfg),
        out_shape=out_shape,
        in_specs=[in_vmem] * (n_z + 4) + [anywhere] * (6 * n_f),
        out_specs=[in_vmem] * len(out_shape),
        scratch_shapes=[
            pltpu.VMEM((half_in, width), BF16),
            pltpu.VMEM((width, ff_half), BF16),
            pltpu.VMEM((ff_half, width), BF16),
            pltpu.VMEM((2 * rows, ff_half), F32),
            pltpu.VMEM((rows, width), F32),
            pltpu.VMEM((rows, width), F32),
            pltpu.VMEM((rows, width), F32),
            pltpu.VMEM((rows, width), F32),
            pltpu.VMEM((rows, width), F32),
            pltpu.VMEM((rows, 128), F32),
            pltpu.SemaphoreType.DMA((3, 2 * n_f)),
            pltpu.SemaphoreType.DMA((6,)),
            pltpu.SemaphoreType.DMA((6,)),
        ],
        compiler_params=pltpu.CompilerParams(
            vmem_limit_bytes=VMEM_MIDDLE, collective_id=0, has_side_effects=True
        ),
        cost_estimate=pl.CostEstimate(
            flops=2 * 2 * rows * width * (2 * half_in + 4 * ff_half),
            bytes_accessed=40 << 20, transcendentals=2 * rows * ff_half,
        ),
        name="middle",
    )(*att, x_own, cot, vectors, bias_half[None], *wo, *wi, *wb)
    return results[:10], results[10:]


def on_device(x_in, w_qkv, w_out, w_in, w_back, vectors, bias_in, cot, *, n_ctx, n_f):
    ctx, fs = lax.axis_index("ctx"), lax.axis_index("fsdp")
    core, zed = ctx % 2, ctx // 2
    n_z = n_ctx // 2
    x_own = x_in[0]
    grad_out = cot[0]
    rows, width = x_own.shape
    hidden = w_back.shape[0]
    half_heads = HEADS // 2
    heads = half_heads // n_z
    wide = heads * HEAD

    def swap(v):
        return lax.ppermute(v, "ctx", [(i, i ^ 1) for i in range(n_ctx)])

    def over_z(v, m):
        return lax.ppermute(v, "ctx", [(i, i ^ (2 * m)) for i in range(n_ctx)])

    def over_f(v, m):
        return lax.ppermute(v, "fsdp", [(i, i ^ m) for i in range(n_f)])

    bits = [1 << b for b in range(n_f.bit_length() - 1)]

    def pair(v):
        return jnp.concatenate([v, swap(v)], axis=0)

    def pair_sum(partial_sum):
        return partial_sum[:rows] + swap(partial_sum[rows:])

    def place(pieces, index, axis):
        count = len(pieces)
        for bit in range(count.bit_length() - 1):
            flag = (index >> bit) & 1
            pieces = [jnp.where(flag, pieces[m ^ (1 << bit)], pieces[m]) for m in range(count)]
        return jnp.concatenate(pieces, axis=axis)

    def gather_cols(shard):
        half = shard.shape[0] // 2
        parts = []
        for piece, order in ((shard[:half], bits), (shard[half:], bits[1:] + bits[:1])):
            held = {0: piece}
            for bit in order:
                for m in list(held):
                    held[m ^ bit] = over_f(held[m], bit)
            parts += [held[m] for m in range(n_f)]
        return parts

    def after(value, *others):
        return lax.optimization_barrier((value,) + others)[0]

    half_in = width // 2
    mine = lax.dynamic_slice_in_dim(w_qkv, core * half_in, half_in, 0)
    pieces = gather_cols(mine)
    all_cols = jnp.concatenate(
        [place(pieces[:n_f], fs, 1), place(pieces[n_f:], fs, 1)], axis=0
    ).reshape(half_in, 3, 2, width // 2)
    keep = lax.dynamic_index_in_dim(all_cols, core, 2, False)
    give = lax.dynamic_index_in_dim(all_cols, 1 - core, 2, False)
    got = swap(give)
    w_attn = place([keep, got], core, 0)
    w_attn = w_attn.reshape(width, 3, n_z, wide).transpose(0, 2, 1, 3).reshape(width, -1)

    ff_part = w_in.shape[1] // 2
    token = w_attn[0, 0]
    wo_mine = lax.dynamic_slice_in_dim(w_out, core * (width // 2), width // 2, 0)
    wo_half = gather_cols(after(wo_mine, got))
    wi_mine = lax.dynamic_slice_in_dim(w_in, core * ff_part, ff_part, 1)
    wi_half = gather_cols(after(wi_mine, wo_half[-1]))
    wb_mine = lax.dynamic_index_in_dim(
        w_back.reshape(n_f, 2, ff_part, w_back.shape[1]), core, 1, False
    ).reshape(n_f * ff_part, -1)
    wb_half = gather_cols(after(wb_mine, wi_half[-1]))

    x_two = pair(x_own)
    span = 3 * wide
    bias_q = vectors[0].reshape(2, n_z, 1, wide)
    bias_v = vectors[1].reshape(2, n_z, 1, wide)
    bias_qkv = jnp.concatenate([bias_q, jnp.zeros_like(bias_q), bias_v], axis=2)
    bias_qkv = lax.dynamic_index_in_dim(bias_qkv.reshape(2, n_z * span), core, 0, False)
    qkv = []
    for m in range(n_z):
        start = (zed ^ m) * span
        w_part = lax.dynamic_slice_in_dim(w_attn, start, span, 1)
        b_part = lax.dynamic_slice_in_dim(bias_qkv, start, span, 0)
        block = (dot(x_two, w_part, NN) + b_part).astype(BF16)
        qkv.append(block if m == 0 else over_z(block, m))
    att, att_full, lse = attend(qkv, heads)
    att = [att[m] if m == 0 else over_z(att[m], m) for m in range(n_z)]
    bias_half = lax.dynamic_index_in_dim(
        bias_in.reshape(n_f, 2, ff_part), core, 1, False
    ).reshape(-1)
    outs, grad_att = middle(
        att, x_own, grad_out, vectors, bias_half, wo_half, wi_half, wb_half, n_f, n_z
    )
    layer_out, grad_one, att_half, h_two, act, g_two, grad_pre_low, g_one, sums_mid, bias_sum = outs
    layer_out = layer_out[None]
    g_att = [grad_att[m] if m == 0 else over_z(grad_att[m], m) for m in range(n_z)]

    def reduce_rows(partial_grad):
        cols = partial_grad.shape[1]
        low = width // (n_ctx * n_f)
        view = partial_grad.reshape((n_z, 2) + (2,) * len(bits) + (low, cols))
        done = []
        for side in range(2):
            now = view[:, side]
            order = bits if side == 0 else bits[1:] + bits[:1]
            left = list(reversed(bits))
            for bit in order:
                axis = 1 + left.index(bit)
                left.remove(bit)
                flag = (fs // bit) % 2
                stay = lax.dynamic_index_in_dim(now, flag, axis, False)
                go = lax.dynamic_index_in_dim(now, 1 - flag, axis, False)
                now = (stay.astype(F32) + over_f(go, bit).astype(F32)).astype(BF16)
            done.append(now)
        both = jnp.stack(done, axis=1)
        total = lax.dynamic_index_in_dim(both, zed, 0, False).astype(F32)
        for m in range(1, n_z):
            part = lax.dynamic_index_in_dim(both, zed ^ m, 0, False)
            total = total + over_z(part, m).astype(F32)
        stay = lax.dynamic_index_in_dim(total, core, 0, False)
        go = lax.dynamic_index_in_dim(total, 1 - core, 0, False)
        return stay, swap(go.astype(BF16)).astype(F32)

    def halves(stay, came, parts):
        low = stay.shape[0]
        first = jnp.where(core == 0, stay, came).reshape(low, parts, 1, -1)
        second = jnp.where(core == 0, came, stay).reshape(low, parts, 1, -1)
        return jnp.concatenate([first, second], axis=2).reshape(low, -1)

    ffn_grad = jnp.concatenate(
        [dot(h_two, grad_pre_low, TN).astype(BF16), dot(g_two, act, TN).astype(BF16)], axis=1
    )
    ffn_grad = after(ffn_grad, g_att[0])
    stay, came = reduce_rows(ffn_grad)
    n_half = hidden // 2
    in_weight_grad = halves(stay[:, :n_half], came[:, :n_half], n_f)
    back_weight_grad = halves(stay[:, n_half:], came[:, n_half:], n_f).T

    att_other = swap(att_half)
    att_other = jnp.concatenate([att_other[rows:], att_other[:rows]], axis=0)
    att_both = place([att_half, att_other], core, 1)
    out_cols = lax.dynamic_slice_in_dim(g_one, core * half_in, half_in, 1)
    out_grad = dot(att_both, out_cols, TN).astype(BF16)

    g_qkv = attend_back(qkv, g_att, att_full, lse, heads)
    g_qkv = [g_qkv[m] if m == 0 else over_z(g_qkv[m], m) for m in range(n_z)]
    g_qkv = place(g_qkv, zed, 1)
    grad_in = grad_one + pair_sum(dot(g_qkv, w_attn, NT))
    attn_grad = jnp.concatenate([dot(x_two, g_qkv, TN).astype(BF16), out_grad], axis=1)
    stay, came = reduce_rows(attn_grad)
    low = stay.shape[0]

    def heads_order(cols):
        return cols.reshape(low, n_z, 3, wide).transpose(0, 2, 1, 3).reshape(low, -1)

    cut = n_z * span
    qkv_weight_grad = halves(heads_order(stay[:, :cut]), heads_order(came[:, :cut]), 3)
    out_weight_grad = halves(stay[:, cut:], came[:, cut:], 1)

    def spread(half_row, parts):
        piece = half_row.reshape(parts, 1, -1)
        empty = jnp.zeros_like(piece)
        both = jnp.where(core == 0, jnp.concatenate([piece, empty], 1), jnp.concatenate([empty, piece], 1))
        return both.reshape(-1)

    sums = jnp.sum(g_qkv.astype(F32), axis=0).reshape(n_z, 3, wide)
    ratio = hidden // width
    early = sums_mid[:6].T
    bias_terms = spread(bias_sum[0], n_f).reshape(width, ratio)
    late = jnp.stack([spread(sums[:, 0], 1), spread(sums[:, 2], 1)], axis=1)
    table = jnp.concatenate([late, early, bias_terms], axis=1)
    kinds = table.shape[1]
    low = width // (n_ctx * n_f)
    now = table.reshape((n_z, 2) + (2,) * len(bits) + (low, kinds))
    now = jnp.swapaxes(now, -1, -2).reshape((n_z, 2) + (2,) * len(bits) + (kinds * low,))
    left = list(reversed(bits))
    for bit in bits:
        axis = 2 + left.index(bit)
        left.remove(bit)
        flag = (fs // bit) % 2
        stay = lax.dynamic_index_in_dim(now, flag, axis, False)
        now = stay + over_f(lax.dynamic_index_in_dim(now, 1 - flag, axis, False), bit)
    total = lax.dynamic_index_in_dim(now, zed, 0, False)
    for m in range(1, n_z):
        total = total + over_z(lax.dynamic_index_in_dim(now, zed ^ m, 0, False), m)
    stay = lax.dynamic_index_in_dim(total, core, 0, False)
    table = stay + swap(lax.dynamic_index_in_dim(total, 1 - core, 0, False))
    table = table.reshape(kinds, low)
    vector_grad = table[:8]
    in_bias_grad = table[8:].T.reshape(-1)
    return (
        layer_out,
        grad_in[None],
        qkv_weight_grad,
        out_weight_grad,
        in_weight_grad,
        back_weight_grad,
        vector_grad,
        in_bias_grad,
    )


def solution(mesh):
    tokens = P("fsdp", "ctx", None)
    cols = P(None, "fsdp")
    shared = P(("ctx", "fsdp"), None)
    return jax.shard_map(
        partial(on_device, n_ctx=mesh.shape["ctx"], n_f=mesh.shape["fsdp"]),
        mesh=mesh,
        in_specs=(tokens, cols, cols, cols, cols, P(), P(), tokens),
        out_specs=(
            tokens,
            tokens,
            shared,
            shared,
            shared,
            P(None, ("ctx", "fsdp")),
            P(None, ("ctx", "fsdp")),
            P(("ctx", "fsdp")),
        ),
        check_vma=False,
    )
```

```python
from functools import partial
import math

import jax
import jax.numpy as jnp
from jax import lax
from jax.experimental import pallas as pl
from jax.experimental.pallas import tpu as pltpu
from jax.sharding import PartitionSpec as P

HEADS = 16
HEAD = 64
EPS = 1e-12
F32 = jnp.float32
BF16 = jnp.bfloat16
NN = (((1,), (0,)), ((), ()))
NT = (((1,), (1,)), ((), ()))
TN = (((0,), (0,)), ((), ()))
VMEM_LIMIT = 50 * 1024 * 1024
VMEM_MIDDLE = 56 * 1024 * 1024
MESH = pl.DeviceIdType.MESH


def dot(left, right, dims):
    return lax.dot_general(left, right, dims, preferred_element_type=F32)


def front_kernel(x_ref, wq_ref, wo_ref, wi_ref, bias_ref, qkv_ref, xf_out, wl_out, wo_out, wi_out, *scratch, n_z, n_f, heads):
    xf, wfull, wloc = scratch[:3]
    own_sem, x_send, x_recv, xs_send, xs_recv, w_send, w_recv, ws_send, ws_recv, o_send, o_recv, i_send, i_recv, out_sem = scratch[3:]
    ctx, fs = lax.axis_index("ctx"), lax.axis_index("fsdp")
    core, zed = ctx % 2, ctx // 2
    bits = [1 << b for b in range(n_f.bit_length() - 1)]
    orders = (bits, bits[1:] + bits[:1])
    rows, width = x_ref.shape
    half = width // 2
    quarter = half // 2
    wide = heads * HEAD
    partner = {"ctx": zed * 2 + (1 - core)}

    barrier = pltpu.get_barrier_semaphore()

    def greet(device):
        pl.semaphore_signal(barrier, inc=1, device_id=device, device_id_type=MESH)

    greet(partner)
    for bit in bits:
        greet({"fsdp": fs ^ bit})

    @pl.when(zed > 0)
    def _():
        greet({"ctx": ctx - 2})

    @pl.when(zed < n_z - 1)
    def _():
        greet({"ctx": ctx + 2})

    edges = (zed == 0).astype(jnp.int32) + (zed == n_z - 1).astype(jnp.int32)
    pl.semaphore_wait(barrier, 3 + len(bits) - edges)

    def remote(src, dst, send, recv, device):
        return pltpu.make_async_remote_copy(
            src_ref=src, dst_ref=dst, send_sem=send, recv_sem=recv, device_id=device, device_id_type=MESH
        )

    def x_move(away, step, first):
        block = zed - step * away
        src = x_ref if first else xf.at[block ^ zed, 0]
        index = (step + 1) // 2
        return remote(
            src, xf.at[block ^ (zed + step), 0], x_send.at[index, away], x_recv.at[block ^ (zed + step)],
            {"ctx": ctx + 2 * step},
        )

    def x_swap(m, first=False):
        src = x_ref if first else xf.at[m, 0]
        return remote(src, xf.at[m, 1], xs_send.at[m], xs_recv.at[m], partner)

    def has(step):
        return zed < n_z - 1 if step == 1 else zed > 0

    def came(away, step):
        return zed - away >= 0 if step == 1 else zed + away <= n_z - 1

    for step in (1, -1):

        @pl.when(has(step))
        def _(step=step):
            x_move(0, step, True).start()

    x_swap(0, True).start()
    own_x = pltpu.make_async_copy(x_ref, xf.at[0, 0], own_sem.at[0])
    own_x.start()

    def x_step(away):
        for step in (1, -1):

            @pl.when(came(away, step))
            def _(step=step):
                block = zed - step * away
                remote(
                    xf.at[block ^ zed, 0], xf.at[block ^ zed, 0], x_send.at[0, 0], x_recv.at[block ^ zed], partner
                ).wait_recv()

                @pl.when(has(step))
                def _():
                    x_move(away, step, False).start()

                x_swap(block ^ zed).start()

    def wq_place(side, origin, which):
        cols = wq_ref.shape[1]
        return wfull.at[
            pl.ds(pl.multiple_of(which * half + side * quarter, quarter), quarter),
            pl.ds(pl.multiple_of(origin * cols, 128), cols),
        ]

    def wq_own(side):
        return wq_ref.at[pl.ds(pl.multiple_of(core * half + side * quarter, quarter), quarter), :]

    def wo_place(side, origin):
        cols = wo_ref.shape[1]
        return wo_out.at[pl.ds(side * quarter, quarter), pl.ds(pl.multiple_of(origin * cols, 128), cols)]

    def wo_own(side):
        return wo_ref.at[pl.ds(pl.multiple_of(core * half + side * quarter, quarter), quarter), :]

    def wq_hop(side, m, bit):
        src = wq_own(side) if m == 0 else wq_place(side, fs ^ m, core)
        return remote(src, wq_place(side, fs ^ m, core), w_send.at[side, m ^ bit], w_recv.at[side, m ^ bit], {"fsdp": fs ^ bit})

    def wo_hop(side, m, bit):
        src = wo_own(side) if m == 0 else wo_place(side, fs ^ m)
        return remote(src, wo_place(side, fs ^ m), o_send.at[side, m ^ bit], o_recv.at[side, m ^ bit], {"fsdp": fs ^ bit})

    def wq_swap(side, m):
        src = wq_own(side) if m == 0 else wq_place(side, fs ^ m, core)
        return remote(src, wq_place(side, fs ^ m, core), ws_send.at[side, m], ws_recv.at[side, m], partner)

    own_w = []
    for side in range(2):
        wq_hop(side, 0, orders[side][0]).start()
        wq_swap(side, 0).start()
        own_w.append(pltpu.make_async_copy(wq_own(side), wq_place(side, fs, core), own_sem.at[1 + side]))
        own_w.append(pltpu.make_async_copy(wo_own(side), wo_place(side, fs), own_sem.at[3 + side]))
    for copy in own_w:
        copy.start()

    part = wi_ref.shape[1] // 2

    def wi_hop(side):
        src = wi_ref.at[pl.ds(side * half, half), pl.ds(pl.multiple_of(core * part, 128), part)]
        return remote(src, wi_out.at[side], i_send.at[side], i_recv.at[side], {"fsdp": fs ^ orders[side][0]})

    def doubling(hop, level, after=None):
        for side in range(2):
            known = [0]
            for bit in orders[side][:level]:
                known = known + [m ^ bit for m in known]
            bit = orders[side][level]
            for m in known:
                hop(side, m, bit).wait_recv()
                if after is not None:
                    after(side, m ^ bit).start()
            if level + 1 < len(bits):
                for m in known + [m ^ bit for m in known]:
                    hop(side, m, orders[side][level + 1]).start()

    doubling(wq_hop, 0, wq_swap)
    for side in range(2):
        wo_hop(side, 0, orders[side][0]).start()
    x_step(1)
    for level in range(1, len(bits)):
        doubling(wq_hop, level, wq_swap)
    for side in range(2):
        wi_hop(side).start()
    doubling(wo_hop, 0)
    for away in range(2, n_z - 1):
        x_step(away)
    for copy in own_w:
        copy.wait()
    for side in range(2):
        for m in range(n_f):
            wq_swap_in = remote(
                wq_place(side, fs ^ m, 1 - core), wq_place(side, fs ^ m, 1 - core),
                ws_send.at[side, m], ws_recv.at[side, m], partner,
            )
            wq_swap_in.wait_recv()
    outs = []
    for j in range(3):
        cols = pl.ds(pl.multiple_of(j * width + core * half, 128), half)
        outs.append(pltpu.make_async_copy(wfull.at[:, cols], wl_out.at[:, pl.ds(j * half, half)], out_sem.at[j]))
    for copy in outs:
        copy.start()
    for j in range(3):
        base = j * width + core * half + zed * wide
        if wide % 128 == 0:
            piece = wfull[:, pl.ds(pl.multiple_of(base, 128), wide)]
        else:
            block = wfull[:, pl.ds(pl.multiple_of(base // 128 * 128, 128), 128)].astype(F32)
            piece = jnp.where(zed % 2 == 1, block[:, wide:], block[:, :wide]).astype(BF16)
        wloc[:, j * wide : (j + 1) * wide] = piece

    def x_ready(m, side):
        remote(xf.at[m, side], xf.at[m, side], xs_send.at[m], xs_recv.at[m], partner).wait_recv()

    def project(m):
        def run(side, carry):
            result = dot(xf[m, side], wloc[...], NN) + bias_ref[...]
            where = pl.ds(pl.multiple_of(side * rows, rows), rows)
            qkv_ref[m, where, :] = result.astype(BF16)
            return carry

        lax.fori_loop(0, 2, run, 0)

    own_x.wait()
    x_ready(0, 1)
    project(0)

    def finish(away):
        def run(i, carry):
            block = zed - (1 - 2 * i) * away

            @pl.when((block >= 0) & (block <= n_z - 1))
            def _():
                x_ready(block ^ zed, 1)
                project(block ^ zed)

            return carry

        lax.fori_loop(0, 2, run, 0)

    for away in range(1, n_z - 1):
        finish(away)
    for level in range(1, len(bits)):
        doubling(wo_hop, level)
    if n_z > 2:
        x_step(n_z - 1)
    finish(n_z - 1)
    x_out = pltpu.make_async_copy(xf, xf_out, own_sem.at[5])
    x_out.start()

    for step in (1, -1):

        @pl.when(has(step))
        def _(step=step):
            x_move(0, step, True).wait_send()
            for away in range(1, n_z):

                @pl.when(came(away, step))
                def _(away=away):
                    x_move(away, step, False).wait_send()

    x_swap(0, True).wait_send()
    for m in range(1, n_z):
        x_swap(m).wait_send()
    for side in range(2):
        known = [0]
        for bit in orders[side]:
            for m in known:
                wq_hop(side, m, bit).wait_send()
                wo_hop(side, m, bit).wait_send()
            known = known + [m ^ bit for m in known]
        for m in range(n_f):
            wq_swap(side, m).wait_send()
        wi_hop(side).wait()
    for copy in outs:
        copy.wait()
    x_out.wait()


def front(x_own, w_qkv, w_out, w_in, bias, n_f, n_z, heads):
    rows, width = x_own.shape
    wide = heads * HEAD
    sds = jax.ShapeDtypeStruct
    in_vmem, anywhere = pl.BlockSpec(memory_space=pltpu.VMEM), pl.BlockSpec(memory_space=pl.ANY)
    part = w_in.shape[1] // 2
    dma = pltpu.SemaphoreType.DMA
    return pl.pallas_call(
        partial(front_kernel, n_z=n_z, n_f=n_f, heads=heads),
        out_shape=[
            sds((n_z, 2 * rows, 3 * wide), BF16),
            sds((n_z, 2, rows, width), BF16),
            sds((width, 3 * width // 2), BF16),
            sds((width // 2, width), BF16),
            sds((2, width // 2, part), BF16),
        ],
        in_specs=[anywhere] * 4 + [in_vmem],
        out_specs=[in_vmem] + [anywhere] * 4,
        scratch_shapes=[
            pltpu.VMEM((n_z, 2, rows, width), BF16),
            pltpu.VMEM((width, 3 * width), BF16),
            pltpu.VMEM((width, 3 * wide), BF16),
            dma((6,)),
            dma((2, n_z)),
            dma((n_z,)),
            dma((n_z,)),
            dma((n_z,)),
            dma((2, n_f)),
            dma((2, n_f)),
            dma((2, n_f)),
            dma((2, n_f)),
            dma((2, n_f)),
            dma((2, n_f)),
            dma((2,)),
            dma((2,)),
            dma((3,)),
        ],
        compiler_params=pltpu.CompilerParams(
            vmem_limit_bytes=VMEM_LIMIT, collective_id=1, has_side_effects=True
        ),
        cost_estimate=pl.CostEstimate(
            flops=4 * n_z * rows * width * 3 * wide, bytes_accessed=30 << 20, transcendentals=0
        ),
        name="front",
    )(x_own, w_qkv, w_out, w_in, bias)


def one_head(block, head, heads):
    if heads == 1:
        return block
    lane = lax.broadcasted_iota(jnp.int32, block.shape, 1)
    return jnp.where(lane // HEAD == head, block, jnp.zeros_like(block))


def merge_heads(parts):
    if len(parts) == 1:
        return parts[0]
    lane = lax.broadcasted_iota(jnp.int32, parts[0].shape, 1)
    result = parts[0]
    for head in range(1, len(parts)):
        result = jnp.where(lane // HEAD == head, parts[head], result)
    return result


def attend_kernel(*refs, blocks, heads, q_rows, k_rows):
    ins, rest = [refs[0].at[b] for b in range(blocks)], refs[1:]
    outs, (full_ref, lse_ref, key_s, value_s) = rest[:blocks], rest[blocks:]
    rows = ins[0].shape[0]
    width = heads * HEAD
    length = rows * blocks
    for b in range(blocks):
        here = slice(b * rows, (b + 1) * rows)
        key_s[here, :] = ins[b][:, width : 2 * width]
        value_s[here, :] = ins[b][:, 2 * width : 3 * width]
    for b in range(blocks):

        def step(i, carry, b=b):
            local = pl.ds(pl.multiple_of(i * q_rows, q_rows), q_rows)
            where = pl.ds(pl.multiple_of(b * rows + i * q_rows, q_rows), q_rows)
            query = ins[b][local, 0:width] * BF16(HEAD**-0.5)
            outputs, sums = [], []
            for head in range(heads):
                masked = one_head(query, head, heads)
                scores = [
                    dot(masked, key_s[j : j + k_rows, :], NT) for j in range(0, length, k_rows)
                ]
                top = None
                for part in scores:
                    part_top = jnp.max(part, axis=1, keepdims=True)
                    top = part_top if top is None else jnp.maximum(top, part_top)
                total = acc = None
                for j, part in enumerate(scores):
                    probs = jnp.exp(part - top)
                    part_total = jnp.sum(probs, axis=1, keepdims=True)
                    value = value_s[j * k_rows : (j + 1) * k_rows, :]
                    part_acc = dot(probs.astype(BF16), value, NN)
                    total = part_total if total is None else total + part_total
                    acc = part_acc if acc is None else acc + part_acc
                outputs.append(acc / total)
                sums.append(jnp.broadcast_to(top + jnp.log(total), (q_rows, width)))
            result = merge_heads(outputs)
            full_ref[where, :] = result
            outs[b][local, :] = result.astype(BF16)
            lse_ref[where, :] = merge_heads(sums)
            return carry

        lax.fori_loop(0, rows // q_rows, step, 0)


def attend(qkv, heads):
    blocks, rows, _ = qkv.shape
    width = heads * HEAD
    length = rows * blocks
    out = [jax.ShapeDtypeStruct((rows, width), BF16)] * blocks
    out += [jax.ShapeDtypeStruct((length, width), F32)] * 2
    results = pl.pallas_call(
        partial(attend_kernel, blocks=blocks, heads=heads, q_rows=256, k_rows=512),
        out_shape=out,
        scratch_shapes=[pltpu.VMEM((length, width), BF16)] * 2,
        compiler_params=pltpu.CompilerParams(vmem_limit_bytes=VMEM_LIMIT),
        cost_estimate=pl.CostEstimate(
            flops=16 * length * length * width, bytes_accessed=10 * length * width,
            transcendentals=heads * length * length,
        ),
        name="attend",
    )(qkv)
    return results[:blocks], results[blocks], results[blocks + 1]


def attend_back_kernel(*refs, blocks, heads, q_rows, k_rows):
    ins = [refs[0].at[b] for b in range(blocks)]
    grads, rest = refs[1 : blocks + 1], refs[blocks + 1 :]
    full_ref, lse_ref, rest = rest[0], rest[1], rest[2:]
    outs, (lse_t, delta_t, gq_t, key_t) = rest[:blocks], rest[blocks:]
    rows = ins[0].shape[0]
    width = heads * HEAD
    scale = HEAD**-0.5
    chunk = 256
    for b in range(blocks):
        for i in range(0, rows, chunk):
            local = slice(i, i + chunk)
            where = slice(b * rows + i, b * rows + i + chunk)
            logs = lse_ref[where, :].T
            terms = (grads[b][local, :].astype(F32) * full_ref[where, :]).T
            for head in range(heads):
                first = head * HEAD
                lse_t[head : head + 1, where] = logs[first : first + 1]
                delta_t[head : head + 1, where] = jnp.sum(
                    terms[first : first + HEAD], axis=0, keepdims=True
                )
        key_t[:, b * rows : (b + 1) * rows] = ins[b][:, width : 2 * width].T
    gq_t[...] = jnp.zeros_like(gq_t)
    for b in range(blocks):

        def step(j, carry, b=b):
            local = pl.ds(pl.multiple_of(j * k_rows, k_rows), k_rows)
            where = pl.ds(pl.multiple_of(b * rows + j * k_rows, k_rows), k_rows)
            key = ins[b][local, width : 2 * width]
            value = ins[b][local, 2 * width : 3 * width]
            key_grads, value_grads = [], []
            for head in range(heads):
                feats = slice(head * HEAD, (head + 1) * HEAD)
                key_h = one_head(key, head, heads) * BF16(scale)
                value_h = one_head(value, head, heads)
                key_grad = value_grad = None
                for other in range(blocks):
                    for i in range(0, rows, q_rows):
                        here = slice(i, i + q_rows)
                        there = slice(other * rows + i, other * rows + i + q_rows)
                        query = ins[other][here, 0:width]
                        grad = grads[other][here, :]
                        scores = dot(key_h, query, NT)
                        probs = jnp.exp(scores - lse_t[head : head + 1, there])
                        grad_probs = dot(value_h, grad, NT)
                        grad_scores = probs * (grad_probs - delta_t[head : head + 1, there])
                        grad_scores = grad_scores.astype(BF16)
                        term = dot(probs.astype(BF16), grad, NN)
                        value_grad = term if value_grad is None else value_grad + term
                        term = dot(grad_scores, query, NN)
                        key_grad = term if key_grad is None else key_grad + term
                        gq_t[feats, there] += dot(key_t[feats, where], grad_scores, NN)
                key_grads.append(key_grad)
                value_grads.append(value_grad)
            outs[b][local, width : 2 * width] = (merge_heads(key_grads) * scale).astype(BF16)
            outs[b][local, 2 * width : 3 * width] = merge_heads(value_grads).astype(BF16)
            return carry

        lax.fori_loop(0, rows // k_rows, step, 0)
    for b in range(blocks):
        for i in range(0, rows, chunk):
            there = slice(b * rows + i, b * rows + i + chunk)
            outs[b][i : i + chunk, 0:width] = (gq_t[:, there].T * scale).astype(BF16)


def attend_back(qkv, grads, full, lse, heads):
    blocks, rows, _ = qkv.shape
    width = heads * HEAD
    length = rows * blocks
    return pl.pallas_call(
        partial(attend_back_kernel, blocks=blocks, heads=heads, q_rows=256, k_rows=rows),
        out_shape=[jax.ShapeDtypeStruct((rows, 3 * width), BF16)] * blocks,
        scratch_shapes=[
            pltpu.VMEM((8, length), F32),
            pltpu.VMEM((8, length), F32),
            pltpu.VMEM((width, length), F32),
            pltpu.VMEM((width, length), BF16),
        ],
        compiler_params=pltpu.CompilerParams(vmem_limit_bytes=VMEM_LIMIT),
        cost_estimate=pl.CostEstimate(
            flops=40 * length * length * width, bytes_accessed=20 * length * width,
            transcendentals=heads * length * length,
        ),
        name="attend_back",
    )(qkv, *grads, full, lse)


def gelu_both(pre):
    slope = math.sqrt(2.0 / math.pi)
    square = pre * pre
    th = jnp.tanh(slope * (pre + 0.044715 * pre * square))
    half = 0.5 * (1.0 + th)
    grad = half + 0.5 * pre * (1.0 - th * th) * (slope * (1.0 + 3 * 0.044715 * square))
    return pre * half, grad


def row_stats(value):
    return jnp.mean(value, axis=1, keepdims=True)


def mid_kernel(*refs, n_f, n_z, cfg):
    att_refs, refs = refs[:n_z], refs[n_z:]
    (x_ref, cot_ref, vec_ref, bias_ref), refs = refs[:4], refs[4:]
    wo_ref, refs = refs[0], refs[1:]
    wi_refs, refs = refs[: 2 * n_f], refs[2 * n_f :]
    wb_refs, refs = refs[: 2 * n_f], refs[2 * n_f :]
    (layer_ref, grad_one_ref, att_ref, h_ref, act_ref, g2_ref, gp_ref, g1_ref), refs = refs[:8], refs[8:]
    (sums_ref, bias_sum_ref), refs = refs[:2], refs[2:]
    ga_refs, refs = refs[:n_z], refs[n_z:]
    (wo_s, wi_s, wb_s, slope_s, normed_s, unit_s, acc_s, send_s, recv_s, rstd_s), refs = refs[:10], refs[10:]
    w_sem, send_sem, recv_sem = refs
    ctx, fs = lax.axis_index("ctx"), lax.axis_index("fsdp")
    core, zed = ctx % 2, ctx // 2
    partner = {"ctx": zed * 2 + (1 - core)}
    rows, width = x_ref.shape
    own, other = slice(0, rows), slice(rows, 2 * rows)
    wide = att_refs[0].shape[1]
    half_in = n_z * wide
    ff_half = wi_s.shape[1]
    step = cfg["step"]
    chunk = cfg["rows"]

    copies = [[pltpu.make_async_copy(wo_ref, wo_s, w_sem.at[0, 0])]]
    copies[0][0].start()
    for pieces, target in ((wi_refs, wi_s), (wb_refs, wb_s)):
        group = []
        for side in range(2):
            for m in range(n_f):
                piece = pieces[side * n_f + m]
                p_rows, p_cols = piece.shape
                where = pl.ds(pl.multiple_of((fs ^ m) * p_cols, p_cols), p_cols)
                copy = pltpu.make_async_copy(
                    piece, target.at[pl.ds(side * p_rows, p_rows), where], w_sem.at[len(copies), side * n_f + m]
                )
                copy.start()
                group.append(copy)
        copies.append(group)
    barrier = pltpu.get_barrier_semaphore()
    pl.semaphore_signal(barrier, inc=1, device_id=partner, device_id_type=MESH)
    pl.semaphore_wait(barrier, 1)

    def exchange(n, src, dst):
        return pltpu.make_async_remote_copy(
            src_ref=src, dst_ref=dst, send_sem=send_sem.at[n], recv_sem=recv_sem.at[n],
            device_id=partner, device_id_type=MESH,
        )

    def over_cols(total, body):
        def run(i, carry):
            body(pl.ds(pl.multiple_of(i * step, step), step))
            return carry

        lax.fori_loop(0, total // step, run, 0)

    def over_rows(body):
        def run(i, carry):
            return body(pl.ds(pl.multiple_of(i * chunk, chunk), chunk), carry)

        zero = jnp.zeros((1, width), F32)
        return lax.fori_loop(0, rows // chunk, run, (zero, zero, zero))

    if wide % 128 == 0:
        for m in range(n_z):
            att_ref[:, pl.ds(pl.multiple_of((zed ^ m) * wide, wide), wide)] = att_refs[m][...]
    else:
        for m in range(0, n_z, 2):
            one, two = att_refs[m][...].astype(F32), att_refs[m + 1][...].astype(F32)
            odd = zed % 2 == 1
            block = jnp.concatenate([jnp.where(odd, two, one), jnp.where(odd, one, two)], axis=1)
            at = pl.ds(pl.multiple_of((zed // 2 ^ (m // 2)) * 2 * wide, 2 * wide), 2 * wide)
            att_ref[:, at] = block.astype(BF16)

    def wait_all(group):
        for copy in group:
            copy.wait()

    wait_all(copies[0])

    def out_other(cols):
        send_s[:, cols] = dot(att_ref[other, :], wo_s[:, cols], NN)

    over_cols(width, out_other)
    move = exchange(0, send_s, recv_s)
    move.start()

    def out_own(cols):
        part = dot(att_ref[own, :], wo_s[:, cols], NN)
        acc_s[:, cols] = part + x_ref[:, cols].astype(F32) + vec_ref[2:3, cols]

    over_cols(width, out_own)
    move.wait()

    def norm_one(r, carry):
        resid = acc_s[r, :] + recv_s[r, :]
        centre = resid - row_stats(resid)
        rstd = lax.rsqrt(row_stats(centre * centre) + EPS)
        unit = centre * rstd
        normed = unit * vec_ref[3:4, :] + vec_ref[4:5, :]
        unit_s[r, :] = unit
        rstd_s[r, :] = jnp.broadcast_to(rstd, (chunk, 128))
        normed_s[r, :] = normed
        h_ref[r, :] = normed.astype(BF16)
        return carry

    over_rows(norm_one)
    move = exchange(1, h_ref.at[own], h_ref.at[other])
    move.start()

    wait_all(copies[1])

    def up(where):
        def body(cols):
            pre = dot(h_ref[where, :], wi_s[:, cols], NN) + bias_ref[0:1, cols]
            act, slope = gelu_both(pre)
            act_ref[where, cols] = act.astype(BF16)
            slope_s[where, cols] = slope

        over_cols(ff_half, body)

    up(own)
    move.wait()
    up(other)
    wait_all(copies[2])

    def down_other(cols):
        send_s[:, cols] = dot(act_ref[other, :], wb_s[:, cols], NN)

    over_cols(width, down_other)
    move = exchange(2, send_s, recv_s)
    move.start()

    def down_own(cols):
        part = dot(act_ref[own, :], wb_s[:, cols], NN)
        acc_s[:, cols] = part + normed_s[:, cols] + vec_ref[5:6, cols]

    over_cols(width, down_own)
    move.wait()

    def norm_two(r, carry):
        resid = acc_s[r, :] + recv_s[r, :]
        centre = resid - row_stats(resid)
        rstd = lax.rsqrt(row_stats(centre * centre) + EPS)
        unit = centre * rstd
        gain = vec_ref[6:7, :]
        layer_ref[r, :] = (unit * gain + vec_ref[7:8, :]).astype(BF16)
        grad = cot_ref[r, :]
        scaled = grad * gain
        back = rstd * (scaled - row_stats(scaled) - unit * row_stats(scaled * unit))
        acc_s[r, :] = back
        g2_ref[r, :] = back.astype(BF16)
        sums = (back, grad * unit, grad)
        return tuple(c + jnp.sum(s, axis=0, keepdims=True) for c, s in zip(carry, sums))

    shift_two = over_rows(norm_two)
    move = exchange(3, g2_ref.at[own], g2_ref.at[other])
    move.start()
    for i, total in enumerate(shift_two):
        sums_ref[3 + i : 4 + i, :] = total

    def back_act(where, first):
        def body(cols):
            grad = dot(g2_ref[where, :], wb_s[cols, :], NT) * slope_s[where, cols]
            gp_ref[where, cols] = grad.astype(BF16)
            total = jnp.sum(grad, axis=0, keepdims=True)
            bias_sum_ref[0:1, cols] = total if first else bias_sum_ref[0:1, cols] + total

        over_cols(ff_half, body)

    back_act(own, True)
    move.wait()
    back_act(other, False)

    def back_other(cols):
        send_s[:, cols] = dot(gp_ref[other, :], wi_s[cols, :], NT)

    over_cols(width, back_other)
    move = exchange(4, send_s, recv_s)
    move.start()

    def back_own(cols):
        acc_s[:, cols] += dot(gp_ref[own, :], wi_s[cols, :], NT)

    over_cols(width, back_own)
    move.wait()

    def back_one(r, carry):
        grad = acc_s[r, :] + recv_s[r, :]
        unit = unit_s[r, :]
        rstd = rstd_s[r, 0:1]
        scaled = grad * vec_ref[3:4, :]
        back = rstd * (scaled - row_stats(scaled) - unit * row_stats(scaled * unit))
        grad_one_ref[r, :] = back
        g1_ref[r, :] = back.astype(BF16)
        sums = (back, grad * unit, grad)
        return tuple(c + jnp.sum(s, axis=0, keepdims=True) for c, s in zip(carry, sums))

    shift_one = over_rows(back_one)
    move = exchange(5, g1_ref.at[own], g1_ref.at[other])
    move.start()
    for i, total in enumerate(shift_one):
        sums_ref[i : 1 + i, :] = total
    sums_ref[6:8, :] = jnp.zeros((2, width), F32)

    for where in (own, other):
        if where is other:
            move.wait()
        for m in range(n_z):
            at = pl.ds(pl.multiple_of((zed ^ m) * wide, wide), wide)
            ga_refs[m][where, :] = dot(g1_ref[where, :], wo_s[at, :], NT).astype(BF16)


def middle(att, x_own, cot, vectors, bias_half, wo, wi, wb, n_f, n_z):
    rows, width = x_own.shape
    wide = att[0].shape[1]
    ff_half = bias_half.shape[0]
    half_in = n_z * wide
    sds = jax.ShapeDtypeStruct
    out_shape = [
        sds((rows, width), BF16),
        sds((rows, width), F32),
        sds((2 * rows, half_in), BF16),
        sds((2 * rows, width), BF16),
        sds((2 * rows, ff_half), BF16),
        sds((2 * rows, width), BF16),
        sds((2 * rows, ff_half), BF16),
        sds((2 * rows, width), BF16),
        sds((8, width), F32),
        sds((1, ff_half), F32),
    ] + [sds((2 * rows, wide), BF16)] * n_z
    in_vmem, anywhere = pl.BlockSpec(memory_space=pltpu.VMEM), pl.BlockSpec(memory_space=pl.ANY)
    cfg = {"step": 512, "rows": 64}
    results = pl.pallas_call(
        partial(mid_kernel, n_f=n_f, n_z=n_z, cfg=cfg),
        out_shape=out_shape,
        in_specs=[in_vmem] * (n_z + 4) + [anywhere] * (4 * n_f + 1),
        out_specs=[in_vmem] * len(out_shape),
        scratch_shapes=[
            pltpu.VMEM((half_in, width), BF16),
            pltpu.VMEM((width, ff_half), BF16),
            pltpu.VMEM((ff_half, width), BF16),
            pltpu.VMEM((2 * rows, ff_half), F32),
            pltpu.VMEM((rows, width), F32),
            pltpu.VMEM((rows, width), F32),
            pltpu.VMEM((rows, width), F32),
            pltpu.VMEM((rows, width), F32),
            pltpu.VMEM((rows, width), F32),
            pltpu.VMEM((rows, 128), F32),
            pltpu.SemaphoreType.DMA((3, 2 * n_f)),
            pltpu.SemaphoreType.DMA((6,)),
            pltpu.SemaphoreType.DMA((6,)),
        ],
        compiler_params=pltpu.CompilerParams(
            vmem_limit_bytes=VMEM_MIDDLE, collective_id=0, has_side_effects=True
        ),
        cost_estimate=pl.CostEstimate(
            flops=2 * 2 * rows * width * (2 * half_in + 4 * ff_half),
            bytes_accessed=40 << 20, transcendentals=2 * rows * ff_half,
        ),
        name="middle",
    )(*att, x_own, cot, vectors, bias_half[None], wo, *wi, *wb)
    return results[:10], results[10:]


def tail_kernel(*refs, n_z):
    g_refs, refs = refs[:n_z], refs[n_z:]
    wl_ref, grad_one_ref, out_ref, cat, send_s, recv_s, send_sem, recv_sem = refs
    ctx = lax.axis_index("ctx")
    core, zed = ctx % 2, ctx // 2
    partner = {"ctx": zed * 2 + (1 - core)}
    rows, width = out_ref.shape
    half = width // 2
    wide = g_refs[0].shape[1] // 3
    barrier = pltpu.get_barrier_semaphore()
    pl.semaphore_signal(barrier, inc=1, device_id=partner, device_id_type=MESH)
    pl.semaphore_wait(barrier, 1)
    for j in range(3):
        part = slice(j * wide, (j + 1) * wide)
        if wide % 128 == 0:
            for m in range(n_z):
                at = pl.ds(pl.multiple_of(j * half + (zed ^ m) * wide, 128), wide)
                cat[:, at] = g_refs[m][:, part]
        else:
            for m in range(0, n_z, 2):
                one, two = g_refs[m][:, part].astype(F32), g_refs[m + 1][:, part].astype(F32)
                odd = zed % 2 == 1
                block = jnp.concatenate([jnp.where(odd, two, one), jnp.where(odd, one, two)], axis=1)
                at = j * half + (zed // 2 ^ (m // 2)) * 2 * wide
                cat[:, pl.ds(pl.multiple_of(at, 128), 2 * wide)] = block.astype(BF16)
    step = 256
    pieces = width // step

    def move(i):
        cols = slice(i * step, (i + 1) * step)
        return pltpu.make_async_remote_copy(
            src_ref=send_s.at[:, cols], dst_ref=recv_s.at[:, cols], send_sem=send_sem.at[i],
            recv_sem=recv_sem.at[i], device_id=partner, device_id_type=MESH,
        )

    for i in range(pieces):
        cols = slice(i * step, (i + 1) * step)
        send_s[:, cols] = dot(cat[rows:, :], wl_ref[cols, :], NT)
        move(i).start()
    for i in range(pieces):
        cols = slice(i * step, (i + 1) * step)
        part = dot(cat[:rows, :], wl_ref[cols, :], NT) + grad_one_ref[:, cols]
        move(i).wait_recv()
        out_ref[:, cols] = part + recv_s[:, cols]
    for i in range(pieces):
        move(i).wait_send()


def tail(grads, w_local, grad_one):
    rows, width = grad_one.shape
    n_z = len(grads)
    return pl.pallas_call(
        partial(tail_kernel, n_z=n_z),
        out_shape=jax.ShapeDtypeStruct((rows, width), F32),
        scratch_shapes=[
            pltpu.VMEM((2 * rows, 3 * width // 2), BF16),
            pltpu.VMEM((rows, width), F32),
            pltpu.VMEM((rows, width), F32),
            pltpu.SemaphoreType.DMA((width // 256,)),
            pltpu.SemaphoreType.DMA((width // 256,)),
        ],
        compiler_params=pltpu.CompilerParams(
            vmem_limit_bytes=VMEM_LIMIT, collective_id=2, has_side_effects=True
        ),
        cost_estimate=pl.CostEstimate(
            flops=6 * rows * width * width, bytes_accessed=12 << 20, transcendentals=0
        ),
        name="tail",
    )(*grads, w_local, grad_one)


def on_device(x_in, w_qkv, w_out, w_in, w_back, vectors, bias_in, cot, *, n_ctx, n_f):
    ctx, fs = lax.axis_index("ctx"), lax.axis_index("fsdp")
    core, zed = ctx % 2, ctx // 2
    n_z = n_ctx // 2
    x_own = x_in[0]
    grad_out = cot[0]
    rows, width = x_own.shape
    hidden = w_back.shape[0]
    half_heads = HEADS // 2
    heads = half_heads // n_z
    wide = heads * HEAD

    def swap(v):
        return lax.ppermute(v, "ctx", [(i, i ^ 1) for i in range(n_ctx)])

    def over_z(v, m):
        return lax.ppermute(v, "ctx", [(i, i ^ (2 * m)) for i in range(n_ctx)])

    def over_f(v, m):
        return lax.ppermute(v, "fsdp", [(i, i ^ m) for i in range(n_f)])

    bits = [1 << b for b in range(n_f.bit_length() - 1)]

    def pair(v):
        return jnp.concatenate([v, swap(v)], axis=0)

    def pair_sum(partial_sum):
        return partial_sum[:rows] + swap(partial_sum[rows:])

    def place(pieces, index, axis):
        count = len(pieces)
        for bit in range(count.bit_length() - 1):
            flag = (index >> bit) & 1
            pieces = [jnp.where(flag, pieces[m ^ (1 << bit)], pieces[m]) for m in range(count)]
        return jnp.concatenate(pieces, axis=axis)

    def gather_cols(shard, begun=None):
        half = shard.shape[0] // 2
        parts = []
        for side, order in enumerate((bits, bits[1:] + bits[:1])):
            held = {0: shard[side * half : (side + 1) * half]}
            for level, bit in enumerate(order):
                if level == 0 and begun is not None:
                    held[bit] = begun[side]
                    continue
                for m in list(held):
                    held[m ^ bit] = over_f(held[m], bit)
            parts += [held[m] for m in range(n_f)]
        return parts

    def after(value, *others):
        return lax.optimization_barrier((value,) + others)[0]

    half_in = width // 2
    first = (core * half_heads + zed * heads) * HEAD
    span = 3 * wide
    bias_qkv = jnp.concatenate(
        [
            lax.dynamic_slice_in_dim(vectors[0], first, wide, 0),
            jnp.zeros((wide,), F32),
            lax.dynamic_slice_in_dim(vectors[1], first, wide, 0),
        ]
    )[None]
    qkv, x_all, w_local, wo_half, wi_got = front(
        x_own, w_qkv, w_out, w_in, bias_qkv, n_f, n_z, heads
    )

    ff_part = w_in.shape[1] // 2
    wi_mine = lax.dynamic_slice_in_dim(w_in, core * ff_part, ff_part, 1)
    wi_half = gather_cols(wi_mine, wi_got)
    wb_mine = lax.dynamic_index_in_dim(
        w_back.reshape(n_f, 2, ff_part, w_back.shape[1]), core, 1, False
    ).reshape(n_f * ff_part, -1)
    wb_half = gather_cols(after(wb_mine, wi_got))

    att, att_full, lse = attend(qkv, heads)
    att = [att[m] if m == 0 else over_z(att[m], m) for m in range(n_z)]
    bias_half = lax.dynamic_index_in_dim(
        bias_in.reshape(n_f, 2, ff_part), core, 1, False
    ).reshape(-1)
    outs, grad_att = middle(
        att, x_own, grad_out, vectors, bias_half, wo_half, wi_half, wb_half, n_f, n_z
    )
    layer_out, grad_one, att_half, h_two, act, g_two, grad_pre_low, g_one, sums_mid, bias_sum = outs
    layer_out = layer_out[None]
    g_att = [grad_att[m] if m == 0 else over_z(grad_att[m], m) for m in range(n_z)]

    low = width // (n_ctx * n_f)

    def over_fsdp(partial_grad):
        cols = partial_grad.shape[1]
        view = partial_grad.reshape((n_z, 2) + (2,) * len(bits) + (low, cols))
        done = []
        for side in range(2):
            now = view[:, side]
            order = bits if side == 0 else bits[1:] + bits[:1]
            left = list(reversed(bits))
            for bit in order:
                axis = 1 + left.index(bit)
                left.remove(bit)
                flag = (fs // bit) % 2
                stay = lax.dynamic_index_in_dim(now, flag, axis, False)
                go = lax.dynamic_index_in_dim(now, 1 - flag, axis, False)
                now = (stay.astype(F32) + over_f(go, bit).astype(F32)).astype(BF16)
            done.append(now)
        return jnp.stack(done, axis=1)

    def over_ctx(both):
        total = lax.dynamic_index_in_dim(both, zed, 0, False).astype(F32)
        for m in range(1, n_z):
            part = lax.dynamic_index_in_dim(both, zed ^ m, 0, False)
            total = total + over_z(part, m).astype(F32)
        stay = lax.dynamic_index_in_dim(total, core, 0, False)
        go = lax.dynamic_index_in_dim(total, 1 - core, 0, False)
        return stay, swap(go.astype(BF16)).astype(F32)

    def halves(stay, came, parts):
        low = stay.shape[0]
        first = jnp.where(core == 0, stay, came).reshape(low, parts, 1, -1)
        second = jnp.where(core == 0, came, stay).reshape(low, parts, 1, -1)
        return jnp.concatenate([first, second], axis=2).reshape(low, -1)

    def reduced(partial_grad):
        return over_ctx(over_fsdp(partial_grad))

    in_weight_grad = halves(*reduced(dot(h_two, grad_pre_low, TN).astype(BF16)), n_f)
    back_weight_grad = halves(*reduced(dot(g_two, act, TN).astype(BF16)), n_f).T
    att_other = swap(att_half)
    att_other = jnp.concatenate([att_other[rows:], att_other[:rows]], axis=0)
    att_both = place([att_half, att_other], core, 0 + 1)
    out_cols = lax.dynamic_slice_in_dim(g_one, core * half_in, half_in, 1)
    out_weight_grad = halves(*reduced(dot(att_both, out_cols, TN).astype(BF16)), 1)

    g_qkv = attend_back(qkv, g_att, att_full, lse, heads)
    g_sent = [g_qkv[m] if m == 0 else over_z(g_qkv[m], m) for m in range(n_z)]
    g_local = jnp.concatenate(g_qkv, axis=0)
    attn_grad = dot(x_all.reshape(-1, width), g_local, TN).astype(BF16)
    both = over_fsdp(attn_grad)
    mine, others = [], []
    for m in range(n_z):
        part = lax.dynamic_index_in_dim(both, zed ^ m, 0, False)
        part = part if m == 0 else over_z(part, m)
        mine.append(lax.dynamic_index_in_dim(part, core, 0, False))
        others.append(lax.dynamic_index_in_dim(part, 1 - core, 0, False))
    others = swap(jnp.stack(others))
    others = [others[m] for m in range(n_z)]

    def heads_order(parts):
        parts = [p.reshape(low, 3, wide) for p in parts]
        return place(parts, zed, 2).astype(F32).reshape(low, -1)

    qkv_weight_grad = halves(heads_order(mine), heads_order(others), 3)
    grad_in = tail(g_sent, w_local, grad_one)

    def spread(half_row, parts):
        piece = half_row.reshape(parts, 1, -1)
        empty = jnp.zeros_like(piece)
        both = jnp.where(core == 0, jnp.concatenate([piece, empty], 1), jnp.concatenate([empty, piece], 1))
        return both.reshape(-1)

    def halve(now):
        left = list(reversed(bits))
        for bit in bits:
            axis = left.index(bit)
            left.remove(bit)
            flag = (fs // bit) % 2
            stay = lax.dynamic_index_in_dim(now, flag, axis, False)
            now = stay + over_f(lax.dynamic_index_in_dim(now, 1 - flag, axis, False), bit)
        return now

    sums = jnp.sum(g_local.astype(F32), axis=0)
    sums = jnp.stack([sums[:wide].reshape(n_f, -1), sums[2 * wide :].reshape(n_f, -1)], axis=1)
    late = halve(sums.reshape((2,) * len(bits) + (-1,)))
    turn = [(2 * z + c, n_z * c + z) for z in range(n_z) for c in range(2)]
    late = lax.ppermute(late, "ctx", turn).reshape(2, -1)
    ratio = hidden // width
    early = sums_mid[:6].T
    bias_terms = spread(bias_sum[0], n_f).reshape(width, ratio)
    table = jnp.concatenate([early, bias_terms], axis=1)
    kinds = table.shape[1]
    now = jnp.swapaxes(table.reshape(n_z * 2, n_f, low, kinds), -1, -2)
    now = jnp.swapaxes(now, 0, 1).reshape((2,) * len(bits) + (n_z, 2, kinds * low))
    now = halve(now)
    total = lax.dynamic_index_in_dim(now, zed, 0, False)
    for m in range(1, n_z):
        total = total + over_z(lax.dynamic_index_in_dim(now, zed ^ m, 0, False), m)
    stay = lax.dynamic_index_in_dim(total, core, 0, False)
    table = stay + swap(lax.dynamic_index_in_dim(total, 1 - core, 0, False))
    table = table.reshape(kinds, low)
    vector_grad = jnp.concatenate([late, table[:6]], axis=0)
    in_bias_grad = table[6:].T.reshape(-1)
    return (
        layer_out,
        grad_in[None],
        qkv_weight_grad,
        out_weight_grad,
        in_weight_grad,
        back_weight_grad,
        vector_grad,
        in_bias_grad,
    )


def solution(mesh):
    tokens = P("fsdp", "ctx", None)
    cols = P(None, "fsdp")
    shared = P(("ctx", "fsdp"), None)
    return jax.shard_map(
        partial(on_device, n_ctx=mesh.shape["ctx"], n_f=mesh.shape["fsdp"]),
        mesh=mesh,
        in_specs=(tokens, cols, cols, cols, cols, P(), P(), tokens),
        out_specs=(
            tokens,
            tokens,
            shared,
            shared,
            shared,
            P(None, ("ctx", "fsdp")),
            P(None, ("ctx", "fsdp")),
            P(("ctx", "fsdp")),
        ),
        check_vma=False,
    )
```

```python
from functools import partial
import math

import jax
import jax.numpy as jnp
from jax import lax
from jax.experimental import pallas as pl
from jax.experimental.pallas import tpu as pltpu
from jax.sharding import PartitionSpec as P

HEADS = 16
HEAD = 64
EPS = 1e-12
F32 = jnp.float32
BF16 = jnp.bfloat16
NN = (((1,), (0,)), ((), ()))
NT = (((1,), (1,)), ((), ()))
TN = (((0,), (0,)), ((), ()))
VMEM_LIMIT = 50 * 1024 * 1024
VMEM_MIDDLE = 56 * 1024 * 1024
MESH = pl.DeviceIdType.MESH


def dot(left, right, dims):
    return lax.dot_general(left, right, dims, preferred_element_type=F32)


def front_kernel(x_ref, wq_ref, wo_ref, wi_ref, bias_ref, qkv_ref, xf_out, wl_out, wo_out, wi_out, *scratch, n_z, n_f, heads):
    xf, wfull, wloc = scratch[:3]
    own_sem, x_send, x_recv, xs_send, xs_recv, w_send, w_recv, ws_send, ws_recv, o_send, o_recv, i_send, i_recv, out_sem = scratch[3:]
    ctx, fs = lax.axis_index("ctx"), lax.axis_index("fsdp")
    core, zed = ctx % 2, ctx // 2
    bits = [1 << b for b in range(n_f.bit_length() - 1)]
    orders = (bits, bits[1:] + bits[:1])
    rows, width = x_ref.shape
    half = width // 2
    quarter = half // 2
    wide = heads * HEAD
    partner = {"ctx": zed * 2 + (1 - core)}

    barrier = pltpu.get_barrier_semaphore()

    def greet(device):
        pl.semaphore_signal(barrier, inc=1, device_id=device, device_id_type=MESH)

    greet(partner)
    for bit in bits:
        greet({"fsdp": fs ^ bit})

    @pl.when(zed > 0)
    def _():
        greet({"ctx": ctx - 2})

    @pl.when(zed < n_z - 1)
    def _():
        greet({"ctx": ctx + 2})

    edges = (zed == 0).astype(jnp.int32) + (zed == n_z - 1).astype(jnp.int32)
    pl.semaphore_wait(barrier, 3 + len(bits) - edges)

    def remote(src, dst, send, recv, device):
        return pltpu.make_async_remote_copy(
            src_ref=src, dst_ref=dst, send_sem=send, recv_sem=recv, device_id=device, device_id_type=MESH
        )

    def x_move(away, step, first):
        block = zed - step * away
        src = x_ref if first else xf.at[block ^ zed, 0]
        index = (step + 1) // 2
        return remote(
            src, xf.at[block ^ (zed + step), 0], x_send.at[index, away], x_recv.at[block ^ (zed + step)],
            {"ctx": ctx + 2 * step},
        )

    def x_swap(m, first=False):
        src = x_ref if first else xf.at[m, 0]
        return remote(src, xf.at[m, 1], xs_send.at[m], xs_recv.at[m], partner)

    def has(step):
        return zed < n_z - 1 if step == 1 else zed > 0

    def came(away, step):
        return zed - away >= 0 if step == 1 else zed + away <= n_z - 1

    for step in (1, -1):

        @pl.when(has(step))
        def _(step=step):
            x_move(0, step, True).start()

    x_swap(0, True).start()
    own_x = pltpu.make_async_copy(x_ref, xf.at[0, 0], own_sem.at[0])
    own_x.start()

    def x_step(away):
        for step in (1, -1):

            @pl.when(came(away, step))
            def _(step=step):
                block = zed - step * away
                remote(
                    xf.at[block ^ zed, 0], xf.at[block ^ zed, 0], x_send.at[0, 0], x_recv.at[block ^ zed], partner
                ).wait_recv()

                @pl.when(has(step))
                def _():
                    x_move(away, step, False).start()

                x_swap(block ^ zed).start()

    def wq_place(side, origin, which):
        cols = wq_ref.shape[1]
        return wfull.at[
            pl.ds(pl.multiple_of(which * half + side * quarter, quarter), quarter),
            pl.ds(pl.multiple_of(origin * cols, 128), cols),
        ]

    def wq_own(side):
        return wq_ref.at[pl.ds(pl.multiple_of(core * half + side * quarter, quarter), quarter), :]

    def wo_place(side, origin):
        cols = wo_ref.shape[1]
        return wo_out.at[pl.ds(side * quarter, quarter), pl.ds(pl.multiple_of(origin * cols, 128), cols)]

    def wo_own(side):
        return wo_ref.at[pl.ds(pl.multiple_of(core * half + side * quarter, quarter), quarter), :]

    def wq_hop(side, m, bit):
        src = wq_own(side) if m == 0 else wq_place(side, fs ^ m, core)
        return remote(src, wq_place(side, fs ^ m, core), w_send.at[side, m ^ bit], w_recv.at[side, m ^ bit], {"fsdp": fs ^ bit})

    def wo_hop(side, m, bit):
        src = wo_own(side) if m == 0 else wo_place(side, fs ^ m)
        return remote(src, wo_place(side, fs ^ m), o_send.at[side, m ^ bit], o_recv.at[side, m ^ bit], {"fsdp": fs ^ bit})

    def wq_swap(side, m):
        src = wq_own(side) if m == 0 else wq_place(side, fs ^ m, core)
        return remote(src, wq_place(side, fs ^ m, core), ws_send.at[side, m], ws_recv.at[side, m], partner)

    own_w = []
    for side in range(2):
        wq_hop(side, 0, orders[side][0]).start()
        wq_swap(side, 0).start()
        own_w.append(pltpu.make_async_copy(wq_own(side), wq_place(side, fs, core), own_sem.at[1 + side]))
        own_w.append(pltpu.make_async_copy(wo_own(side), wo_place(side, fs), own_sem.at[3 + side]))
    for copy in own_w:
        copy.start()

    part = wi_ref.shape[1] // 2

    def wi_hop(side):
        src = wi_ref.at[pl.ds(side * half, half), pl.ds(pl.multiple_of(core * part, 128), part)]
        return remote(src, wi_out.at[side], i_send.at[side], i_recv.at[side], {"fsdp": fs ^ orders[side][0]})

    def doubling(hop, level, after=None):
        for side in range(2):
            known = [0]
            for bit in orders[side][:level]:
                known = known + [m ^ bit for m in known]
            bit = orders[side][level]
            for m in known:
                hop(side, m, bit).wait_recv()
                if after is not None:
                    after(side, m ^ bit).start()
            if level + 1 < len(bits):
                for m in known + [m ^ bit for m in known]:
                    hop(side, m, orders[side][level + 1]).start()

    doubling(wq_hop, 0, wq_swap)
    for side in range(2):
        wo_hop(side, 0, orders[side][0]).start()
    x_step(1)
    for level in range(1, len(bits)):
        doubling(wq_hop, level, wq_swap)
    for side in range(2):
        wi_hop(side).start()
    doubling(wo_hop, 0)
    for away in range(2, n_z - 1):
        x_step(away)
    for copy in own_w:
        copy.wait()
    for side in range(2):
        for m in range(n_f):
            wq_swap_in = remote(
                wq_place(side, fs ^ m, 1 - core), wq_place(side, fs ^ m, 1 - core),
                ws_send.at[side, m], ws_recv.at[side, m], partner,
            )
            wq_swap_in.wait_recv()
    outs = []
    for j in range(3):
        cols = pl.ds(pl.multiple_of(j * width + core * half, 128), half)
        outs.append(pltpu.make_async_copy(wfull.at[:, cols], wl_out.at[:, pl.ds(j * half, half)], out_sem.at[j]))
    for copy in outs:
        copy.start()
    for j in range(3):
        base = j * width + core * half + zed * wide
        if wide % 128 == 0:
            piece = wfull[:, pl.ds(pl.multiple_of(base, 128), wide)]
        else:
            block = wfull[:, pl.ds(pl.multiple_of(base // 128 * 128, 128), 128)].astype(F32)
            piece = jnp.where(zed % 2 == 1, block[:, wide:], block[:, :wide]).astype(BF16)
        wloc[:, j * wide : (j + 1) * wide] = piece

    def x_ready(m, side):
        remote(xf.at[m, side], xf.at[m, side], xs_send.at[m], xs_recv.at[m], partner).wait_recv()

    def project(m):
        def run(side, carry):
            result = dot(xf[m, side], wloc[...], NN) + bias_ref[...]
            where = pl.ds(pl.multiple_of(side * rows, rows), rows)
            qkv_ref[m, where, :] = result.astype(BF16)
            return carry

        lax.fori_loop(0, 2, run, 0)

    own_x.wait()
    x_ready(0, 1)
    project(0)

    def finish(away):
        def run(i, carry):
            block = zed - (1 - 2 * i) * away

            @pl.when((block >= 0) & (block <= n_z - 1))
            def _():
                x_ready(block ^ zed, 1)
                project(block ^ zed)

            return carry

        lax.fori_loop(0, 2, run, 0)

    for away in range(1, n_z - 1):
        finish(away)
    for level in range(1, len(bits)):
        doubling(wo_hop, level)
    if n_z > 2:
        x_step(n_z - 1)
    finish(n_z - 1)
    x_out = pltpu.make_async_copy(xf, xf_out, own_sem.at[5])
    x_out.start()

    for step in (1, -1):

        @pl.when(has(step))
        def _(step=step):
            x_move(0, step, True).wait_send()
            for away in range(1, n_z):

                @pl.when(came(away, step))
                def _(away=away):
                    x_move(away, step, False).wait_send()

    x_swap(0, True).wait_send()
    for m in range(1, n_z):
        x_swap(m).wait_send()
    for side in range(2):
        known = [0]
        for bit in orders[side]:
            for m in known:
                wq_hop(side, m, bit).wait_send()
                wo_hop(side, m, bit).wait_send()
            known = known + [m ^ bit for m in known]
        for m in range(n_f):
            wq_swap(side, m).wait_send()
        wi_hop(side).wait()
    for copy in outs:
        copy.wait()
    x_out.wait()


def front(x_own, w_qkv, w_out, w_in, bias, n_f, n_z, heads):
    rows, width = x_own.shape
    wide = heads * HEAD
    sds = jax.ShapeDtypeStruct
    in_vmem, anywhere = pl.BlockSpec(memory_space=pltpu.VMEM), pl.BlockSpec(memory_space=pl.ANY)
    part = w_in.shape[1] // 2
    dma = pltpu.SemaphoreType.DMA
    return pl.pallas_call(
        partial(front_kernel, n_z=n_z, n_f=n_f, heads=heads),
        out_shape=[
            sds((n_z, 2 * rows, 3 * wide), BF16),
            sds((n_z, 2, rows, width), BF16),
            sds((width, 3 * width // 2), BF16),
            sds((width // 2, width), BF16),
            sds((2, width // 2, part), BF16),
        ],
        in_specs=[anywhere] * 4 + [in_vmem],
        out_specs=[in_vmem] + [anywhere] * 4,
        scratch_shapes=[
            pltpu.VMEM((n_z, 2, rows, width), BF16),
            pltpu.VMEM((width, 3 * width), BF16),
            pltpu.VMEM((width, 3 * wide), BF16),
            dma((6,)),
            dma((2, n_z)),
            dma((n_z,)),
            dma((n_z,)),
            dma((n_z,)),
            dma((2, n_f)),
            dma((2, n_f)),
            dma((2, n_f)),
            dma((2, n_f)),
            dma((2, n_f)),
            dma((2, n_f)),
            dma((2,)),
            dma((2,)),
            dma((3,)),
        ],
        compiler_params=pltpu.CompilerParams(
            vmem_limit_bytes=VMEM_LIMIT, collective_id=1, has_side_effects=True
        ),
        cost_estimate=pl.CostEstimate(
            flops=4 * n_z * rows * width * 3 * wide, bytes_accessed=30 << 20, transcendentals=0
        ),
        name="front",
    )(x_own, w_qkv, w_out, w_in, bias)


def one_head(block, head, heads):
    if heads == 1:
        return block
    lane = lax.broadcasted_iota(jnp.int32, block.shape, 1)
    return jnp.where(lane // HEAD == head, block, jnp.zeros_like(block))


def merge_heads(parts):
    if len(parts) == 1:
        return parts[0]
    lane = lax.broadcasted_iota(jnp.int32, parts[0].shape, 1)
    result = parts[0]
    for head in range(1, len(parts)):
        result = jnp.where(lane // HEAD == head, parts[head], result)
    return result


def remote(src, dst, send, recv, device):
    return pltpu.make_async_remote_copy(
        src_ref=src, dst_ref=dst, send_sem=send, recv_sem=recv, device_id=device, device_id_type=MESH
    )


def greet(barrier, devices):
    for device in devices:
        pl.semaphore_signal(barrier, inc=1, device_id=device, device_id_type=MESH)
    pl.semaphore_wait(barrier, len(devices))


def fsdp_orders(n_f):
    bits = [1 << b for b in range(n_f.bit_length() - 1)]
    return bits, (bits, bits[1:] + bits[:1])


def known_at(order, level):
    known = [0]
    for bit in order[:level]:
        known = known + [m ^ bit for m in known]
    return known


def attend_kernel(*refs, blocks, heads, n_f, q_rows, k_rows):
    qkv_ref, wi_ref, got_ref, wb_ref = refs[:4]
    att_ref, full_ref, lse_ref, wi_out, wb_out = refs[4:9]
    key_s, value_s, send_s, a_send, a_recv, i_send, i_recv, b_send, b_recv, own_sem = refs[9:]
    ins = [qkv_ref.at[b] for b in range(blocks)]
    rows = ins[0].shape[0]
    width = heads * HEAD
    length = rows * blocks
    ctx, fs = lax.axis_index("ctx"), lax.axis_index("fsdp")
    core, zed = ctx % 2, ctx // 2
    bits, orders = fsdp_orders(n_f)
    greet(
        pltpu.get_barrier_semaphore(),
        [{"fsdp": fs ^ bit} for bit in bits] + [{"ctx": (zed ^ m) * 2 + core} for m in range(1, blocks)],
    )

    half, part = got_ref.shape[1:]

    def wi_place(side, m):
        return wi_out.at[pl.ds(side * half, half), pl.ds(pl.multiple_of((fs ^ m) * part, 128), part)]

    def wi_source(side, m):
        if m == 0:
            return wi_ref.at[pl.ds(side * half, half), pl.ds(pl.multiple_of(core * part, 128), part)]
        return got_ref.at[side] if m == orders[side][0] else wi_place(side, m)

    def wi_hop(side, m, bit):
        return remote(
            wi_source(side, m), wi_place(side, m), i_send.at[side, m ^ bit], i_recv.at[side, m ^ bit], {"fsdp": fs ^ bit}
        )

    def wb_hop(seg):
        return remote(
            wb_ref.at[seg, core], wb_out.at[seg], b_send.at[seg], b_recv.at[seg],
            {"fsdp": fs ^ orders[seg * 2 // n_f][0]},
        )

    def level(number, act):
        for side in range(2):
            for m in known_at(orders[side], number):
                act(wi_hop(side, m, orders[side][number]))

    locals_ = []
    for side in range(2):
        for i, m in enumerate((0, orders[side][0])):
            locals_.append(pltpu.make_async_copy(wi_source(side, m), wi_place(side, m), own_sem.at[2 * side + i]))
    for copy in locals_:
        copy.start()
    level(1, lambda hop: hop.start())
    for seg in range(n_f):
        wb_hop(seg).start()

    def att_hop(b):
        return remote(send_s.at[b - 1], att_ref.at[b], a_send.at[b], a_recv.at[b], {"ctx": (zed ^ b) * 2 + core})

    for b in range(blocks):
        here = slice(b * rows, (b + 1) * rows)
        key_s[here, :] = ins[b][:, width : 2 * width]
        value_s[here, :] = ins[b][:, 2 * width : 3 * width]
    for turn, b in enumerate(list(range(blocks - 1, 0, -1)) + [0]):

        def step(i, carry, b=b):
            local = pl.ds(pl.multiple_of(i * q_rows, q_rows), q_rows)
            where = pl.ds(pl.multiple_of(b * rows + i * q_rows, q_rows), q_rows)
            query = ins[b][local, 0:width] * BF16(HEAD**-0.5)
            outputs, sums = [], []
            for head in range(heads):
                masked = one_head(query, head, heads)
                scores = [
                    dot(masked, key_s[j : j + k_rows, :], NT) for j in range(0, length, k_rows)
                ]
                top = None
                for part in scores:
                    part_top = jnp.max(part, axis=1, keepdims=True)
                    top = part_top if top is None else jnp.maximum(top, part_top)
                total = acc = None
                for j, part in enumerate(scores):
                    probs = jnp.exp(part - top)
                    part_total = jnp.sum(probs, axis=1, keepdims=True)
                    value = value_s[j * k_rows : (j + 1) * k_rows, :]
                    part_acc = dot(probs.astype(BF16), value, NN)
                    total = part_total if total is None else total + part_total
                    acc = part_acc if acc is None else acc + part_acc
                outputs.append(acc / total)
                sums.append(jnp.broadcast_to(top + jnp.log(total), (q_rows, width)))
            result = merge_heads(outputs)
            full_ref[where, :] = result
            if b == 0:
                att_ref[0, local, :] = result.astype(BF16)
            else:
                send_s[b - 1, local, :] = result.astype(BF16)
            lse_ref[where, :] = merge_heads(sums)
            return carry

        lax.fori_loop(0, rows // q_rows, step, 0)
        if b > 0:
            att_hop(b).start()
        if 0 < turn < len(bits) - 1:
            level(turn, lambda hop: hop.wait_recv())
            level(turn + 1, lambda hop: hop.start())
    level(len(bits) - 1, lambda hop: hop.wait_recv())
    for number in range(1, len(bits)):
        level(number, lambda hop: hop.wait_send())
    for seg in range(n_f):
        wb_hop(seg).wait()
    for b in range(1, blocks):
        att_hop(b).wait()
    for copy in locals_:
        copy.wait()


def attend(qkv, w_in, wi_got, w_back4, heads, n_f):
    blocks, rows, _ = qkv.shape
    width = heads * HEAD
    length = rows * blocks
    _, half, part = wi_got.shape
    _, _, seg_rows, seg_cols = w_back4.shape
    sds = jax.ShapeDtypeStruct
    in_vmem, anywhere = pl.BlockSpec(memory_space=pltpu.VMEM), pl.BlockSpec(memory_space=pl.ANY)
    dma = pltpu.SemaphoreType.DMA
    return pl.pallas_call(
        partial(attend_kernel, blocks=blocks, heads=heads, n_f=n_f, q_rows=256, k_rows=512),
        out_shape=[
            sds((blocks, rows, width), BF16),
            sds((length, width), F32),
            sds((length, width), F32),
            sds((2 * half, n_f * part), BF16),
            sds((n_f, seg_rows, seg_cols), BF16),
        ],
        in_specs=[in_vmem] + [anywhere] * 3,
        out_specs=[in_vmem] * 3 + [anywhere] * 2,
        scratch_shapes=[pltpu.VMEM((length, width), BF16)] * 2
        + [
            pltpu.VMEM((blocks - 1, rows, width), BF16),
            dma((blocks,)),
            dma((blocks,)),
            dma((2, n_f)),
            dma((2, n_f)),
            dma((n_f,)),
            dma((n_f,)),
            dma((4,)),
        ],
        compiler_params=pltpu.CompilerParams(
            vmem_limit_bytes=VMEM_LIMIT, collective_id=3, has_side_effects=True
        ),
        cost_estimate=pl.CostEstimate(
            flops=16 * length * length * width, bytes_accessed=10 * length * width,
            transcendentals=heads * length * length,
        ),
        name="attend",
    )(qkv, w_in, wi_got, w_back4)


def attend_back_kernel(*refs, blocks, heads, q_rows, k_rows):
    ins = [refs[0].at[b] for b in range(blocks)]
    grads, rest = [refs[1].at[b] for b in range(blocks)], refs[2:]
    full_ref, lse_ref, rest = rest[0], rest[1], rest[2:]
    outs, (lse_t, delta_t, gq_t, key_t) = rest[:blocks], rest[blocks:]
    rows = ins[0].shape[0]
    width = heads * HEAD
    scale = HEAD**-0.5
    chunk = 256
    for b in range(blocks):
        for i in range(0, rows, chunk):
            local = slice(i, i + chunk)
            where = slice(b * rows + i, b * rows + i + chunk)
            logs = lse_ref[where, :].T
            terms = (grads[b][local, :].astype(F32) * full_ref[where, :]).T
            for head in range(heads):
                first = head * HEAD
                lse_t[head : head + 1, where] = logs[first : first + 1]
                delta_t[head : head + 1, where] = jnp.sum(
                    terms[first : first + HEAD], axis=0, keepdims=True
                )
        key_t[:, b * rows : (b + 1) * rows] = ins[b][:, width : 2 * width].T
    gq_t[...] = jnp.zeros_like(gq_t)
    for b in range(blocks):

        def step(j, carry, b=b):
            local = pl.ds(pl.multiple_of(j * k_rows, k_rows), k_rows)
            where = pl.ds(pl.multiple_of(b * rows + j * k_rows, k_rows), k_rows)
            key = ins[b][local, width : 2 * width]
            value = ins[b][local, 2 * width : 3 * width]
            key_grads, value_grads = [], []
            for head in range(heads):
                feats = slice(head * HEAD, (head + 1) * HEAD)
                key_h = one_head(key, head, heads) * BF16(scale)
                value_h = one_head(value, head, heads)
                key_grad = value_grad = None
                for other in range(blocks):
                    for i in range(0, rows, q_rows):
                        here = slice(i, i + q_rows)
                        there = slice(other * rows + i, other * rows + i + q_rows)
                        query = ins[other][here, 0:width]
                        grad = grads[other][here, :]
                        scores = dot(key_h, query, NT)
                        probs = jnp.exp(scores - lse_t[head : head + 1, there])
                        grad_probs = dot(value_h, grad, NT)
                        grad_scores = probs * (grad_probs - delta_t[head : head + 1, there])
                        grad_scores = grad_scores.astype(BF16)
                        term = dot(probs.astype(BF16), grad, NN)
                        value_grad = term if value_grad is None else value_grad + term
                        term = dot(grad_scores, query, NN)
                        key_grad = term if key_grad is None else key_grad + term
                        gq_t[feats, there] += dot(key_t[feats, where], grad_scores, NN)
                key_grads.append(key_grad)
                value_grads.append(value_grad)
            outs[b][local, width : 2 * width] = (merge_heads(key_grads) * scale).astype(BF16)
            outs[b][local, 2 * width : 3 * width] = merge_heads(value_grads).astype(BF16)
            return carry

        lax.fori_loop(0, rows // k_rows, step, 0)
    for b in range(blocks):
        for i in range(0, rows, chunk):
            there = slice(b * rows + i, b * rows + i + chunk)
            outs[b][i : i + chunk, 0:width] = (gq_t[:, there].T * scale).astype(BF16)


def attend_back(qkv, grads, full, lse, heads):
    blocks, rows, _ = qkv.shape
    width = heads * HEAD
    length = rows * blocks
    return pl.pallas_call(
        partial(attend_back_kernel, blocks=blocks, heads=heads, q_rows=256, k_rows=rows),
        out_shape=[jax.ShapeDtypeStruct((rows, 3 * width), BF16)] * blocks,
        scratch_shapes=[
            pltpu.VMEM((8, length), F32),
            pltpu.VMEM((8, length), F32),
            pltpu.VMEM((width, length), F32),
            pltpu.VMEM((width, length), BF16),
        ],
        compiler_params=pltpu.CompilerParams(vmem_limit_bytes=VMEM_LIMIT),
        cost_estimate=pl.CostEstimate(
            flops=40 * length * length * width, bytes_accessed=20 * length * width,
            transcendentals=heads * length * length,
        ),
        name="attend_back",
    )(qkv, grads, full, lse)


def gelu_both(pre):
    slope = math.sqrt(2.0 / math.pi)
    square = pre * pre
    th = jnp.tanh(slope * (pre + 0.044715 * pre * square))
    half = 0.5 * (1.0 + th)
    grad = half + 0.5 * pre * (1.0 - th * th) * (slope * (1.0 + 3 * 0.044715 * square))
    return pre * half, grad


def row_stats(value):
    return jnp.mean(value, axis=1, keepdims=True)


def mid_kernel(*refs, n_f, n_z, cfg):
    att_in, x_ref, cot_ref, vec_ref, bias_ref, wo_ref, wi_ref, wb_ref, got_ref = refs[:9]
    layer_ref, grad_one_ref, ga_ref, sums_ref, bias_sum_ref, grads_out = refs[9:15]
    att_ref, att2_s, h_ref, act_ref, g2_ref, gp_ref, g1_ref, ga_s, turned_s, og_s = refs[15:25]
    wo_s, wi_s, wb_s, slope_s, normed_s, unit_s, acc_s, send_s, recv_s, rstd_s = refs[25:35]
    w_sem, send_sem, recv_sem, b_send, b_recv, a_send, a_recv, g_sem = refs[35:]
    ctx, fs = lax.axis_index("ctx"), lax.axis_index("fsdp")
    core, zed = ctx % 2, ctx // 2
    partner = {"ctx": zed * 2 + (1 - core)}
    rows, width = x_ref.shape
    own, other = slice(0, rows), slice(rows, 2 * rows)
    wide = att_in.shape[2]
    half_in = n_z * wide
    ff_half = wi_s.shape[1]
    step = cfg["step"]
    chunk = cfg["rows"]
    bits, orders = fsdp_orders(n_f)
    _, _, seg_rows, seg_cols = wb_ref.shape

    def wb_place(seg, m):
        return wb_s.at[
            pl.ds(seg * seg_rows, seg_rows), pl.ds(pl.multiple_of((fs ^ m) * seg_cols, 128), seg_cols)
        ]

    def wb_order(seg):
        return orders[seg * 2 // n_f]

    def wb_source(seg, m):
        if m == 0:
            return wb_ref.at[seg, core]
        return got_ref.at[seg] if m == wb_order(seg)[0] else wb_place(seg, m)

    def wb_hop(seg, m, bit):
        return remote(
            wb_source(seg, m), wb_place(seg, m), b_send.at[seg, m ^ bit], b_recv.at[seg, m ^ bit], {"fsdp": fs ^ bit}
        )

    def wb_level(number, act):
        for seg in range(n_f):
            for m in known_at(wb_order(seg), number):
                act(wb_hop(seg, m, wb_order(seg)[number]))

    copies = [
        [pltpu.make_async_copy(wo_ref, wo_s, w_sem.at[0])],
        [pltpu.make_async_copy(wi_ref, wi_s, w_sem.at[1])],
        [],
    ]
    for seg in range(n_f):
        for i, m in enumerate((0, wb_order(seg)[0])):
            copies[2].append(pltpu.make_async_copy(wb_source(seg, m), wb_place(seg, m), w_sem.at[2 + 2 * seg + i]))
    for copy in copies[0] + copies[1]:
        copy.start()
    greet(
        pltpu.get_barrier_semaphore(),
        [partner] + [{"fsdp": fs ^ bit} for bit in bits] + [{"ctx": (zed ^ m) * 2 + core} for m in range(1, n_z)],
    )
    wb_level(1, lambda hop: hop.start())
    for copy in copies[2]:
        copy.start()

    def exchange(n, src, dst):
        return remote(src, dst, send_sem.at[n], recv_sem.at[n], partner)

    def over_cols(total, body):
        def run(i, carry):
            body(pl.ds(pl.multiple_of(i * step, step), step))
            return carry

        lax.fori_loop(0, total // step, run, 0)

    def over_rows(body):
        def run(i, carry):
            return body(pl.ds(pl.multiple_of(i * chunk, chunk), chunk), carry)

        zero = jnp.zeros((1, width), F32)
        return lax.fori_loop(0, rows // chunk, run, (zero, zero, zero))

    if wide % 128 == 0:
        for m in range(n_z):
            att_ref[:, pl.ds(pl.multiple_of((zed ^ m) * wide, wide), wide)] = att_in[m]
    else:
        for m in range(0, n_z, 2):
            one, two = att_in[m].astype(F32), att_in[m + 1].astype(F32)
            odd = zed % 2 == 1
            block = jnp.concatenate([jnp.where(odd, two, one), jnp.where(odd, one, two)], axis=1)
            at = pl.ds(pl.multiple_of((zed // 2 ^ (m // 2)) * 2 * wide, 2 * wide), 2 * wide)
            att_ref[:, at] = block.astype(BF16)

    def wait_all(group):
        for copy in group:
            copy.wait()

    att_move = exchange(6, att_ref, att2_s)
    att_move.start()

    wait_all(copies[0])

    def out_other(cols):
        send_s[:, cols] = dot(att_ref[other, :], wo_s[:, cols], NN)

    over_cols(width, out_other)
    move = exchange(0, send_s, recv_s)
    move.start()

    def out_own(cols):
        part = dot(att_ref[own, :], wo_s[:, cols], NN)
        acc_s[:, cols] = part + x_ref[:, cols].astype(F32) + vec_ref[2:3, cols]

    over_cols(width, out_own)
    move.wait()

    def norm_one(r, carry):
        resid = acc_s[r, :] + recv_s[r, :]
        centre = resid - row_stats(resid)
        rstd = lax.rsqrt(row_stats(centre * centre) + EPS)
        unit = centre * rstd
        normed = unit * vec_ref[3:4, :] + vec_ref[4:5, :]
        unit_s[r, :] = unit
        rstd_s[r, :] = jnp.broadcast_to(rstd, (chunk, 128))
        normed_s[r, :] = normed
        h_ref[r, :] = normed.astype(BF16)
        return carry

    over_rows(norm_one)
    move = exchange(1, h_ref.at[own], h_ref.at[other])
    move.start()

    wait_all(copies[1])

    def up(where):
        def body(cols):
            pre = dot(h_ref[where, :], wi_s[:, cols], NN) + bias_ref[0:1, cols]
            act, slope = gelu_both(pre)
            act_ref[where, cols] = act.astype(BF16)
            slope_s[where, cols] = slope

        over_cols(ff_half, body)

    up(own)
    move.wait()
    up(other)
    for number in range(1, len(bits)):
        wb_level(number, lambda hop: hop.wait_recv())
        if number + 1 < len(bits):
            wb_level(number + 1, lambda hop: hop.start())
    wait_all(copies[2])

    def down_other(cols):
        send_s[:, cols] = dot(act_ref[other, :], wb_s[:, cols], NN)

    over_cols(width, down_other)
    move = exchange(2, send_s, recv_s)
    move.start()

    def down_own(cols):
        part = dot(act_ref[own, :], wb_s[:, cols], NN)
        acc_s[:, cols] = part + normed_s[:, cols] + vec_ref[5:6, cols]

    over_cols(width, down_own)
    move.wait()

    def norm_two(r, carry):
        resid = acc_s[r, :] + recv_s[r, :]
        centre = resid - row_stats(resid)
        rstd = lax.rsqrt(row_stats(centre * centre) + EPS)
        unit = centre * rstd
        gain = vec_ref[6:7, :]
        layer_ref[r, :] = (unit * gain + vec_ref[7:8, :]).astype(BF16)
        grad = cot_ref[r, :]
        scaled = grad * gain
        back = rstd * (scaled - row_stats(scaled) - unit * row_stats(scaled * unit))
        acc_s[r, :] = back
        g2_ref[r, :] = back.astype(BF16)
        sums = (back, grad * unit, grad)
        return tuple(c + jnp.sum(s, axis=0, keepdims=True) for c, s in zip(carry, sums))

    shift_two = over_rows(norm_two)
    move = exchange(3, g2_ref.at[own], g2_ref.at[other])
    move.start()
    for i, total in enumerate(shift_two):
        sums_ref[3 + i : 4 + i, :] = total

    def back_act(where, first):
        def body(cols):
            grad = dot(g2_ref[where, :], wb_s[cols, :], NT) * slope_s[where, cols]
            gp_ref[where, cols] = grad.astype(BF16)
            total = jnp.sum(grad, axis=0, keepdims=True)
            bias_sum_ref[0:1, cols] = total if first else bias_sum_ref[0:1, cols] + total

        over_cols(ff_half, body)

    back_act(own, True)
    move.wait()
    back_act(other, False)

    def back_other(cols):
        send_s[:, cols] = dot(gp_ref[other, :], wi_s[cols, :], NT)

    over_cols(width, back_other)
    move = exchange(4, send_s, recv_s)
    move.start()

    def back_own(cols):
        acc_s[:, cols] += dot(gp_ref[own, :], wi_s[cols, :], NT)

    over_cols(width, back_own)
    move.wait()

    def back_one(r, carry):
        grad = acc_s[r, :] + recv_s[r, :]
        unit = unit_s[r, :]
        rstd = rstd_s[r, 0:1]
        scaled = grad * vec_ref[3:4, :]
        back = rstd * (scaled - row_stats(scaled) - unit * row_stats(scaled * unit))
        grad_one_ref[r, :] = back
        g1_ref[r, :] = back.astype(BF16)
        sums = (back, grad * unit, grad)
        return tuple(c + jnp.sum(s, axis=0, keepdims=True) for c, s in zip(carry, sums))

    shift_one = over_rows(back_one)
    move = exchange(5, g1_ref.at[own], g1_ref.at[other])
    move.start()
    for i, total in enumerate(shift_one):
        sums_ref[i : 1 + i, :] = total
    sums_ref[6:8, :] = jnp.zeros((2, width), F32)

    def att_hop(m):
        return remote(ga_s.at[m - 1], ga_ref.at[m], a_send.at[m], a_recv.at[m], {"ctx": (zed ^ m) * 2 + core})

    move.wait()
    for m in list(range(n_z - 1, 0, -1)) + [0]:
        at = pl.ds(pl.multiple_of((zed ^ m) * wide, wide), wide)
        block = dot(g1_ref[...], wo_s[at, :], NT).astype(BF16)
        if m == 0:
            ga_ref[0] = block
        else:
            ga_s[m - 1] = block
            att_hop(m).start()

    def out_grad(i):
        return pltpu.make_async_copy(
            wi_s.at[:, pl.ds(i % n_out * step, step)], grads_out.at[:, pl.ds(i * step, step)], g_sem.at[i]
        )

    n_out = ff_half // step
    for which, (left, right) in enumerate(((h_ref, gp_ref), (g2_ref, act_ref))):
        for i in range(0, width, 256):
            turned_s[i : i + 256, :] = left[:, i : i + 256].T
        for i in range(n_out):
            if which == 1:
                out_grad(i).wait()

            def rows_of(j, carry, i=i, right=right):
                part = pl.ds(pl.multiple_of(j * 256, 256), 256)
                cols = slice(i * step, (i + 1) * step)
                wi_s[part, cols] = dot(turned_s[part, :], right[:, cols], NN).astype(BF16)
                return carry

            lax.fori_loop(0, width // 256, rows_of, 0)
            out_grad(which * n_out + i).start()
    att_move.wait()
    half = width // 2
    cols = pl.ds(pl.multiple_of(core * half, 128), half)
    for i in range(0, half_in, 256):
        at = pl.ds(pl.multiple_of(core * half + i, 128), 256)
        og_s[at, :] = dot(att_ref[:, i : i + 256].T, g1_ref[:, cols], NN).astype(BF16)
        at = pl.ds(pl.multiple_of((1 - core) * half + i, 128), 256)
        turned = att2_s[:, i : i + 256].T
        og_s[at, :] = (
            dot(turned[:, :rows], g1_ref[rows:, cols], NN) + dot(turned[:, rows:], g1_ref[:rows, cols], NN)
        ).astype(BF16)
    out_move = pltpu.make_async_copy(og_s, grads_out.at[:, pl.ds(2 * ff_half, half)], g_sem.at[2 * n_out])
    out_move.start()
    for number in range(1, len(bits)):
        wb_level(number, lambda hop: hop.wait_send())
    for m in range(1, n_z):
        att_hop(m).wait()
    for i in range(n_out):
        out_grad(n_out + i).wait()
    out_move.wait()


def middle(att, x_own, cot, vectors, bias_half, wo, wi, wb4, got, n_f, n_z):
    rows, width = x_own.shape
    wide = att.shape[2]
    ff_half = bias_half.shape[0]
    half_in = n_z * wide
    sds = jax.ShapeDtypeStruct
    vmem, dma = pltpu.VMEM, pltpu.SemaphoreType.DMA
    in_vmem, anywhere = pl.BlockSpec(memory_space=pltpu.VMEM), pl.BlockSpec(memory_space=pl.ANY)
    cfg = {"step": 512, "rows": 64}
    return pl.pallas_call(
        partial(mid_kernel, n_f=n_f, n_z=n_z, cfg=cfg),
        out_shape=[
            sds((rows, width), BF16),
            sds((rows, width), F32),
            sds((n_z, 2 * rows, wide), BF16),
            sds((8, width), F32),
            sds((1, ff_half), F32),
            sds((width, 2 * ff_half + width // 2), BF16),
        ],
        in_specs=[in_vmem] * 5 + [anywhere] * 4,
        out_specs=[in_vmem] * 5 + [anywhere],
        scratch_shapes=[
            vmem((2 * rows, half_in), BF16),
            vmem((2 * rows, half_in), BF16),
            vmem((2 * rows, width), BF16),
            vmem((2 * rows, ff_half), BF16),
            vmem((2 * rows, width), BF16),
            vmem((2 * rows, ff_half), BF16),
            vmem((2 * rows, width), BF16),
            vmem((n_z - 1, 2 * rows, wide), BF16),
            vmem((width, 2 * rows), BF16),
            vmem((width, width // 2), BF16),
            vmem((half_in, width), BF16),
            vmem((width, ff_half), BF16),
            vmem((ff_half, width), BF16),
            vmem((2 * rows, ff_half), F32),
            vmem((rows, width), F32),
            vmem((rows, width), F32),
            vmem((rows, width), F32),
            vmem((rows, width), F32),
            vmem((rows, width), F32),
            vmem((rows, 128), F32),
            dma((2 + 2 * n_f,)),
            dma((7,)),
            dma((7,)),
            dma((n_f, n_f)),
            dma((n_f, n_f)),
            dma((n_z,)),
            dma((n_z,)),
            dma((2 * (ff_half // cfg["step"]) + 1,)),
        ],
        compiler_params=pltpu.CompilerParams(
            vmem_limit_bytes=VMEM_MIDDLE, collective_id=0, has_side_effects=True
        ),
        cost_estimate=pl.CostEstimate(
            flops=2 * 2 * rows * width * (3 * half_in + 6 * ff_half),
            bytes_accessed=40 << 20, transcendentals=2 * rows * ff_half,
        ),
        name="middle",
    )(att, x_own, cot, vectors, bias_half[None], wo, wi, wb4, got)


def tail_kernel(*refs, n_z):
    g_refs, refs = refs[:n_z], refs[n_z:]
    wl_ref, grad_one_ref, out_ref, cat, send_s, recv_s, send_sem, recv_sem = refs
    ctx = lax.axis_index("ctx")
    core, zed = ctx % 2, ctx // 2
    partner = {"ctx": zed * 2 + (1 - core)}
    rows, width = out_ref.shape
    half = width // 2
    wide = g_refs[0].shape[1] // 3
    barrier = pltpu.get_barrier_semaphore()
    pl.semaphore_signal(barrier, inc=1, device_id=partner, device_id_type=MESH)
    pl.semaphore_wait(barrier, 1)
    for j in range(3):
        part = slice(j * wide, (j + 1) * wide)
        if wide % 128 == 0:
            for m in range(n_z):
                at = pl.ds(pl.multiple_of(j * half + (zed ^ m) * wide, 128), wide)
                cat[:, at] = g_refs[m][:, part]
        else:
            for m in range(0, n_z, 2):
                one, two = g_refs[m][:, part].astype(F32), g_refs[m + 1][:, part].astype(F32)
                odd = zed % 2 == 1
                block = jnp.concatenate([jnp.where(odd, two, one), jnp.where(odd, one, two)], axis=1)
                at = j * half + (zed // 2 ^ (m // 2)) * 2 * wide
                cat[:, pl.ds(pl.multiple_of(at, 128), 2 * wide)] = block.astype(BF16)
    step = 256
    pieces = width // step

    def move(i):
        cols = slice(i * step, (i + 1) * step)
        return pltpu.make_async_remote_copy(
            src_ref=send_s.at[:, cols], dst_ref=recv_s.at[:, cols], send_sem=send_sem.at[i],
            recv_sem=recv_sem.at[i], device_id=partner, device_id_type=MESH,
        )

    for i in range(pieces):
        cols = slice(i * step, (i + 1) * step)
        send_s[:, cols] = dot(cat[rows:, :], wl_ref[cols, :], NT)
        move(i).start()
    for i in range(pieces):
        cols = slice(i * step, (i + 1) * step)
        part = dot(cat[:rows, :], wl_ref[cols, :], NT) + grad_one_ref[:, cols]
        move(i).wait_recv()
        out_ref[:, cols] = part + recv_s[:, cols]
    for i in range(pieces):
        move(i).wait_send()


def tail(grads, w_local, grad_one):
    rows, width = grad_one.shape
    n_z = len(grads)
    return pl.pallas_call(
        partial(tail_kernel, n_z=n_z),
        out_shape=jax.ShapeDtypeStruct((rows, width), F32),
        scratch_shapes=[
            pltpu.VMEM((2 * rows, 3 * width // 2), BF16),
            pltpu.VMEM((rows, width), F32),
            pltpu.VMEM((rows, width), F32),
            pltpu.SemaphoreType.DMA((width // 256,)),
            pltpu.SemaphoreType.DMA((width // 256,)),
        ],
        compiler_params=pltpu.CompilerParams(
            vmem_limit_bytes=VMEM_LIMIT, collective_id=2, has_side_effects=True
        ),
        cost_estimate=pl.CostEstimate(
            flops=6 * rows * width * width, bytes_accessed=12 << 20, transcendentals=0
        ),
        name="tail",
    )(*grads, w_local, grad_one)


def on_device(x_in, w_qkv, w_out, w_in, w_back, vectors, bias_in, cot, *, n_ctx, n_f):
    ctx, fs = lax.axis_index("ctx"), lax.axis_index("fsdp")
    core, zed = ctx % 2, ctx // 2
    n_z = n_ctx // 2
    x_own = x_in[0]
    grad_out = cot[0]
    rows, width = x_own.shape
    hidden = w_back.shape[0]
    half_heads = HEADS // 2
    heads = half_heads // n_z
    wide = heads * HEAD

    def swap(v):
        return lax.ppermute(v, "ctx", [(i, i ^ 1) for i in range(n_ctx)])

    def over_z(v, m):
        return lax.ppermute(v, "ctx", [(i, i ^ (2 * m)) for i in range(n_ctx)])

    def over_f(v, m):
        return lax.ppermute(v, "fsdp", [(i, i ^ m) for i in range(n_f)])

    bits = [1 << b for b in range(n_f.bit_length() - 1)]

    def place(pieces, index, axis):
        count = len(pieces)
        for bit in range(count.bit_length() - 1):
            flag = (index >> bit) & 1
            pieces = [jnp.where(flag, pieces[m ^ (1 << bit)], pieces[m]) for m in range(count)]
        return jnp.concatenate(pieces, axis=axis)

    half_in = width // 2
    first = (core * half_heads + zed * heads) * HEAD
    span = 3 * wide
    bias_qkv = jnp.concatenate(
        [
            lax.dynamic_slice_in_dim(vectors[0], first, wide, 0),
            jnp.zeros((wide,), F32),
            lax.dynamic_slice_in_dim(vectors[1], first, wide, 0),
        ]
    )[None]
    qkv, x_all, w_local, wo_half, wi_got = front(
        x_own, w_qkv, w_out, w_in, bias_qkv, n_f, n_z, heads
    )

    ff_part = w_in.shape[1] // 2
    w_back4 = w_back.reshape(n_f, 2, ff_part, w_back.shape[1])
    att, att_full, lse, wi_half, wb_got = attend(qkv, w_in, wi_got, w_back4, heads, n_f)
    bias_half = lax.dynamic_index_in_dim(
        bias_in.reshape(n_f, 2, ff_part), core, 1, False
    ).reshape(-1)
    layer_out, grad_one, g_att, sums_mid, bias_sum, mid_grads = middle(
        att, x_own, grad_out, vectors, bias_half, wo_half, wi_half, w_back4, wb_got, n_f, n_z
    )
    layer_out = layer_out[None]

    low = width // (n_ctx * n_f)

    def over_fsdp(partial_grad):
        cols = partial_grad.shape[1]
        view = partial_grad.reshape((n_z, 2) + (2,) * len(bits) + (low, cols))
        done = []
        for side in range(2):
            now = view[:, side]
            order = bits if side == 0 else bits[1:] + bits[:1]
            left = list(reversed(bits))
            for bit in order:
                axis = 1 + left.index(bit)
                left.remove(bit)
                flag = (fs // bit) % 2
                stay = lax.dynamic_index_in_dim(now, flag, axis, False)
                go = lax.dynamic_index_in_dim(now, 1 - flag, axis, False)
                now = (stay.astype(F32) + over_f(go, bit).astype(F32)).astype(BF16)
            done.append(now)
        return jnp.stack(done, axis=1)

    def over_ctx(both):
        total = lax.dynamic_index_in_dim(both, zed, 0, False).astype(F32)
        for m in range(1, n_z):
            part = lax.dynamic_index_in_dim(both, zed ^ m, 0, False)
            total = total + over_z(part, m).astype(F32)
        stay = lax.dynamic_index_in_dim(total, core, 0, False)
        go = lax.dynamic_index_in_dim(total, 1 - core, 0, False)
        return stay, swap(go.astype(BF16)).astype(F32)

    def halves(stay, came, parts):
        low = stay.shape[0]
        first = jnp.where(core == 0, stay, came).reshape(low, parts, 1, -1)
        second = jnp.where(core == 0, came, stay).reshape(low, parts, 1, -1)
        return jnp.concatenate([first, second], axis=2).reshape(low, -1)

    def reduced(partial_grad):
        return over_ctx(over_fsdp(partial_grad))

    stay, came = reduced(mid_grads)
    n_half = hidden // 2
    in_weight_grad = halves(stay[:, :n_half], came[:, :n_half], n_f)
    back_weight_grad = halves(stay[:, n_half : 2 * n_half], came[:, n_half : 2 * n_half], n_f).T
    out_weight_grad = halves(stay[:, 2 * n_half :], came[:, 2 * n_half :], 1)

    g_qkv = attend_back(qkv, g_att, att_full, lse, heads)
    g_sent = [g_qkv[m] if m == 0 else over_z(g_qkv[m], m) for m in range(n_z)]
    g_local = jnp.concatenate(g_qkv, axis=0)
    attn_grad = dot(x_all.reshape(-1, width), g_local, TN).astype(BF16)
    both = over_fsdp(attn_grad)
    mine, others = [], []
    for m in range(n_z):
        part = lax.dynamic_index_in_dim(both, zed ^ m, 0, False)
        part = part if m == 0 else over_z(part, m)
        mine.append(lax.dynamic_index_in_dim(part, core, 0, False))
        others.append(lax.dynamic_index_in_dim(part, 1 - core, 0, False))
    others = swap(jnp.stack(others))
    others = [others[m] for m in range(n_z)]

    def heads_order(parts):
        parts = [p.reshape(low, 3, wide) for p in parts]
        return place(parts, zed, 2).astype(F32).reshape(low, -1)

    qkv_weight_grad = halves(heads_order(mine), heads_order(others), 3)
    grad_in = tail(g_sent, w_local, grad_one)

    def spread(half_row, parts):
        piece = half_row.reshape(parts, 1, -1)
        empty = jnp.zeros_like(piece)
        both = jnp.where(core == 0, jnp.concatenate([piece, empty], 1), jnp.concatenate([empty, piece], 1))
        return both.reshape(-1)

    def halve(now):
        left = list(reversed(bits))
        for bit in bits:
            axis = left.index(bit)
            left.remove(bit)
            flag = (fs // bit) % 2
            stay = lax.dynamic_index_in_dim(now, flag, axis, False)
            now = stay + over_f(lax.dynamic_index_in_dim(now, 1 - flag, axis, False), bit)
        return now

    sums = jnp.sum(g_local.astype(F32), axis=0)
    sums = jnp.stack([sums[:wide].reshape(n_f, -1), sums[2 * wide :].reshape(n_f, -1)], axis=1)
    late = halve(sums.reshape((2,) * len(bits) + (-1,)))
    turn = [(2 * z + c, n_z * c + z) for z in range(n_z) for c in range(2)]
    late = lax.ppermute(late, "ctx", turn).reshape(2, -1)
    ratio = hidden // width
    early = sums_mid[:6].T
    bias_terms = spread(bias_sum[0], n_f).reshape(width, ratio)
    table = jnp.concatenate([early, bias_terms], axis=1)
    kinds = table.shape[1]
    now = jnp.swapaxes(table.reshape(n_z * 2, n_f, low, kinds), -1, -2)
    now = jnp.swapaxes(now, 0, 1).reshape((2,) * len(bits) + (n_z, 2, kinds * low))
    now = halve(now)
    total = lax.dynamic_index_in_dim(now, zed, 0, False)
    for m in range(1, n_z):
        total = total + over_z(lax.dynamic_index_in_dim(now, zed ^ m, 0, False), m)
    stay = lax.dynamic_index_in_dim(total, core, 0, False)
    table = stay + swap(lax.dynamic_index_in_dim(total, 1 - core, 0, False))
    table = table.reshape(kinds, low)
    vector_grad = jnp.concatenate([late, table[:6]], axis=0)
    in_bias_grad = table[6:].T.reshape(-1)
    return (
        layer_out,
        grad_in[None],
        qkv_weight_grad,
        out_weight_grad,
        in_weight_grad,
        back_weight_grad,
        vector_grad,
        in_bias_grad,
    )


def solution(mesh):
    tokens = P("fsdp", "ctx", None)
    cols = P(None, "fsdp")
    shared = P(("ctx", "fsdp"), None)
    return jax.shard_map(
        partial(on_device, n_ctx=mesh.shape["ctx"], n_f=mesh.shape["fsdp"]),
        mesh=mesh,
        in_specs=(tokens, cols, cols, cols, cols, P(), P(), tokens),
        out_specs=(
            tokens,
            tokens,
            shared,
            shared,
            shared,
            P(None, ("ctx", "fsdp")),
            P(None, ("ctx", "fsdp")),
            P(("ctx", "fsdp")),
        ),
        check_vma=False,
    )
```

```python
from functools import partial
import math

import jax
import jax.numpy as jnp
from jax import lax
from jax.experimental import pallas as pl
from jax.experimental.pallas import tpu as pltpu
from jax.sharding import PartitionSpec as P

HEADS = 16
HEAD = 64
EPS = 1e-12
F32 = jnp.float32
BF16 = jnp.bfloat16
NN = (((1,), (0,)), ((), ()))
NT = (((1,), (1,)), ((), ()))
TN = (((0,), (0,)), ((), ()))
VMEM_LIMIT = 50 * 1024 * 1024
VMEM_MIDDLE = 56 * 1024 * 1024
MESH = pl.DeviceIdType.MESH


def dot(left, right, dims):
    return lax.dot_general(left, right, dims, preferred_element_type=F32)


def front_kernel(x_ref, wq_ref, wo_ref, wi_ref, bias_ref, qkv_ref, xf_out, wl_out, wo_out, wi_out, *scratch, n_z, n_f, heads):
    xf, wfull, wloc = scratch[:3]
    own_sem, x_send, x_recv, xs_send, xs_recv, w_send, w_recv, ws_send, ws_recv, o_send, o_recv, i_send, i_recv, out_sem = scratch[3:]
    ctx, fs = lax.axis_index("ctx"), lax.axis_index("fsdp")
    core, zed = ctx % 2, ctx // 2
    bits = [1 << b for b in range(n_f.bit_length() - 1)]
    orders = (bits, bits[1:] + bits[:1])
    rows, width = x_ref.shape
    half = width // 2
    quarter = half // 2
    wide = heads * HEAD
    partner = {"ctx": zed * 2 + (1 - core)}

    barrier = pltpu.get_barrier_semaphore()

    def greet(device):
        pl.semaphore_signal(barrier, inc=1, device_id=device, device_id_type=MESH)

    greet(partner)
    for bit in bits:
        greet({"fsdp": fs ^ bit})

    @pl.when(zed > 0)
    def _():
        greet({"ctx": ctx - 2})

    @pl.when(zed < n_z - 1)
    def _():
        greet({"ctx": ctx + 2})

    edges = (zed == 0).astype(jnp.int32) + (zed == n_z - 1).astype(jnp.int32)
    pl.semaphore_wait(barrier, 3 + len(bits) - edges)

    def remote(src, dst, send, recv, device):
        return pltpu.make_async_remote_copy(
            src_ref=src, dst_ref=dst, send_sem=send, recv_sem=recv, device_id=device, device_id_type=MESH
        )

    def x_move(away, step, first):
        block = zed - step * away
        src = x_ref if first else xf.at[block ^ zed, 0]
        index = (step + 1) // 2
        return remote(
            src, xf.at[block ^ (zed + step), 0], x_send.at[index, away], x_recv.at[block ^ (zed + step)],
            {"ctx": ctx + 2 * step},
        )

    def x_swap(m, first=False):
        src = x_ref if first else xf.at[m, 0]
        return remote(src, xf.at[m, 1], xs_send.at[m], xs_recv.at[m], partner)

    def has(step):
        return zed < n_z - 1 if step == 1 else zed > 0

    def came(away, step):
        return zed - away >= 0 if step == 1 else zed + away <= n_z - 1

    for step in (1, -1):

        @pl.when(has(step))
        def _(step=step):
            x_move(0, step, True).start()

    x_swap(0, True).start()
    own_x = pltpu.make_async_copy(x_ref, xf.at[0, 0], own_sem.at[0])
    own_x.start()

    def x_step(away):
        for step in (1, -1):

            @pl.when(came(away, step))
            def _(step=step):
                block = zed - step * away
                remote(
                    xf.at[block ^ zed, 0], xf.at[block ^ zed, 0], x_send.at[0, 0], x_recv.at[block ^ zed], partner
                ).wait_recv()

                @pl.when(has(step))
                def _():
                    x_move(away, step, False).start()

                x_swap(block ^ zed).start()

    def wq_place(side, origin, which):
        cols = wq_ref.shape[1]
        return wfull.at[
            pl.ds(pl.multiple_of(which * half + side * quarter, quarter), quarter),
            pl.ds(pl.multiple_of(origin * cols, 128), cols),
        ]

    def wq_own(side):
        return wq_ref.at[pl.ds(pl.multiple_of(core * half + side * quarter, quarter), quarter), :]

    def wo_place(side, origin):
        cols = wo_ref.shape[1]
        return wo_out.at[pl.ds(side * quarter, quarter), pl.ds(pl.multiple_of(origin * cols, 128), cols)]

    def wo_own(side):
        return wo_ref.at[pl.ds(pl.multiple_of(core * half + side * quarter, quarter), quarter), :]

    def wq_hop(side, m, bit):
        src = wq_own(side) if m == 0 else wq_place(side, fs ^ m, core)
        return remote(src, wq_place(side, fs ^ m, core), w_send.at[side, m ^ bit], w_recv.at[side, m ^ bit], {"fsdp": fs ^ bit})

    def wo_hop(side, m, bit):
        src = wo_own(side) if m == 0 else wo_place(side, fs ^ m)
        return remote(src, wo_place(side, fs ^ m), o_send.at[side, m ^ bit], o_recv.at[side, m ^ bit], {"fsdp": fs ^ bit})

    def wq_swap(side, m):
        src = wq_own(side) if m == 0 else wq_place(side, fs ^ m, core)
        return remote(src, wq_place(side, fs ^ m, core), ws_send.at[side, m], ws_recv.at[side, m], partner)

    own_w = []
    for side in range(2):
        wq_hop(side, 0, orders[side][0]).start()
        wq_swap(side, 0).start()
        own_w.append(pltpu.make_async_copy(wq_own(side), wq_place(side, fs, core), own_sem.at[1 + side]))
        own_w.append(pltpu.make_async_copy(wo_own(side), wo_place(side, fs), own_sem.at[3 + side]))
    for copy in own_w:
        copy.start()

    part = wi_ref.shape[1] // 2

    def wi_hop(side):
        src = wi_ref.at[pl.ds(side * half, half), pl.ds(pl.multiple_of(core * part, 128), part)]
        return remote(src, wi_out.at[side], i_send.at[side], i_recv.at[side], {"fsdp": fs ^ orders[side][0]})

    def doubling(hop, level, after=None):
        for side in range(2):
            known = [0]
            for bit in orders[side][:level]:
                known = known + [m ^ bit for m in known]
            bit = orders[side][level]
            for m in known:
                hop(side, m, bit).wait_recv()
                if after is not None:
                    after(side, m ^ bit).start()
            if level + 1 < len(bits):
                for m in known + [m ^ bit for m in known]:
                    hop(side, m, orders[side][level + 1]).start()

    doubling(wq_hop, 0, wq_swap)
    for side in range(2):
        wo_hop(side, 0, orders[side][0]).start()
    x_step(1)
    for level in range(1, len(bits)):
        doubling(wq_hop, level, wq_swap)
    for side in range(2):
        wi_hop(side).start()
    doubling(wo_hop, 0)
    for away in range(2, n_z - 1):
        x_step(away)
    for copy in own_w:
        copy.wait()
    for side in range(2):
        for m in range(n_f):
            wq_swap_in = remote(
                wq_place(side, fs ^ m, 1 - core), wq_place(side, fs ^ m, 1 - core),
                ws_send.at[side, m], ws_recv.at[side, m], partner,
            )
            wq_swap_in.wait_recv()
    outs = []
    for j in range(3):
        cols = pl.ds(pl.multiple_of(j * width + core * half, 128), half)
        outs.append(pltpu.make_async_copy(wfull.at[:, cols], wl_out.at[:, pl.ds(j * half, half)], out_sem.at[j]))
    for copy in outs:
        copy.start()
    for j in range(3):
        base = j * width + core * half + zed * wide
        if wide % 128 == 0:
            piece = wfull[:, pl.ds(pl.multiple_of(base, 128), wide)]
        else:
            block = wfull[:, pl.ds(pl.multiple_of(base // 128 * 128, 128), 128)].astype(F32)
            piece = jnp.where(zed % 2 == 1, block[:, wide:], block[:, :wide]).astype(BF16)
        wloc[:, j * wide : (j + 1) * wide] = piece

    def x_ready(m, side):
        remote(xf.at[m, side], xf.at[m, side], xs_send.at[m], xs_recv.at[m], partner).wait_recv()

    def project(m):
        def run(side, carry):
            result = dot(xf[m, side], wloc[...], NN) + bias_ref[...]
            where = pl.ds(pl.multiple_of(side * rows, rows), rows)
            qkv_ref[m, where, :] = result.astype(BF16)
            return carry

        lax.fori_loop(0, 2, run, 0)

    own_x.wait()
    x_ready(0, 1)
    project(0)

    def finish(away):
        def run(i, carry):
            block = zed - (1 - 2 * i) * away

            @pl.when((block >= 0) & (block <= n_z - 1))
            def _():
                x_ready(block ^ zed, 1)
                project(block ^ zed)

            return carry

        lax.fori_loop(0, 2, run, 0)

    for away in range(1, n_z - 1):
        finish(away)
    for level in range(1, len(bits)):
        doubling(wo_hop, level)
    if n_z > 2:
        x_step(n_z - 1)
    finish(n_z - 1)
    x_out = pltpu.make_async_copy(xf, xf_out, own_sem.at[5])
    x_out.start()

    for step in (1, -1):

        @pl.when(has(step))
        def _(step=step):
            x_move(0, step, True).wait_send()
            for away in range(1, n_z):

                @pl.when(came(away, step))
                def _(away=away):
                    x_move(away, step, False).wait_send()

    x_swap(0, True).wait_send()
    for m in range(1, n_z):
        x_swap(m).wait_send()
    for side in range(2):
        known = [0]
        for bit in orders[side]:
            for m in known:
                wq_hop(side, m, bit).wait_send()
                wo_hop(side, m, bit).wait_send()
            known = known + [m ^ bit for m in known]
        for m in range(n_f):
            wq_swap(side, m).wait_send()
        wi_hop(side).wait()
    for copy in outs:
        copy.wait()
    x_out.wait()


def front(x_own, w_qkv, w_out, w_in, bias, n_f, n_z, heads):
    rows, width = x_own.shape
    wide = heads * HEAD
    sds = jax.ShapeDtypeStruct
    in_vmem, anywhere = pl.BlockSpec(memory_space=pltpu.VMEM), pl.BlockSpec(memory_space=pl.ANY)
    part = w_in.shape[1] // 2
    dma = pltpu.SemaphoreType.DMA
    return pl.pallas_call(
        partial(front_kernel, n_z=n_z, n_f=n_f, heads=heads),
        out_shape=[
            sds((n_z, 2 * rows, 3 * wide), BF16),
            sds((n_z, 2, rows, width), BF16),
            sds((width, 3 * width // 2), BF16),
            sds((width // 2, width), BF16),
            sds((2, width // 2, part), BF16),
        ],
        in_specs=[anywhere] * 4 + [in_vmem],
        out_specs=[in_vmem] + [anywhere] * 4,
        scratch_shapes=[
            pltpu.VMEM((n_z, 2, rows, width), BF16),
            pltpu.VMEM((width, 3 * width), BF16),
            pltpu.VMEM((width, 3 * wide), BF16),
            dma((6,)),
            dma((2, n_z)),
            dma((n_z,)),
            dma((n_z,)),
            dma((n_z,)),
            dma((2, n_f)),
            dma((2, n_f)),
            dma((2, n_f)),
            dma((2, n_f)),
            dma((2, n_f)),
            dma((2, n_f)),
            dma((2,)),
            dma((2,)),
            dma((3,)),
        ],
        compiler_params=pltpu.CompilerParams(
            vmem_limit_bytes=VMEM_LIMIT, collective_id=1, has_side_effects=True
        ),
        cost_estimate=pl.CostEstimate(
            flops=4 * n_z * rows * width * 3 * wide, bytes_accessed=30 << 20, transcendentals=0
        ),
        name="front",
    )(x_own, w_qkv, w_out, w_in, bias)


def one_head(block, head, heads):
    if heads == 1:
        return block
    lane = lax.broadcasted_iota(jnp.int32, block.shape, 1)
    return jnp.where(lane // HEAD == head, block, jnp.zeros_like(block))


def merge_heads(parts):
    if len(parts) == 1:
        return parts[0]
    lane = lax.broadcasted_iota(jnp.int32, parts[0].shape, 1)
    result = parts[0]
    for head in range(1, len(parts)):
        result = jnp.where(lane // HEAD == head, parts[head], result)
    return result


def remote(src, dst, send, recv, device):
    return pltpu.make_async_remote_copy(
        src_ref=src, dst_ref=dst, send_sem=send, recv_sem=recv, device_id=device, device_id_type=MESH
    )


def greet(barrier, devices):
    for device in devices:
        pl.semaphore_signal(barrier, inc=1, device_id=device, device_id_type=MESH)
    pl.semaphore_wait(barrier, len(devices))


def fsdp_orders(n_f):
    bits = [1 << b for b in range(n_f.bit_length() - 1)]
    return bits, (bits, bits[1:] + bits[:1])


def known_at(order, level):
    known = [0]
    for bit in order[:level]:
        known = known + [m ^ bit for m in known]
    return known


def attend_kernel(*refs, blocks, heads, n_f, q_rows, k_rows):
    qkv_ref, wi_ref, got_ref, wb_ref = refs[:4]
    att_ref, full_ref, lse_ref, wi_out, wb_out = refs[4:9]
    key_s, value_s, send_s, a_send, a_recv, i_send, i_recv, b_send, b_recv, own_sem = refs[9:]
    ins = [qkv_ref.at[b] for b in range(blocks)]
    rows = ins[0].shape[0]
    width = heads * HEAD
    length = rows * blocks
    ctx, fs = lax.axis_index("ctx"), lax.axis_index("fsdp")
    core, zed = ctx % 2, ctx // 2
    bits, orders = fsdp_orders(n_f)
    greet(
        pltpu.get_barrier_semaphore(),
        [{"fsdp": fs ^ bit} for bit in bits] + [{"ctx": (zed ^ m) * 2 + core} for m in range(1, blocks)],
    )

    half, part = got_ref.shape[1:]

    def wi_place(side, m):
        return wi_out.at[pl.ds(side * half, half), pl.ds(pl.multiple_of((fs ^ m) * part, 128), part)]

    def wi_source(side, m):
        if m == 0:
            return wi_ref.at[pl.ds(side * half, half), pl.ds(pl.multiple_of(core * part, 128), part)]
        return got_ref.at[side] if m == orders[side][0] else wi_place(side, m)

    def wi_hop(side, m, bit):
        return remote(
            wi_source(side, m), wi_place(side, m), i_send.at[side, m ^ bit], i_recv.at[side, m ^ bit], {"fsdp": fs ^ bit}
        )

    def wb_hop(seg):
        return remote(
            wb_ref.at[seg, core], wb_out.at[seg], b_send.at[seg], b_recv.at[seg],
            {"fsdp": fs ^ orders[seg * 2 // n_f][0]},
        )

    def level(number, act):
        for side in range(2):
            for m in known_at(orders[side], number):
                act(wi_hop(side, m, orders[side][number]))

    locals_ = []
    for side in range(2):
        for i, m in enumerate((0, orders[side][0])):
            locals_.append(pltpu.make_async_copy(wi_source(side, m), wi_place(side, m), own_sem.at[2 * side + i]))
    for copy in locals_:
        copy.start()
    level(1, lambda hop: hop.start())
    for seg in range(n_f):
        wb_hop(seg).start()

    def att_hop(b):
        return remote(send_s.at[b - 1], att_ref.at[b], a_send.at[b], a_recv.at[b], {"ctx": (zed ^ b) * 2 + core})

    for b in range(blocks):
        here = slice(b * rows, (b + 1) * rows)
        key_s[here, :] = ins[b][:, width : 2 * width]
        value_s[here, :] = ins[b][:, 2 * width : 3 * width]
    for turn, b in enumerate(list(range(blocks - 1, 0, -1)) + [0]):

        def step(i, carry, b=b):
            local = pl.ds(pl.multiple_of(i * q_rows, q_rows), q_rows)
            where = pl.ds(pl.multiple_of(b * rows + i * q_rows, q_rows), q_rows)
            query = ins[b][local, 0:width] * BF16(HEAD**-0.5)
            outputs, sums = [], []
            for head in range(heads):
                masked = one_head(query, head, heads)
                scores = [
                    dot(masked, key_s[j : j + k_rows, :], NT) for j in range(0, length, k_rows)
                ]
                top = None
                for part in scores:
                    part_top = jnp.max(part, axis=1, keepdims=True)
                    top = part_top if top is None else jnp.maximum(top, part_top)
                total = acc = None
                for j, part in enumerate(scores):
                    probs = jnp.exp(part - top)
                    part_total = jnp.sum(probs, axis=1, keepdims=True)
                    value = value_s[j * k_rows : (j + 1) * k_rows, :]
                    part_acc = dot(probs.astype(BF16), value, NN)
                    total = part_total if total is None else total + part_total
                    acc = part_acc if acc is None else acc + part_acc
                outputs.append(acc / total)
                sums.append(jnp.broadcast_to(top + jnp.log(total), (q_rows, width)))
            result = merge_heads(outputs)
            full_ref[where, :] = result
            if b == 0:
                att_ref[0, local, :] = result.astype(BF16)
            else:
                send_s[b - 1, local, :] = result.astype(BF16)
            lse_ref[where, :] = merge_heads(sums)
            return carry

        lax.fori_loop(0, rows // q_rows, step, 0)
        if b > 0:
            att_hop(b).start()
        if 0 < turn < len(bits) - 1:
            level(turn, lambda hop: hop.wait_recv())
            level(turn + 1, lambda hop: hop.start())
    level(len(bits) - 1, lambda hop: hop.wait_recv())
    for number in range(1, len(bits)):
        level(number, lambda hop: hop.wait_send())
    for seg in range(n_f):
        wb_hop(seg).wait()
    for b in range(1, blocks):
        att_hop(b).wait()
    for copy in locals_:
        copy.wait()


def attend(qkv, w_in, wi_got, w_back4, heads, n_f):
    blocks, rows, _ = qkv.shape
    width = heads * HEAD
    length = rows * blocks
    _, half, part = wi_got.shape
    _, _, seg_rows, seg_cols = w_back4.shape
    sds = jax.ShapeDtypeStruct
    in_vmem, anywhere = pl.BlockSpec(memory_space=pltpu.VMEM), pl.BlockSpec(memory_space=pl.ANY)
    dma = pltpu.SemaphoreType.DMA
    return pl.pallas_call(
        partial(attend_kernel, blocks=blocks, heads=heads, n_f=n_f, q_rows=256, k_rows=512),
        out_shape=[
            sds((blocks, rows, width), BF16),
            sds((length, width), F32),
            sds((length, width), F32),
            sds((2 * half, n_f * part), BF16),
            sds((n_f, seg_rows, seg_cols), BF16),
        ],
        in_specs=[in_vmem] + [anywhere] * 3,
        out_specs=[in_vmem] * 3 + [anywhere] * 2,
        scratch_shapes=[pltpu.VMEM((length, width), BF16)] * 2
        + [
            pltpu.VMEM((blocks - 1, rows, width), BF16),
            dma((blocks,)),
            dma((blocks,)),
            dma((2, n_f)),
            dma((2, n_f)),
            dma((n_f,)),
            dma((n_f,)),
            dma((4,)),
        ],
        compiler_params=pltpu.CompilerParams(
            vmem_limit_bytes=VMEM_LIMIT, collective_id=3, has_side_effects=True
        ),
        cost_estimate=pl.CostEstimate(
            flops=16 * length * length * width, bytes_accessed=10 * length * width,
            transcendentals=heads * length * length,
        ),
        name="attend",
    )(qkv, w_in, wi_got, w_back4)


def gelu_both(pre):
    slope = math.sqrt(2.0 / math.pi)
    square = pre * pre
    th = jnp.tanh(slope * (pre + 0.044715 * pre * square))
    half = 0.5 * (1.0 + th)
    grad = half + 0.5 * pre * (1.0 - th * th) * (slope * (1.0 + 3 * 0.044715 * square))
    return pre * half, grad


def row_stats(value):
    return jnp.mean(value, axis=1, keepdims=True)


def mid_kernel(*refs, n_f, n_z, cfg):
    att_in, x_ref, cot_ref, vec_ref, bias_ref, wo_ref, wi_ref, wb_ref, got_ref = refs[:9]
    layer_ref, grad_one_ref, ga_ref, sums_ref, bias_sum_ref, grads_out = refs[9:15]
    att_ref, att2_s, h_ref, act_ref, g2_ref, gp_ref, g1_ref, ga_s, turned_s, og_s = refs[15:25]
    wo_s, wi_s, wb_s, slope_s, normed_s, unit_s, acc_s, send_s, recv_s, rstd_s = refs[25:35]
    w_sem, send_sem, recv_sem, b_send, b_recv, a_send, a_recv, g_sem = refs[35:]
    ctx, fs = lax.axis_index("ctx"), lax.axis_index("fsdp")
    core, zed = ctx % 2, ctx // 2
    partner = {"ctx": zed * 2 + (1 - core)}
    rows, width = x_ref.shape
    own, other = slice(0, rows), slice(rows, 2 * rows)
    wide = att_in.shape[2]
    half_in = n_z * wide
    ff_half = wi_s.shape[1]
    step = cfg["step"]
    chunk = cfg["rows"]
    bits, orders = fsdp_orders(n_f)
    _, _, seg_rows, seg_cols = wb_ref.shape

    def wb_place(seg, m):
        return wb_s.at[
            pl.ds(seg * seg_rows, seg_rows), pl.ds(pl.multiple_of((fs ^ m) * seg_cols, 128), seg_cols)
        ]

    def wb_order(seg):
        return orders[seg * 2 // n_f]

    def wb_source(seg, m):
        if m == 0:
            return wb_ref.at[seg, core]
        return got_ref.at[seg] if m == wb_order(seg)[0] else wb_place(seg, m)

    def wb_hop(seg, m, bit):
        return remote(
            wb_source(seg, m), wb_place(seg, m), b_send.at[seg, m ^ bit], b_recv.at[seg, m ^ bit], {"fsdp": fs ^ bit}
        )

    def wb_level(number, act):
        for seg in range(n_f):
            for m in known_at(wb_order(seg), number):
                act(wb_hop(seg, m, wb_order(seg)[number]))

    copies = [
        [pltpu.make_async_copy(wo_ref, wo_s, w_sem.at[0])],
        [pltpu.make_async_copy(wi_ref, wi_s, w_sem.at[1])],
        [],
    ]
    for seg in range(n_f):
        for i, m in enumerate((0, wb_order(seg)[0])):
            copies[2].append(pltpu.make_async_copy(wb_source(seg, m), wb_place(seg, m), w_sem.at[2 + 2 * seg + i]))
    for copy in copies[0] + copies[1]:
        copy.start()
    greet(
        pltpu.get_barrier_semaphore(),
        [partner] + [{"fsdp": fs ^ bit} for bit in bits] + [{"ctx": (zed ^ m) * 2 + core} for m in range(1, n_z)],
    )
    wb_level(1, lambda hop: hop.start())
    for copy in copies[2]:
        copy.start()

    def exchange(n, src, dst):
        return remote(src, dst, send_sem.at[n], recv_sem.at[n], partner)

    def over_cols(total, body):
        def run(i, carry):
            body(pl.ds(pl.multiple_of(i * step, step), step))
            return carry

        lax.fori_loop(0, total // step, run, 0)

    def over_rows(body):
        def run(i, carry):
            return body(pl.ds(pl.multiple_of(i * chunk, chunk), chunk), carry)

        zero = jnp.zeros((1, width), F32)
        return lax.fori_loop(0, rows // chunk, run, (zero, zero, zero))

    if wide % 128 == 0:
        for m in range(n_z):
            att_ref[:, pl.ds(pl.multiple_of((zed ^ m) * wide, wide), wide)] = att_in[m]
    else:
        for m in range(0, n_z, 2):
            one, two = att_in[m].astype(F32), att_in[m + 1].astype(F32)
            odd = zed % 2 == 1
            block = jnp.concatenate([jnp.where(odd, two, one), jnp.where(odd, one, two)], axis=1)
            at = pl.ds(pl.multiple_of((zed // 2 ^ (m // 2)) * 2 * wide, 2 * wide), 2 * wide)
            att_ref[:, at] = block.astype(BF16)

    def wait_all(group):
        for copy in group:
            copy.wait()

    att_move = exchange(6, att_ref, att2_s)
    att_move.start()

    wait_all(copies[0])

    def out_other(cols):
        send_s[:, cols] = dot(att_ref[other, :], wo_s[:, cols], NN)

    over_cols(width, out_other)
    move = exchange(0, send_s, recv_s)
    move.start()

    def out_own(cols):
        part = dot(att_ref[own, :], wo_s[:, cols], NN)
        acc_s[:, cols] = part + x_ref[:, cols].astype(F32) + vec_ref[2:3, cols]

    over_cols(width, out_own)
    move.wait()

    def norm_one(r, carry):
        resid = acc_s[r, :] + recv_s[r, :]
        centre = resid - row_stats(resid)
        rstd = lax.rsqrt(row_stats(centre * centre) + EPS)
        unit = centre * rstd
        normed = unit * vec_ref[3:4, :] + vec_ref[4:5, :]
        unit_s[r, :] = unit
        rstd_s[r, :] = jnp.broadcast_to(rstd, (chunk, 128))
        normed_s[r, :] = normed
        h_ref[r, :] = normed.astype(BF16)
        return carry

    over_rows(norm_one)
    move = exchange(1, h_ref.at[own], h_ref.at[other])
    move.start()

    wait_all(copies[1])

    def up(where):
        def body(cols):
            pre = dot(h_ref[where, :], wi_s[:, cols], NN) + bias_ref[0:1, cols]
            act, slope = gelu_both(pre)
            act_ref[where, cols] = act.astype(BF16)
            slope_s[where, cols] = slope

        over_cols(ff_half, body)

    up(own)
    move.wait()
    up(other)
    for number in range(1, len(bits)):
        wb_level(number, lambda hop: hop.wait_recv())
        if number + 1 < len(bits):
            wb_level(number + 1, lambda hop: hop.start())
    wait_all(copies[2])

    def down_other(cols):
        send_s[:, cols] = dot(act_ref[other, :], wb_s[:, cols], NN)

    over_cols(width, down_other)
    move = exchange(2, send_s, recv_s)
    move.start()

    def down_own(cols):
        part = dot(act_ref[own, :], wb_s[:, cols], NN)
        acc_s[:, cols] = part + normed_s[:, cols] + vec_ref[5:6, cols]

    over_cols(width, down_own)
    move.wait()

    def norm_two(r, carry):
        resid = acc_s[r, :] + recv_s[r, :]
        centre = resid - row_stats(resid)
        rstd = lax.rsqrt(row_stats(centre * centre) + EPS)
        unit = centre * rstd
        gain = vec_ref[6:7, :]
        layer_ref[r, :] = (unit * gain + vec_ref[7:8, :]).astype(BF16)
        grad = cot_ref[r, :]
        scaled = grad * gain
        back = rstd * (scaled - row_stats(scaled) - unit * row_stats(scaled * unit))
        acc_s[r, :] = back
        g2_ref[r, :] = back.astype(BF16)
        sums = (back, grad * unit, grad)
        return tuple(c + jnp.sum(s, axis=0, keepdims=True) for c, s in zip(carry, sums))

    shift_two = over_rows(norm_two)
    move = exchange(3, g2_ref.at[own], g2_ref.at[other])
    move.start()
    for i, total in enumerate(shift_two):
        sums_ref[3 + i : 4 + i, :] = total

    def back_act(where, first):
        def body(cols):
            grad = dot(g2_ref[where, :], wb_s[cols, :], NT) * slope_s[where, cols]
            gp_ref[where, cols] = grad.astype(BF16)
            total = jnp.sum(grad, axis=0, keepdims=True)
            bias_sum_ref[0:1, cols] = total if first else bias_sum_ref[0:1, cols] + total

        over_cols(ff_half, body)

    back_act(own, True)
    move.wait()
    back_act(other, False)

    def back_other(cols):
        send_s[:, cols] = dot(gp_ref[other, :], wi_s[cols, :], NT)

    over_cols(width, back_other)
    move = exchange(4, send_s, recv_s)
    move.start()

    def back_own(cols):
        acc_s[:, cols] += dot(gp_ref[own, :], wi_s[cols, :], NT)

    over_cols(width, back_own)
    move.wait()

    def back_one(r, carry):
        grad = acc_s[r, :] + recv_s[r, :]
        unit = unit_s[r, :]
        rstd = rstd_s[r, 0:1]
        scaled = grad * vec_ref[3:4, :]
        back = rstd * (scaled - row_stats(scaled) - unit * row_stats(scaled * unit))
        grad_one_ref[r, :] = back
        g1_ref[r, :] = back.astype(BF16)
        sums = (back, grad * unit, grad)
        return tuple(c + jnp.sum(s, axis=0, keepdims=True) for c, s in zip(carry, sums))

    shift_one = over_rows(back_one)
    move = exchange(5, g1_ref.at[own], g1_ref.at[other])
    move.start()
    for i, total in enumerate(shift_one):
        sums_ref[i : 1 + i, :] = total
    sums_ref[6:8, :] = jnp.zeros((2, width), F32)

    def att_hop(m):
        return remote(ga_s.at[m - 1], ga_ref.at[m], a_send.at[m], a_recv.at[m], {"ctx": (zed ^ m) * 2 + core})

    move.wait()
    for m in list(range(n_z - 1, 0, -1)) + [0]:
        at = pl.ds(pl.multiple_of((zed ^ m) * wide, wide), wide)
        block = dot(g1_ref[...], wo_s[at, :], NT).astype(BF16)
        if m == 0:
            ga_ref[0] = block
        else:
            ga_s[m - 1] = block
            att_hop(m).start()

    def out_grad(i):
        return pltpu.make_async_copy(
            wi_s.at[:, pl.ds(i % n_out * step, step)], grads_out.at[:, pl.ds(i * step, step)], g_sem.at[i]
        )

    n_out = ff_half // step
    for which, (left, right) in enumerate(((h_ref, gp_ref), (g2_ref, act_ref))):
        for i in range(0, width, 256):
            turned_s[i : i + 256, :] = left[:, i : i + 256].T
        for i in range(n_out):
            if which == 1:
                out_grad(i).wait()

            def rows_of(j, carry, i=i, right=right):
                part = pl.ds(pl.multiple_of(j * 256, 256), 256)
                cols = slice(i * step, (i + 1) * step)
                wi_s[part, cols] = dot(turned_s[part, :], right[:, cols], NN).astype(BF16)
                return carry

            lax.fori_loop(0, width // 256, rows_of, 0)
            out_grad(which * n_out + i).start()
    att_move.wait()
    half = width // 2
    cols = pl.ds(pl.multiple_of(core * half, 128), half)
    for i in range(0, half_in, 256):
        at = pl.ds(pl.multiple_of(core * half + i, 128), 256)
        og_s[at, :] = dot(att_ref[:, i : i + 256].T, g1_ref[:, cols], NN).astype(BF16)
        at = pl.ds(pl.multiple_of((1 - core) * half + i, 128), 256)
        turned = att2_s[:, i : i + 256].T
        og_s[at, :] = (
            dot(turned[:, :rows], g1_ref[rows:, cols], NN) + dot(turned[:, rows:], g1_ref[:rows, cols], NN)
        ).astype(BF16)
    out_move = pltpu.make_async_copy(og_s, grads_out.at[:, pl.ds(2 * ff_half, half)], g_sem.at[2 * n_out])
    out_move.start()
    for number in range(1, len(bits)):
        wb_level(number, lambda hop: hop.wait_send())
    for m in range(1, n_z):
        att_hop(m).wait()
    for i in range(n_out):
        out_grad(n_out + i).wait()
    out_move.wait()


def middle(att, x_own, cot, vectors, bias_half, wo, wi, wb4, got, n_f, n_z):
    rows, width = x_own.shape
    wide = att.shape[2]
    ff_half = bias_half.shape[0]
    half_in = n_z * wide
    sds = jax.ShapeDtypeStruct
    vmem, dma = pltpu.VMEM, pltpu.SemaphoreType.DMA
    in_vmem, anywhere = pl.BlockSpec(memory_space=pltpu.VMEM), pl.BlockSpec(memory_space=pl.ANY)
    cfg = {"step": 512, "rows": 64}
    return pl.pallas_call(
        partial(mid_kernel, n_f=n_f, n_z=n_z, cfg=cfg),
        out_shape=[
            sds((rows, width), BF16),
            sds((rows, width), F32),
            sds((n_z, 2 * rows, wide), BF16),
            sds((8, width), F32),
            sds((1, ff_half), F32),
            sds((width, 2 * ff_half + width // 2), BF16),
        ],
        in_specs=[in_vmem] * 5 + [anywhere] * 4,
        out_specs=[in_vmem] * 5 + [anywhere],
        scratch_shapes=[
            vmem((2 * rows, half_in), BF16),
            vmem((2 * rows, half_in), BF16),
            vmem((2 * rows, width), BF16),
            vmem((2 * rows, ff_half), BF16),
            vmem((2 * rows, width), BF16),
            vmem((2 * rows, ff_half), BF16),
            vmem((2 * rows, width), BF16),
            vmem((n_z - 1, 2 * rows, wide), BF16),
            vmem((width, 2 * rows), BF16),
            vmem((width, width // 2), BF16),
            vmem((half_in, width), BF16),
            vmem((width, ff_half), BF16),
            vmem((ff_half, width), BF16),
            vmem((2 * rows, ff_half), F32),
            vmem((rows, width), F32),
            vmem((rows, width), F32),
            vmem((rows, width), F32),
            vmem((rows, width), F32),
            vmem((rows, width), F32),
            vmem((rows, 128), F32),
            dma((2 + 2 * n_f,)),
            dma((7,)),
            dma((7,)),
            dma((n_f, n_f)),
            dma((n_f, n_f)),
            dma((n_z,)),
            dma((n_z,)),
            dma((2 * (ff_half // cfg["step"]) + 1,)),
        ],
        compiler_params=pltpu.CompilerParams(
            vmem_limit_bytes=VMEM_MIDDLE, collective_id=0, has_side_effects=True
        ),
        cost_estimate=pl.CostEstimate(
            flops=2 * 2 * rows * width * (3 * half_in + 6 * ff_half),
            bytes_accessed=40 << 20, transcendentals=2 * rows * ff_half,
        ),
        name="middle",
    )(att, x_own, cot, vectors, bias_half[None], wo, wi, wb4, got)


class Reduction:
    def __init__(self, src, cols, acc, got, far, sems, n_f, n_z):
        self.src, self.cols, self.acc, self.got, self.far = src, cols, acc, got, far
        self.load_sem, self.f_send, self.f_recv, self.z_send, self.z_recv = sems
        self.n_z = n_z
        ctx, self.fs = lax.axis_index("ctx"), lax.axis_index("fsdp")
        self.core, self.zed = ctx % 2, ctx // 2
        self.bits, self.orders = fsdp_orders(n_f)
        self.last = len(self.bits) - 1

    def targets(self, side, level):
        found = [0]
        for bit in reversed(self.orders[side][level + 1 :]):
            found = found + [d ^ bit for d in found]
        return found

    def part(self, side, target):
        return self.src.at[:, side, target, :, self.cols]

    def load(self, side, i):
        d = self.targets(side, 0)[i]
        return pltpu.make_async_copy(self.part(side, self.fs ^ d), self.acc.at[side, i], self.load_sem.at[side, i])

    def hop(self, side, level, i):
        bit = self.orders[side][level]
        first = sum(len(self.targets(side, l)) for l in range(level))
        if level == 0:
            src = self.part(side, self.fs ^ bit ^ self.targets(side, 0)[i])
        else:
            src = self.acc.at[side, len(self.targets(side, level)) + i]
        return remote(
            src, self.got.at[side, first + i], self.f_send.at[side, first + i], self.f_recv.at[side, first + i],
            {"fsdp": self.fs ^ bit},
        )

    def every(self, level, act):
        for side in range(2):
            for i in range(len(self.targets(side, level))):
                act(self.hop(side, level, i))

    def loads(self, act):
        for side in range(2):
            for i in range(len(self.targets(side, 0))):
                act(self.load(side, i))

    def start(self):
        self.every(0, lambda hop: hop.start())
        self.loads(lambda copy: copy.start())

    def level(self, level):
        if level == 0:
            self.loads(lambda copy: copy.wait())
        self.every(level, lambda hop: hop.wait_recv())
        first = sum(len(self.targets(0, l)) for l in range(level))
        count = len(self.targets(0, level))

        def add(n, carry):
            side, rest = n // (count * self.n_z), n % (count * self.n_z)
            i, z = rest // self.n_z, rest % self.n_z
            total = self.acc[side, i, z].astype(F32) + self.got[side, first + i, z].astype(F32)
            self.acc[side, i, z] = total.astype(BF16)
            return carry

        lax.fori_loop(0, 2 * count * self.n_z, add, 0)
        if level < self.last:
            self.every(level + 1, lambda hop: hop.start())
        else:
            self.z_every(lambda hop: hop.start())

    def z_every(self, act):
        for m in range(self.n_z - 1, 0, -1):
            for side in range(2):
                act(
                    remote(
                        self.acc.at[side, 0, self.zed ^ m], self.far.at[side, m - 1], self.z_send.at[side, m - 1],
                        self.z_recv.at[side, m - 1], {"ctx": (self.zed ^ m) * 2 + self.core},
                    )
                )

    def arrived(self):
        self.z_every(lambda hop: hop.wait_recv())

    def total(self, side):
        result = self.acc[side, 0, self.zed].astype(F32)
        for m in range(1, self.n_z):
            result = result + self.far[side, m - 1].astype(F32)
        return result

    def sent(self):
        for level in range(self.last + 1):
            self.every(level, lambda hop: hop.wait_send())
        self.z_every(lambda hop: hop.wait_send())


def back_kernel(*refs, blocks, heads, n_f, reduce, cut, q_rows, steps_per):
    refs = list(refs)

    def take(count):
        taken = refs[:count]
        del refs[:count]
        return taken

    qkv_ref, ga_ref, full_ref, lse_ref, grad_one_ref, wl_hbm = take(6)
    if reduce:
        x_hbm, g_hbm = take(2)
    out_ref, sums_ref = take(2)
    if reduce:
        stay_ref, came_ref, mine_ref, others_ref = take(4)
        (stage,) = take(1)
    else:
        (stage,) = take(1)
    lse_t, delta_t, gq_t, key_t, gin, wl_s, cat, send_s, recv_s = take(9)
    kv_send, kv_recv, q_send, q_recv, t_send, t_recv, own_sem = take(7)
    if reduce:
        x_s, gq_src, give_s, c_send, c_recv, o_send, o_recv = take(7)
        bufs = [take(8) for _ in range(3)]
    ctx, fs = lax.axis_index("ctx"), lax.axis_index("fsdp")
    core, zed = ctx % 2, ctx // 2
    partner = {"ctx": zed * 2 + (1 - core)}
    bits, orders = fsdp_orders(n_f)
    rows = qkv_ref.shape[1]
    width = heads * HEAD
    scale = HEAD**-0.5
    chunk = 256
    half = wl_s.shape[1] // 3
    greeted = [partner] + [{"ctx": (zed ^ m) * 2 + core} for m in range(1, blocks)]
    if reduce:
        greeted += [{"fsdp": fs ^ bit} for bit in bits]
    greet(pltpu.get_barrier_semaphore(), greeted)
    wl_copy = pltpu.make_async_copy(wl_hbm, wl_s, own_sem.at[0])
    wl_copy.start()
    if reduce:
        columns = g_hbm.shape[-1]
        early, late, attn = [
            Reduction(src, cols, buf[0], buf[1], buf[2], buf[3:], n_f, blocks)
            for buf, src, cols in zip(
                bufs,
                (g_hbm, g_hbm, gq_src),
                (pl.ds(0, cut), pl.ds(cut, columns - cut), pl.ds(0, 3 * width)),
            )
        ]
        early.start()
        x_copy = pltpu.make_async_copy(x_hbm, x_s, own_sem.at[1])
        x_copy.start()

    for b in range(blocks):
        for i in range(0, rows, chunk):
            local = slice(i, i + chunk)
            where = slice(b * rows + i, b * rows + i + chunk)
            logs = lse_ref[where, :].T
            terms = (ga_ref[b, local, :].astype(F32) * full_ref[where, :]).T
            for head in range(heads):
                first = head * HEAD
                lse_t[head : head + 1, where] = logs[first : first + 1]
                delta_t[head : head + 1, where] = jnp.sum(
                    terms[first : first + HEAD], axis=0, keepdims=True
                )
        key_t[:, b * rows : (b + 1) * rows] = qkv_ref[b, :, width : 2 * width].T
    gq_t[...] = jnp.zeros_like(gq_t)

    split = width % 128 == 0

    def kv_hop(m):
        return remote(
            stage.at[m, :, pl.ds(width, 2 * width)], gin.at[m, :, pl.ds(width, 2 * width)], kv_send.at[m], kv_recv.at[m],
            {"ctx": (zed ^ m) * 2 + core},
        )

    def q_hop(m):
        cols = pl.ds(0, width if split else 3 * width)
        return remote(
            stage.at[m, :, cols], gin.at[m, :, cols], q_send.at[m], q_recv.at[m], {"ctx": (zed ^ m) * 2 + core}
        )

    k_rows = rows // steps_per

    def step(n, carry):
        b = blocks - 1 - n // steps_per
        start = n % steps_per * k_rows
        local = pl.ds(pl.multiple_of(start, 128), k_rows)
        where = pl.ds(pl.multiple_of(b * rows + start, 128), k_rows)
        key = qkv_ref[b, local, width : 2 * width]
        value = qkv_ref[b, local, 2 * width : 3 * width]
        key_grads, value_grads = [], []
        for head in range(heads):
            feats = slice(head * HEAD, (head + 1) * HEAD)
            key_h = one_head(key, head, heads) * BF16(scale)
            value_h = one_head(value, head, heads)
            key_grad = value_grad = None
            for other in range(blocks):
                for i in range(0, rows, q_rows):
                    here = slice(i, i + q_rows)
                    there = slice(other * rows + i, other * rows + i + q_rows)
                    query = qkv_ref[other, here, 0:width]
                    grad = ga_ref[other, here, :]
                    scores = dot(key_h, query, NT)
                    probs = jnp.exp(scores - lse_t[head : head + 1, there])
                    grad_probs = dot(value_h, grad, NT)
                    grad_scores = probs * (grad_probs - delta_t[head : head + 1, there])
                    grad_scores = grad_scores.astype(BF16)
                    term = dot(probs.astype(BF16), grad, NN)
                    value_grad = term if value_grad is None else value_grad + term
                    term = dot(grad_scores, query, NN)
                    key_grad = term if key_grad is None else key_grad + term
                    gq_t[feats, there] += dot(key_t[feats, where], grad_scores, NN)
            key_grads.append(key_grad)
            value_grads.append(value_grad)
        stage[b, local, width : 2 * width] = (merge_heads(key_grads) * scale).astype(BF16)
        stage[b, local, 2 * width : 3 * width] = merge_heads(value_grads).astype(BF16)
        if split:

            @pl.when((n % steps_per == steps_per - 1) & (b > 0))
            def _():
                kv_hop(b).start()

        if reduce:

            @pl.when(n == 3)
            def _():
                early.level(0)

            @pl.when(n == 5)
            def _():
                for level in range(1, len(bits)):
                    early.level(level)
                late.start()

        return carry

    lax.fori_loop(0, blocks * steps_per, step, 0)
    for b in range(blocks - 1, -1, -1):
        for i in range(0, rows, chunk):
            there = slice(b * rows + i, b * rows + i + chunk)
            stage[b, i : i + chunk, 0:width] = (gq_t[:, there].T * scale).astype(BF16)
        if b > 0:
            q_hop(b).start()
    gin[0] = stage[0]
    sums = jnp.zeros((1, 3 * width), F32)
    for b in range(blocks):
        sums = sums + jnp.sum(stage[b].astype(F32), axis=0, keepdims=True)
    sums_ref[...] = sums

    if reduce:
        x_copy.wait()
        d_rows = x_s.shape[-1] // blocks
        low = gq_src.shape[3]
        for b in range(blocks):
            cat[0 : 3 * width, b * rows : (b + 1) * rows] = stage[b].T
        for z in range(blocks):
            cols = slice(z * d_rows, (z + 1) * d_rows)
            total = None
            for b in range(blocks):
                x_block = x_s[b, :, :, cols].reshape(rows, d_rows)
                term = dot(cat[0 : 3 * width, b * rows : (b + 1) * rows], x_block, NN)
                total = term if total is None else total + term
            gq_src[z] = total.T.astype(BF16).reshape(2, n_f, low, 3 * width)
        attn.start()
        late.level(0)
        for level in range(len(bits)):
            attn.level(level)
        for level in range(1, len(bits)):
            late.level(level)

    for m in range(blocks - 1, 0, -1):
        if split:
            kv_hop(m).wait()
        q_hop(m).wait()
    wl_copy.wait()
    for j in range(3):
        part = slice(j * width, (j + 1) * width)
        if split:
            for m in range(blocks):
                at = pl.ds(pl.multiple_of(j * half + (zed ^ m) * width, 128), width)
                cat[0:rows, at] = gin[m, :, part]
        else:
            for m in range(0, blocks, 2):
                one, two = gin[m, :, part].astype(F32), gin[m + 1, :, part].astype(F32)
                odd = zed % 2 == 1
                block = jnp.concatenate([jnp.where(odd, two, one), jnp.where(odd, one, two)], axis=1)
                at = j * half + (zed // 2 ^ (m // 2)) * 2 * width
                cat[0:rows, pl.ds(pl.multiple_of(at, 128), 2 * width)] = block.astype(BF16)
    tokens, dim = out_ref.shape
    pieces = dim // 256

    def swap_hop(i):
        cols = slice(i * 256, (i + 1) * 256)
        return remote(send_s.at[:, cols], recv_s.at[:, cols], t_send.at[i], t_recv.at[i], partner)

    for i in range(pieces):
        cols = slice(i * 256, (i + 1) * 256)
        send_s[:, cols] = dot(cat[tokens:rows, 0 : 3 * half], wl_s[cols, :], NT)
        swap_hop(i).start()
    for i in range(pieces):
        cols = slice(i * 256, (i + 1) * 256)
        out_ref[:, cols] = dot(cat[0:tokens, 0 : 3 * half], wl_s[cols, :], NT) + grad_one_ref[:, cols]
    for i in range(pieces):
        cols = slice(i * 256, (i + 1) * 256)
        swap_hop(i).wait_recv()
        out_ref[:, cols] += recv_s[:, cols]
    for i in range(pieces):
        swap_hop(i).wait_send()

    if reduce:
        attn.arrived()

        def other_hop(m):
            src = attn.acc.at[1 - core, 0, zed] if m == 0 else attn.far.at[1 - core, m - 1]
            return remote(src, others_ref.at[m], o_send.at[m], o_recv.at[m], partner)

        for m in range(blocks):
            other_hop(m).start()
            mine_ref[m] = attn.acc[core, 0, zed] if m == 0 else attn.far[core, m - 1]

        def give_hop(i, cols):
            return remote(give_s.at[:, cols], came_ref.at[:, cols], c_send.at[i], c_recv.at[i], partner)

        for i, which in enumerate((early, late)):
            which.arrived()
            give_s[:, which.cols] = which.total(1 - core)
            give_hop(i, which.cols).start()
            stay_ref[:, which.cols] = which.total(core)
        for which in (early, late, attn):
            which.sent()
        for i, which in enumerate((early, late)):
            give_hop(i, which.cols).wait()
        for m in range(blocks):
            other_hop(m).wait()


def back(qkv, grads, full, lse, grad_one, w_local, x_all, mid_grads, heads, n_f, reduce, cut=0):
    blocks, rows, _ = qkv.shape
    width = heads * HEAD
    length = rows * blocks
    tokens, dim = grad_one.shape
    sds = jax.ShapeDtypeStruct
    vmem, dma = pltpu.VMEM, pltpu.SemaphoreType.DMA
    in_vmem, anywhere = pl.BlockSpec(memory_space=pltpu.VMEM), pl.BlockSpec(memory_space=pl.ANY)
    operands = [qkv, grads, full, lse, grad_one, w_local]
    out_shape = [sds((tokens, dim), F32), sds((1, 3 * width), F32)]
    staged = (blocks, rows, 3 * width)
    scratch = [
        vmem((8, length), F32),
        vmem((8, length), F32),
        vmem((width, length), F32),
        vmem((width, length), BF16),
        vmem(staged, BF16),
        vmem(w_local.shape, BF16),
        vmem((rows, max(length, w_local.shape[1])), BF16),
        vmem((tokens, dim), F32),
        vmem((tokens, dim), F32),
        dma((blocks,)),
        dma((blocks,)),
        dma((blocks,)),
        dma((blocks,)),
        dma((dim // 256,)),
        dma((dim // 256,)),
        dma((2,)),
    ]
    if reduce:
        _, _, _, low, columns = mid_grads.shape
        operands += [x_all, mid_grads]
        out_shape += [sds((low, columns), F32)] * 2 + [sds((blocks, low, 3 * width), BF16)] * 2
        scratch = [vmem(staged, BF16)] + scratch
        scratch += [
            vmem(x_all.shape, BF16),
            vmem((blocks, 2, n_f, low, 3 * width), BF16),
            vmem((low, columns), F32),
            dma((2,)),
            dma((2,)),
            dma((blocks,)),
            dma((blocks,)),
        ]
        for cols in (cut, columns - cut, 3 * width):
            scratch += [
                vmem((2, n_f // 2, blocks, low, cols), BF16),
                vmem((2, n_f - 1, blocks, low, cols), BF16),
                vmem((2, blocks - 1, low, cols), BF16),
                dma((2, n_f // 2)),
                dma((2, n_f - 1)),
                dma((2, n_f - 1)),
                dma((2, blocks - 1)),
                dma((2, blocks - 1)),
            ]
    else:
        out_shape += [sds(staged, BF16)]
    return pl.pallas_call(
        partial(
            back_kernel, blocks=blocks, heads=heads, n_f=n_f, reduce=reduce, cut=cut, q_rows=256, steps_per=2
        ),
        out_shape=out_shape,
        in_specs=[in_vmem] * 5 + [anywhere] * (len(operands) - 5),
        out_specs=[in_vmem] * len(out_shape),
        scratch_shapes=scratch,
        compiler_params=pltpu.CompilerParams(
            vmem_limit_bytes=VMEM_MIDDLE, collective_id=2, has_side_effects=True
        ),
        cost_estimate=pl.CostEstimate(
            flops=40 * length * length * width, bytes_accessed=30 << 20,
            transcendentals=heads * length * length,
        ),
        name="back",
    )(*operands)


def on_device(x_in, w_qkv, w_out, w_in, w_back, vectors, bias_in, cot, *, n_ctx, n_f):
    ctx, fs = lax.axis_index("ctx"), lax.axis_index("fsdp")
    core, zed = ctx % 2, ctx // 2
    n_z = n_ctx // 2
    x_own = x_in[0]
    grad_out = cot[0]
    rows, width = x_own.shape
    hidden = w_back.shape[0]
    half_heads = HEADS // 2
    heads = half_heads // n_z
    wide = heads * HEAD

    def swap(v):
        return lax.ppermute(v, "ctx", [(i, i ^ 1) for i in range(n_ctx)])

    def over_z(v, m):
        return lax.ppermute(v, "ctx", [(i, i ^ (2 * m)) for i in range(n_ctx)])

    def over_f(v, m):
        return lax.ppermute(v, "fsdp", [(i, i ^ m) for i in range(n_f)])

    bits = [1 << b for b in range(n_f.bit_length() - 1)]

    def place(pieces, index, axis):
        count = len(pieces)
        for bit in range(count.bit_length() - 1):
            flag = (index >> bit) & 1
            pieces = [jnp.where(flag, pieces[m ^ (1 << bit)], pieces[m]) for m in range(count)]
        return jnp.concatenate(pieces, axis=axis)

    half_in = width // 2
    first = (core * half_heads + zed * heads) * HEAD
    span = 3 * wide
    bias_qkv = jnp.concatenate(
        [
            lax.dynamic_slice_in_dim(vectors[0], first, wide, 0),
            jnp.zeros((wide,), F32),
            lax.dynamic_slice_in_dim(vectors[1], first, wide, 0),
        ]
    )[None]
    qkv, x_all, w_local, wo_half, wi_got = front(
        x_own, w_qkv, w_out, w_in, bias_qkv, n_f, n_z, heads
    )

    ff_part = w_in.shape[1] // 2
    w_back4 = w_back.reshape(n_f, 2, ff_part, w_back.shape[1])
    att, att_full, lse, wi_half, wb_got = attend(qkv, w_in, wi_got, w_back4, heads, n_f)
    bias_half = lax.dynamic_index_in_dim(
        bias_in.reshape(n_f, 2, ff_part), core, 1, False
    ).reshape(-1)
    layer_out, grad_one, g_att, sums_mid, bias_sum, mid_grads = middle(
        att, x_own, grad_out, vectors, bias_half, wo_half, wi_half, w_back4, wb_got, n_f, n_z
    )
    layer_out = layer_out[None]

    low = width // (n_ctx * n_f)

    def over_fsdp(partial_grad):
        cols = partial_grad.shape[1]
        view = partial_grad.reshape((n_z, 2) + (2,) * len(bits) + (low, cols))
        done = []
        for side in range(2):
            now = view[:, side]
            order = bits if side == 0 else bits[1:] + bits[:1]
            left = list(reversed(bits))
            for bit in order:
                axis = 1 + left.index(bit)
                left.remove(bit)
                flag = (fs // bit) % 2
                stay = lax.dynamic_index_in_dim(now, flag, axis, False)
                go = lax.dynamic_index_in_dim(now, 1 - flag, axis, False)
                now = (stay.astype(F32) + over_f(go, bit).astype(F32)).astype(BF16)
            done.append(now)
        return jnp.stack(done, axis=1)

    def over_ctx(both):
        total = lax.dynamic_index_in_dim(both, zed, 0, False).astype(F32)
        for m in range(1, n_z):
            part = lax.dynamic_index_in_dim(both, zed ^ m, 0, False)
            total = total + over_z(part, m).astype(F32)
        stay = lax.dynamic_index_in_dim(total, core, 0, False)
        go = lax.dynamic_index_in_dim(total, 1 - core, 0, False)
        return stay, swap(go.astype(BF16)).astype(F32)

    def halves(stay, came, parts):
        low = stay.shape[0]
        first = jnp.where(core == 0, stay, came).reshape(low, parts, 1, -1)
        second = jnp.where(core == 0, came, stay).reshape(low, parts, 1, -1)
        return jnp.concatenate([first, second], axis=2).reshape(low, -1)

    def reduced(partial_grad):
        return over_ctx(over_fsdp(partial_grad))

    in_kernel = low % 16 == 0 and wide % 128 == 0
    if in_kernel:
        grad_in, sums, stay, came, mine, others = back(
            qkv, g_att, att_full, lse, grad_one, w_local, x_all,
            mid_grads.reshape(n_z, 2, n_f, low, -1), heads, n_f, True, hidden // 2,
        )
        mine = [mine[m] for m in range(n_z)]
        others = [others[m] for m in range(n_z)]
    else:
        stay, came = reduced(mid_grads)
        grad_in, sums, g_local = back(
            qkv, g_att, att_full, lse, grad_one, w_local, None, None, heads, n_f, False
        )
        attn_grad = dot(x_all.reshape(-1, width), g_local.reshape(-1, span), TN).astype(BF16)
        both = over_fsdp(attn_grad)
        mine, others = [], []
        for m in range(n_z):
            part = lax.dynamic_index_in_dim(both, zed ^ m, 0, False)
            part = part if m == 0 else over_z(part, m)
            mine.append(lax.dynamic_index_in_dim(part, core, 0, False))
            others.append(lax.dynamic_index_in_dim(part, 1 - core, 0, False))
        others = swap(jnp.stack(others))
        others = [others[m] for m in range(n_z)]
    n_half = hidden // 2
    in_weight_grad = halves(stay[:, :n_half], came[:, :n_half], n_f)
    back_weight_grad = halves(stay[:, n_half : 2 * n_half], came[:, n_half : 2 * n_half], n_f).T
    out_weight_grad = halves(stay[:, 2 * n_half :], came[:, 2 * n_half :], 1)

    def heads_order(parts):
        parts = [p.reshape(low, 3, wide) for p in parts]
        return place(parts, zed, 2).astype(F32).reshape(low, -1)

    qkv_weight_grad = halves(heads_order(mine), heads_order(others), 3)

    def spread(half_row, parts):
        piece = half_row.reshape(parts, 1, -1)
        empty = jnp.zeros_like(piece)
        both = jnp.where(core == 0, jnp.concatenate([piece, empty], 1), jnp.concatenate([empty, piece], 1))
        return both.reshape(-1)

    def halve(now):
        left = list(reversed(bits))
        for bit in bits:
            axis = left.index(bit)
            left.remove(bit)
            flag = (fs // bit) % 2
            stay = lax.dynamic_index_in_dim(now, flag, axis, False)
            now = stay + over_f(lax.dynamic_index_in_dim(now, 1 - flag, axis, False), bit)
        return now

    sums = sums[0]
    sums = jnp.stack([sums[:wide].reshape(n_f, -1), sums[2 * wide :].reshape(n_f, -1)], axis=1)
    late = halve(sums.reshape((2,) * len(bits) + (-1,)))
    turn = [(2 * z + c, n_z * c + z) for z in range(n_z) for c in range(2)]
    late = lax.ppermute(late, "ctx", turn).reshape(2, -1)
    ratio = hidden // width
    early = sums_mid[:6].T
    bias_terms = spread(bias_sum[0], n_f).reshape(width, ratio)
    table = jnp.concatenate([early, bias_terms], axis=1)
    kinds = table.shape[1]
    now = jnp.swapaxes(table.reshape(n_z * 2, n_f, low, kinds), -1, -2)
    now = jnp.swapaxes(now, 0, 1).reshape((2,) * len(bits) + (n_z, 2, kinds * low))
    now = halve(now)
    total = lax.dynamic_index_in_dim(now, zed, 0, False)
    for m in range(1, n_z):
        total = total + over_z(lax.dynamic_index_in_dim(now, zed ^ m, 0, False), m)
    stay = lax.dynamic_index_in_dim(total, core, 0, False)
    table = stay + swap(lax.dynamic_index_in_dim(total, 1 - core, 0, False))
    table = table.reshape(kinds, low)
    vector_grad = jnp.concatenate([late, table[:6]], axis=0)
    in_bias_grad = table[6:].T.reshape(-1)
    return (
        layer_out,
        grad_in[None],
        qkv_weight_grad,
        out_weight_grad,
        in_weight_grad,
        back_weight_grad,
        vector_grad,
        in_bias_grad,
    )


def solution(mesh):
    tokens = P("fsdp", "ctx", None)
    cols = P(None, "fsdp")
    shared = P(("ctx", "fsdp"), None)
    return jax.shard_map(
        partial(on_device, n_ctx=mesh.shape["ctx"], n_f=mesh.shape["fsdp"]),
        mesh=mesh,
        in_specs=(tokens, cols, cols, cols, cols, P(), P(), tokens),
        out_specs=(
            tokens,
            tokens,
            shared,
            shared,
            shared,
            P(None, ("ctx", "fsdp")),
            P(None, ("ctx", "fsdp")),
            P(("ctx", "fsdp")),
        ),
        check_vma=False,
    )
```

```python
from functools import partial
import math

import jax
import jax.numpy as jnp
from jax import lax
from jax.experimental import pallas as pl
from jax.experimental.pallas import tpu as pltpu
from jax.sharding import PartitionSpec as P

HEADS = 16
HEAD = 64
EPS = 1e-12
F32 = jnp.float32
BF16 = jnp.bfloat16
NN = (((1,), (0,)), ((), ()))
NT = (((1,), (1,)), ((), ()))
TN = (((0,), (0,)), ((), ()))
VMEM_LIMIT = 50 * 1024 * 1024
VMEM_MIDDLE = 56 * 1024 * 1024
MESH = pl.DeviceIdType.MESH


def dot(left, right, dims):
    return lax.dot_general(left, right, dims, preferred_element_type=F32)


def front_kernel(
    x_ref, wq_ref, wo_ref, wi_ref, wb_ref, bias_ref, qkv_ref, xf_out, wl_out, wo_out, wi_out, wb_out, *scratch, n_z, n_f, heads
):
    xf, wfull, wloc = scratch[:3]
    own_sem, x_send, x_recv, xs_send, xs_recv, w_send, w_recv, ws_send, ws_recv, o_send, o_recv, i_send, i_recv, b_send, b_recv, out_sem = scratch[3:]
    ctx, fs = lax.axis_index("ctx"), lax.axis_index("fsdp")
    core, zed = ctx % 2, ctx // 2
    bits = [1 << b for b in range(n_f.bit_length() - 1)]
    orders = (bits, bits[1:] + bits[:1])
    rows, width = x_ref.shape
    half = width // 2
    quarter = half // 2
    wide = heads * HEAD
    partner = {"ctx": zed * 2 + (1 - core)}

    barrier = pltpu.get_barrier_semaphore()

    def greet(device):
        pl.semaphore_signal(barrier, inc=1, device_id=device, device_id_type=MESH)

    greet(partner)
    for bit in bits:
        greet({"fsdp": fs ^ bit})

    @pl.when(zed > 0)
    def _():
        greet({"ctx": ctx - 2})

    @pl.when(zed < n_z - 1)
    def _():
        greet({"ctx": ctx + 2})

    edges = (zed == 0).astype(jnp.int32) + (zed == n_z - 1).astype(jnp.int32)
    pl.semaphore_wait(barrier, 3 + len(bits) - edges)

    def remote(src, dst, send, recv, device):
        return pltpu.make_async_remote_copy(
            src_ref=src, dst_ref=dst, send_sem=send, recv_sem=recv, device_id=device, device_id_type=MESH
        )

    def x_move(away, step, first):
        block = zed - step * away
        src = x_ref if first else xf.at[block ^ zed, 0]
        index = (step + 1) // 2
        return remote(
            src, xf.at[block ^ (zed + step), 0], x_send.at[index, away], x_recv.at[block ^ (zed + step)],
            {"ctx": ctx + 2 * step},
        )

    def x_swap(m, first=False):
        src = x_ref if first else xf.at[m, 0]
        return remote(src, xf.at[m, 1], xs_send.at[m], xs_recv.at[m], partner)

    def has(step):
        return zed < n_z - 1 if step == 1 else zed > 0

    def came(away, step):
        return zed - away >= 0 if step == 1 else zed + away <= n_z - 1

    for step in (1, -1):

        @pl.when(has(step))
        def _(step=step):
            x_move(0, step, True).start()

    x_swap(0, True).start()
    own_x = pltpu.make_async_copy(x_ref, xf.at[0, 0], own_sem.at[0])
    own_x.start()

    def x_step(away):
        for step in (1, -1):

            @pl.when(came(away, step))
            def _(step=step):
                block = zed - step * away
                remote(
                    xf.at[block ^ zed, 0], xf.at[block ^ zed, 0], x_send.at[0, 0], x_recv.at[block ^ zed], partner
                ).wait_recv()

                @pl.when(has(step))
                def _():
                    x_move(away, step, False).start()

                x_swap(block ^ zed).start()

    def wq_place(side, origin, which):
        cols = wq_ref.shape[1]
        return wfull.at[
            pl.ds(pl.multiple_of(which * half + side * quarter, quarter), quarter),
            pl.ds(pl.multiple_of(origin * cols, 128), cols),
        ]

    def wq_own(side):
        return wq_ref.at[pl.ds(pl.multiple_of(core * half + side * quarter, quarter), quarter), :]

    def wo_place(side, origin):
        cols = wo_ref.shape[1]
        return wo_out.at[pl.ds(side * quarter, quarter), pl.ds(pl.multiple_of(origin * cols, 128), cols)]

    def wo_own(side):
        return wo_ref.at[pl.ds(pl.multiple_of(core * half + side * quarter, quarter), quarter), :]

    def wq_hop(side, m, bit):
        src = wq_own(side) if m == 0 else wq_place(side, fs ^ m, core)
        return remote(src, wq_place(side, fs ^ m, core), w_send.at[side, m ^ bit], w_recv.at[side, m ^ bit], {"fsdp": fs ^ bit})

    def wo_hop(side, m, bit):
        src = wo_own(side) if m == 0 else wo_place(side, fs ^ m)
        return remote(src, wo_place(side, fs ^ m), o_send.at[side, m ^ bit], o_recv.at[side, m ^ bit], {"fsdp": fs ^ bit})

    def wq_swap(side, m):
        src = wq_own(side) if m == 0 else wq_place(side, fs ^ m, core)
        return remote(src, wq_place(side, fs ^ m, core), ws_send.at[side, m], ws_recv.at[side, m], partner)

    own_w = []
    for side in range(2):
        wq_hop(side, 0, orders[side][0]).start()
        wq_swap(side, 0).start()
        own_w.append(pltpu.make_async_copy(wq_own(side), wq_place(side, fs, core), own_sem.at[1 + side]))
        own_w.append(pltpu.make_async_copy(wo_own(side), wo_place(side, fs), own_sem.at[3 + side]))
    for copy in own_w:
        copy.start()

    part = wi_ref.shape[1] // 2

    def wi_hop(side):
        src = wi_ref.at[pl.ds(side * half, half), pl.ds(pl.multiple_of(core * part, 128), part)]
        return remote(src, wi_out.at[side], i_send.at[side], i_recv.at[side], {"fsdp": fs ^ orders[side][0]})

    def wb_hop(seg):
        return remote(
            wb_ref.at[seg, core], wb_out.at[seg], b_send.at[seg], b_recv.at[seg],
            {"fsdp": fs ^ orders[seg * 2 // n_f][0]},
        )

    def doubling(hop, level, after=None):
        for side in range(2):
            known = [0]
            for bit in orders[side][:level]:
                known = known + [m ^ bit for m in known]
            bit = orders[side][level]
            for m in known:
                hop(side, m, bit).wait_recv()
                if after is not None:
                    after(side, m ^ bit).start()
            if level + 1 < len(bits):
                for m in known + [m ^ bit for m in known]:
                    hop(side, m, orders[side][level + 1]).start()

    doubling(wq_hop, 0, wq_swap)
    for side in range(2):
        wo_hop(side, 0, orders[side][0]).start()
    x_step(1)
    for level in range(1, len(bits)):
        doubling(wq_hop, level, wq_swap)
    for side in range(2):
        wi_hop(side).start()
    doubling(wo_hop, 0)
    for seg in range(n_f):
        wb_hop(seg).start()
    for away in range(2, n_z - 1):
        x_step(away)
    for copy in own_w:
        copy.wait()
    for side in range(2):
        for m in range(n_f):
            wq_swap_in = remote(
                wq_place(side, fs ^ m, 1 - core), wq_place(side, fs ^ m, 1 - core),
                ws_send.at[side, m], ws_recv.at[side, m], partner,
            )
            wq_swap_in.wait_recv()
    outs = []
    for j in range(3):
        cols = pl.ds(pl.multiple_of(j * width + core * half, 128), half)
        outs.append(pltpu.make_async_copy(wfull.at[:, cols], wl_out.at[:, pl.ds(j * half, half)], out_sem.at[j]))
    for copy in outs:
        copy.start()
    for j in range(3):
        base = j * width + core * half + zed * wide
        if wide % 128 == 0:
            piece = wfull[:, pl.ds(pl.multiple_of(base, 128), wide)]
        else:
            block = wfull[:, pl.ds(pl.multiple_of(base // 128 * 128, 128), 128)].astype(F32)
            piece = jnp.where(zed % 2 == 1, block[:, wide:], block[:, :wide]).astype(BF16)
        wloc[:, j * wide : (j + 1) * wide] = piece

    def x_ready(m, side):
        remote(xf.at[m, side], xf.at[m, side], xs_send.at[m], xs_recv.at[m], partner).wait_recv()

    def project(m):
        def run(side, carry):
            result = dot(xf[m, side], wloc[...], NN) + bias_ref[...]
            where = pl.ds(pl.multiple_of(side * rows, rows), rows)
            qkv_ref[m, where, :] = result.astype(BF16)
            return carry

        lax.fori_loop(0, 2, run, 0)

    own_x.wait()
    x_ready(0, 1)
    project(0)

    def finish(away):
        def run(i, carry):
            block = zed - (1 - 2 * i) * away

            @pl.when((block >= 0) & (block <= n_z - 1))
            def _():
                x_ready(block ^ zed, 1)
                project(block ^ zed)

            return carry

        lax.fori_loop(0, 2, run, 0)

    for away in range(1, n_z - 1):
        finish(away)
    for level in range(1, len(bits)):
        doubling(wo_hop, level)
    if n_z > 2:
        x_step(n_z - 1)
    finish(n_z - 1)
    x_out = pltpu.make_async_copy(xf, xf_out, own_sem.at[5])
    x_out.start()

    for step in (1, -1):

        @pl.when(has(step))
        def _(step=step):
            x_move(0, step, True).wait_send()
            for away in range(1, n_z):

                @pl.when(came(away, step))
                def _(away=away):
                    x_move(away, step, False).wait_send()

    x_swap(0, True).wait_send()
    for m in range(1, n_z):
        x_swap(m).wait_send()
    for side in range(2):
        known = [0]
        for bit in orders[side]:
            for m in known:
                wq_hop(side, m, bit).wait_send()
                wo_hop(side, m, bit).wait_send()
            known = known + [m ^ bit for m in known]
        for m in range(n_f):
            wq_swap(side, m).wait_send()
        wi_hop(side).wait()
    for seg in range(n_f):
        wb_hop(seg).wait()
    for copy in outs:
        copy.wait()
    x_out.wait()


def front(x_own, w_qkv, w_out, w_in, w_back4, bias, n_f, n_z, heads):
    rows, width = x_own.shape
    wide = heads * HEAD
    sds = jax.ShapeDtypeStruct
    in_vmem, anywhere = pl.BlockSpec(memory_space=pltpu.VMEM), pl.BlockSpec(memory_space=pl.ANY)
    part = w_in.shape[1] // 2
    dma = pltpu.SemaphoreType.DMA
    return pl.pallas_call(
        partial(front_kernel, n_z=n_z, n_f=n_f, heads=heads),
        out_shape=[
            sds((n_z, 2 * rows, 3 * wide), BF16),
            sds((n_z, 2, rows, width), BF16),
            sds((width, 3 * width // 2), BF16),
            sds((width // 2, width), BF16),
            sds((2, width // 2, part), BF16),
            sds((n_f,) + w_back4.shape[2:], BF16),
        ],
        in_specs=[anywhere] * 5 + [in_vmem],
        out_specs=[in_vmem] + [anywhere] * 5,
        scratch_shapes=[
            pltpu.VMEM((n_z, 2, rows, width), BF16),
            pltpu.VMEM((width, 3 * width), BF16),
            pltpu.VMEM((width, 3 * wide), BF16),
            dma((6,)),
            dma((2, n_z)),
            dma((n_z,)),
            dma((n_z,)),
            dma((n_z,)),
            dma((2, n_f)),
            dma((2, n_f)),
            dma((2, n_f)),
            dma((2, n_f)),
            dma((2, n_f)),
            dma((2, n_f)),
            dma((2,)),
            dma((2,)),
            dma((n_f,)),
            dma((n_f,)),
            dma((3,)),
        ],
        compiler_params=pltpu.CompilerParams(
            vmem_limit_bytes=VMEM_LIMIT, collective_id=1, has_side_effects=True
        ),
        cost_estimate=pl.CostEstimate(
            flops=4 * n_z * rows * width * 3 * wide, bytes_accessed=30 << 20, transcendentals=0
        ),
        name="front",
    )(x_own, w_qkv, w_out, w_in, w_back4, bias)


def one_head(block, head, heads):
    if heads == 1:
        return block
    lane = lax.broadcasted_iota(jnp.int32, block.shape, 1)
    return jnp.where(lane // HEAD == head, block, jnp.zeros_like(block))


def merge_heads(parts):
    if len(parts) == 1:
        return parts[0]
    lane = lax.broadcasted_iota(jnp.int32, parts[0].shape, 1)
    result = parts[0]
    for head in range(1, len(parts)):
        result = jnp.where(lane // HEAD == head, parts[head], result)
    return result


def remote(src, dst, send, recv, device):
    return pltpu.make_async_remote_copy(
        src_ref=src, dst_ref=dst, send_sem=send, recv_sem=recv, device_id=device, device_id_type=MESH
    )


def greet(barrier, devices):
    for device in devices:
        pl.semaphore_signal(barrier, inc=1, device_id=device, device_id_type=MESH)
    pl.semaphore_wait(barrier, len(devices))


def fsdp_orders(n_f):
    bits = [1 << b for b in range(n_f.bit_length() - 1)]
    return bits, (bits, bits[1:] + bits[:1])


def known_at(order, level):
    known = [0]
    for bit in order[:level]:
        known = known + [m ^ bit for m in known]
    return known


def attend_kernel(*refs, blocks, heads, n_f, q_rows, k_rows):
    qkv_ref, wi_ref, got_ref, wb_ref = refs[:4]
    att_ref, full_ref, lse_ref, wi_out, wb_out = refs[4:9]
    key_s, value_s, send_s, a_send, a_recv, i_send, i_recv, b_send, b_recv, own_sem = refs[9:]
    ins = [qkv_ref.at[b] for b in range(blocks)]
    rows = ins[0].shape[0]
    width = heads * HEAD
    length = rows * blocks
    ctx, fs = lax.axis_index("ctx"), lax.axis_index("fsdp")
    core, zed = ctx % 2, ctx // 2
    bits, orders = fsdp_orders(n_f)
    greet(
        pltpu.get_barrier_semaphore(),
        [{"fsdp": fs ^ bit} for bit in bits] + [{"ctx": (zed ^ m) * 2 + core} for m in range(1, blocks)],
    )

    half, part = got_ref.shape[1:]

    def wi_place(side, m):
        return wi_out.at[pl.ds(side * half, half), pl.ds(pl.multiple_of((fs ^ m) * part, 128), part)]

    def wi_source(side, m):
        if m == 0:
            return wi_ref.at[pl.ds(side * half, half), pl.ds(pl.multiple_of(core * part, 128), part)]
        return got_ref.at[side] if m == orders[side][0] else wi_place(side, m)

    def wi_hop(side, m, bit):
        return remote(
            wi_source(side, m), wi_place(side, m), i_send.at[side, m ^ bit], i_recv.at[side, m ^ bit], {"fsdp": fs ^ bit}
        )

    def wb_hop(seg):
        return remote(
            wb_ref.at[seg, core], wb_out.at[seg], b_send.at[seg], b_recv.at[seg],
            {"fsdp": fs ^ orders[seg * 2 // n_f][1]},
        )

    def level(number, act):
        for side in range(2):
            for m in known_at(orders[side], number):
                act(wi_hop(side, m, orders[side][number]))

    locals_ = []
    for side in range(2):
        for i, m in enumerate((0, orders[side][0])):
            locals_.append(pltpu.make_async_copy(wi_source(side, m), wi_place(side, m), own_sem.at[2 * side + i]))
    for copy in locals_:
        copy.start()
    level(1, lambda hop: hop.start())
    for seg in range(n_f):
        wb_hop(seg).start()

    def att_hop(b):
        return remote(send_s.at[b - 1], att_ref.at[b], a_send.at[b], a_recv.at[b], {"ctx": (zed ^ b) * 2 + core})

    for b in range(blocks):
        here = slice(b * rows, (b + 1) * rows)
        key_s[here, :] = ins[b][:, width : 2 * width]
        value_s[here, :] = ins[b][:, 2 * width : 3 * width]
    for turn, b in enumerate(list(range(blocks - 1, 0, -1)) + [0]):

        def step(i, carry, b=b):
            local = pl.ds(pl.multiple_of(i * q_rows, q_rows), q_rows)
            where = pl.ds(pl.multiple_of(b * rows + i * q_rows, q_rows), q_rows)
            query = ins[b][local, 0:width] * BF16(HEAD**-0.5)
            outputs, sums = [], []
            for head in range(heads):
                masked = one_head(query, head, heads)
                scores = [
                    dot(masked, key_s[j : j + k_rows, :], NT) for j in range(0, length, k_rows)
                ]
                top = None
                for part in scores:
                    part_top = jnp.max(part, axis=1, keepdims=True)
                    top = part_top if top is None else jnp.maximum(top, part_top)
                total = acc = None
                for j, part in enumerate(scores):
                    probs = jnp.exp(part - top)
                    part_total = jnp.sum(probs, axis=1, keepdims=True)
                    value = value_s[j * k_rows : (j + 1) * k_rows, :]
                    part_acc = dot(probs.astype(BF16), value, NN)
                    total = part_total if total is None else total + part_total
                    acc = part_acc if acc is None else acc + part_acc
                outputs.append(acc / total)
                sums.append(jnp.broadcast_to(top + jnp.log(total), (q_rows, width)))
            result = merge_heads(outputs)
            full_ref[where, :] = result
            if b == 0:
                att_ref[0, local, :] = result.astype(BF16)
            else:
                send_s[b - 1, local, :] = result.astype(BF16)
            lse_ref[where, :] = merge_heads(sums)
            return carry

        lax.fori_loop(0, rows // q_rows, step, 0)
        if b > 0:
            att_hop(b).start()
        if 0 < turn < len(bits) - 1:
            level(turn, lambda hop: hop.wait_recv())
            level(turn + 1, lambda hop: hop.start())
    level(len(bits) - 1, lambda hop: hop.wait_recv())
    for number in range(1, len(bits)):
        level(number, lambda hop: hop.wait_send())
    for seg in range(n_f):
        wb_hop(seg).wait()
    for b in range(1, blocks):
        att_hop(b).wait()
    for copy in locals_:
        copy.wait()


def attend(qkv, w_in, wi_got, w_back4, heads, n_f):
    blocks, rows, _ = qkv.shape
    width = heads * HEAD
    length = rows * blocks
    _, half, part = wi_got.shape
    _, _, seg_rows, seg_cols = w_back4.shape
    sds = jax.ShapeDtypeStruct
    in_vmem, anywhere = pl.BlockSpec(memory_space=pltpu.VMEM), pl.BlockSpec(memory_space=pl.ANY)
    dma = pltpu.SemaphoreType.DMA
    return pl.pallas_call(
        partial(attend_kernel, blocks=blocks, heads=heads, n_f=n_f, q_rows=256, k_rows=512),
        out_shape=[
            sds((blocks, rows, width), BF16),
            sds((length, width), F32),
            sds((length, width), F32),
            sds((2 * half, n_f * part), BF16),
            sds((n_f, seg_rows, seg_cols), BF16),
        ],
        in_specs=[in_vmem] + [anywhere] * 3,
        out_specs=[in_vmem] * 3 + [anywhere] * 2,
        scratch_shapes=[pltpu.VMEM((length, width), BF16)] * 2
        + [
            pltpu.VMEM((blocks - 1, rows, width), BF16),
            dma((blocks,)),
            dma((blocks,)),
            dma((2, n_f)),
            dma((2, n_f)),
            dma((n_f,)),
            dma((n_f,)),
            dma((4,)),
        ],
        compiler_params=pltpu.CompilerParams(
            vmem_limit_bytes=VMEM_LIMIT, collective_id=3, has_side_effects=True
        ),
        cost_estimate=pl.CostEstimate(
            flops=16 * length * length * width, bytes_accessed=10 * length * width,
            transcendentals=heads * length * length,
        ),
        name="attend",
    )(qkv, w_in, wi_got, w_back4)


def gelu_both(pre):
    slope = math.sqrt(2.0 / math.pi)
    square = pre * pre
    th = jnp.tanh(slope * (pre + 0.044715 * pre * square))
    half = 0.5 * (1.0 + th)
    grad = half + 0.5 * pre * (1.0 - th * th) * (slope * (1.0 + 3 * 0.044715 * square))
    return pre * half, grad


class Reduction:
    def __init__(self, src, cols, acc, got, far, sems, n_f, n_z, begin=0, summed=True):
        self.begin, self.summed = begin, summed
        self.z_bits = [1 << i for i in range(n_z.bit_length() - 1)]
        self.src, self.cols, self.acc, self.got, self.far = src, cols, acc, got, far
        self.load_sem, self.f_send, self.f_recv, self.z_send, self.z_recv = sems
        self.n_z = n_z
        ctx, self.fs = lax.axis_index("ctx"), lax.axis_index("fsdp")
        self.core, self.zed = ctx % 2, ctx // 2
        self.bits, self.orders = fsdp_orders(n_f)
        self.last = len(self.bits) - 1

    def targets(self, side, level):
        found = [0]
        for bit in reversed(self.orders[side][level + 1 :]):
            found = found + [d ^ bit for d in found]
        return found

    def part(self, side, target):
        return self.src.at[:, side, target, :, self.cols]

    def load(self, side, i):
        d = self.targets(side, 0)[i]
        return pltpu.make_async_copy(self.part(side, self.fs ^ d), self.acc.at[side, i], self.load_sem.at[side, i])

    def hop(self, side, level, i):
        bit = self.orders[side][level]
        first = sum(len(self.targets(side, l)) for l in range(level))
        if level == 0:
            src = self.part(side, self.fs ^ bit ^ self.targets(side, 0)[i])
        else:
            src = self.acc.at[side, len(self.targets(side, level)) + i]
        return remote(
            src, self.got.at[side, first + i], self.f_send.at[side, first + i], self.f_recv.at[side, first + i],
            {"fsdp": self.fs ^ bit},
        )

    def every(self, level, act):
        for side in range(2):
            for i in range(len(self.targets(side, level))):
                act(self.hop(side, level, i))

    def loads(self, act):
        for side in range(2):
            for i in range(len(self.targets(side, 0))):
                act(self.load(side, i))

    def start(self):
        self.every(0, lambda hop: hop.start())
        self.loads(lambda copy: copy.start())

    def level(self, level, go=True):
        if level == 0:
            self.loads(lambda copy: copy.wait())
        self.every(level, lambda hop: hop.wait_recv())
        first = sum(len(self.targets(0, l)) for l in range(level))
        count = len(self.targets(0, level))

        def add(n, carry):
            side, rest = n // (count * self.n_z), n % (count * self.n_z)
            i, z = rest // self.n_z, rest % self.n_z
            total = self.acc[side, i, z].astype(F32) + self.got[side, first + i, z].astype(F32)
            self.acc[side, i, z] = total.astype(BF16)
            return carry

        lax.fori_loop(0, 2 * count * self.n_z, add, 0)
        if not go:
            return
        if level < self.last:
            self.every(level + 1, lambda hop: hop.start())
        elif self.far is not None:
            self.z_start()

    def z_targets(self, level):
        found = [0]
        for bit in reversed(self.z_bits[level + 1 :]):
            found = found + [d ^ bit for d in found]
        return found

    def z_hops(self, level):
        hops = []
        if self.summed:
            bit = self.z_bits[level]
            first = sum(len(self.z_targets(l)) for l in range(level))
            moves = [(bit ^ d, bit, first + i) for i, d in enumerate(self.z_targets(level))]
        else:
            moves = [(m, m, m - 1) for m in range(self.n_z - 1, 0, -1)]
        for block, away, slot in moves:
            for side in range(2):
                hops.append(
                    remote(
                        self.acc.at[side, 0, self.zed ^ block], self.far.at[side, slot], self.z_send.at[side, slot],
                        self.z_recv.at[side, slot], {"ctx": (self.zed ^ away) * 2 + self.core},
                    )
                )
        return hops

    def z_start(self, level=0):
        for hop in self.z_hops(level):
            hop.start()

    def z_level(self, level):
        for hop in self.z_hops(level):
            hop.wait_recv()
        if level == len(self.z_bits) - 1:
            return
        first = sum(len(self.z_targets(l)) for l in range(level))
        for i, d in enumerate(self.z_targets(level)):
            for side in range(2):
                total = self.acc[side, 0, self.zed ^ d].astype(F32) + self.far[side, first + i].astype(F32)
                self.acc[side, 0, self.zed ^ d] = total.astype(BF16)
        self.z_start(level + 1)

    def arrived(self):
        for hop in self.z_hops(0):
            hop.wait_recv()

    def total(self, side):
        return self.acc[side, 0, self.zed].astype(F32) + self.far[side, self.n_z - 2].astype(F32)

    def sent(self, end=None):
        for level in range(self.begin, self.last + 1 if end is None else end):
            self.every(level, lambda hop: hop.wait_send())
        if self.far is not None:
            for level in range(len(self.z_bits) if self.summed else 1):
                for hop in self.z_hops(level):
                    hop.wait_send()


def row_stats(value):
    return jnp.mean(value, axis=1, keepdims=True)


def mid_kernel(*refs, n_f, n_z, reduce, cfg):
    refs = list(refs)
    red_refs = [refs.pop() for _ in range(6)][::-1] if reduce else None
    sum_out = refs.pop(16) if reduce else None
    att_in, x_ref, cot_ref, vec_ref, bias_ref, wo_ref, wi_ref, wb_ref, got_ref, got2_ref = refs[:10]
    layer_ref, grad_one_ref, ga_ref, sums_ref, bias_sum_ref, grads_out = refs[10:16]
    att_ref, att2_s, h_ref, act_ref, g2_ref, gp_ref, g1_ref, ga_s, turned_s, og_s = refs[16:26]
    wo_s, wi_s, wb_s, slope_s, normed_s, unit_s, acc_s, send_s, recv_s, rstd_s = refs[26:36]
    w_sem, send_sem, recv_sem, b_send, b_recv, a_send, a_recv, g_sem = refs[36:]
    ctx, fs = lax.axis_index("ctx"), lax.axis_index("fsdp")
    core, zed = ctx % 2, ctx // 2
    partner = {"ctx": zed * 2 + (1 - core)}
    rows, width = x_ref.shape
    own, other = slice(0, rows), slice(rows, 2 * rows)
    wide = att_in.shape[2]
    half_in = n_z * wide
    ff_half = wi_s.shape[1]
    step = cfg["step"]
    chunk = cfg["rows"]
    bits, orders = fsdp_orders(n_f)
    _, _, seg_rows, seg_cols = wb_ref.shape

    def wb_place(seg, m):
        return wb_s.at[
            pl.ds(seg * seg_rows, seg_rows), pl.ds(pl.multiple_of((fs ^ m) * seg_cols, 128), seg_cols)
        ]

    def wb_order(seg):
        return orders[seg * 2 // n_f]

    def wb_source(seg, m):
        if m == 0:
            return wb_ref.at[seg, core]
        if m == wb_order(seg)[1]:
            return got2_ref.at[seg]
        return got_ref.at[seg] if m == wb_order(seg)[0] else wb_place(seg, m)

    def wb_hop(seg, m, bit):
        return remote(
            wb_source(seg, m), wb_place(seg, m), b_send.at[seg, m ^ bit], b_recv.at[seg, m ^ bit], {"fsdp": fs ^ bit}
        )

    def wb_level(number, act):
        for seg in range(n_f):
            for m in known_at(wb_order(seg), number)[1 if number == 1 else 0 :]:
                act(wb_hop(seg, m, wb_order(seg)[number]))

    copies = [
        [pltpu.make_async_copy(wo_ref, wo_s, w_sem.at[0])],
        [pltpu.make_async_copy(wi_ref, wi_s, w_sem.at[1])],
        [],
    ]
    for seg in range(n_f):
        for i, m in enumerate((0, wb_order(seg)[0], wb_order(seg)[1])):
            copies[2].append(pltpu.make_async_copy(wb_source(seg, m), wb_place(seg, m), w_sem.at[2 + 3 * seg + i]))
    for copy in copies[0] + copies[1]:
        copy.start()
    greet(
        pltpu.get_barrier_semaphore(),
        [partner] + [{"fsdp": fs ^ bit} for bit in bits] + [{"ctx": (zed ^ m) * 2 + core} for m in range(1, n_z)],
    )
    wb_level(1, lambda hop: hop.start())
    for copy in copies[2]:
        copy.start()

    def exchange(n, src, dst):
        return remote(src, dst, send_sem.at[n], recv_sem.at[n], partner)

    def over_cols(total, body):
        def run(i, carry):
            body(pl.ds(pl.multiple_of(i * step, step), step))
            return carry

        lax.fori_loop(0, total // step, run, 0)

    def over_rows(body):
        def run(i, carry):
            return body(pl.ds(pl.multiple_of(i * chunk, chunk), chunk), carry)

        zero = jnp.zeros((1, width), F32)
        return lax.fori_loop(0, rows // chunk, run, (zero, zero, zero))

    if wide % 128 == 0:
        for m in range(n_z):
            att_ref[:, pl.ds(pl.multiple_of((zed ^ m) * wide, wide), wide)] = att_in[m]
    else:
        for m in range(0, n_z, 2):
            one, two = att_in[m].astype(F32), att_in[m + 1].astype(F32)
            odd = zed % 2 == 1
            block = jnp.concatenate([jnp.where(odd, two, one), jnp.where(odd, one, two)], axis=1)
            at = pl.ds(pl.multiple_of((zed // 2 ^ (m // 2)) * 2 * wide, 2 * wide), 2 * wide)
            att_ref[:, at] = block.astype(BF16)

    def wait_all(group):
        for copy in group:
            copy.wait()

    att_move = exchange(6, att_ref, att2_s)
    att_move.start()

    wait_all(copies[0])

    def out_other(cols):
        send_s[:, cols] = dot(att_ref[other, :], wo_s[:, cols], NN)

    over_cols(width, out_other)
    move = exchange(0, send_s, recv_s)
    move.start()

    def out_own(cols):
        part = dot(att_ref[own, :], wo_s[:, cols], NN)
        acc_s[:, cols] = part + x_ref[:, cols].astype(F32) + vec_ref[2:3, cols]

    over_cols(width, out_own)
    move.wait()

    def norm_one(r, carry):
        resid = acc_s[r, :] + recv_s[r, :]
        centre = resid - row_stats(resid)
        rstd = lax.rsqrt(row_stats(centre * centre) + EPS)
        unit = centre * rstd
        normed = unit * vec_ref[3:4, :] + vec_ref[4:5, :]
        unit_s[r, :] = unit
        rstd_s[r, :] = jnp.broadcast_to(rstd, (chunk, 128))
        normed_s[r, :] = normed
        h_ref[r, :] = normed.astype(BF16)
        return carry

    over_rows(norm_one)
    move = exchange(1, h_ref.at[own], h_ref.at[other])
    move.start()

    wait_all(copies[1])

    def up(where):
        def body(cols):
            pre = dot(h_ref[where, :], wi_s[:, cols], NN) + bias_ref[0:1, cols]
            act, slope = gelu_both(pre)
            act_ref[where, cols] = act.astype(BF16)
            slope_s[where, cols] = slope

        over_cols(ff_half, body)

    up(own)
    move.wait()
    up(other)
    for number in range(1, len(bits)):
        wb_level(number, lambda hop: hop.wait_recv())
        if number + 1 < len(bits):
            wb_level(number + 1, lambda hop: hop.start())
    wait_all(copies[2])

    def down_other(cols):
        send_s[:, cols] = dot(act_ref[other, :], wb_s[:, cols], NN)

    over_cols(width, down_other)
    move = exchange(2, send_s, recv_s)
    move.start()

    def down_own(cols):
        part = dot(act_ref[own, :], wb_s[:, cols], NN)
        acc_s[:, cols] = part + normed_s[:, cols] + vec_ref[5:6, cols]

    over_cols(width, down_own)
    move.wait()

    def norm_two(r, carry):
        resid = acc_s[r, :] + recv_s[r, :]
        centre = resid - row_stats(resid)
        rstd = lax.rsqrt(row_stats(centre * centre) + EPS)
        unit = centre * rstd
        gain = vec_ref[6:7, :]
        layer_ref[r, :] = (unit * gain + vec_ref[7:8, :]).astype(BF16)
        grad = cot_ref[r, :]
        scaled = grad * gain
        back = rstd * (scaled - row_stats(scaled) - unit * row_stats(scaled * unit))
        acc_s[r, :] = back
        g2_ref[r, :] = back.astype(BF16)
        sums = (back, grad * unit, grad)
        return tuple(c + jnp.sum(s, axis=0, keepdims=True) for c, s in zip(carry, sums))

    shift_two = over_rows(norm_two)
    move = exchange(3, g2_ref.at[own], g2_ref.at[other])
    move.start()
    for i, total in enumerate(shift_two):
        sums_ref[3 + i : 4 + i, :] = total

    def back_act(where, first):
        def body(cols):
            grad = dot(g2_ref[where, :], wb_s[cols, :], NT) * slope_s[where, cols]
            gp_ref[where, cols] = grad.astype(BF16)
            total = jnp.sum(grad, axis=0, keepdims=True)
            bias_sum_ref[0:1, cols] = total if first else bias_sum_ref[0:1, cols] + total

        over_cols(ff_half, body)

    back_act(own, True)
    move.wait()
    n_out = ff_half // step
    d_rows = width // n_z

    def product(left, right, store):
        for i in range(0, width, 256):
            turned_s[i : i + 256, :] = left[:, i : i + 256].T

        def cols_of(i, carry):
            cols = pl.ds(pl.multiple_of(i * step, step), step)
            store(i, cols, dot(turned_s[...], right[:, cols], NN).astype(BF16))
            return carry

        lax.fori_loop(0, n_out, cols_of, 0)

    if reduce:
        gb_s, acc_r, got_r, load_sem, f_send, f_recv = red_refs
        sums = Reduction(gb_s, pl.ds(0, ff_half), acc_r, got_r, None, (load_sem, f_send, f_recv, None, None), n_f, n_z)
        low = gb_s.shape[3]

        def store_back(i, cols, value):
            gb_s[:, :, :, :, cols] = value.reshape(n_z, 2, n_f, low, step)

        product(g2_ref, act_ref, store_back)
        sums.start()
    back_act(other, False)

    def back_other(cols):
        send_s[:, cols] = dot(gp_ref[other, :], wi_s[cols, :], NT)

    over_cols(width, back_other)
    move = exchange(4, send_s, recv_s)
    move.start()

    def back_own(cols):
        acc_s[:, cols] += dot(gp_ref[own, :], wi_s[cols, :], NT)

    over_cols(width, back_own)
    move.wait()

    def back_one(r, carry):
        grad = acc_s[r, :] + recv_s[r, :]
        unit = unit_s[r, :]
        rstd = rstd_s[r, 0:1]
        scaled = grad * vec_ref[3:4, :]
        back = rstd * (scaled - row_stats(scaled) - unit * row_stats(scaled * unit))
        grad_one_ref[r, :] = back
        g1_ref[r, :] = back.astype(BF16)
        sums = (back, grad * unit, grad)
        return tuple(c + jnp.sum(s, axis=0, keepdims=True) for c, s in zip(carry, sums))

    shift_one = over_rows(back_one)
    move = exchange(5, g1_ref.at[own], g1_ref.at[other])
    move.start()
    for i, total in enumerate(shift_one):
        sums_ref[i : 1 + i, :] = total
    sums_ref[6:8, :] = jnp.zeros((2, width), F32)

    def att_hop(m):
        return remote(ga_s.at[m - 1], ga_ref.at[m], a_send.at[m], a_recv.at[m], {"ctx": (zed ^ m) * 2 + core})

    move.wait()
    for m in list(range(n_z - 1, 0, -1)) + [0]:
        at = pl.ds(pl.multiple_of((zed ^ m) * wide, wide), wide)
        block = dot(g1_ref[...], wo_s[at, :], NT).astype(BF16)
        if m == 0:
            ga_ref[0] = block
        else:
            ga_s[m - 1] = block
            att_hop(m).start()

    def out_grad(i, which):
        cols = pl.ds(pl.multiple_of(i * step, step), step)
        there = pl.ds(pl.multiple_of(which * ff_half + i * step, step), step)
        return pltpu.make_async_copy(wi_s.at[:, cols], grads_out.at[:, there], g_sem.at[which * n_out + i])

    def store_staged(which):
        def store(i, cols, value):
            if which == 1:
                out_grad(i, 0).wait()
            wi_s[:, cols] = value
            out_grad(i, which).start()

        return store

    product(h_ref, gp_ref, store_staged(0))
    wide_out = ff_half
    if not reduce:
        product(g2_ref, act_ref, store_staged(1))
        wide_out = 2 * ff_half
    att_move.wait()
    half = width // 2
    cols = pl.ds(pl.multiple_of(core * half, 128), half)
    for i in range(0, half_in, 256):
        at = pl.ds(pl.multiple_of(core * half + i, 128), 256)
        og_s[at, :] = dot(att_ref[:, i : i + 256].T, g1_ref[:, cols], NN).astype(BF16)
        at = pl.ds(pl.multiple_of((1 - core) * half + i, 128), 256)
        turned = att2_s[:, i : i + 256].T
        og_s[at, :] = (
            dot(turned[:, :rows], g1_ref[rows:, cols], NN) + dot(turned[:, rows:], g1_ref[:rows, cols], NN)
        ).astype(BF16)
    out_move = pltpu.make_async_copy(og_s, grads_out.at[:, pl.ds(wide_out, half)], g_sem.at[2 * n_out])
    out_move.start()
    for number in range(1, len(bits)):
        wb_level(number, lambda hop: hop.wait_send())
    for m in range(1, n_z):
        att_hop(m).wait()
    for i in range(n_out):
        out_grad(i, 0 if reduce else 1).wait()
    out_move.wait()
    if reduce:
        sums.level(0, False)
        final = pltpu.make_async_copy(acc_r, sum_out, load_sem.at[0, 0])
        final.start()
        sums.sent(1)
        final.wait()


def middle(att, x_own, cot, vectors, bias_half, wo, wi, wb4, got, got2, n_f, n_z, reduce):
    rows, width = x_own.shape
    wide = att.shape[2]
    ff_half = bias_half.shape[0]
    half_in = n_z * wide
    sds = jax.ShapeDtypeStruct
    vmem, dma = pltpu.VMEM, pltpu.SemaphoreType.DMA
    in_vmem, anywhere = pl.BlockSpec(memory_space=pltpu.VMEM), pl.BlockSpec(memory_space=pl.ANY)
    cfg = {"step": 512, "rows": 64}
    low = width // (2 * n_z * n_f)
    extra_out, extra = [], []
    if reduce:
        extra_out = [sds((2, n_f // 2, n_z, low, ff_half), BF16)]
        extra = [
            vmem((n_z, 2, n_f, low, ff_half), BF16),
            vmem((2, n_f // 2, n_z, low, ff_half), BF16),
            vmem((2, n_f - 1, n_z, low, ff_half), BF16),
            dma((2, n_f // 2)),
            dma((2, n_f - 1)),
            dma((2, n_f - 1)),
        ]
    return pl.pallas_call(
        partial(mid_kernel, n_f=n_f, n_z=n_z, reduce=reduce, cfg=cfg),
        out_shape=[
            sds((rows, width), BF16),
            sds((rows, width), F32),
            sds((n_z, 2 * rows, wide), BF16),
            sds((8, width), F32),
            sds((1, ff_half), F32),
            sds((width, (1 if reduce else 2) * ff_half + width // 2), BF16),
        ]
        + extra_out,
        in_specs=[in_vmem] * 5 + [anywhere] * 5,
        out_specs=[in_vmem] * 5 + [anywhere] * (1 + len(extra_out)),
        scratch_shapes=[
            vmem((2 * rows, half_in), BF16),
            vmem((2 * rows, half_in), BF16),
            vmem((2 * rows, width), BF16),
            vmem((2 * rows, ff_half), BF16),
            vmem((2 * rows, width), BF16),
            vmem((2 * rows, ff_half), BF16),
            vmem((2 * rows, width), BF16),
            vmem((n_z - 1, 2 * rows, wide), BF16),
            vmem((width, 2 * rows), BF16),
            vmem((width, width // 2), BF16),
            vmem((half_in, width), BF16),
            vmem((width, ff_half), BF16),
            vmem((ff_half, width), BF16),
            vmem((2 * rows, ff_half), F32),
            vmem((rows, width), F32),
            vmem((rows, width), F32),
            vmem((rows, width), F32),
            vmem((rows, width), F32),
            vmem((rows, width), F32),
            vmem((rows, 128), F32),
            dma((2 + 3 * n_f,)),
            dma((7,)),
            dma((7,)),
            dma((n_f, n_f)),
            dma((n_f, n_f)),
            dma((n_z,)),
            dma((n_z,)),
            dma((2 * (ff_half // cfg["step"]) + 1,)),
        ]
        + extra,
        compiler_params=pltpu.CompilerParams(
            vmem_limit_bytes=VMEM_MIDDLE, collective_id=0, has_side_effects=True
        ),
        cost_estimate=pl.CostEstimate(
            flops=2 * 2 * rows * width * (3 * half_in + 6 * ff_half),
            bytes_accessed=40 << 20, transcendentals=2 * rows * ff_half,
        ),
        name="middle",
    )(att, x_own, cot, vectors, bias_half[None], wo, wi, wb4, got, got2)


def back_kernel(*refs, blocks, heads, n_f, reduce, q_rows, steps_per):
    refs = list(refs)

    def take(count):
        taken = refs[:count]
        del refs[:count]
        return taken

    qkv_ref, ga_ref, full_ref, lse_ref, grad_one_ref = take(5)
    if reduce:
        mid_ref, bias_ref = take(2)
    (wl_hbm,) = take(1)
    if reduce:
        x_hbm, g_hbm, back_hbm = take(3)
    out_ref, sums_ref = take(2)
    if reduce:
        in_ref, back_ref, og_ref, qg_ref = take(4)
    (stage,) = take(1)
    lse_t, delta_t, gq_t, key_t, gin, wl_s, cat, send_s, recv_s = take(9)
    kv_send, kv_recv, q_send, q_recv, t_send, t_recv, own_sem = take(7)
    if reduce:
        x_s, gq_src, give_s, others, table_r, c_send, c_recv, o_send, o_recv, s_send, s_recv = take(11)
        bufs = [take(8) for _ in range(3)]
    ctx, fs = lax.axis_index("ctx"), lax.axis_index("fsdp")
    core, zed = ctx % 2, ctx // 2
    partner = {"ctx": zed * 2 + (1 - core)}
    bits, orders = fsdp_orders(n_f)
    rows = qkv_ref.shape[1]
    width = heads * HEAD
    scale = HEAD**-0.5
    chunk = 256
    half = wl_s.shape[1] // 3
    greeted = [partner] + [{"ctx": (zed ^ m) * 2 + core} for m in range(1, blocks)]
    if reduce:
        greeted += [{"fsdp": fs ^ bit} for bit in bits]
    greet(pltpu.get_barrier_semaphore(), greeted)
    wl_copy = pltpu.make_async_copy(wl_hbm, wl_s, own_sem.at[0])
    wl_copy.start()
    if reduce:
        early, attn, lone = [
            Reduction(
                src, pl.ds(0, buf[0].shape[-1]), buf[0], buf[1], buf[2], buf[3:], n_f, blocks, begin, summed
            )
            for buf, src, begin, summed in zip(bufs, (g_hbm, gq_src, None), (0, 0, 1), (True, False, True))
        ]
        lone_copy = pltpu.make_async_copy(back_hbm, lone.acc, own_sem.at[2])
        lone_copy.start()
        lone_copy.wait()
        lone.every(1, lambda hop: hop.start())
        early.start()
        x_copy = pltpu.make_async_copy(x_hbm, x_s, own_sem.at[1])
        x_copy.start()

    for b in range(blocks):
        for i in range(0, rows, chunk):
            local = slice(i, i + chunk)
            where = slice(b * rows + i, b * rows + i + chunk)
            logs = lse_ref[where, :].T
            terms = (ga_ref[b, local, :].astype(F32) * full_ref[where, :]).T
            for head in range(heads):
                first = head * HEAD
                lse_t[head : head + 1, where] = logs[first : first + 1]
                delta_t[head : head + 1, where] = jnp.sum(
                    terms[first : first + HEAD], axis=0, keepdims=True
                )
        key_t[:, b * rows : (b + 1) * rows] = qkv_ref[b, :, width : 2 * width].T
    gq_t[...] = jnp.zeros_like(gq_t)

    split = width % 128 == 0

    def kv_hop(m):
        return remote(
            stage.at[m, :, pl.ds(width, 2 * width)], gin.at[m, :, pl.ds(width, 2 * width)], kv_send.at[m], kv_recv.at[m],
            {"ctx": (zed ^ m) * 2 + core},
        )

    def q_hop(m):
        cols = pl.ds(0, width if split else 3 * width)
        return remote(
            stage.at[m, :, cols], gin.at[m, :, cols], q_send.at[m], q_recv.at[m], {"ctx": (zed ^ m) * 2 + core}
        )

    k_rows = rows // steps_per

    def step(n, carry):
        b = blocks - 1 - n // steps_per
        start = n % steps_per * k_rows
        local = pl.ds(pl.multiple_of(start, 128), k_rows)
        where = pl.ds(pl.multiple_of(b * rows + start, 128), k_rows)
        key = qkv_ref[b, local, width : 2 * width]
        value = qkv_ref[b, local, 2 * width : 3 * width]
        key_grads, value_grads = [], []
        for head in range(heads):
            feats = slice(head * HEAD, (head + 1) * HEAD)
            key_h = one_head(key, head, heads) * BF16(scale)
            value_h = one_head(value, head, heads)
            key_grad = value_grad = None
            for other in range(blocks):
                for i in range(0, rows, q_rows):
                    here = slice(i, i + q_rows)
                    there = slice(other * rows + i, other * rows + i + q_rows)
                    query = qkv_ref[other, here, 0:width]
                    grad = ga_ref[other, here, :]
                    scores = dot(key_h, query, NT)
                    probs = jnp.exp(scores - lse_t[head : head + 1, there])
                    grad_probs = dot(value_h, grad, NT)
                    grad_scores = probs * (grad_probs - delta_t[head : head + 1, there])
                    grad_scores = grad_scores.astype(BF16)
                    term = dot(probs.astype(BF16), grad, NN)
                    value_grad = term if value_grad is None else value_grad + term
                    term = dot(grad_scores, query, NN)
                    key_grad = term if key_grad is None else key_grad + term
                    gq_t[feats, there] += dot(key_t[feats, where], grad_scores, NN)
            key_grads.append(key_grad)
            value_grads.append(value_grad)
        stage[b, local, width : 2 * width] = (merge_heads(key_grads) * scale).astype(BF16)
        stage[b, local, 2 * width : 3 * width] = merge_heads(value_grads).astype(BF16)
        if split:

            @pl.when((n % steps_per == steps_per - 1) & (b > 0))
            def _():
                kv_hop(b).start()

        if reduce:

            @pl.when(n == 2)
            def _():
                for level in range(1, len(bits)):
                    lone.level(level)

            @pl.when(n == 5)
            def _():
                early.level(0)
                lone.z_level(0)

        return carry

    lax.fori_loop(0, blocks * steps_per, step, 0)
    for b in range(blocks - 1, -1, -1):
        for i in range(0, rows, chunk):
            there = slice(b * rows + i, b * rows + i + chunk)
            stage[b, i : i + chunk, 0:width] = (gq_t[:, there].T * scale).astype(BF16)
        if b > 0:
            q_hop(b).start()
    gin[0] = stage[0]
    sums = jnp.zeros((1, 3 * width), F32)
    for b in range(blocks):
        sums = sums + jnp.sum(stage[b].astype(F32), axis=0, keepdims=True)
    if reduce:
        dim = out_ref.shape[1]
        hidden_half = bias_ref.shape[1] // n_f
        sums_ref[...] = jnp.zeros_like(sums_ref)
        first = pl.ds(pl.multiple_of(core * half + zed * width, 128), width)
        sums_ref[0:1, first] = sums[:, 0:width]
        sums_ref[1:2, first] = sums[:, 2 * width :]
        sums_ref[2:8, :] = mid_ref[0:6, :]
        for f in range(n_f):
            at = pl.ds(pl.multiple_of(core * hidden_half, 128), hidden_half)
            sums_ref[8 + f : 9 + f, at] = bias_ref[:, f * hidden_half : (f + 1) * hidden_half]
        peers = [{"fsdp": fs ^ bit} for bit in bits]
        peers += [{"ctx": (zed ^ (1 << i)) * 2 + core} for i in range(blocks.bit_length() - 1)] + [partner]

        def table_hop(k):
            return remote(sums_ref, table_r.at[k], s_send.at[k], s_recv.at[k], peers[k])

        def table_step(k):
            if k < len(peers):
                table_hop(k).wait()
                sums_ref[...] += table_r[k]
                if k + 1 < len(peers):
                    table_hop(k + 1).start()

        table_hop(0).start()
    else:
        sums_ref[...] = sums

    if reduce:
        x_copy.wait()
        d_rows = x_s.shape[-1] // blocks
        low = gq_src.shape[3]
        for b in range(blocks):
            cat[0 : 3 * width, b * rows : (b + 1) * rows] = stage[b].T
        for z in range(blocks):
            cols = slice(z * d_rows, (z + 1) * d_rows)
            total = None
            for b in range(blocks):
                x_block = x_s[b, :, :, cols].reshape(rows, d_rows)
                term = dot(cat[0 : 3 * width, b * rows : (b + 1) * rows], x_block, NN)
                total = term if total is None else total + term
            gq_src[z] = total.T.astype(BF16).reshape(2, n_f, low, 3 * width)
        attn.start()
        for level in range(1, len(bits)):
            early.level(level)
        table_step(0)
        for level in range(len(bits)):
            attn.level(level)
            table_step(1 + level)

    for m in range(blocks - 1, 0, -1):
        if split:
            kv_hop(m).wait()
        q_hop(m).wait()
    wl_copy.wait()
    for j in range(3):
        part = slice(j * width, (j + 1) * width)
        if split:
            for m in range(blocks):
                at = pl.ds(pl.multiple_of(j * half + (zed ^ m) * width, 128), width)
                cat[0:rows, at] = gin[m, :, part]
        else:
            for m in range(0, blocks, 2):
                one, two = gin[m, :, part].astype(F32), gin[m + 1, :, part].astype(F32)
                odd = zed % 2 == 1
                block = jnp.concatenate([jnp.where(odd, two, one), jnp.where(odd, one, two)], axis=1)
                at = j * half + (zed // 2 ^ (m // 2)) * 2 * width
                cat[0:rows, pl.ds(pl.multiple_of(at, 128), 2 * width)] = block.astype(BF16)
    tokens, dim = out_ref.shape
    pieces = dim // 256
    if reduce:
        for k in range(1 + len(bits), len(peers)):
            table_step(k)
        for level in range(1, len(lone.z_bits)):
            lone.z_level(level)
        early.z_level(0)

    def swap_hop(i):
        cols = slice(i * 256, (i + 1) * 256)
        return remote(send_s.at[:, cols], recv_s.at[:, cols], t_send.at[i], t_recv.at[i], partner)

    for i in range(pieces):
        cols = slice(i * 256, (i + 1) * 256)
        send_s[:, cols] = dot(cat[tokens:rows, 0 : 3 * half], wl_s[cols, :], NT)
        swap_hop(i).start()
    for i in range(pieces):
        cols = slice(i * 256, (i + 1) * 256)
        out_ref[:, cols] = dot(cat[0:tokens, 0 : 3 * half], wl_s[cols, :], NT) + grad_one_ref[:, cols]
    for i in range(pieces):
        cols = slice(i * 256, (i + 1) * 256)
        swap_hop(i).wait_recv()
        out_ref[:, cols] += recv_s[:, cols]
    for i in range(pieces):
        swap_hop(i).wait_send()

    if reduce:
        attn.arrived()

        def other_hop(m):
            src = attn.acc.at[1 - core, 0, zed] if m == 0 else attn.far.at[1 - core, m - 1]
            return remote(src, others.at[m], o_send.at[m], o_recv.at[m], partner)

        def put_heads(m, value, which):
            for j in range(3):
                at = pl.ds(pl.multiple_of(j * dim + which * half + (zed ^ m) * width, 128), width)
                qg_ref[:, at] = value[:, j * width : (j + 1) * width].astype(F32)

        for m in range(blocks):
            other_hop(m).start()
        for m in range(blocks):
            put_heads(m, attn.acc[core, 0, zed] if m == 0 else attn.far[core, m - 1], core)

        hops = []

        def settle(which, offset, places):
            count = which.acc.shape[-1]
            give_s[:, offset : offset + count] = which.total(1 - core)
            kept = which.total(core)
            start = 0
            for target, at, size in places:
                cols = pl.ds(pl.multiple_of(at, 128), size)
                hop = remote(
                    give_s.at[:, pl.ds(offset + start, size)], target.at[:, cols], c_send.at[len(hops)],
                    c_recv.at[len(hops)], partner,
                )
                hop.start()
                hops.append(hop)
                target[:, cols] = kept[:, start : start + size]
                start += size

        def units(target):
            return [(target, (2 * f + core) * hidden_half, hidden_half) for f in range(n_f)]

        settle(lone, 0, units(back_ref))
        for level in range(1, len(early.z_bits)):
            early.z_level(level)
        settle(early, lone.acc.shape[-1], units(in_ref) + [(og_ref, core * half, half)])
        for m in range(blocks):
            other_hop(m).wait()
            put_heads(m, others[m], 1 - core)
        for which in (early, attn, lone):
            which.sent()
        for hop in hops:
            hop.wait()


def back(qkv, grads, full, lse, grad_one, w_local, x_all, mid_grads, heads, n_f, reduce, back_sums=None, sums_mid=None, bias_sum=None):
    blocks, rows, _ = qkv.shape
    width = heads * HEAD
    length = rows * blocks
    tokens, dim = grad_one.shape
    sds = jax.ShapeDtypeStruct
    vmem, dma = pltpu.VMEM, pltpu.SemaphoreType.DMA
    in_vmem, anywhere = pl.BlockSpec(memory_space=pltpu.VMEM), pl.BlockSpec(memory_space=pl.ANY)
    operands = [qkv, grads, full, lse, grad_one]
    if reduce:
        operands += [sums_mid, bias_sum]
    inner = len(operands)
    operands += [w_local]
    out_shape = [sds((tokens, dim), F32), sds((16, dim) if reduce else (1, 3 * width), F32)]
    staged = (blocks, rows, 3 * width)
    scratch = [
        vmem((8, length), F32),
        vmem((8, length), F32),
        vmem((width, length), F32),
        vmem((width, length), BF16),
        vmem(staged, BF16),
        vmem(w_local.shape, BF16),
        vmem((rows, max(length, w_local.shape[1])), BF16),
        vmem((tokens, dim), F32),
        vmem((tokens, dim), F32),
        dma((blocks,)),
        dma((blocks,)),
        dma((blocks,)),
        dma((blocks,)),
        dma((dim // 256,)),
        dma((dim // 256,)),
        dma((3,)),
    ]
    if reduce:
        _, _, _, low, columns = mid_grads.shape
        operands += [x_all, mid_grads, back_sums]
        hidden_half = back_sums.shape[-1]
        out_shape += [sds((low, 2 * hidden_half), F32)] * 2 + [sds((low, dim), F32), sds((low, 3 * dim), F32)]
        n_peers = n_f.bit_length() + blocks.bit_length() - 1
        scratch = [vmem(staged, BF16)] + scratch
        scratch += [
            vmem(x_all.shape, BF16),
            vmem((blocks, 2, n_f, low, 3 * width), BF16),
            vmem((low, columns + hidden_half), F32),
            vmem((blocks, low, 3 * width), BF16),
            vmem((n_peers, 16, dim), F32),
            dma((2 * n_f + 1,)),
            dma((2 * n_f + 1,)),
            dma((blocks,)),
            dma((blocks,)),
            dma((n_peers,)),
            dma((n_peers,)),
        ]
        for cols in (columns, 3 * width, hidden_half):
            scratch += [
                vmem((2, n_f // 2, blocks, low, cols), BF16),
                vmem((2, n_f - 1, blocks, low, cols), BF16),
                vmem((2, blocks - 1, low, cols), BF16),
                dma((2, n_f // 2)),
                dma((2, n_f - 1)),
                dma((2, n_f - 1)),
                dma((2, blocks - 1)),
                dma((2, blocks - 1)),
            ]
    else:
        out_shape += [sds(staged, BF16)]
    return pl.pallas_call(
        partial(
            back_kernel, blocks=blocks, heads=heads, n_f=n_f, reduce=reduce, q_rows=256, steps_per=2
        ),
        out_shape=out_shape,
        in_specs=[in_vmem] * inner + [anywhere] * (len(operands) - inner),
        out_specs=[in_vmem] * len(out_shape),
        scratch_shapes=scratch,
        compiler_params=pltpu.CompilerParams(
            vmem_limit_bytes=VMEM_MIDDLE, collective_id=2, has_side_effects=True
        ),
        cost_estimate=pl.CostEstimate(
            flops=40 * length * length * width, bytes_accessed=30 << 20,
            transcendentals=heads * length * length,
        ),
        name="back",
    )(*operands)


def on_device(x_in, w_qkv, w_out, w_in, w_back, vectors, bias_in, cot, *, n_ctx, n_f):
    ctx, fs = lax.axis_index("ctx"), lax.axis_index("fsdp")
    core, zed = ctx % 2, ctx // 2
    n_z = n_ctx // 2
    x_own = x_in[0]
    grad_out = cot[0]
    rows, width = x_own.shape
    hidden = w_back.shape[0]
    half_heads = HEADS // 2
    heads = half_heads // n_z
    wide = heads * HEAD

    def swap(v):
        return lax.ppermute(v, "ctx", [(i, i ^ 1) for i in range(n_ctx)])

    def over_z(v, m):
        return lax.ppermute(v, "ctx", [(i, i ^ (2 * m)) for i in range(n_ctx)])

    def over_f(v, m):
        return lax.ppermute(v, "fsdp", [(i, i ^ m) for i in range(n_f)])

    bits = [1 << b for b in range(n_f.bit_length() - 1)]

    def place(pieces, index, axis):
        count = len(pieces)
        for bit in range(count.bit_length() - 1):
            flag = (index >> bit) & 1
            pieces = [jnp.where(flag, pieces[m ^ (1 << bit)], pieces[m]) for m in range(count)]
        return jnp.concatenate(pieces, axis=axis)

    half_in = width // 2
    first = (core * half_heads + zed * heads) * HEAD
    span = 3 * wide
    bias_qkv = jnp.concatenate(
        [
            lax.dynamic_slice_in_dim(vectors[0], first, wide, 0),
            jnp.zeros((wide,), F32),
            lax.dynamic_slice_in_dim(vectors[1], first, wide, 0),
        ]
    )[None]
    ff_part = w_in.shape[1] // 2
    w_back4 = w_back.reshape(n_f, 2, ff_part, w_back.shape[1])
    qkv, x_all, w_local, wo_half, wi_got, wb_got = front(
        x_own, w_qkv, w_out, w_in, w_back4, bias_qkv, n_f, n_z, heads
    )

    att, att_full, lse, wi_half, wb_got2 = attend(qkv, w_in, wi_got, w_back4, heads, n_f)
    bias_half = lax.dynamic_index_in_dim(
        bias_in.reshape(n_f, 2, ff_part), core, 1, False
    ).reshape(-1)
    low = width // (n_ctx * n_f)
    in_kernel = low % 16 == 0 and wide % 128 == 0 and hidden == n_f * width and min(n_z, n_f) >= 4
    layer_out, grad_one, g_att, sums_mid, bias_sum, mid_grads, *back_sums = middle(
        att, x_own, grad_out, vectors, bias_half, wo_half, wi_half, w_back4, wb_got, wb_got2, n_f, n_z, in_kernel
    )
    layer_out = layer_out[None]


    def over_fsdp(partial_grad):
        cols = partial_grad.shape[1]
        view = partial_grad.reshape((n_z, 2) + (2,) * len(bits) + (low, cols))
        done = []
        for side in range(2):
            now = view[:, side]
            order = bits if side == 0 else bits[1:] + bits[:1]
            left = list(reversed(bits))
            for bit in order:
                axis = 1 + left.index(bit)
                left.remove(bit)
                flag = (fs // bit) % 2
                stay = lax.dynamic_index_in_dim(now, flag, axis, False)
                go = lax.dynamic_index_in_dim(now, 1 - flag, axis, False)
                now = (stay.astype(F32) + over_f(go, bit).astype(F32)).astype(BF16)
            done.append(now)
        return jnp.stack(done, axis=1)

    def over_ctx(both):
        total = lax.dynamic_index_in_dim(both, zed, 0, False).astype(F32)
        for m in range(1, n_z):
            part = lax.dynamic_index_in_dim(both, zed ^ m, 0, False)
            total = total + over_z(part, m).astype(F32)
        stay = lax.dynamic_index_in_dim(total, core, 0, False)
        go = lax.dynamic_index_in_dim(total, 1 - core, 0, False)
        return stay, swap(go.astype(BF16)).astype(F32)

    def halves(stay, came, parts):
        low = stay.shape[0]
        first = jnp.where(core == 0, stay, came).reshape(low, parts, 1, -1)
        second = jnp.where(core == 0, came, stay).reshape(low, parts, 1, -1)
        return jnp.concatenate([first, second], axis=2).reshape(low, -1)

    def reduced(partial_grad):
        return over_ctx(over_fsdp(partial_grad))

    if in_kernel:
        grad_in, table, in_weight_grad, back_turned, out_weight_grad, qkv_weight_grad = back(
            qkv, g_att, att_full, lse, grad_one, w_local, x_all,
            mid_grads.reshape(n_z, 2, n_f, low, -1), heads, n_f, True, back_sums[0], sums_mid, bias_sum,
        )
        mine_at = (ctx * n_f + fs) * low
        vector_grad = lax.dynamic_slice_in_dim(table[:8], mine_at, low, 1)
        share = hidden // (n_ctx * n_f)
        in_bias_grad = lax.dynamic_slice_in_dim(table[8 : 8 + n_f].reshape(-1), mine_at // low * share, share, 0)
        return (
            layer_out,
            grad_in[None],
            qkv_weight_grad,
            out_weight_grad,
            in_weight_grad,
            back_turned.T,
            vector_grad,
            in_bias_grad,
        )
    stay, came = reduced(mid_grads)
    grad_in, sums, g_local = back(
        qkv, g_att, att_full, lse, grad_one, w_local, None, None, heads, n_f, False
    )
    attn_grad = dot(x_all.reshape(-1, width), g_local.reshape(-1, span), TN).astype(BF16)
    both = over_fsdp(attn_grad)
    mine, others = [], []
    for m in range(n_z):
        part = lax.dynamic_index_in_dim(both, zed ^ m, 0, False)
        part = part if m == 0 else over_z(part, m)
        mine.append(lax.dynamic_index_in_dim(part, core, 0, False))
        others.append(lax.dynamic_index_in_dim(part, 1 - core, 0, False))
    others = swap(jnp.stack(others))
    others = [others[m] for m in range(n_z)]
    n_half = hidden // 2
    in_weight_grad = halves(stay[:, :n_half], came[:, :n_half], n_f)
    back_weight_grad = halves(stay[:, n_half : 2 * n_half], came[:, n_half : 2 * n_half], n_f).T
    out_weight_grad = halves(stay[:, 2 * n_half :], came[:, 2 * n_half :], 1)

    def heads_order(parts):
        parts = [p.reshape(low, 3, wide) for p in parts]
        return place(parts, zed, 2).astype(F32).reshape(low, -1)

    qkv_weight_grad = halves(heads_order(mine), heads_order(others), 3)

    def spread(half_row, parts):
        piece = half_row.reshape(parts, 1, -1)
        empty = jnp.zeros_like(piece)
        both = jnp.where(core == 0, jnp.concatenate([piece, empty], 1), jnp.concatenate([empty, piece], 1))
        return both.reshape(-1)

    def halve(now):
        left = list(reversed(bits))
        for bit in bits:
            axis = left.index(bit)
            left.remove(bit)
            flag = (fs // bit) % 2
            stay = lax.dynamic_index_in_dim(now, flag, axis, False)
            now = stay + over_f(lax.dynamic_index_in_dim(now, 1 - flag, axis, False), bit)
        return now

    sums = sums[0]
    sums = jnp.stack([sums[:wide].reshape(n_f, -1), sums[2 * wide :].reshape(n_f, -1)], axis=1)
    late = halve(sums.reshape((2,) * len(bits) + (-1,)))
    turn = [(2 * z + c, n_z * c + z) for z in range(n_z) for c in range(2)]
    late = lax.ppermute(late, "ctx", turn).reshape(2, -1)
    ratio = hidden // width
    early = sums_mid[:6].T
    bias_terms = spread(bias_sum[0], n_f).reshape(width, ratio)
    table = jnp.concatenate([early, bias_terms], axis=1)
    kinds = table.shape[1]
    now = jnp.swapaxes(table.reshape(n_z * 2, n_f, low, kinds), -1, -2)
    now = jnp.swapaxes(now, 0, 1).reshape((2,) * len(bits) + (n_z, 2, kinds * low))
    now = halve(now)
    total = lax.dynamic_index_in_dim(now, zed, 0, False)
    for m in range(1, n_z):
        total = total + over_z(lax.dynamic_index_in_dim(now, zed ^ m, 0, False), m)
    stay = lax.dynamic_index_in_dim(total, core, 0, False)
    table = stay + swap(lax.dynamic_index_in_dim(total, 1 - core, 0, False))
    table = table.reshape(kinds, low)
    vector_grad = jnp.concatenate([late, table[:6]], axis=0)
    in_bias_grad = table[6:].T.reshape(-1)
    return (
        layer_out,
        grad_in[None],
        qkv_weight_grad,
        out_weight_grad,
        in_weight_grad,
        back_weight_grad,
        vector_grad,
        in_bias_grad,
    )


def solution(mesh):
    tokens = P("fsdp", "ctx", None)
    cols = P(None, "fsdp")
    shared = P(("ctx", "fsdp"), None)
    return jax.shard_map(
        partial(on_device, n_ctx=mesh.shape["ctx"], n_f=mesh.shape["fsdp"]),
        mesh=mesh,
        in_specs=(tokens, cols, cols, cols, cols, P(), P(), tokens),
        out_specs=(
            tokens,
            tokens,
            shared,
            shared,
            shared,
            P(None, ("ctx", "fsdp")),
            P(None, ("ctx", "fsdp")),
            P(("ctx", "fsdp")),
        ),
        check_vma=False,
    )
```

```python
from functools import partial
import math

import jax
import jax.numpy as jnp
from jax import lax
from jax.experimental import pallas as pl
from jax.experimental.pallas import tpu as pltpu
from jax.sharding import PartitionSpec as P

HEADS = 16
HEAD = 64
EPS = 1e-12
F32 = jnp.float32
BF16 = jnp.bfloat16
NN = (((1,), (0,)), ((), ()))
NT = (((1,), (1,)), ((), ()))
TN = (((0,), (0,)), ((), ()))
VMEM_LIMIT = 50 * 1024 * 1024
VMEM_MIDDLE = 56 * 1024 * 1024
MESH = pl.DeviceIdType.MESH


def dot(left, right, dims):
    return lax.dot_general(left, right, dims, preferred_element_type=F32)


def front_kernel(
    x_ref, wq_ref, wo_ref, wi_ref, wb_ref, bias_ref, qkv_ref, xf_out, wl_out, wo_out, wi_out, wb_out, *scratch, n_z, n_f, heads
):
    xf, wfull, wloc = scratch[:3]
    own_sem, x_send, x_recv, xs_send, xs_recv, w_send, w_recv, ws_send, ws_recv, o_send, o_recv, i_send, i_recv, b_send, b_recv, out_sem = scratch[3:]
    ctx, fs = lax.axis_index("ctx"), lax.axis_index("fsdp")
    core, zed = ctx % 2, ctx // 2
    bits = [1 << b for b in range(n_f.bit_length() - 1)]
    orders = (bits, bits[1:] + bits[:1])
    rows, width = x_ref.shape
    half = width // 2
    quarter = half // 2
    wide = heads * HEAD
    partner = {"ctx": zed * 2 + (1 - core)}

    barrier = pltpu.get_barrier_semaphore()

    def greet(device):
        pl.semaphore_signal(barrier, inc=1, device_id=device, device_id_type=MESH)

    greet(partner)
    for bit in bits:
        greet({"fsdp": fs ^ bit})

    @pl.when(zed > 0)
    def _():
        greet({"ctx": ctx - 2})

    @pl.when(zed < n_z - 1)
    def _():
        greet({"ctx": ctx + 2})

    edges = (zed == 0).astype(jnp.int32) + (zed == n_z - 1).astype(jnp.int32)
    pl.semaphore_wait(barrier, 3 + len(bits) - edges)

    def remote(src, dst, send, recv, device):
        return pltpu.make_async_remote_copy(
            src_ref=src, dst_ref=dst, send_sem=send, recv_sem=recv, device_id=device, device_id_type=MESH
        )

    def x_move(away, step, first):
        block = zed - step * away
        src = x_ref if first else xf.at[block ^ zed, 0]
        index = (step + 1) // 2
        return remote(
            src, xf.at[block ^ (zed + step), 0], x_send.at[index, away], x_recv.at[block ^ (zed + step)],
            {"ctx": ctx + 2 * step},
        )

    def x_swap(m, first=False):
        src = x_ref if first else xf.at[m, 0]
        return remote(src, xf.at[m, 1], xs_send.at[m], xs_recv.at[m], partner)

    def has(step):
        return zed < n_z - 1 if step == 1 else zed > 0

    def came(away, step):
        return zed - away >= 0 if step == 1 else zed + away <= n_z - 1

    for step in (1, -1):

        @pl.when(has(step))
        def _(step=step):
            x_move(0, step, True).start()

    x_swap(0, True).start()
    own_x = pltpu.make_async_copy(x_ref, xf.at[0, 0], own_sem.at[0])
    own_x.start()

    def x_step(away):
        for step in (1, -1):

            @pl.when(came(away, step))
            def _(step=step):
                block = zed - step * away
                remote(
                    xf.at[block ^ zed, 0], xf.at[block ^ zed, 0], x_send.at[0, 0], x_recv.at[block ^ zed], partner
                ).wait_recv()

                @pl.when(has(step))
                def _():
                    x_move(away, step, False).start()

                x_swap(block ^ zed).start()

    def wq_place(side, origin, which):
        cols = wq_ref.shape[1]
        return wfull.at[
            pl.ds(pl.multiple_of(which * half + side * quarter, quarter), quarter),
            pl.ds(pl.multiple_of(origin * cols, 128), cols),
        ]

    def wq_own(side):
        return wq_ref.at[pl.ds(pl.multiple_of(core * half + side * quarter, quarter), quarter), :]

    def wo_place(side, origin):
        cols = wo_ref.shape[1]
        return wo_out.at[pl.ds(side * quarter, quarter), pl.ds(pl.multiple_of(origin * cols, 128), cols)]

    def wo_own(side):
        return wo_ref.at[pl.ds(pl.multiple_of(core * half + side * quarter, quarter), quarter), :]

    def wq_hop(side, m, bit):
        src = wq_own(side) if m == 0 else wq_place(side, fs ^ m, core)
        return remote(src, wq_place(side, fs ^ m, core), w_send.at[side, m ^ bit], w_recv.at[side, m ^ bit], {"fsdp": fs ^ bit})

    def wo_hop(side, m, bit):
        src = wo_own(side) if m == 0 else wo_place(side, fs ^ m)
        return remote(src, wo_place(side, fs ^ m), o_send.at[side, m ^ bit], o_recv.at[side, m ^ bit], {"fsdp": fs ^ bit})

    def wq_swap(side, m):
        src = wq_own(side) if m == 0 else wq_place(side, fs ^ m, core)
        return remote(src, wq_place(side, fs ^ m, core), ws_send.at[side, m], ws_recv.at[side, m], partner)

    own_w = []
    for side in range(2):
        wq_hop(side, 0, orders[side][0]).start()
        wq_swap(side, 0).start()
        own_w.append(pltpu.make_async_copy(wq_own(side), wq_place(side, fs, core), own_sem.at[1 + side]))
        own_w.append(pltpu.make_async_copy(wo_own(side), wo_place(side, fs), own_sem.at[3 + side]))
    for copy in own_w:
        copy.start()

    part = wi_ref.shape[1] // 2

    def wi_hop(side):
        src = wi_ref.at[pl.ds(side * half, half), pl.ds(pl.multiple_of(core * part, 128), part)]
        return remote(src, wi_out.at[side], i_send.at[side], i_recv.at[side], {"fsdp": fs ^ orders[side][0]})

    def wb_hop(seg):
        return remote(
            wb_ref.at[seg, core], wb_out.at[seg], b_send.at[seg], b_recv.at[seg],
            {"fsdp": fs ^ orders[seg * 2 // n_f][0]},
        )

    def doubling(hop, level, after=None):
        for side in range(2):
            known = [0]
            for bit in orders[side][:level]:
                known = known + [m ^ bit for m in known]
            bit = orders[side][level]
            for m in known:
                hop(side, m, bit).wait_recv()
                if after is not None:
                    after(side, m ^ bit).start()
            if level + 1 < len(bits):
                for m in known + [m ^ bit for m in known]:
                    hop(side, m, orders[side][level + 1]).start()

    doubling(wq_hop, 0, wq_swap)
    for side in range(2):
        wo_hop(side, 0, orders[side][0]).start()
    x_step(1)
    for level in range(1, len(bits)):
        doubling(wq_hop, level, wq_swap)
    for side in range(2):
        wi_hop(side).start()
    doubling(wo_hop, 0)
    for seg in range(n_f):
        wb_hop(seg).start()
    for away in range(2, n_z - 1):
        x_step(away)
    for copy in own_w:
        copy.wait()
    for side in range(2):
        for m in range(n_f):
            wq_swap_in = remote(
                wq_place(side, fs ^ m, 1 - core), wq_place(side, fs ^ m, 1 - core),
                ws_send.at[side, m], ws_recv.at[side, m], partner,
            )
            wq_swap_in.wait_recv()
    outs = []
    for j in range(3):
        cols = pl.ds(pl.multiple_of(j * width + core * half, 128), half)
        outs.append(pltpu.make_async_copy(wfull.at[:, cols], wl_out.at[:, pl.ds(j * half, half)], out_sem.at[j]))
    for copy in outs:
        copy.start()
    for j in range(3):
        base = j * width + core * half + zed * wide
        if wide % 128 == 0:
            piece = wfull[:, pl.ds(pl.multiple_of(base, 128), wide)]
        else:
            block = wfull[:, pl.ds(pl.multiple_of(base // 128 * 128, 128), 128)].astype(F32)
            piece = jnp.where(zed % 2 == 1, block[:, wide:], block[:, :wide]).astype(BF16)
        wloc[:, j * wide : (j + 1) * wide] = piece

    def x_ready(m, side):
        remote(xf.at[m, side], xf.at[m, side], xs_send.at[m], xs_recv.at[m], partner).wait_recv()

    def project(m):
        def run(side, carry):
            result = dot(xf[m, side], wloc[...], NN) + bias_ref[...]
            where = pl.ds(pl.multiple_of(side * rows, rows), rows)
            qkv_ref[m, where, :] = result.astype(BF16)
            return carry

        lax.fori_loop(0, 2, run, 0)

    own_x.wait()
    x_ready(0, 1)
    project(0)

    def finish(away):
        def run(i, carry):
            block = zed - (1 - 2 * i) * away

            @pl.when((block >= 0) & (block <= n_z - 1))
            def _():
                x_ready(block ^ zed, 1)
                project(block ^ zed)

            return carry

        lax.fori_loop(0, 2, run, 0)

    for away in range(1, n_z - 1):
        finish(away)
    for level in range(1, len(bits)):
        doubling(wo_hop, level)
    if n_z > 2:
        x_step(n_z - 1)
    finish(n_z - 1)
    x_out = pltpu.make_async_copy(xf, xf_out, own_sem.at[5])
    x_out.start()

    for step in (1, -1):

        @pl.when(has(step))
        def _(step=step):
            x_move(0, step, True).wait_send()
            for away in range(1, n_z):

                @pl.when(came(away, step))
                def _(away=away):
                    x_move(away, step, False).wait_send()

    x_swap(0, True).wait_send()
    for m in range(1, n_z):
        x_swap(m).wait_send()
    for side in range(2):
        known = [0]
        for bit in orders[side]:
            for m in known:
                wq_hop(side, m, bit).wait_send()
                wo_hop(side, m, bit).wait_send()
            known = known + [m ^ bit for m in known]
        for m in range(n_f):
            wq_swap(side, m).wait_send()
        wi_hop(side).wait()
    for seg in range(n_f):
        wb_hop(seg).wait()
    for copy in outs:
        copy.wait()
    x_out.wait()


def front(x_own, w_qkv, w_out, w_in, w_back4, bias, n_f, n_z, heads):
    rows, width = x_own.shape
    wide = heads * HEAD
    sds = jax.ShapeDtypeStruct
    in_vmem, anywhere = pl.BlockSpec(memory_space=pltpu.VMEM), pl.BlockSpec(memory_space=pl.ANY)
    part = w_in.shape[1] // 2
    dma = pltpu.SemaphoreType.DMA
    return pl.pallas_call(
        partial(front_kernel, n_z=n_z, n_f=n_f, heads=heads),
        out_shape=[
            sds((n_z, 2 * rows, 3 * wide), BF16),
            sds((n_z, 2, rows, width), BF16),
            sds((width, 3 * width // 2), BF16),
            sds((width // 2, width), BF16),
            sds((2, width // 2, part), BF16),
            sds((n_f,) + w_back4.shape[2:], BF16),
        ],
        in_specs=[anywhere] * 5 + [in_vmem],
        out_specs=[in_vmem] + [anywhere] * 5,
        scratch_shapes=[
            pltpu.VMEM((n_z, 2, rows, width), BF16),
            pltpu.VMEM((width, 3 * width), BF16),
            pltpu.VMEM((width, 3 * wide), BF16),
            dma((6,)),
            dma((2, n_z)),
            dma((n_z,)),
            dma((n_z,)),
            dma((n_z,)),
            dma((2, n_f)),
            dma((2, n_f)),
            dma((2, n_f)),
            dma((2, n_f)),
            dma((2, n_f)),
            dma((2, n_f)),
            dma((2,)),
            dma((2,)),
            dma((n_f,)),
            dma((n_f,)),
            dma((3,)),
        ],
        compiler_params=pltpu.CompilerParams(
            vmem_limit_bytes=VMEM_LIMIT, collective_id=1, has_side_effects=True
        ),
        cost_estimate=pl.CostEstimate(
            flops=4 * n_z * rows * width * 3 * wide, bytes_accessed=30 << 20, transcendentals=0
        ),
        name="front",
    )(x_own, w_qkv, w_out, w_in, w_back4, bias)


def one_head(block, head, heads):
    if heads == 1:
        return block
    lane = lax.broadcasted_iota(jnp.int32, block.shape, 1)
    return jnp.where(lane // HEAD == head, block, jnp.zeros_like(block))


def merge_heads(parts):
    if len(parts) == 1:
        return parts[0]
    lane = lax.broadcasted_iota(jnp.int32, parts[0].shape, 1)
    result = parts[0]
    for head in range(1, len(parts)):
        result = jnp.where(lane // HEAD == head, parts[head], result)
    return result


def remote(src, dst, send, recv, device):
    return pltpu.make_async_remote_copy(
        src_ref=src, dst_ref=dst, send_sem=send, recv_sem=recv, device_id=device, device_id_type=MESH
    )


def greet(barrier, devices):
    for device in devices:
        pl.semaphore_signal(barrier, inc=1, device_id=device, device_id_type=MESH)
    pl.semaphore_wait(barrier, len(devices))


def fsdp_orders(n_f):
    bits = [1 << b for b in range(n_f.bit_length() - 1)]
    return bits, (bits, bits[1:] + bits[:1])


def known_at(order, level):
    known = [0]
    for bit in order[:level]:
        known = known + [m ^ bit for m in known]
    return known


def attend_kernel(*refs, blocks, heads, n_f, q_rows, k_rows):
    qkv_ref, wi_ref, got_ref, wb_ref = refs[:4]
    att_ref, full_ref, lse_ref, wi_out, wb_out = refs[4:9]
    key_s, value_s, send_s, a_send, a_recv, i_send, i_recv, b_send, b_recv, own_sem = refs[9:]
    ins = [qkv_ref.at[b] for b in range(blocks)]
    rows = ins[0].shape[0]
    width = heads * HEAD
    length = rows * blocks
    ctx, fs = lax.axis_index("ctx"), lax.axis_index("fsdp")
    core, zed = ctx % 2, ctx // 2
    bits, orders = fsdp_orders(n_f)
    greet(
        pltpu.get_barrier_semaphore(),
        [{"fsdp": fs ^ bit} for bit in bits] + [{"ctx": (zed ^ m) * 2 + core} for m in range(1, blocks)],
    )

    half, part = got_ref.shape[1:]

    def wi_place(side, m):
        return wi_out.at[pl.ds(side * half, half), pl.ds(pl.multiple_of((fs ^ m) * part, 128), part)]

    def wi_source(side, m):
        if m == 0:
            return wi_ref.at[pl.ds(side * half, half), pl.ds(pl.multiple_of(core * part, 128), part)]
        return got_ref.at[side] if m == orders[side][0] else wi_place(side, m)

    def wi_hop(side, m, bit):
        return remote(
            wi_source(side, m), wi_place(side, m), i_send.at[side, m ^ bit], i_recv.at[side, m ^ bit], {"fsdp": fs ^ bit}
        )

    def wb_hop(seg):
        return remote(
            wb_ref.at[seg, core], wb_out.at[seg], b_send.at[seg], b_recv.at[seg],
            {"fsdp": fs ^ orders[seg * 2 // n_f][1]},
        )

    def level(number, act):
        for side in range(2):
            for m in known_at(orders[side], number):
                act(wi_hop(side, m, orders[side][number]))

    locals_ = []
    for side in range(2):
        for i, m in enumerate((0, orders[side][0])):
            locals_.append(pltpu.make_async_copy(wi_source(side, m), wi_place(side, m), own_sem.at[2 * side + i]))
    for copy in locals_:
        copy.start()
    level(1, lambda hop: hop.start())
    for seg in range(n_f):
        wb_hop(seg).start()

    def att_hop(b):
        return remote(send_s.at[b - 1], att_ref.at[b], a_send.at[b], a_recv.at[b], {"ctx": (zed ^ b) * 2 + core})

    for b in range(blocks):
        here = slice(b * rows, (b + 1) * rows)
        key_s[here, :] = ins[b][:, width : 2 * width]
        value_s[here, :] = ins[b][:, 2 * width : 3 * width]
    for turn, b in enumerate(list(range(blocks - 1, 0, -1)) + [0]):

        def step(i, carry, b=b):
            local = pl.ds(pl.multiple_of(i * q_rows, q_rows), q_rows)
            where = pl.ds(pl.multiple_of(b * rows + i * q_rows, q_rows), q_rows)
            query = ins[b][local, 0:width] * BF16(HEAD**-0.5)
            outputs, sums = [], []
            for head in range(heads):
                masked = one_head(query, head, heads)
                scores = [
                    dot(masked, key_s[j : j + k_rows, :], NT) for j in range(0, length, k_rows)
                ]
                top = None
                for part in scores:
                    part_top = jnp.max(part, axis=1, keepdims=True)
                    top = part_top if top is None else jnp.maximum(top, part_top)
                total = acc = None
                for j, part in enumerate(scores):
                    probs = jnp.exp(part - top)
                    part_total = jnp.sum(probs, axis=1, keepdims=True)
                    value = value_s[j * k_rows : (j + 1) * k_rows, :]
                    part_acc = dot(probs.astype(BF16), value, NN)
                    total = part_total if total is None else total + part_total
                    acc = part_acc if acc is None else acc + part_acc
                outputs.append(acc / total)
                sums.append(jnp.broadcast_to(top + jnp.log(total), (q_rows, width)))
            result = merge_heads(outputs)
            full_ref[where, :] = result
            if b == 0:
                att_ref[0, local, :] = result.astype(BF16)
            else:
                send_s[b - 1, local, :] = result.astype(BF16)
            lse_ref[where, :] = merge_heads(sums)
            return carry

        lax.fori_loop(0, rows // q_rows, step, 0)
        if b > 0:
            att_hop(b).start()
        if 0 < turn < len(bits) - 1:
            level(turn, lambda hop: hop.wait_recv())
            level(turn + 1, lambda hop: hop.start())
    level(len(bits) - 1, lambda hop: hop.wait_recv())
    for number in range(1, len(bits)):
        level(number, lambda hop: hop.wait_send())
    for seg in range(n_f):
        wb_hop(seg).wait()
    for b in range(1, blocks):
        att_hop(b).wait()
    for copy in locals_:
        copy.wait()


def attend(qkv, w_in, wi_got, w_back4, heads, n_f):
    blocks, rows, _ = qkv.shape
    width = heads * HEAD
    length = rows * blocks
    _, half, part = wi_got.shape
    _, _, seg_rows, seg_cols = w_back4.shape
    sds = jax.ShapeDtypeStruct
    in_vmem, anywhere = pl.BlockSpec(memory_space=pltpu.VMEM), pl.BlockSpec(memory_space=pl.ANY)
    dma = pltpu.SemaphoreType.DMA
    return pl.pallas_call(
        partial(attend_kernel, blocks=blocks, heads=heads, n_f=n_f, q_rows=256, k_rows=512),
        out_shape=[
            sds((blocks, rows, width), BF16),
            sds((length, width), F32),
            sds((length, width), F32),
            sds((2 * half, n_f * part), BF16),
            sds((n_f, seg_rows, seg_cols), BF16),
        ],
        in_specs=[in_vmem] + [anywhere] * 3,
        out_specs=[in_vmem] * 3 + [anywhere] * 2,
        scratch_shapes=[pltpu.VMEM((length, width), BF16)] * 2
        + [
            pltpu.VMEM((blocks - 1, rows, width), BF16),
            dma((blocks,)),
            dma((blocks,)),
            dma((2, n_f)),
            dma((2, n_f)),
            dma((n_f,)),
            dma((n_f,)),
            dma((4,)),
        ],
        compiler_params=pltpu.CompilerParams(
            vmem_limit_bytes=VMEM_LIMIT, collective_id=3, has_side_effects=True
        ),
        cost_estimate=pl.CostEstimate(
            flops=16 * length * length * width, bytes_accessed=10 * length * width,
            transcendentals=heads * length * length,
        ),
        name="attend",
    )(qkv, w_in, wi_got, w_back4)


def gelu_both(pre):
    slope = math.sqrt(2.0 / math.pi)
    square = pre * pre
    th = jnp.tanh(slope * (pre + 0.044715 * pre * square))
    half = 0.5 * (1.0 + th)
    grad = half + 0.5 * pre * (1.0 - th * th) * (slope * (1.0 + 3 * 0.044715 * square))
    return pre * half, grad


class Reduction:
    def __init__(self, src, cols, acc, got, far, sems, n_f, n_z, begin=0, summed=True):
        self.begin, self.summed = begin, summed
        self.z_bits = [1 << i for i in range(n_z.bit_length() - 1)]
        self.src, self.cols, self.acc, self.got, self.far = src, cols, acc, got, far
        self.load_sem, self.f_send, self.f_recv, self.z_send, self.z_recv = sems
        self.n_z = n_z
        ctx, self.fs = lax.axis_index("ctx"), lax.axis_index("fsdp")
        self.core, self.zed = ctx % 2, ctx // 2
        self.bits, self.orders = fsdp_orders(n_f)
        self.last = len(self.bits) - 1

    def targets(self, side, level):
        found = [0]
        for bit in reversed(self.orders[side][level + 1 :]):
            found = found + [d ^ bit for d in found]
        return found

    def part(self, side, target):
        return self.src.at[:, side, target, :, self.cols]

    def load(self, side, i):
        d = self.targets(side, 0)[i]
        return pltpu.make_async_copy(self.part(side, self.fs ^ d), self.acc.at[side, i], self.load_sem.at[side, i])

    def hop(self, side, level, i):
        bit = self.orders[side][level]
        first = sum(len(self.targets(side, l)) for l in range(level))
        if level == 0:
            src = self.part(side, self.fs ^ bit ^ self.targets(side, 0)[i])
        else:
            src = self.acc.at[side, len(self.targets(side, level)) + i]
        return remote(
            src, self.got.at[side, first + i], self.f_send.at[side, first + i], self.f_recv.at[side, first + i],
            {"fsdp": self.fs ^ bit},
        )

    def every(self, level, act):
        for side in range(2):
            for i in range(len(self.targets(side, level))):
                act(self.hop(side, level, i))

    def loads(self, act):
        for side in range(2):
            for i in range(len(self.targets(side, 0))):
                act(self.load(side, i))

    def start(self):
        self.every(0, lambda hop: hop.start())
        self.loads(lambda copy: copy.start())

    def level(self, level):
        if level == 0:
            self.loads(lambda copy: copy.wait())
        self.every(level, lambda hop: hop.wait_recv())
        first = sum(len(self.targets(0, l)) for l in range(level))
        count = len(self.targets(0, level))

        def add(n, carry):
            side, rest = n // (count * self.n_z), n % (count * self.n_z)
            i, z = rest // self.n_z, rest % self.n_z
            total = self.acc[side, i, z].astype(F32) + self.got[side, first + i, z].astype(F32)
            self.acc[side, i, z] = total.astype(BF16)
            return carry

        lax.fori_loop(0, 2 * count * self.n_z, add, 0)
        if level < self.last:
            self.every(level + 1, lambda hop: hop.start())
        elif self.far is not None:
            self.z_start()

    def z_targets(self, level):
        found = [0]
        for bit in reversed(self.z_bits[level + 1 :]):
            found = found + [d ^ bit for d in found]
        return found

    def z_hops(self, level):
        hops = []
        if self.summed:
            bit = self.z_bits[level]
            first = sum(len(self.z_targets(l)) for l in range(level))
            moves = [(bit ^ d, bit, first + i) for i, d in enumerate(self.z_targets(level))]
        else:
            moves = [(m, m, m - 1) for m in range(self.n_z - 1, 0, -1)]
        for block, away, slot in moves:
            for side in range(2):
                hops.append(
                    remote(
                        self.acc.at[side, 0, self.zed ^ block], self.far.at[side, slot], self.z_send.at[side, slot],
                        self.z_recv.at[side, slot], {"ctx": (self.zed ^ away) * 2 + self.core},
                    )
                )
        return hops

    def z_start(self, level=0):
        for hop in self.z_hops(level):
            hop.start()

    def z_level(self, level):
        for hop in self.z_hops(level):
            hop.wait_recv()
        if level == len(self.z_bits) - 1:
            return
        first = sum(len(self.z_targets(l)) for l in range(level))
        for i, d in enumerate(self.z_targets(level)):
            for side in range(2):
                total = self.acc[side, 0, self.zed ^ d].astype(F32) + self.far[side, first + i].astype(F32)
                self.acc[side, 0, self.zed ^ d] = total.astype(BF16)
        self.z_start(level + 1)

    def arrived(self):
        for hop in self.z_hops(0):
            hop.wait_recv()

    def total(self, side):
        return self.acc[side, 0, self.zed].astype(F32) + self.far[side, self.n_z - 2].astype(F32)

    def sent(self):
        for level in range(self.begin, self.last + 1):
            self.every(level, lambda hop: hop.wait_send())
        if self.far is not None:
            for level in range(len(self.z_bits) if self.summed else 1):
                for hop in self.z_hops(level):
                    hop.wait_send()


def row_stats(value):
    return jnp.mean(value, axis=1, keepdims=True)


def mid_kernel(*refs, n_f, n_z, reduce, cfg):
    refs = list(refs)
    red_refs = [refs.pop() for _ in range(6)][::-1] if reduce else None
    sum_out = refs.pop(16) if reduce else None
    att_in, x_ref, cot_ref, vec_ref, bias_ref, wo_ref, wi_ref, wb_ref, got_ref, got2_ref = refs[:10]
    layer_ref, grad_one_ref, ga_ref, sums_ref, bias_sum_ref, grads_out = refs[10:16]
    att_ref, att2_s, h_ref, act_ref, g2_ref, gp_ref, g1_ref, ga_s, turned_s, og_s = refs[16:26]
    wo_s, wi_s, wb_s, slope_s, normed_s, unit_s, acc_s, send_s, recv_s, rstd_s = refs[26:36]
    w_sem, send_sem, recv_sem, b_send, b_recv, a_send, a_recv, g_sem = refs[36:]
    ctx, fs = lax.axis_index("ctx"), lax.axis_index("fsdp")
    core, zed = ctx % 2, ctx // 2
    partner = {"ctx": zed * 2 + (1 - core)}
    rows, width = x_ref.shape
    own, other = slice(0, rows), slice(rows, 2 * rows)
    wide = att_in.shape[2]
    half_in = n_z * wide
    ff_half = wi_s.shape[1]
    step = cfg["step"]
    chunk = cfg["rows"]
    bits, orders = fsdp_orders(n_f)
    _, _, seg_rows, seg_cols = wb_ref.shape

    def wb_place(seg, m):
        return wb_s.at[
            pl.ds(seg * seg_rows, seg_rows), pl.ds(pl.multiple_of((fs ^ m) * seg_cols, 128), seg_cols)
        ]

    def wb_order(seg):
        return orders[seg * 2 // n_f]

    def wb_source(seg, m):
        if m == 0:
            return wb_ref.at[seg, core]
        if m == wb_order(seg)[1]:
            return got2_ref.at[seg]
        return got_ref.at[seg] if m == wb_order(seg)[0] else wb_place(seg, m)

    def wb_hop(seg, m, bit):
        return remote(
            wb_source(seg, m), wb_place(seg, m), b_send.at[seg, m ^ bit], b_recv.at[seg, m ^ bit], {"fsdp": fs ^ bit}
        )

    def wb_level(number, act):
        for seg in range(n_f):
            for m in known_at(wb_order(seg), number)[1 if number == 1 else 0 :]:
                act(wb_hop(seg, m, wb_order(seg)[number]))

    copies = [
        [pltpu.make_async_copy(wo_ref, wo_s, w_sem.at[0])],
        [pltpu.make_async_copy(wi_ref, wi_s, w_sem.at[1])],
        [],
    ]
    for seg in range(n_f):
        for i, m in enumerate((0, wb_order(seg)[0], wb_order(seg)[1])):
            copies[2].append(pltpu.make_async_copy(wb_source(seg, m), wb_place(seg, m), w_sem.at[2 + 3 * seg + i]))
    for copy in copies[0] + copies[1]:
        copy.start()
    greet(
        pltpu.get_barrier_semaphore(),
        [partner] + [{"fsdp": fs ^ bit} for bit in bits] + [{"ctx": (zed ^ m) * 2 + core} for m in range(1, n_z)],
    )
    wb_level(1, lambda hop: hop.start())
    for copy in copies[2]:
        copy.start()

    def exchange(n, src, dst):
        return remote(src, dst, send_sem.at[n], recv_sem.at[n], partner)

    def over_cols(total, body):
        def run(i, carry):
            body(pl.ds(pl.multiple_of(i * step, step), step))
            return carry

        lax.fori_loop(0, total // step, run, 0)

    def over_rows(body):
        def run(i, carry):
            return body(pl.ds(pl.multiple_of(i * chunk, chunk), chunk), carry)

        zero = jnp.zeros((1, width), F32)
        return lax.fori_loop(0, rows // chunk, run, (zero, zero, zero))

    if wide % 128 == 0:
        for m in range(n_z):
            att_ref[:, pl.ds(pl.multiple_of((zed ^ m) * wide, wide), wide)] = att_in[m]
    else:
        for m in range(0, n_z, 2):
            one, two = att_in[m].astype(F32), att_in[m + 1].astype(F32)
            odd = zed % 2 == 1
            block = jnp.concatenate([jnp.where(odd, two, one), jnp.where(odd, one, two)], axis=1)
            at = pl.ds(pl.multiple_of((zed // 2 ^ (m // 2)) * 2 * wide, 2 * wide), 2 * wide)
            att_ref[:, at] = block.astype(BF16)

    def wait_all(group):
        for copy in group:
            copy.wait()

    att_move = exchange(6, att_ref, att2_s)
    att_move.start()

    wait_all(copies[0])

    def out_other(cols):
        send_s[:, cols] = dot(att_ref[other, :], wo_s[:, cols], NN)

    over_cols(width, out_other)
    move = exchange(0, send_s, recv_s)
    move.start()

    def out_own(cols):
        part = dot(att_ref[own, :], wo_s[:, cols], NN)
        acc_s[:, cols] = part + x_ref[:, cols].astype(F32) + vec_ref[2:3, cols]

    over_cols(width, out_own)
    move.wait()

    def norm_one(r, carry):
        resid = acc_s[r, :] + recv_s[r, :]
        centre = resid - row_stats(resid)
        rstd = lax.rsqrt(row_stats(centre * centre) + EPS)
        unit = centre * rstd
        normed = unit * vec_ref[3:4, :] + vec_ref[4:5, :]
        unit_s[r, :] = unit
        rstd_s[r, :] = jnp.broadcast_to(rstd, (chunk, 128))
        normed_s[r, :] = normed
        h_ref[r, :] = normed.astype(BF16)
        return carry

    over_rows(norm_one)
    move = exchange(1, h_ref.at[own], h_ref.at[other])
    move.start()

    wait_all(copies[1])

    def up(where):
        def body(cols):
            pre = dot(h_ref[where, :], wi_s[:, cols], NN) + bias_ref[0:1, cols]
            act, slope = gelu_both(pre)
            act_ref[where, cols] = act.astype(BF16)
            slope_s[where, cols] = slope

        over_cols(ff_half, body)

    up(own)
    move.wait()
    up(other)
    for number in range(1, len(bits)):
        wb_level(number, lambda hop: hop.wait_recv())
        if number + 1 < len(bits):
            wb_level(number + 1, lambda hop: hop.start())
    wait_all(copies[2])

    def down_other(cols):
        send_s[:, cols] = dot(act_ref[other, :], wb_s[:, cols], NN)

    over_cols(width, down_other)
    move = exchange(2, send_s, recv_s)
    move.start()

    def down_own(cols):
        part = dot(act_ref[own, :], wb_s[:, cols], NN)
        acc_s[:, cols] = part + normed_s[:, cols] + vec_ref[5:6, cols]

    over_cols(width, down_own)
    move.wait()

    def norm_two(r, carry):
        resid = acc_s[r, :] + recv_s[r, :]
        centre = resid - row_stats(resid)
        rstd = lax.rsqrt(row_stats(centre * centre) + EPS)
        unit = centre * rstd
        gain = vec_ref[6:7, :]
        layer_ref[r, :] = (unit * gain + vec_ref[7:8, :]).astype(BF16)
        grad = cot_ref[r, :]
        scaled = grad * gain
        back = rstd * (scaled - row_stats(scaled) - unit * row_stats(scaled * unit))
        acc_s[r, :] = back
        g2_ref[r, :] = back.astype(BF16)
        sums = (back, grad * unit, grad)
        return tuple(c + jnp.sum(s, axis=0, keepdims=True) for c, s in zip(carry, sums))

    shift_two = over_rows(norm_two)
    move = exchange(3, g2_ref.at[own], g2_ref.at[other])
    move.start()
    for i, total in enumerate(shift_two):
        sums_ref[3 + i : 4 + i, :] = total

    def back_act(where, first):
        def body(cols):
            grad = dot(g2_ref[where, :], wb_s[cols, :], NT) * slope_s[where, cols]
            gp_ref[where, cols] = grad.astype(BF16)
            total = jnp.sum(grad, axis=0, keepdims=True)
            bias_sum_ref[0:1, cols] = total if first else bias_sum_ref[0:1, cols] + total

        over_cols(ff_half, body)

    back_act(own, True)
    move.wait()
    n_out = ff_half // step
    d_rows = width // n_z

    def product(left, right, store):
        for i in range(0, width, 256):
            turned_s[i : i + 256, :] = left[:, i : i + 256].T

        def cols_of(i, carry):
            cols = pl.ds(pl.multiple_of(i * step, step), step)
            store(i, cols, dot(turned_s[...], right[:, cols], NN).astype(BF16))
            return carry

        lax.fori_loop(0, n_out, cols_of, 0)

    if reduce:
        gb_s, acc_r, got_r, load_sem, f_send, f_recv = red_refs
        sums = Reduction(gb_s, pl.ds(0, ff_half), acc_r, got_r, None, (load_sem, f_send, f_recv, None, None), n_f, n_z)
        low = gb_s.shape[3]

        def store_back(i, cols, value):
            gb_s[:, :, :, :, cols] = value.reshape(n_z, 2, n_f, low, step)

        product(g2_ref, act_ref, store_back)
        sums.start()
    back_act(other, False)

    def back_other(cols):
        send_s[:, cols] = dot(gp_ref[other, :], wi_s[cols, :], NT)

    over_cols(width, back_other)
    move = exchange(4, send_s, recv_s)
    move.start()

    def back_own(cols):
        acc_s[:, cols] += dot(gp_ref[own, :], wi_s[cols, :], NT)

    over_cols(width, back_own)
    move.wait()

    def back_one(r, carry):
        grad = acc_s[r, :] + recv_s[r, :]
        unit = unit_s[r, :]
        rstd = rstd_s[r, 0:1]
        scaled = grad * vec_ref[3:4, :]
        back = rstd * (scaled - row_stats(scaled) - unit * row_stats(scaled * unit))
        grad_one_ref[r, :] = back
        g1_ref[r, :] = back.astype(BF16)
        sums = (back, grad * unit, grad)
        return tuple(c + jnp.sum(s, axis=0, keepdims=True) for c, s in zip(carry, sums))

    shift_one = over_rows(back_one)
    move = exchange(5, g1_ref.at[own], g1_ref.at[other])
    move.start()
    for i, total in enumerate(shift_one):
        sums_ref[i : 1 + i, :] = total
    sums_ref[6:8, :] = jnp.zeros((2, width), F32)

    def att_hop(m):
        return remote(ga_s.at[m - 1], ga_ref.at[m], a_send.at[m], a_recv.at[m], {"ctx": (zed ^ m) * 2 + core})

    move.wait()
    for m in list(range(n_z - 1, 0, -1)) + [0]:
        at = pl.ds(pl.multiple_of((zed ^ m) * wide, wide), wide)
        block = dot(g1_ref[...], wo_s[at, :], NT).astype(BF16)
        if m == 0:
            ga_ref[0] = block
        else:
            ga_s[m - 1] = block
            att_hop(m).start()

    if reduce:
        sums.level(0)

    def out_grad(i, which):
        cols = pl.ds(pl.multiple_of(i * step, step), step)
        there = pl.ds(pl.multiple_of(which * ff_half + i * step, step), step)
        return pltpu.make_async_copy(wi_s.at[:, cols], grads_out.at[:, there], g_sem.at[which * n_out + i])

    def store_staged(which):
        def store(i, cols, value):
            if which == 1:
                out_grad(i, 0).wait()
            wi_s[:, cols] = value
            out_grad(i, which).start()

        return store

    product(h_ref, gp_ref, store_staged(0))
    wide_out = ff_half
    if not reduce:
        product(g2_ref, act_ref, store_staged(1))
        wide_out = 2 * ff_half
    att_move.wait()
    half = width // 2
    cols = pl.ds(pl.multiple_of(core * half, 128), half)
    for i in range(0, half_in, 256):
        at = pl.ds(pl.multiple_of(core * half + i, 128), 256)
        og_s[at, :] = dot(att_ref[:, i : i + 256].T, g1_ref[:, cols], NN).astype(BF16)
        at = pl.ds(pl.multiple_of((1 - core) * half + i, 128), 256)
        turned = att2_s[:, i : i + 256].T
        og_s[at, :] = (
            dot(turned[:, :rows], g1_ref[rows:, cols], NN) + dot(turned[:, rows:], g1_ref[:rows, cols], NN)
        ).astype(BF16)
    out_move = pltpu.make_async_copy(og_s, grads_out.at[:, pl.ds(wide_out, half)], g_sem.at[2 * n_out])
    out_move.start()
    for number in range(1, len(bits)):
        wb_level(number, lambda hop: hop.wait_send())
    for m in range(1, n_z):
        att_hop(m).wait()
    for i in range(n_out):
        out_grad(i, 0 if reduce else 1).wait()
    out_move.wait()
    if reduce:
        for level in range(1, len(bits)):
            sums.level(level)
        final = pltpu.make_async_copy(acc_r.at[:, pl.ds(0, 1)], sum_out, load_sem.at[0, 0])
        final.start()
        sums.sent()
        final.wait()


def middle(att, x_own, cot, vectors, bias_half, wo, wi, wb4, got, got2, n_f, n_z, reduce):
    rows, width = x_own.shape
    wide = att.shape[2]
    ff_half = bias_half.shape[0]
    half_in = n_z * wide
    sds = jax.ShapeDtypeStruct
    vmem, dma = pltpu.VMEM, pltpu.SemaphoreType.DMA
    in_vmem, anywhere = pl.BlockSpec(memory_space=pltpu.VMEM), pl.BlockSpec(memory_space=pl.ANY)
    cfg = {"step": 512, "rows": 64}
    low = width // (2 * n_z * n_f)
    extra_out, extra = [], []
    if reduce:
        extra_out = [sds((2, 1, n_z, low, ff_half), BF16)]
        extra = [
            vmem((n_z, 2, n_f, low, ff_half), BF16),
            vmem((2, n_f // 2, n_z, low, ff_half), BF16),
            vmem((2, n_f - 1, n_z, low, ff_half), BF16),
            dma((2, n_f // 2)),
            dma((2, n_f - 1)),
            dma((2, n_f - 1)),
        ]
    return pl.pallas_call(
        partial(mid_kernel, n_f=n_f, n_z=n_z, reduce=reduce, cfg=cfg),
        out_shape=[
            sds((rows, width), BF16),
            sds((rows, width), F32),
            sds((n_z, 2 * rows, wide), BF16),
            sds((8, width), F32),
            sds((1, ff_half), F32),
            sds((width, (1 if reduce else 2) * ff_half + width // 2), BF16),
        ]
        + extra_out,
        in_specs=[in_vmem] * 5 + [anywhere] * 5,
        out_specs=[in_vmem] * 5 + [anywhere] * (1 + len(extra_out)),
        scratch_shapes=[
            vmem((2 * rows, half_in), BF16),
            vmem((2 * rows, half_in), BF16),
            vmem((2 * rows, width), BF16),
            vmem((2 * rows, ff_half), BF16),
            vmem((2 * rows, width), BF16),
            vmem((2 * rows, ff_half), BF16),
            vmem((2 * rows, width), BF16),
            vmem((n_z - 1, 2 * rows, wide), BF16),
            vmem((width, 2 * rows), BF16),
            vmem((width, width // 2), BF16),
            vmem((half_in, width), BF16),
            vmem((width, ff_half), BF16),
            vmem((ff_half, width), BF16),
            vmem((2 * rows, ff_half), F32),
            vmem((rows, width), F32),
            vmem((rows, width), F32),
            vmem((rows, width), F32),
            vmem((rows, width), F32),
            vmem((rows, width), F32),
            vmem((rows, 128), F32),
            dma((2 + 3 * n_f,)),
            dma((7,)),
            dma((7,)),
            dma((n_f, n_f)),
            dma((n_f, n_f)),
            dma((n_z,)),
            dma((n_z,)),
            dma((2 * (ff_half // cfg["step"]) + 1,)),
        ]
        + extra,
        compiler_params=pltpu.CompilerParams(
            vmem_limit_bytes=VMEM_MIDDLE, collective_id=0, has_side_effects=True
        ),
        cost_estimate=pl.CostEstimate(
            flops=2 * 2 * rows * width * (3 * half_in + 6 * ff_half),
            bytes_accessed=40 << 20, transcendentals=2 * rows * ff_half,
        ),
        name="middle",
    )(att, x_own, cot, vectors, bias_half[None], wo, wi, wb4, got, got2)


def back_kernel(*refs, blocks, heads, n_f, reduce, q_rows, steps_per):
    refs = list(refs)

    def take(count):
        taken = refs[:count]
        del refs[:count]
        return taken

    qkv_ref, ga_ref, full_ref, lse_ref, grad_one_ref = take(5)
    if reduce:
        mid_ref, bias_ref = take(2)
    (wl_hbm,) = take(1)
    if reduce:
        x_hbm, g_hbm, back_hbm = take(3)
    out_ref, sums_ref = take(2)
    if reduce:
        in_ref, back_ref, og_ref, qg_ref = take(4)
    (stage,) = take(1)
    lse_t, delta_t, gq_t, key_t, gin, wl_s, cat, send_s, recv_s = take(9)
    kv_send, kv_recv, q_send, q_recv, t_send, t_recv, own_sem = take(7)
    if reduce:
        x_s, gq_src, give_s, others, table_r, c_send, c_recv, o_send, o_recv, s_send, s_recv = take(11)
        bufs = [take(8) for _ in range(4)]
    ctx, fs = lax.axis_index("ctx"), lax.axis_index("fsdp")
    core, zed = ctx % 2, ctx // 2
    partner = {"ctx": zed * 2 + (1 - core)}
    bits, orders = fsdp_orders(n_f)
    rows = qkv_ref.shape[1]
    width = heads * HEAD
    scale = HEAD**-0.5
    chunk = 256
    half = wl_s.shape[1] // 3
    greeted = [partner] + [{"ctx": (zed ^ m) * 2 + core} for m in range(1, blocks)]
    if reduce:
        greeted += [{"fsdp": fs ^ bit} for bit in bits]
    greet(pltpu.get_barrier_semaphore(), greeted)
    wl_copy = pltpu.make_async_copy(wl_hbm, wl_s, own_sem.at[0])
    wl_copy.start()
    if reduce:
        cut = bufs[0][0].shape[-1]
        early, late, attn, lone = [
            Reduction(
                src, pl.ds(first, buf[0].shape[-1]), buf[0], buf[1], buf[2], buf[3:], n_f, blocks, begin, summed
            )
            for buf, src, first, begin, summed in zip(
                bufs, (g_hbm, g_hbm, gq_src, None), (0, cut, 0, 0), (0, 0, 0, len(bits)), (True, True, False, True)
            )
        ]
        lone_copy = pltpu.make_async_copy(back_hbm, lone.acc, own_sem.at[2])
        lone_copy.start()
        lone_copy.wait()
        lone.z_start()
        early.start()
        x_copy = pltpu.make_async_copy(x_hbm, x_s, own_sem.at[1])
        x_copy.start()

    for b in range(blocks):
        for i in range(0, rows, chunk):
            local = slice(i, i + chunk)
            where = slice(b * rows + i, b * rows + i + chunk)
            logs = lse_ref[where, :].T
            terms = (ga_ref[b, local, :].astype(F32) * full_ref[where, :]).T
            for head in range(heads):
                first = head * HEAD
                lse_t[head : head + 1, where] = logs[first : first + 1]
                delta_t[head : head + 1, where] = jnp.sum(
                    terms[first : first + HEAD], axis=0, keepdims=True
                )
        key_t[:, b * rows : (b + 1) * rows] = qkv_ref[b, :, width : 2 * width].T
    gq_t[...] = jnp.zeros_like(gq_t)

    split = width % 128 == 0

    def kv_hop(m, piece):
        at = pl.ds(pl.multiple_of(piece * (rows // steps_per), 128), rows // steps_per)
        cols = pl.ds(width, 2 * width)
        return remote(
            stage.at[m, at, cols], gin.at[m, at, cols], kv_send.at[m, piece], kv_recv.at[m, piece],
            {"ctx": (zed ^ m) * 2 + core},
        )

    def q_hop(m):
        cols = pl.ds(0, width if split else 3 * width)
        return remote(
            stage.at[m, :, cols], gin.at[m, :, cols], q_send.at[m], q_recv.at[m], {"ctx": (zed ^ m) * 2 + core}
        )

    k_rows = rows // steps_per

    def step(n, carry):
        b = blocks - 1 - n // steps_per
        start = n % steps_per * k_rows
        local = pl.ds(pl.multiple_of(start, 128), k_rows)
        where = pl.ds(pl.multiple_of(b * rows + start, 128), k_rows)
        key = qkv_ref[b, local, width : 2 * width]
        value = qkv_ref[b, local, 2 * width : 3 * width]
        key_grads, value_grads = [], []
        for head in range(heads):
            feats = slice(head * HEAD, (head + 1) * HEAD)
            key_h = one_head(key, head, heads) * BF16(scale)
            value_h = one_head(value, head, heads)
            key_grad = value_grad = None
            for other in range(blocks):
                for i in range(0, rows, q_rows):
                    here = slice(i, i + q_rows)
                    there = slice(other * rows + i, other * rows + i + q_rows)
                    query = qkv_ref[other, here, 0:width]
                    grad = ga_ref[other, here, :]
                    scores = dot(key_h, query, NT)
                    probs = jnp.exp(scores - lse_t[head : head + 1, there])
                    grad_probs = dot(value_h, grad, NT)
                    grad_scores = probs * (grad_probs - delta_t[head : head + 1, there])
                    grad_scores = grad_scores.astype(BF16)
                    term = dot(probs.astype(BF16), grad, NN)
                    value_grad = term if value_grad is None else value_grad + term
                    term = dot(grad_scores, query, NN)
                    key_grad = term if key_grad is None else key_grad + term
                    gq_t[feats, there] += dot(key_t[feats, where], grad_scores, NN)
            key_grads.append(key_grad)
            value_grads.append(value_grad)
        stage[b, local, width : 2 * width] = (merge_heads(key_grads) * scale).astype(BF16)
        stage[b, local, 2 * width : 3 * width] = merge_heads(value_grads).astype(BF16)
        if split:

            @pl.when(b > 0)
            def _():
                kv_hop(b, n % steps_per).start()

        if reduce:

            @pl.when(n == 1)
            def _():
                lone.z_level(0)
                early.level(0)

            @pl.when(n == 2)
            def _():
                late.start()

            @pl.when(n == 3)
            def _():
                for level in range(1, len(bits)):
                    early.level(level)

            @pl.when(n == 4)
            def _():
                late.level(0)

            @pl.when(n == 5)
            def _():
                early.z_level(0)
                for level in range(1, len(bits)):
                    late.level(level)

        return carry

    lax.fori_loop(0, blocks * steps_per, step, 0)
    for b in range(blocks - 1, -1, -1):
        for i in range(0, rows, chunk):
            there = slice(b * rows + i, b * rows + i + chunk)
            stage[b, i : i + chunk, 0:width] = (gq_t[:, there].T * scale).astype(BF16)
        if b > 0:
            q_hop(b).start()
    gin[0] = stage[0]
    sums = jnp.zeros((1, 3 * width), F32)
    for b in range(blocks):
        sums = sums + jnp.sum(stage[b].astype(F32), axis=0, keepdims=True)
    if reduce:
        dim = out_ref.shape[1]
        hidden_half = bias_ref.shape[1] // n_f
        sums_ref[...] = jnp.zeros_like(sums_ref)
        first = pl.ds(pl.multiple_of(core * half + zed * width, 128), width)
        sums_ref[0:1, first] = sums[:, 0:width]
        sums_ref[1:2, first] = sums[:, 2 * width :]
        sums_ref[2:8, :] = mid_ref[0:6, :]
        for f in range(n_f):
            at = pl.ds(pl.multiple_of(core * hidden_half, 128), hidden_half)
            sums_ref[8 + f : 9 + f, at] = bias_ref[:, f * hidden_half : (f + 1) * hidden_half]
        peers = [{"fsdp": fs ^ bit} for bit in bits]
        peers += [{"ctx": (zed ^ (1 << i)) * 2 + core} for i in range(blocks.bit_length() - 1)] + [partner]

        def table_hop(k):
            return remote(sums_ref, table_r.at[k], s_send.at[k], s_recv.at[k], peers[k])

        def table_step(k):
            if k < len(peers):
                table_hop(k).wait()
                sums_ref[...] += table_r[k]
                if k + 1 < len(peers):
                    table_hop(k + 1).start()

        table_hop(0).start()
    else:
        sums_ref[...] = sums

    if reduce:
        x_copy.wait()
        d_rows = x_s.shape[-1] // blocks
        low = gq_src.shape[3]
        for b in range(blocks):
            cat[0 : 3 * width, b * rows : (b + 1) * rows] = stage[b].T
        for z in range(blocks):
            cols = slice(z * d_rows, (z + 1) * d_rows)
            total = None
            for b in range(blocks):
                x_block = x_s[b, :, :, cols].reshape(rows, d_rows)
                term = dot(cat[0 : 3 * width, b * rows : (b + 1) * rows], x_block, NN)
                total = term if total is None else total + term
            gq_src[z] = total.T.astype(BF16).reshape(2, n_f, low, 3 * width)
        attn.start()
        table_step(0)
        late.z_level(0)

    tokens, dim = out_ref.shape
    pieces = dim // 256

    def collect(j):
        part = slice(j * width, (j + 1) * width)
        if split:
            for m in range(blocks):
                at = pl.ds(pl.multiple_of(j * half + (zed ^ m) * width, 128), width)
                cat[0:rows, at] = gin[m, :, part]
        else:
            for m in range(0, blocks, 2):
                one, two = gin[m, :, part].astype(F32), gin[m + 1, :, part].astype(F32)
                odd = zed % 2 == 1
                block = jnp.concatenate([jnp.where(odd, two, one), jnp.where(odd, one, two)], axis=1)
                at = j * half + (zed // 2 ^ (m // 2)) * 2 * width
                cat[0:rows, pl.ds(pl.multiple_of(at, 128), 2 * width)] = block.astype(BF16)

    def swap_hop(i):
        cols = slice(i * 256, (i + 1) * 256)
        return remote(send_s.at[:, cols], recv_s.at[:, cols], t_send.at[i], t_recv.at[i], partner)

    for m in range(blocks - 1, 0, -1):
        if split:
            for piece in range(steps_per):
                kv_hop(m, piece).wait()
        else:
            q_hop(m).wait()
    wl_copy.wait()
    collect(1)
    collect(2)
    keys = slice(half, 3 * half)
    for i in range(pieces):
        cols = slice(i * 256, (i + 1) * 256)
        send_s[:, cols] = dot(cat[tokens:rows, keys], wl_s[cols, keys], NT)
        out_ref[:, cols] = dot(cat[0:tokens, keys], wl_s[cols, keys], NT) + grad_one_ref[:, cols]
    if reduce:
        hops = []

        def settle(which, offset, places):
            count = which.acc.shape[-1]
            give_s[:, offset : offset + count] = which.total(1 - core)
            kept = which.total(core)
            start = 0
            for target, at, size in places:
                cols = pl.ds(pl.multiple_of(at, 128), size)
                hop = remote(
                    give_s.at[:, pl.ds(offset + start, size)], target.at[:, cols], c_send.at[len(hops)],
                    c_recv.at[len(hops)], partner,
                )
                hop.start()
                hops.append(hop)
                target[:, cols] = kept[:, start : start + size]
                start += size

        def units(target):
            return [(target, (2 * f + core) * hidden_half, hidden_half) for f in range(n_f)]

        for level in range(len(bits)):
            attn.level(level)
            table_step(1 + level)
        for level in range(1, len(lone.z_bits)):
            lone.z_level(level)
        settle(lone, 0, units(back_ref))
    if split:
        for m in range(blocks - 1, 0, -1):
            q_hop(m).wait()
    collect(0)
    for i in range(pieces):
        cols = slice(i * 256, (i + 1) * 256)
        send_s[:, cols] += dot(cat[tokens:rows, 0:half], wl_s[cols, 0:half], NT)
        swap_hop(i).start()
    for i in range(pieces):
        cols = slice(i * 256, (i + 1) * 256)
        out_ref[:, cols] += dot(cat[0:tokens, 0:half], wl_s[cols, 0:half], NT)
    if reduce:
        for k in range(1 + len(bits), len(peers)):
            table_step(k)
    for i in range(pieces):
        cols = slice(i * 256, (i + 1) * 256)
        swap_hop(i).wait_recv()
        out_ref[:, cols] += recv_s[:, cols]
    for i in range(pieces):
        swap_hop(i).wait_send()

    if reduce:
        attn.arrived()

        def other_hop(m):
            src = attn.acc.at[1 - core, 0, zed] if m == 0 else attn.far.at[1 - core, m - 1]
            return remote(src, others.at[m], o_send.at[m], o_recv.at[m], partner)

        def put_heads(m, value, which):
            for j in range(3):
                at = pl.ds(pl.multiple_of(j * dim + which * half + (zed ^ m) * width, 128), width)
                qg_ref[:, at] = value[:, j * width : (j + 1) * width].astype(F32)

        for m in range(blocks):
            other_hop(m).start()
        for m in range(blocks):
            put_heads(m, attn.acc[core, 0, zed] if m == 0 else attn.far[core, m - 1], core)

        places = units(in_ref) + [(og_ref, core * half, half)]
        offset = lone.acc.shape[-1]
        for which, some in ((early, places[: n_f - 1]), (late, places[n_f - 1 :])):
            for level in range(1, len(which.z_bits)):
                which.z_level(level)
            settle(which, offset, some)
            offset += cut
        for m in range(blocks):
            other_hop(m).wait()
            put_heads(m, others[m], 1 - core)
        for which in (early, late, attn, lone):
            which.sent()
        for hop in hops:
            hop.wait()


def back(qkv, grads, full, lse, grad_one, w_local, x_all, mid_grads, heads, n_f, reduce, back_sums=None, sums_mid=None, bias_sum=None):
    blocks, rows, _ = qkv.shape
    width = heads * HEAD
    length = rows * blocks
    tokens, dim = grad_one.shape
    sds = jax.ShapeDtypeStruct
    vmem, dma = pltpu.VMEM, pltpu.SemaphoreType.DMA
    in_vmem, anywhere = pl.BlockSpec(memory_space=pltpu.VMEM), pl.BlockSpec(memory_space=pl.ANY)
    operands = [qkv, grads, full, lse, grad_one]
    if reduce:
        operands += [sums_mid, bias_sum]
    inner = len(operands)
    operands += [w_local]
    out_shape = [sds((tokens, dim), F32), sds((16, dim) if reduce else (1, 3 * width), F32)]
    staged = (blocks, rows, 3 * width)
    scratch = [
        vmem((8, length), F32),
        vmem((8, length), F32),
        vmem((width, length), F32),
        vmem((width, length), BF16),
        vmem(staged, BF16),
        vmem(w_local.shape, BF16),
        vmem((rows, max(length, w_local.shape[1])), BF16),
        vmem((tokens, dim), F32),
        vmem((tokens, dim), F32),
        dma((blocks, 2)),
        dma((blocks, 2)),
        dma((blocks,)),
        dma((blocks,)),
        dma((dim // 256,)),
        dma((dim // 256,)),
        dma((3,)),
    ]
    if reduce:
        _, _, _, low, columns = mid_grads.shape
        operands += [x_all, mid_grads, back_sums]
        hidden_half = back_sums.shape[-1]
        out_shape += [sds((low, 2 * hidden_half), F32)] * 2 + [sds((low, dim), F32), sds((low, 3 * dim), F32)]
        n_peers = n_f.bit_length() + blocks.bit_length() - 1
        scratch = [vmem(staged, BF16)] + scratch
        scratch += [
            vmem(x_all.shape, BF16),
            vmem((blocks, 2, n_f, low, 3 * width), BF16),
            vmem((low, columns + hidden_half), F32),
            vmem((blocks, low, 3 * width), BF16),
            vmem((n_peers, 16, dim), F32),
            dma((2 * n_f + 1,)),
            dma((2 * n_f + 1,)),
            dma((blocks,)),
            dma((blocks,)),
            dma((n_peers,)),
            dma((n_peers,)),
        ]
        cut = (n_f - 1) * (hidden_half // n_f)
        for cols in (cut, columns - cut, 3 * width, hidden_half):
            halved = cols == hidden_half
            scratch += [
                vmem((2, 1 if halved else n_f // 2, blocks, low, cols), BF16),
                vmem((2, 1, 1, 16, 128) if halved else (2, n_f - 1, blocks, low, cols), BF16),
                vmem((2, blocks - 1, low, cols), BF16),
                dma((2, n_f // 2)),
                dma((2, n_f - 1)),
                dma((2, n_f - 1)),
                dma((2, blocks - 1)),
                dma((2, blocks - 1)),
            ]
    else:
        out_shape += [sds(staged, BF16)]
    return pl.pallas_call(
        partial(
            back_kernel, blocks=blocks, heads=heads, n_f=n_f, reduce=reduce, q_rows=256, steps_per=2
        ),
        out_shape=out_shape,
        in_specs=[in_vmem] * inner + [anywhere] * (len(operands) - inner),
        out_specs=[in_vmem] * len(out_shape),
        scratch_shapes=scratch,
        compiler_params=pltpu.CompilerParams(
            vmem_limit_bytes=VMEM_MIDDLE, collective_id=2, has_side_effects=True
        ),
        cost_estimate=pl.CostEstimate(
            flops=40 * length * length * width, bytes_accessed=30 << 20,
            transcendentals=heads * length * length,
        ),
        name="back",
    )(*operands)


def on_device(x_in, w_qkv, w_out, w_in, w_back, vectors, bias_in, cot, *, n_ctx, n_f):
    ctx, fs = lax.axis_index("ctx"), lax.axis_index("fsdp")
    core, zed = ctx % 2, ctx // 2
    n_z = n_ctx // 2
    x_own = x_in[0]
    grad_out = cot[0]
    rows, width = x_own.shape
    hidden = w_back.shape[0]
    half_heads = HEADS // 2
    heads = half_heads // n_z
    wide = heads * HEAD

    def swap(v):
        return lax.ppermute(v, "ctx", [(i, i ^ 1) for i in range(n_ctx)])

    def over_z(v, m):
        return lax.ppermute(v, "ctx", [(i, i ^ (2 * m)) for i in range(n_ctx)])

    def over_f(v, m):
        return lax.ppermute(v, "fsdp", [(i, i ^ m) for i in range(n_f)])

    bits = [1 << b for b in range(n_f.bit_length() - 1)]

    def place(pieces, index, axis):
        count = len(pieces)
        for bit in range(count.bit_length() - 1):
            flag = (index >> bit) & 1
            pieces = [jnp.where(flag, pieces[m ^ (1 << bit)], pieces[m]) for m in range(count)]
        return jnp.concatenate(pieces, axis=axis)

    half_in = width // 2
    first = (core * half_heads + zed * heads) * HEAD
    span = 3 * wide
    bias_qkv = jnp.concatenate(
        [
            lax.dynamic_slice_in_dim(vectors[0], first, wide, 0),
            jnp.zeros((wide,), F32),
            lax.dynamic_slice_in_dim(vectors[1], first, wide, 0),
        ]
    )[None]
    ff_part = w_in.shape[1] // 2
    w_back4 = w_back.reshape(n_f, 2, ff_part, w_back.shape[1])
    qkv, x_all, w_local, wo_half, wi_got, wb_got = front(
        x_own, w_qkv, w_out, w_in, w_back4, bias_qkv, n_f, n_z, heads
    )

    att, att_full, lse, wi_half, wb_got2 = attend(qkv, w_in, wi_got, w_back4, heads, n_f)
    bias_half = lax.dynamic_index_in_dim(
        bias_in.reshape(n_f, 2, ff_part), core, 1, False
    ).reshape(-1)
    low = width // (n_ctx * n_f)
    in_kernel = low % 16 == 0 and wide % 128 == 0 and hidden == n_f * width and min(n_z, n_f) >= 4
    layer_out, grad_one, g_att, sums_mid, bias_sum, mid_grads, *back_sums = middle(
        att, x_own, grad_out, vectors, bias_half, wo_half, wi_half, w_back4, wb_got, wb_got2, n_f, n_z, in_kernel
    )
    layer_out = layer_out[None]


    def over_fsdp(partial_grad):
        cols = partial_grad.shape[1]
        view = partial_grad.reshape((n_z, 2) + (2,) * len(bits) + (low, cols))
        done = []
        for side in range(2):
            now = view[:, side]
            order = bits if side == 0 else bits[1:] + bits[:1]
            left = list(reversed(bits))
            for bit in order:
                axis = 1 + left.index(bit)
                left.remove(bit)
                flag = (fs // bit) % 2
                stay = lax.dynamic_index_in_dim(now, flag, axis, False)
                go = lax.dynamic_index_in_dim(now, 1 - flag, axis, False)
                now = (stay.astype(F32) + over_f(go, bit).astype(F32)).astype(BF16)
            done.append(now)
        return jnp.stack(done, axis=1)

    def over_ctx(both):
        total = lax.dynamic_index_in_dim(both, zed, 0, False).astype(F32)
        for m in range(1, n_z):
            part = lax.dynamic_index_in_dim(both, zed ^ m, 0, False)
            total = total + over_z(part, m).astype(F32)
        stay = lax.dynamic_index_in_dim(total, core, 0, False)
        go = lax.dynamic_index_in_dim(total, 1 - core, 0, False)
        return stay, swap(go.astype(BF16)).astype(F32)

    def halves(stay, came, parts):
        low = stay.shape[0]
        first = jnp.where(core == 0, stay, came).reshape(low, parts, 1, -1)
        second = jnp.where(core == 0, came, stay).reshape(low, parts, 1, -1)
        return jnp.concatenate([first, second], axis=2).reshape(low, -1)

    def reduced(partial_grad):
        return over_ctx(over_fsdp(partial_grad))

    if in_kernel:
        grad_in, table, in_weight_grad, back_turned, out_weight_grad, qkv_weight_grad = back(
            qkv, g_att, att_full, lse, grad_one, w_local, x_all,
            mid_grads.reshape(n_z, 2, n_f, low, -1), heads, n_f, True, back_sums[0], sums_mid, bias_sum,
        )
        mine_at = (ctx * n_f + fs) * low
        vector_grad = lax.dynamic_slice_in_dim(table[:8], mine_at, low, 1)
        share = hidden // (n_ctx * n_f)
        in_bias_grad = lax.dynamic_slice_in_dim(table[8 : 8 + n_f].reshape(-1), mine_at // low * share, share, 0)
        return (
            layer_out,
            grad_in[None],
            qkv_weight_grad,
            out_weight_grad,
            in_weight_grad,
            back_turned.T,
            vector_grad,
            in_bias_grad,
        )
    stay, came = reduced(mid_grads)
    grad_in, sums, g_local = back(
        qkv, g_att, att_full, lse, grad_one, w_local, None, None, heads, n_f, False
    )
    attn_grad = dot(x_all.reshape(-1, width), g_local.reshape(-1, span), TN).astype(BF16)
    both = over_fsdp(attn_grad)
    mine, others = [], []
    for m in range(n_z):
        part = lax.dynamic_index_in_dim(both, zed ^ m, 0, False)
        part = part if m == 0 else over_z(part, m)
        mine.append(lax.dynamic_index_in_dim(part, core, 0, False))
        others.append(lax.dynamic_index_in_dim(part, 1 - core, 0, False))
    others = swap(jnp.stack(others))
    others = [others[m] for m in range(n_z)]
    n_half = hidden // 2
    in_weight_grad = halves(stay[:, :n_half], came[:, :n_half], n_f)
    back_weight_grad = halves(stay[:, n_half : 2 * n_half], came[:, n_half : 2 * n_half], n_f).T
    out_weight_grad = halves(stay[:, 2 * n_half :], came[:, 2 * n_half :], 1)

    def heads_order(parts):
        parts = [p.reshape(low, 3, wide) for p in parts]
        return place(parts, zed, 2).astype(F32).reshape(low, -1)

    qkv_weight_grad = halves(heads_order(mine), heads_order(others), 3)

    def spread(half_row, parts):
        piece = half_row.reshape(parts, 1, -1)
        empty = jnp.zeros_like(piece)
        both = jnp.where(core == 0, jnp.concatenate([piece, empty], 1), jnp.concatenate([empty, piece], 1))
        return both.reshape(-1)

    def halve(now):
        left = list(reversed(bits))
        for bit in bits:
            axis = left.index(bit)
            left.remove(bit)
            flag = (fs // bit) % 2
            stay = lax.dynamic_index_in_dim(now, flag, axis, False)
            now = stay + over_f(lax.dynamic_index_in_dim(now, 1 - flag, axis, False), bit)
        return now

    sums = sums[0]
    sums = jnp.stack([sums[:wide].reshape(n_f, -1), sums[2 * wide :].reshape(n_f, -1)], axis=1)
    late = halve(sums.reshape((2,) * len(bits) + (-1,)))
    turn = [(2 * z + c, n_z * c + z) for z in range(n_z) for c in range(2)]
    late = lax.ppermute(late, "ctx", turn).reshape(2, -1)
    ratio = hidden // width
    early = sums_mid[:6].T
    bias_terms = spread(bias_sum[0], n_f).reshape(width, ratio)
    table = jnp.concatenate([early, bias_terms], axis=1)
    kinds = table.shape[1]
    now = jnp.swapaxes(table.reshape(n_z * 2, n_f, low, kinds), -1, -2)
    now = jnp.swapaxes(now, 0, 1).reshape((2,) * len(bits) + (n_z, 2, kinds * low))
    now = halve(now)
    total = lax.dynamic_index_in_dim(now, zed, 0, False)
    for m in range(1, n_z):
        total = total + over_z(lax.dynamic_index_in_dim(now, zed ^ m, 0, False), m)
    stay = lax.dynamic_index_in_dim(total, core, 0, False)
    table = stay + swap(lax.dynamic_index_in_dim(total, 1 - core, 0, False))
    table = table.reshape(kinds, low)
    vector_grad = jnp.concatenate([late, table[:6]], axis=0)
    in_bias_grad = table[6:].T.reshape(-1)
    return (
        layer_out,
        grad_in[None],
        qkv_weight_grad,
        out_weight_grad,
        in_weight_grad,
        back_weight_grad,
        vector_grad,
        in_bias_grad,
    )


def solution(mesh):
    tokens = P("fsdp", "ctx", None)
    cols = P(None, "fsdp")
    shared = P(("ctx", "fsdp"), None)
    return jax.shard_map(
        partial(on_device, n_ctx=mesh.shape["ctx"], n_f=mesh.shape["fsdp"]),
        mesh=mesh,
        in_specs=(tokens, cols, cols, cols, cols, P(), P(), tokens),
        out_specs=(
            tokens,
            tokens,
            shared,
            shared,
            shared,
            P(None, ("ctx", "fsdp")),
            P(None, ("ctx", "fsdp")),
            P(("ctx", "fsdp")),
        ),
        check_vma=False,
    )
```

```python
from functools import partial
import math

import jax
import jax.numpy as jnp
from jax import lax
from jax.experimental import pallas as pl
from jax.experimental.pallas import tpu as pltpu
from jax.sharding import PartitionSpec as P

HEADS = 16
HEAD = 64
EPS = 1e-12
F32 = jnp.float32
BF16 = jnp.bfloat16
NN = (((1,), (0,)), ((), ()))
NT = (((1,), (1,)), ((), ()))
TN = (((0,), (0,)), ((), ()))
VMEM_LIMIT = 50 * 1024 * 1024
VMEM_MIDDLE = 56 * 1024 * 1024
MESH = pl.DeviceIdType.MESH


def dot(left, right, dims):
    return lax.dot_general(left, right, dims, preferred_element_type=F32)


def front_kernel(
    x_ref, wq_ref, wo_ref, wi_ref, wb_ref, bias_ref, qkv_ref, xf_out, wl_out, wo_out, wi_out, wb_out, *scratch, n_z, n_f, heads
):
    xf, wfull, wloc = scratch[:3]
    own_sem, x_send, x_recv, xs_send, xs_recv, w_send, w_recv, ws_send, ws_recv, o_send, o_recv, i_send, i_recv, b_send, b_recv, out_sem = scratch[3:]
    ctx, fs = lax.axis_index("ctx"), lax.axis_index("fsdp")
    core, zed = ctx % 2, ctx // 2
    bits = [1 << b for b in range(n_f.bit_length() - 1)]
    orders = (bits, bits[1:] + bits[:1])
    rows, width = x_ref.shape
    half = width // 2
    quarter = half // 2
    wide = heads * HEAD
    partner = {"ctx": zed * 2 + (1 - core)}

    barrier = pltpu.get_barrier_semaphore()

    def greet(device):
        pl.semaphore_signal(barrier, inc=1, device_id=device, device_id_type=MESH)

    greet(partner)
    for bit in bits:
        greet({"fsdp": fs ^ bit})

    @pl.when(zed > 0)
    def _():
        greet({"ctx": ctx - 2})

    @pl.when(zed < n_z - 1)
    def _():
        greet({"ctx": ctx + 2})

    edges = (zed == 0).astype(jnp.int32) + (zed == n_z - 1).astype(jnp.int32)
    pl.semaphore_wait(barrier, 3 + len(bits) - edges)

    def remote(src, dst, send, recv, device):
        return pltpu.make_async_remote_copy(
            src_ref=src, dst_ref=dst, send_sem=send, recv_sem=recv, device_id=device, device_id_type=MESH
        )

    def x_move(away, step, first):
        block = zed - step * away
        src = x_ref if first else xf.at[block ^ zed, 0]
        index = (step + 1) // 2
        return remote(
            src, xf.at[block ^ (zed + step), 0], x_send.at[index, away], x_recv.at[block ^ (zed + step)],
            {"ctx": ctx + 2 * step},
        )

    def x_swap(m, first=False):
        src = x_ref if first else xf.at[m, 0]
        return remote(src, xf.at[m, 1], xs_send.at[m], xs_recv.at[m], partner)

    def has(step):
        return zed < n_z - 1 if step == 1 else zed > 0

    def came(away, step):
        return zed - away >= 0 if step == 1 else zed + away <= n_z - 1

    for step in (1, -1):

        @pl.when(has(step))
        def _(step=step):
            x_move(0, step, True).start()

    x_swap(0, True).start()
    own_x = pltpu.make_async_copy(x_ref, xf.at[0, 0], own_sem.at[0])
    own_x.start()

    def x_step(away):
        for step in (1, -1):

            @pl.when(came(away, step))
            def _(step=step):
                block = zed - step * away
                remote(
                    xf.at[block ^ zed, 0], xf.at[block ^ zed, 0], x_send.at[0, 0], x_recv.at[block ^ zed], partner
                ).wait_recv()

                @pl.when(has(step))
                def _():
                    x_move(away, step, False).start()

                x_swap(block ^ zed).start()

    def wq_place(side, origin, which):
        cols = wq_ref.shape[1]
        return wfull.at[
            pl.ds(pl.multiple_of(which * half + side * quarter, quarter), quarter),
            pl.ds(pl.multiple_of(origin * cols, 128), cols),
        ]

    def wq_own(side):
        return wq_ref.at[pl.ds(pl.multiple_of(core * half + side * quarter, quarter), quarter), :]

    def wo_place(side, origin):
        cols = wo_ref.shape[1]
        return wo_out.at[pl.ds(side * quarter, quarter), pl.ds(pl.multiple_of(origin * cols, 128), cols)]

    def wo_own(side):
        return wo_ref.at[pl.ds(pl.multiple_of(core * half + side * quarter, quarter), quarter), :]

    def wq_hop(side, m, bit):
        src = wq_own(side) if m == 0 else wq_place(side, fs ^ m, core)
        return remote(src, wq_place(side, fs ^ m, core), w_send.at[side, m ^ bit], w_recv.at[side, m ^ bit], {"fsdp": fs ^ bit})

    def wo_hop(side, m, bit):
        src = wo_own(side) if m == 0 else wo_place(side, fs ^ m)
        return remote(src, wo_place(side, fs ^ m), o_send.at[side, m ^ bit], o_recv.at[side, m ^ bit], {"fsdp": fs ^ bit})

    def wq_swap(side, m):
        src = wq_own(side) if m == 0 else wq_place(side, fs ^ m, core)
        return remote(src, wq_place(side, fs ^ m, core), ws_send.at[side, m], ws_recv.at[side, m], partner)

    own_w = []
    for side in range(2):
        wq_hop(side, 0, orders[side][0]).start()
        wq_swap(side, 0).start()
        own_w.append(pltpu.make_async_copy(wq_own(side), wq_place(side, fs, core), own_sem.at[1 + side]))
        own_w.append(pltpu.make_async_copy(wo_own(side), wo_place(side, fs), own_sem.at[3 + side]))
    for copy in own_w:
        copy.start()

    part = wi_ref.shape[1] // 2

    def wi_hop(side):
        src = wi_ref.at[pl.ds(side * half, half), pl.ds(pl.multiple_of(core * part, 128), part)]
        return remote(src, wi_out.at[side], i_send.at[side], i_recv.at[side], {"fsdp": fs ^ orders[side][0]})

    def wb_hop(seg):
        return remote(
            wb_ref.at[seg, core], wb_out.at[seg], b_send.at[seg], b_recv.at[seg],
            {"fsdp": fs ^ orders[seg * 2 // n_f][0]},
        )

    def doubling(hop, level, after=None):
        for side in range(2):
            known = [0]
            for bit in orders[side][:level]:
                known = known + [m ^ bit for m in known]
            bit = orders[side][level]
            for m in known:
                hop(side, m, bit).wait_recv()
                if after is not None:
                    after(side, m ^ bit).start()
            if level + 1 < len(bits):
                for m in known + [m ^ bit for m in known]:
                    hop(side, m, orders[side][level + 1]).start()

    doubling(wq_hop, 0, wq_swap)
    for side in range(2):
        wo_hop(side, 0, orders[side][0]).start()
    x_step(1)
    for level in range(1, len(bits)):
        doubling(wq_hop, level, wq_swap)
    for side in range(2):
        wi_hop(side).start()
    doubling(wo_hop, 0)
    for seg in range(n_f):
        wb_hop(seg).start()
    for away in range(2, n_z - 1):
        x_step(away)
    for copy in own_w:
        copy.wait()
    for side in range(2):
        for m in range(n_f):
            wq_swap_in = remote(
                wq_place(side, fs ^ m, 1 - core), wq_place(side, fs ^ m, 1 - core),
                ws_send.at[side, m], ws_recv.at[side, m], partner,
            )
            wq_swap_in.wait_recv()
    outs = []
    for j in range(3):
        cols = pl.ds(pl.multiple_of(j * width + core * half, 128), half)
        outs.append(pltpu.make_async_copy(wfull.at[:, cols], wl_out.at[:, pl.ds(j * half, half)], out_sem.at[j]))
    for copy in outs:
        copy.start()
    for j in range(3):
        base = j * width + core * half + zed * wide
        if wide % 128 == 0:
            piece = wfull[:, pl.ds(pl.multiple_of(base, 128), wide)]
        else:
            block = wfull[:, pl.ds(pl.multiple_of(base // 128 * 128, 128), 128)].astype(F32)
            piece = jnp.where(zed % 2 == 1, block[:, wide:], block[:, :wide]).astype(BF16)
        wloc[:, j * wide : (j + 1) * wide] = piece

    def x_ready(m, side):
        remote(xf.at[m, side], xf.at[m, side], xs_send.at[m], xs_recv.at[m], partner).wait_recv()

    def project(m):
        def run(side, carry):
            result = dot(xf[m, side], wloc[...], NN) + bias_ref[...]
            where = pl.ds(pl.multiple_of(side * rows, rows), rows)
            qkv_ref[m, where, :] = result.astype(BF16)
            return carry

        lax.fori_loop(0, 2, run, 0)

    own_x.wait()
    x_ready(0, 1)
    project(0)

    def finish(away):
        def run(i, carry):
            block = zed - (1 - 2 * i) * away

            @pl.when((block >= 0) & (block <= n_z - 1))
            def _():
                x_ready(block ^ zed, 1)
                project(block ^ zed)

            return carry

        lax.fori_loop(0, 2, run, 0)

    for away in range(1, n_z - 1):
        finish(away)
    for level in range(1, len(bits)):
        doubling(wo_hop, level)
    if n_z > 2:
        x_step(n_z - 1)
    finish(n_z - 1)
    x_out = pltpu.make_async_copy(xf, xf_out, own_sem.at[5])
    x_out.start()

    for step in (1, -1):

        @pl.when(has(step))
        def _(step=step):
            x_move(0, step, True).wait_send()
            for away in range(1, n_z):

                @pl.when(came(away, step))
                def _(away=away):
                    x_move(away, step, False).wait_send()

    x_swap(0, True).wait_send()
    for m in range(1, n_z):
        x_swap(m).wait_send()
    for side in range(2):
        known = [0]
        for bit in orders[side]:
            for m in known:
                wq_hop(side, m, bit).wait_send()
                wo_hop(side, m, bit).wait_send()
            known = known + [m ^ bit for m in known]
        for m in range(n_f):
            wq_swap(side, m).wait_send()
        wi_hop(side).wait()
    for seg in range(n_f):
        wb_hop(seg).wait()
    for copy in outs:
        copy.wait()
    x_out.wait()


def front(x_own, w_qkv, w_out, w_in, w_back4, bias, n_f, n_z, heads):
    rows, width = x_own.shape
    wide = heads * HEAD
    sds = jax.ShapeDtypeStruct
    in_vmem, anywhere = pl.BlockSpec(memory_space=pltpu.VMEM), pl.BlockSpec(memory_space=pl.ANY)
    part = w_in.shape[1] // 2
    dma = pltpu.SemaphoreType.DMA
    return pl.pallas_call(
        partial(front_kernel, n_z=n_z, n_f=n_f, heads=heads),
        out_shape=[
            sds((n_z, 2 * rows, 3 * wide), BF16),
            sds((n_z, 2, rows, width), BF16),
            sds((width, 3 * width // 2), BF16),
            sds((width // 2, width), BF16),
            sds((2, width // 2, part), BF16),
            sds((n_f,) + w_back4.shape[2:], BF16),
        ],
        in_specs=[anywhere] * 5 + [in_vmem],
        out_specs=[in_vmem] + [anywhere] * 5,
        scratch_shapes=[
            pltpu.VMEM((n_z, 2, rows, width), BF16),
            pltpu.VMEM((width, 3 * width), BF16),
            pltpu.VMEM((width, 3 * wide), BF16),
            dma((6,)),
            dma((2, n_z)),
            dma((n_z,)),
            dma((n_z,)),
            dma((n_z,)),
            dma((2, n_f)),
            dma((2, n_f)),
            dma((2, n_f)),
            dma((2, n_f)),
            dma((2, n_f)),
            dma((2, n_f)),
            dma((2,)),
            dma((2,)),
            dma((n_f,)),
            dma((n_f,)),
            dma((3,)),
        ],
        compiler_params=pltpu.CompilerParams(
            vmem_limit_bytes=VMEM_LIMIT, collective_id=1, has_side_effects=True
        ),
        cost_estimate=pl.CostEstimate(
            flops=4 * n_z * rows * width * 3 * wide, bytes_accessed=30 << 20, transcendentals=0
        ),
        name="front",
    )(x_own, w_qkv, w_out, w_in, w_back4, bias)


def one_head(block, head, heads):
    if heads == 1:
        return block
    lane = lax.broadcasted_iota(jnp.int32, block.shape, 1)
    return jnp.where(lane // HEAD == head, block, jnp.zeros_like(block))


def merge_heads(parts):
    if len(parts) == 1:
        return parts[0]
    lane = lax.broadcasted_iota(jnp.int32, parts[0].shape, 1)
    result = parts[0]
    for head in range(1, len(parts)):
        result = jnp.where(lane // HEAD == head, parts[head], result)
    return result


def remote(src, dst, send, recv, device):
    return pltpu.make_async_remote_copy(
        src_ref=src, dst_ref=dst, send_sem=send, recv_sem=recv, device_id=device, device_id_type=MESH
    )


def greet(barrier, devices):
    for device in devices:
        pl.semaphore_signal(barrier, inc=1, device_id=device, device_id_type=MESH)
    pl.semaphore_wait(barrier, len(devices))


def fsdp_orders(n_f):
    bits = [1 << b for b in range(n_f.bit_length() - 1)]
    return bits, (bits, bits[1:] + bits[:1])


def known_at(order, level):
    known = [0]
    for bit in order[:level]:
        known = known + [m ^ bit for m in known]
    return known


def attend_kernel(*refs, blocks, heads, n_f, q_rows, k_rows):
    qkv_ref, wi_ref, got_ref, wb_ref = refs[:4]
    att_ref, full_ref, lse_ref, wi_out, wb_out = refs[4:9]
    key_s, value_s, send_s, a_send, a_recv, i_send, i_recv, b_send, b_recv, own_sem = refs[9:]
    ins = [qkv_ref.at[b] for b in range(blocks)]
    rows = ins[0].shape[0]
    width = heads * HEAD
    length = rows * blocks
    ctx, fs = lax.axis_index("ctx"), lax.axis_index("fsdp")
    core, zed = ctx % 2, ctx // 2
    bits, orders = fsdp_orders(n_f)
    greet(
        pltpu.get_barrier_semaphore(),
        [{"fsdp": fs ^ bit} for bit in bits] + [{"ctx": (zed ^ m) * 2 + core} for m in range(1, blocks)],
    )

    half, part = got_ref.shape[1:]

    def wi_place(side, m):
        return wi_out.at[pl.ds(side * half, half), pl.ds(pl.multiple_of((fs ^ m) * part, 128), part)]

    def wi_source(side, m):
        if m == 0:
            return wi_ref.at[pl.ds(side * half, half), pl.ds(pl.multiple_of(core * part, 128), part)]
        return got_ref.at[side] if m == orders[side][0] else wi_place(side, m)

    def wi_hop(side, m, bit):
        return remote(
            wi_source(side, m), wi_place(side, m), i_send.at[side, m ^ bit], i_recv.at[side, m ^ bit], {"fsdp": fs ^ bit}
        )

    def wb_hop(seg):
        return remote(
            wb_ref.at[seg, core], wb_out.at[seg], b_send.at[seg], b_recv.at[seg],
            {"fsdp": fs ^ orders[seg * 2 // n_f][1]},
        )

    def level(number, act):
        for side in range(2):
            for m in known_at(orders[side], number):
                act(wi_hop(side, m, orders[side][number]))

    locals_ = []
    for side in range(2):
        for i, m in enumerate((0, orders[side][0])):
            locals_.append(pltpu.make_async_copy(wi_source(side, m), wi_place(side, m), own_sem.at[2 * side + i]))
    for copy in locals_:
        copy.start()
    level(1, lambda hop: hop.start())
    for seg in range(n_f):
        wb_hop(seg).start()

    def att_hop(b):
        return remote(send_s.at[b - 1], att_ref.at[b], a_send.at[b], a_recv.at[b], {"ctx": (zed ^ b) * 2 + core})

    for b in range(blocks):
        here = slice(b * rows, (b + 1) * rows)
        key_s[here, :] = ins[b][:, width : 2 * width]
        value_s[here, :] = ins[b][:, 2 * width : 3 * width]
    for turn, b in enumerate(list(range(blocks - 1, 0, -1)) + [0]):

        def step(i, carry, b=b):
            local = pl.ds(pl.multiple_of(i * q_rows, q_rows), q_rows)
            where = pl.ds(pl.multiple_of(b * rows + i * q_rows, q_rows), q_rows)
            query = ins[b][local, 0:width] * BF16(HEAD**-0.5)
            outputs, sums = [], []
            for head in range(heads):
                masked = one_head(query, head, heads)
                scores = [
                    dot(masked, key_s[j : j + k_rows, :], NT) for j in range(0, length, k_rows)
                ]
                top = None
                for part in scores:
                    part_top = jnp.max(part, axis=1, keepdims=True)
                    top = part_top if top is None else jnp.maximum(top, part_top)
                total = acc = None
                for j, part in enumerate(scores):
                    probs = jnp.exp(part - top)
                    part_total = jnp.sum(probs, axis=1, keepdims=True)
                    value = value_s[j * k_rows : (j + 1) * k_rows, :]
                    part_acc = dot(probs.astype(BF16), value, NN)
                    total = part_total if total is None else total + part_total
                    acc = part_acc if acc is None else acc + part_acc
                outputs.append(acc / total)
                sums.append(jnp.broadcast_to(top + jnp.log(total), (q_rows, width)))
            result = merge_heads(outputs)
            full_ref[where, :] = result
            if b == 0:
                att_ref[0, local, :] = result.astype(BF16)
            else:
                send_s[b - 1, local, :] = result.astype(BF16)
            lse_ref[where, :] = merge_heads(sums)
            return carry

        lax.fori_loop(0, rows // q_rows, step, 0)
        if b > 0:
            att_hop(b).start()
        if 0 < turn < len(bits) - 1:
            level(turn, lambda hop: hop.wait_recv())
            level(turn + 1, lambda hop: hop.start())
    level(len(bits) - 1, lambda hop: hop.wait_recv())
    for number in range(1, len(bits)):
        level(number, lambda hop: hop.wait_send())
    for seg in range(n_f):
        wb_hop(seg).wait()
    for b in range(1, blocks):
        att_hop(b).wait()
    for copy in locals_:
        copy.wait()


def attend(qkv, w_in, wi_got, w_back4, heads, n_f):
    blocks, rows, _ = qkv.shape
    width = heads * HEAD
    length = rows * blocks
    _, half, part = wi_got.shape
    _, _, seg_rows, seg_cols = w_back4.shape
    sds = jax.ShapeDtypeStruct
    in_vmem, anywhere = pl.BlockSpec(memory_space=pltpu.VMEM), pl.BlockSpec(memory_space=pl.ANY)
    dma = pltpu.SemaphoreType.DMA
    return pl.pallas_call(
        partial(attend_kernel, blocks=blocks, heads=heads, n_f=n_f, q_rows=256, k_rows=512),
        out_shape=[
            sds((blocks, rows, width), BF16),
            sds((length, width), F32),
            sds((length, width), F32),
            sds((2 * half, n_f * part), BF16),
            sds((n_f, seg_rows, seg_cols), BF16),
        ],
        in_specs=[in_vmem] + [anywhere] * 3,
        out_specs=[in_vmem] * 3 + [anywhere] * 2,
        scratch_shapes=[pltpu.VMEM((length, width), BF16)] * 2
        + [
            pltpu.VMEM((blocks - 1, rows, width), BF16),
            dma((blocks,)),
            dma((blocks,)),
            dma((2, n_f)),
            dma((2, n_f)),
            dma((n_f,)),
            dma((n_f,)),
            dma((4,)),
        ],
        compiler_params=pltpu.CompilerParams(
            vmem_limit_bytes=VMEM_LIMIT, collective_id=3, has_side_effects=True
        ),
        cost_estimate=pl.CostEstimate(
            flops=16 * length * length * width, bytes_accessed=10 * length * width,
            transcendentals=heads * length * length,
        ),
        name="attend",
    )(qkv, w_in, wi_got, w_back4)


def gelu_both(pre):
    slope = math.sqrt(2.0 / math.pi)
    square = pre * pre
    th = jnp.tanh(slope * (pre + 0.044715 * pre * square))
    half = 0.5 * (1.0 + th)
    grad = half + 0.5 * pre * (1.0 - th * th) * (slope * (1.0 + 3 * 0.044715 * square))
    return pre * half, grad


class Reduction:
    def __init__(self, src, cols, acc, got, far, sems, n_f, n_z, begin=0, summed=True):
        self.begin, self.summed = begin, summed
        self.z_bits = [1 << i for i in range(n_z.bit_length() - 1)]
        self.src, self.cols, self.acc, self.got, self.far = src, cols, acc, got, far
        self.load_sem, self.f_send, self.f_recv, self.z_send, self.z_recv = sems
        self.n_z = n_z
        ctx, self.fs = lax.axis_index("ctx"), lax.axis_index("fsdp")
        self.core, self.zed = ctx % 2, ctx // 2
        self.bits, self.orders = fsdp_orders(n_f)
        self.last = len(self.bits) - 1

    def targets(self, side, level):
        found = [0]
        for bit in reversed(self.orders[side][level + 1 :]):
            found = found + [d ^ bit for d in found]
        return found

    def part(self, side, target):
        return self.src.at[:, side, target, :, self.cols]

    def load(self, side, i):
        d = self.targets(side, 0)[i]
        return pltpu.make_async_copy(self.part(side, self.fs ^ d), self.acc.at[side, i], self.load_sem.at[side, i])

    def hop(self, side, level, i):
        bit = self.orders[side][level]
        first = sum(len(self.targets(side, l)) for l in range(level))
        if level == 0:
            src = self.part(side, self.fs ^ bit ^ self.targets(side, 0)[i])
        else:
            src = self.acc.at[side, len(self.targets(side, level)) + i]
        return remote(
            src, self.got.at[side, first + i], self.f_send.at[side, first + i], self.f_recv.at[side, first + i],
            {"fsdp": self.fs ^ bit},
        )

    def every(self, level, act):
        for side in range(2):
            for i in range(len(self.targets(side, level))):
                act(self.hop(side, level, i))

    def loads(self, act):
        for side in range(2):
            for i in range(len(self.targets(side, 0))):
                act(self.load(side, i))

    def start(self):
        self.every(0, lambda hop: hop.start())
        self.loads(lambda copy: copy.start())

    def level(self, level):
        if level == 0:
            self.loads(lambda copy: copy.wait())
        self.every(level, lambda hop: hop.wait_recv())
        first = sum(len(self.targets(0, l)) for l in range(level))
        count = len(self.targets(0, level))

        def add(n, carry):
            side, rest = n // (count * self.n_z), n % (count * self.n_z)
            i, z = rest // self.n_z, rest % self.n_z
            total = self.acc[side, i, z].astype(F32) + self.got[side, first + i, z].astype(F32)
            self.acc[side, i, z] = total.astype(BF16)
            return carry

        lax.fori_loop(0, 2 * count * self.n_z, add, 0)
        if level < self.last:
            self.every(level + 1, lambda hop: hop.start())
        elif self.far is not None:
            self.z_start()

    def z_targets(self, level):
        found = [0]
        for bit in reversed(self.z_bits[level + 1 :]):
            found = found + [d ^ bit for d in found]
        return found

    def z_hops(self, level):
        hops = []
        if self.summed:
            bit = self.z_bits[level]
            first = sum(len(self.z_targets(l)) for l in range(level))
            moves = [(bit ^ d, bit, first + i) for i, d in enumerate(self.z_targets(level))]
        else:
            moves = [(m, m, m - 1) for m in range(self.n_z - 1, 0, -1)]
        for block, away, slot in moves:
            for side in range(2):
                hops.append(
                    remote(
                        self.acc.at[side, 0, self.zed ^ block], self.far.at[side, slot], self.z_send.at[side, slot],
                        self.z_recv.at[side, slot], {"ctx": (self.zed ^ away) * 2 + self.core},
                    )
                )
        return hops

    def z_start(self, level=0):
        for hop in self.z_hops(level):
            hop.start()

    def z_level(self, level):
        for hop in self.z_hops(level):
            hop.wait_recv()
        if level == len(self.z_bits) - 1:
            return
        first = sum(len(self.z_targets(l)) for l in range(level))
        for i, d in enumerate(self.z_targets(level)):
            for side in range(2):
                total = self.acc[side, 0, self.zed ^ d].astype(F32) + self.far[side, first + i].astype(F32)
                self.acc[side, 0, self.zed ^ d] = total.astype(BF16)
        self.z_start(level + 1)

    def arrived(self):
        for hop in self.z_hops(0):
            hop.wait_recv()

    def total(self, side):
        return self.acc[side, 0, self.zed].astype(F32) + self.far[side, self.n_z - 2].astype(F32)

    def sent(self):
        for level in range(self.begin, self.last + 1):
            self.every(level, lambda hop: hop.wait_send())
        if self.far is not None:
            for level in range(len(self.z_bits) if self.summed else 1):
                for hop in self.z_hops(level):
                    hop.wait_send()


def row_stats(value):
    return jnp.mean(value, axis=1, keepdims=True)


def mid_kernel(*refs, n_f, n_z, reduce, cfg):
    refs = list(refs)
    red_refs = [refs.pop() for _ in range(6)][::-1] if reduce else None
    sum_out = refs.pop(16) if reduce else None
    att_in, x_ref, cot_ref, vec_ref, bias_ref, wo_ref, wi_ref, wb_ref, got_ref, got2_ref = refs[:10]
    layer_ref, grad_one_ref, ga_ref, sums_ref, bias_sum_ref, grads_out = refs[10:16]
    att_ref, att2_s, h_ref, act_ref, g2_ref, gp_ref, g1_ref, ga_s, turned_s, og_s = refs[16:26]
    wo_s, wi_s, wb_s, slope_s, normed_s, unit_s, acc_s, send_s, recv_s, rstd_s = refs[26:36]
    w_sem, send_sem, recv_sem, b_send, b_recv, a_send, a_recv, g_sem = refs[36:]
    ctx, fs = lax.axis_index("ctx"), lax.axis_index("fsdp")
    core, zed = ctx % 2, ctx // 2
    partner = {"ctx": zed * 2 + (1 - core)}
    rows, width = x_ref.shape
    own, other = slice(0, rows), slice(rows, 2 * rows)
    wide = att_in.shape[2]
    half_in = n_z * wide
    ff_half = wi_s.shape[1]
    step = cfg["step"]
    chunk = cfg["rows"]
    bits, orders = fsdp_orders(n_f)
    _, _, seg_rows, seg_cols = wb_ref.shape

    def wb_place(seg, m):
        return wb_s.at[
            pl.ds(seg * seg_rows, seg_rows), pl.ds(pl.multiple_of((fs ^ m) * seg_cols, 128), seg_cols)
        ]

    def wb_order(seg):
        return orders[seg * 2 // n_f]

    def wb_source(seg, m):
        if m == 0:
            return wb_ref.at[seg, core]
        if m == wb_order(seg)[1]:
            return got2_ref.at[seg]
        return got_ref.at[seg] if m == wb_order(seg)[0] else wb_place(seg, m)

    def wb_hop(seg, m, bit):
        return remote(
            wb_source(seg, m), wb_place(seg, m), b_send.at[seg, m ^ bit], b_recv.at[seg, m ^ bit], {"fsdp": fs ^ bit}
        )

    def wb_level(number, act):
        for seg in range(n_f):
            for m in known_at(wb_order(seg), number)[1 if number == 1 else 0 :]:
                act(wb_hop(seg, m, wb_order(seg)[number]))

    copies = [
        [pltpu.make_async_copy(wo_ref, wo_s, w_sem.at[0])],
        [pltpu.make_async_copy(wi_ref, wi_s, w_sem.at[1])],
        [],
    ]
    for seg in range(n_f):
        for i, m in enumerate((0, wb_order(seg)[0], wb_order(seg)[1])):
            copies[2].append(pltpu.make_async_copy(wb_source(seg, m), wb_place(seg, m), w_sem.at[2 + 3 * seg + i]))
    for copy in copies[0] + copies[1]:
        copy.start()
    greet(
        pltpu.get_barrier_semaphore(),
        [partner] + [{"fsdp": fs ^ bit} for bit in bits] + [{"ctx": (zed ^ m) * 2 + core} for m in range(1, n_z)],
    )
    wb_level(1, lambda hop: hop.start())
    for copy in copies[2]:
        copy.start()

    def exchange(n, src, dst):
        return remote(src, dst, send_sem.at[n], recv_sem.at[n], partner)

    def over_cols(total, body):
        def run(i, carry):
            body(pl.ds(pl.multiple_of(i * step, step), step))
            return carry

        lax.fori_loop(0, total // step, run, 0)

    def over_rows(body):
        def run(i, carry):
            return body(pl.ds(pl.multiple_of(i * chunk, chunk), chunk), carry)

        zero = jnp.zeros((1, width), F32)
        return lax.fori_loop(0, rows // chunk, run, (zero, zero, zero))

    if wide % 128 == 0:
        for m in range(n_z):
            att_ref[:, pl.ds(pl.multiple_of((zed ^ m) * wide, wide), wide)] = att_in[m]
    else:
        for m in range(0, n_z, 2):
            one, two = att_in[m].astype(F32), att_in[m + 1].astype(F32)
            odd = zed % 2 == 1
            block = jnp.concatenate([jnp.where(odd, two, one), jnp.where(odd, one, two)], axis=1)
            at = pl.ds(pl.multiple_of((zed // 2 ^ (m // 2)) * 2 * wide, 2 * wide), 2 * wide)
            att_ref[:, at] = block.astype(BF16)

    def wait_all(group):
        for copy in group:
            copy.wait()

    att_move = exchange(6, att_ref, att2_s)
    att_move.start()

    wait_all(copies[0])

    def out_other(cols):
        send_s[:, cols] = dot(att_ref[other, :], wo_s[:, cols], NN)

    over_cols(width, out_other)
    move = exchange(0, send_s, recv_s)
    move.start()

    def out_own(cols):
        part = dot(att_ref[own, :], wo_s[:, cols], NN)
        acc_s[:, cols] = part + x_ref[:, cols].astype(F32) + vec_ref[2:3, cols]

    over_cols(width, out_own)
    move.wait()

    def norm_one(r, carry):
        resid = acc_s[r, :] + recv_s[r, :]
        centre = resid - row_stats(resid)
        rstd = lax.rsqrt(row_stats(centre * centre) + EPS)
        unit = centre * rstd
        normed = unit * vec_ref[3:4, :] + vec_ref[4:5, :]
        unit_s[r, :] = unit
        rstd_s[r, :] = jnp.broadcast_to(rstd, (chunk, 128))
        normed_s[r, :] = normed
        h_ref[r, :] = normed.astype(BF16)
        return carry

    over_rows(norm_one)
    move = exchange(1, h_ref.at[own], h_ref.at[other])
    move.start()

    wait_all(copies[1])

    def up(where):
        def body(cols):
            pre = dot(h_ref[where, :], wi_s[:, cols], NN) + bias_ref[0:1, cols]
            act, slope = gelu_both(pre)
            act_ref[where, cols] = act.astype(BF16)
            slope_s[where, cols] = slope

        over_cols(ff_half, body)

    up(own)
    move.wait()
    up(other)
    for number in range(1, len(bits)):
        wb_level(number, lambda hop: hop.wait_recv())
        if number + 1 < len(bits):
            wb_level(number + 1, lambda hop: hop.start())
    wait_all(copies[2])

    def down_other(cols):
        send_s[:, cols] = dot(act_ref[other, :], wb_s[:, cols], NN)

    over_cols(width, down_other)
    move = exchange(2, send_s, recv_s)
    move.start()

    def down_own(cols):
        part = dot(act_ref[own, :], wb_s[:, cols], NN)
        acc_s[:, cols] = part + normed_s[:, cols] + vec_ref[5:6, cols]

    over_cols(width, down_own)
    move.wait()

    def norm_two(r, carry):
        resid = acc_s[r, :] + recv_s[r, :]
        centre = resid - row_stats(resid)
        rstd = lax.rsqrt(row_stats(centre * centre) + EPS)
        unit = centre * rstd
        gain = vec_ref[6:7, :]
        layer_ref[r, :] = (unit * gain + vec_ref[7:8, :]).astype(BF16)
        grad = cot_ref[r, :]
        scaled = grad * gain
        back = rstd * (scaled - row_stats(scaled) - unit * row_stats(scaled * unit))
        acc_s[r, :] = back
        g2_ref[r, :] = back.astype(BF16)
        sums = (back, grad * unit, grad)
        return tuple(c + jnp.sum(s, axis=0, keepdims=True) for c, s in zip(carry, sums))

    shift_two = over_rows(norm_two)
    move = exchange(3, g2_ref.at[own], g2_ref.at[other])
    move.start()
    for i, total in enumerate(shift_two):
        sums_ref[3 + i : 4 + i, :] = total

    def back_act(where, first):
        def body(cols):
            grad = dot(g2_ref[where, :], wb_s[cols, :], NT) * slope_s[where, cols]
            gp_ref[where, cols] = grad.astype(BF16)
            total = jnp.sum(grad, axis=0, keepdims=True)
            bias_sum_ref[0:1, cols] = total if first else bias_sum_ref[0:1, cols] + total

        over_cols(ff_half, body)

    back_act(own, True)
    move.wait()
    n_out = ff_half // step
    d_rows = width // n_z

    def product(left, right, store):
        for i in range(0, width, 256):
            turned_s[i : i + 256, :] = left[:, i : i + 256].T

        def cols_of(i, carry):
            cols = pl.ds(pl.multiple_of(i * step, step), step)
            store(i, cols, dot(turned_s[...], right[:, cols], NN).astype(BF16))
            return carry

        lax.fori_loop(0, n_out, cols_of, 0)

    if reduce:
        gb_s, acc_r, got_r, load_sem, f_send, f_recv = red_refs
        sums = Reduction(gb_s, pl.ds(0, ff_half), acc_r, got_r, None, (load_sem, f_send, f_recv, None, None), n_f, n_z)
        low = gb_s.shape[3]

        def store_back(i, cols, value):
            gb_s[:, :, :, :, cols] = value.reshape(n_z, 2, n_f, low, step)

        product(g2_ref, act_ref, store_back)
        sums.start()
    back_act(other, False)

    def back_other(cols):
        send_s[:, cols] = dot(gp_ref[other, :], wi_s[cols, :], NT)

    over_cols(width, back_other)
    move = exchange(4, send_s, recv_s)
    move.start()

    def back_own(cols):
        acc_s[:, cols] += dot(gp_ref[own, :], wi_s[cols, :], NT)

    over_cols(width, back_own)
    move.wait()

    def back_one(r, carry):
        grad = acc_s[r, :] + recv_s[r, :]
        unit = unit_s[r, :]
        rstd = rstd_s[r, 0:1]
        scaled = grad * vec_ref[3:4, :]
        back = rstd * (scaled - row_stats(scaled) - unit * row_stats(scaled * unit))
        grad_one_ref[r, :] = back
        g1_ref[r, :] = back.astype(BF16)
        sums = (back, grad * unit, grad)
        return tuple(c + jnp.sum(s, axis=0, keepdims=True) for c, s in zip(carry, sums))

    shift_one = over_rows(back_one)
    move = exchange(5, g1_ref.at[own], g1_ref.at[other])
    move.start()
    for i, total in enumerate(shift_one):
        sums_ref[i : 1 + i, :] = total
    sums_ref[6:8, :] = jnp.zeros((2, width), F32)

    def att_hop(m):
        return remote(ga_s.at[m - 1], ga_ref.at[m], a_send.at[m], a_recv.at[m], {"ctx": (zed ^ m) * 2 + core})

    move.wait()
    for m in list(range(n_z - 1, 0, -1)) + [0]:
        at = pl.ds(pl.multiple_of((zed ^ m) * wide, wide), wide)
        block = dot(g1_ref[...], wo_s[at, :], NT).astype(BF16)
        if m == 0:
            ga_ref[0] = block
        else:
            ga_s[m - 1] = block
            att_hop(m).start()

    if reduce:
        sums.level(0)

    def out_grad(i, which):
        cols = pl.ds(pl.multiple_of(i * step, step), step)
        there = pl.ds(pl.multiple_of(which * ff_half + i * step, step), step)
        return pltpu.make_async_copy(wi_s.at[:, cols], grads_out.at[:, there], g_sem.at[which * n_out + i])

    def store_staged(which):
        def store(i, cols, value):
            if which == 1:
                out_grad(i, 0).wait()
            wi_s[:, cols] = value
            out_grad(i, which).start()

        return store

    product(h_ref, gp_ref, store_staged(0))
    wide_out = ff_half
    if not reduce:
        product(g2_ref, act_ref, store_staged(1))
        wide_out = 2 * ff_half
    att_move.wait()
    half = width // 2
    cols = pl.ds(pl.multiple_of(core * half, 128), half)
    for i in range(0, half_in, 256):
        at = pl.ds(pl.multiple_of(core * half + i, 128), 256)
        og_s[at, :] = dot(att_ref[:, i : i + 256].T, g1_ref[:, cols], NN).astype(BF16)
        at = pl.ds(pl.multiple_of((1 - core) * half + i, 128), 256)
        turned = att2_s[:, i : i + 256].T
        og_s[at, :] = (
            dot(turned[:, :rows], g1_ref[rows:, cols], NN) + dot(turned[:, rows:], g1_ref[:rows, cols], NN)
        ).astype(BF16)
    out_move = pltpu.make_async_copy(og_s, grads_out.at[:, pl.ds(wide_out, half)], g_sem.at[2 * n_out])
    out_move.start()
    for number in range(1, len(bits)):
        wb_level(number, lambda hop: hop.wait_send())
    for m in range(1, n_z):
        att_hop(m).wait()
    for i in range(n_out):
        out_grad(i, 0 if reduce else 1).wait()
    out_move.wait()
    if reduce:
        for level in range(1, len(bits)):
            sums.level(level)
        final = pltpu.make_async_copy(acc_r.at[:, pl.ds(0, 1)], sum_out, load_sem.at[0, 0])
        final.start()
        sums.sent()
        final.wait()


def middle(att, x_own, cot, vectors, bias_half, wo, wi, wb4, got, got2, n_f, n_z, reduce):
    rows, width = x_own.shape
    wide = att.shape[2]
    ff_half = bias_half.shape[0]
    half_in = n_z * wide
    sds = jax.ShapeDtypeStruct
    vmem, dma = pltpu.VMEM, pltpu.SemaphoreType.DMA
    in_vmem, anywhere = pl.BlockSpec(memory_space=pltpu.VMEM), pl.BlockSpec(memory_space=pl.ANY)
    cfg = {"step": 512, "rows": 128}
    low = width // (2 * n_z * n_f)
    extra_out, extra = [], []
    if reduce:
        extra_out = [sds((2, 1, n_z, low, ff_half), BF16)]
        extra = [
            vmem((n_z, 2, n_f, low, ff_half), BF16),
            vmem((2, n_f // 2, n_z, low, ff_half), BF16),
            vmem((2, n_f - 1, n_z, low, ff_half), BF16),
            dma((2, n_f // 2)),
            dma((2, n_f - 1)),
            dma((2, n_f - 1)),
        ]
    return pl.pallas_call(
        partial(mid_kernel, n_f=n_f, n_z=n_z, reduce=reduce, cfg=cfg),
        out_shape=[
            sds((rows, width), BF16),
            sds((rows, width), F32),
            sds((n_z, 2 * rows, wide), BF16),
            sds((8, width), F32),
            sds((1, ff_half), F32),
            sds((width, (1 if reduce else 2) * ff_half + width // 2), BF16),
        ]
        + extra_out,
        in_specs=[in_vmem] * 5 + [anywhere] * 5,
        out_specs=[in_vmem] * 5 + [anywhere] * (1 + len(extra_out)),
        scratch_shapes=[
            vmem((2 * rows, half_in), BF16),
            vmem((2 * rows, half_in), BF16),
            vmem((2 * rows, width), BF16),
            vmem((2 * rows, ff_half), BF16),
            vmem((2 * rows, width), BF16),
            vmem((2 * rows, ff_half), BF16),
            vmem((2 * rows, width), BF16),
            vmem((n_z - 1, 2 * rows, wide), BF16),
            vmem((width, 2 * rows), BF16),
            vmem((width, width // 2), BF16),
            vmem((half_in, width), BF16),
            vmem((width, ff_half), BF16),
            vmem((ff_half, width), BF16),
            vmem((2 * rows, ff_half), F32),
            vmem((rows, width), F32),
            vmem((rows, width), F32),
            vmem((rows, width), F32),
            vmem((rows, width), F32),
            vmem((rows, width), F32),
            vmem((rows, 128), F32),
            dma((2 + 3 * n_f,)),
            dma((7,)),
            dma((7,)),
            dma((n_f, n_f)),
            dma((n_f, n_f)),
            dma((n_z,)),
            dma((n_z,)),
            dma((2 * (ff_half // cfg["step"]) + 1,)),
        ]
        + extra,
        compiler_params=pltpu.CompilerParams(
            vmem_limit_bytes=VMEM_MIDDLE, collective_id=0, has_side_effects=True
        ),
        cost_estimate=pl.CostEstimate(
            flops=2 * 2 * rows * width * (3 * half_in + 6 * ff_half),
            bytes_accessed=40 << 20, transcendentals=2 * rows * ff_half,
        ),
        name="middle",
    )(att, x_own, cot, vectors, bias_half[None], wo, wi, wb4, got, got2)


def back_kernel(*refs, blocks, heads, n_f, reduce, q_rows, steps_per):
    refs = list(refs)

    def take(count):
        taken = refs[:count]
        del refs[:count]
        return taken

    qkv_ref, ga_ref, full_ref, lse_ref, grad_one_ref = take(5)
    if reduce:
        mid_ref, bias_ref = take(2)
    (wl_hbm,) = take(1)
    if reduce:
        x_hbm, g_hbm, back_hbm = take(3)
    out_ref, sums_ref = take(2)
    if reduce:
        in_ref, back_ref, og_ref, qg_ref = take(4)
    (stage,) = take(1)
    lse_t, delta_t, gq_t, key_t, gin, wl_s, cat, send_s, recv_s = take(9)
    kv_send, kv_recv, q_send, q_recv, t_send, t_recv, own_sem = take(7)
    if reduce:
        x_s, gq_src, give_s, others, table_r, c_send, c_recv, o_send, o_recv, s_send, s_recv = take(11)
        bufs = [take(8) for _ in range(4)]
    ctx, fs = lax.axis_index("ctx"), lax.axis_index("fsdp")
    core, zed = ctx % 2, ctx // 2
    partner = {"ctx": zed * 2 + (1 - core)}
    bits, orders = fsdp_orders(n_f)
    rows = qkv_ref.shape[1]
    width = heads * HEAD
    scale = HEAD**-0.5
    chunk = 256
    half = wl_s.shape[1] // 3
    greeted = [partner] + [{"ctx": (zed ^ m) * 2 + core} for m in range(1, blocks)]
    if reduce:
        greeted += [{"fsdp": fs ^ bit} for bit in bits]
    greet(pltpu.get_barrier_semaphore(), greeted)
    wl_copy = pltpu.make_async_copy(wl_hbm, wl_s, own_sem.at[0])
    wl_copy.start()
    if reduce:
        cut = bufs[0][0].shape[-1]
        early, late, attn, lone = [
            Reduction(
                src, pl.ds(first, buf[0].shape[-1]), buf[0], buf[1], buf[2], buf[3:], n_f, blocks, begin, summed
            )
            for buf, src, first, begin, summed in zip(
                bufs, (g_hbm, g_hbm, gq_src, None), (0, cut, 0, 0), (0, 0, 0, len(bits)), (True, True, False, True)
            )
        ]
        lone_copy = pltpu.make_async_copy(back_hbm, lone.acc, own_sem.at[2])
        lone_copy.start()
        lone_copy.wait()
        lone.z_start()
        early.start()
        x_copy = pltpu.make_async_copy(x_hbm, x_s, own_sem.at[1])
        x_copy.start()

    for b in range(blocks):
        for i in range(0, rows, chunk):
            local = slice(i, i + chunk)
            where = slice(b * rows + i, b * rows + i + chunk)
            logs = lse_ref[where, :].T
            terms = (ga_ref[b, local, :].astype(F32) * full_ref[where, :]).T
            for head in range(heads):
                first = head * HEAD
                lse_t[head : head + 1, where] = logs[first : first + 1]
                delta_t[head : head + 1, where] = jnp.sum(
                    terms[first : first + HEAD], axis=0, keepdims=True
                )
        key_t[:, b * rows : (b + 1) * rows] = qkv_ref[b, :, width : 2 * width].T
    gq_t[...] = jnp.zeros_like(gq_t)

    split = width % 128 == 0

    def kv_hop(m, piece):
        at = pl.ds(pl.multiple_of(piece * (rows // steps_per), 128), rows // steps_per)
        cols = pl.ds(width, 2 * width)
        return remote(
            stage.at[m, at, cols], gin.at[m, at, cols], kv_send.at[m, piece], kv_recv.at[m, piece],
            {"ctx": (zed ^ m) * 2 + core},
        )

    def q_hop(m):
        cols = pl.ds(0, width if split else 3 * width)
        return remote(
            stage.at[m, :, cols], gin.at[m, :, cols], q_send.at[m], q_recv.at[m], {"ctx": (zed ^ m) * 2 + core}
        )

    k_rows = rows // steps_per

    def step(n, carry):
        b = blocks - 1 - n // steps_per
        start = n % steps_per * k_rows
        local = pl.ds(pl.multiple_of(start, 128), k_rows)
        where = pl.ds(pl.multiple_of(b * rows + start, 128), k_rows)
        key = qkv_ref[b, local, width : 2 * width]
        value = qkv_ref[b, local, 2 * width : 3 * width]
        key_grads, value_grads = [], []
        for head in range(heads):
            feats = slice(head * HEAD, (head + 1) * HEAD)
            key_h = one_head(key, head, heads) * BF16(scale)
            value_h = one_head(value, head, heads)
            key_grad = value_grad = None
            for other in range(blocks):
                for i in range(0, rows, q_rows):
                    here = slice(i, i + q_rows)
                    there = slice(other * rows + i, other * rows + i + q_rows)
                    query = qkv_ref[other, here, 0:width]
                    grad = ga_ref[other, here, :]
                    scores = dot(key_h, query, NT)
                    probs = jnp.exp(scores - lse_t[head : head + 1, there])
                    grad_probs = dot(value_h, grad, NT)
                    grad_scores = probs * (grad_probs - delta_t[head : head + 1, there])
                    grad_scores = grad_scores.astype(BF16)
                    term = dot(probs.astype(BF16), grad, NN)
                    value_grad = term if value_grad is None else value_grad + term
                    term = dot(grad_scores, query, NN)
                    key_grad = term if key_grad is None else key_grad + term
                    gq_t[feats, there] += dot(key_t[feats, where], grad_scores, NN)
            key_grads.append(key_grad)
            value_grads.append(value_grad)
        stage[b, local, width : 2 * width] = (merge_heads(key_grads) * scale).astype(BF16)
        stage[b, local, 2 * width : 3 * width] = merge_heads(value_grads).astype(BF16)
        if split:

            @pl.when(b > 0)
            def _():
                kv_hop(b, n % steps_per).start()

        if reduce:

            @pl.when(n == 1)
            def _():
                early.level(0)

            @pl.when(n == 2)
            def _():
                late.start()

            @pl.when(n == 3)
            def _():
                lone.z_level(0)
                for level in range(1, len(bits)):
                    early.level(level)

            @pl.when(n == 4)
            def _():
                late.level(0)

            @pl.when(n == 5)
            def _():
                early.z_level(0)
                for level in range(1, len(bits)):
                    late.level(level)

        return carry

    lax.fori_loop(0, blocks * steps_per, step, 0)
    for b in range(blocks - 1, -1, -1):
        for i in range(0, rows, chunk):
            there = slice(b * rows + i, b * rows + i + chunk)
            stage[b, i : i + chunk, 0:width] = (gq_t[:, there].T * scale).astype(BF16)
        if b > 0:
            q_hop(b).start()
    gin[0] = stage[0]
    sums = jnp.zeros((1, 3 * width), F32)
    for b in range(blocks):
        sums = sums + jnp.sum(stage[b].astype(F32), axis=0, keepdims=True)
    if reduce:
        dim = out_ref.shape[1]
        hidden_half = bias_ref.shape[1] // n_f
        sums_ref[...] = jnp.zeros_like(sums_ref)
        first = pl.ds(pl.multiple_of(core * half + zed * width, 128), width)
        sums_ref[0:1, first] = sums[:, 0:width]
        sums_ref[1:2, first] = sums[:, 2 * width :]
        sums_ref[2:8, :] = mid_ref[0:6, :]
        for f in range(n_f):
            at = pl.ds(pl.multiple_of(core * hidden_half, 128), hidden_half)
            sums_ref[8 + f : 9 + f, at] = bias_ref[:, f * hidden_half : (f + 1) * hidden_half]
        peers = [{"fsdp": fs ^ bit} for bit in bits]
        peers += [{"ctx": (zed ^ (1 << i)) * 2 + core} for i in range(blocks.bit_length() - 1)] + [partner]

        def table_hop(k):
            return remote(sums_ref, table_r.at[k], s_send.at[k], s_recv.at[k], peers[k])

        def table_step(k):
            if k < len(peers):
                table_hop(k).wait()
                sums_ref[...] += table_r[k]
                if k + 1 < len(peers):
                    table_hop(k + 1).start()

        table_hop(0).start()
    else:
        sums_ref[...] = sums

    if reduce:
        x_copy.wait()
        d_rows = x_s.shape[-1] // blocks
        low = gq_src.shape[3]
        for b in range(blocks):
            cat[0 : 3 * width, b * rows : (b + 1) * rows] = stage[b].T
        for z in range(blocks):
            cols = slice(z * d_rows, (z + 1) * d_rows)
            total = None
            for b in range(blocks):
                x_block = x_s[b, :, :, cols].reshape(rows, d_rows)
                term = dot(cat[0 : 3 * width, b * rows : (b + 1) * rows], x_block, NN)
                total = term if total is None else total + term
            gq_src[z] = total.T.astype(BF16).reshape(2, n_f, low, 3 * width)
        attn.start()
        table_step(0)
        late.z_level(0)

    tokens, dim = out_ref.shape
    pieces = dim // 256

    def collect(j):
        part = slice(j * width, (j + 1) * width)
        if split:
            for m in range(blocks):
                at = pl.ds(pl.multiple_of(j * half + (zed ^ m) * width, 128), width)
                cat[0:rows, at] = gin[m, :, part]
        else:
            for m in range(0, blocks, 2):
                one, two = gin[m, :, part].astype(F32), gin[m + 1, :, part].astype(F32)
                odd = zed % 2 == 1
                block = jnp.concatenate([jnp.where(odd, two, one), jnp.where(odd, one, two)], axis=1)
                at = j * half + (zed // 2 ^ (m // 2)) * 2 * width
                cat[0:rows, pl.ds(pl.multiple_of(at, 128), 2 * width)] = block.astype(BF16)

    def swap_hop(i):
        cols = slice(i * 256, (i + 1) * 256)
        return remote(send_s.at[:, cols], recv_s.at[:, cols], t_send.at[i], t_recv.at[i], partner)

    for m in range(blocks - 1, 0, -1):
        if split:
            for piece in range(steps_per):
                kv_hop(m, piece).wait()
        else:
            q_hop(m).wait()
    wl_copy.wait()
    collect(1)
    collect(2)
    keys = slice(half, 3 * half)
    for i in range(pieces):
        cols = slice(i * 256, (i + 1) * 256)
        send_s[:, cols] = dot(cat[tokens:rows, keys], wl_s[cols, keys], NT)
        out_ref[:, cols] = dot(cat[0:tokens, keys], wl_s[cols, keys], NT) + grad_one_ref[:, cols]
    if reduce:
        hops = []

        def settle(which, offset, places):
            count = which.acc.shape[-1]
            give_s[:, offset : offset + count] = which.total(1 - core)
            kept = which.total(core)
            start = 0
            for target, at, size in places:
                cols = pl.ds(pl.multiple_of(at, 128), size)
                hop = remote(
                    give_s.at[:, pl.ds(offset + start, size)], target.at[:, cols], c_send.at[len(hops)],
                    c_recv.at[len(hops)], partner,
                )
                hop.start()
                hops.append(hop)
                target[:, cols] = kept[:, start : start + size]
                start += size

        def units(target):
            return [(target, (2 * f + core) * hidden_half, hidden_half) for f in range(n_f)]

        for level in range(len(bits)):
            attn.level(level)
            table_step(1 + level)
        for level in range(1, len(lone.z_bits)):
            lone.z_level(level)
        settle(lone, 0, units(back_ref))
    if split:
        for m in range(blocks - 1, 0, -1):
            q_hop(m).wait()
    collect(0)
    for i in range(pieces):
        cols = slice(i * 256, (i + 1) * 256)
        send_s[:, cols] += dot(cat[tokens:rows, 0:half], wl_s[cols, 0:half], NT)
        swap_hop(i).start()
    for i in range(pieces):
        cols = slice(i * 256, (i + 1) * 256)
        out_ref[:, cols] += dot(cat[0:tokens, 0:half], wl_s[cols, 0:half], NT)
    if reduce:
        for k in range(1 + len(bits), len(peers)):
            table_step(k)
    for i in range(pieces):
        cols = slice(i * 256, (i + 1) * 256)
        swap_hop(i).wait_recv()
        out_ref[:, cols] += recv_s[:, cols]
    for i in range(pieces):
        swap_hop(i).wait_send()

    if reduce:
        attn.arrived()

        def other_hop(m):
            src = attn.acc.at[1 - core, 0, zed] if m == 0 else attn.far.at[1 - core, m - 1]
            return remote(src, others.at[m], o_send.at[m], o_recv.at[m], partner)

        def put_heads(m, value, which):
            for j in range(3):
                at = pl.ds(pl.multiple_of(j * dim + which * half + (zed ^ m) * width, 128), width)
                qg_ref[:, at] = value[:, j * width : (j + 1) * width].astype(F32)

        for m in range(blocks):
            other_hop(m).start()
        for m in range(blocks):
            put_heads(m, attn.acc[core, 0, zed] if m == 0 else attn.far[core, m - 1], core)

        places = units(in_ref) + [(og_ref, core * half, half)]
        offset = lone.acc.shape[-1]
        for which, some in ((early, places[: n_f - 1]), (late, places[n_f - 1 :])):
            for level in range(1, len(which.z_bits)):
                which.z_level(level)
            settle(which, offset, some)
            offset += cut
        for m in range(blocks):
            other_hop(m).wait()
            put_heads(m, others[m], 1 - core)
        for which in (early, late, attn, lone):
            which.sent()
        for hop in hops:
            hop.wait()


def back(qkv, grads, full, lse, grad_one, w_local, x_all, mid_grads, heads, n_f, reduce, back_sums=None, sums_mid=None, bias_sum=None):
    blocks, rows, _ = qkv.shape
    width = heads * HEAD
    length = rows * blocks
    tokens, dim = grad_one.shape
    sds = jax.ShapeDtypeStruct
    vmem, dma = pltpu.VMEM, pltpu.SemaphoreType.DMA
    in_vmem, anywhere = pl.BlockSpec(memory_space=pltpu.VMEM), pl.BlockSpec(memory_space=pl.ANY)
    operands = [qkv, grads, full, lse, grad_one]
    if reduce:
        operands += [sums_mid, bias_sum]
    inner = len(operands)
    operands += [w_local]
    out_shape = [sds((tokens, dim), F32), sds((16, dim) if reduce else (1, 3 * width), F32)]
    staged = (blocks, rows, 3 * width)
    scratch = [
        vmem((8, length), F32),
        vmem((8, length), F32),
        vmem((width, length), F32),
        vmem((width, length), BF16),
        vmem(staged, BF16),
        vmem(w_local.shape, BF16),
        vmem((rows, max(length, w_local.shape[1])), BF16),
        vmem((tokens, dim), F32),
        vmem((tokens, dim), F32),
        dma((blocks, 2)),
        dma((blocks, 2)),
        dma((blocks,)),
        dma((blocks,)),
        dma((dim // 256,)),
        dma((dim // 256,)),
        dma((3,)),
    ]
    if reduce:
        _, _, _, low, columns = mid_grads.shape
        operands += [x_all, mid_grads, back_sums]
        hidden_half = back_sums.shape[-1]
        out_shape += [sds((low, 2 * hidden_half), F32)] * 2 + [sds((low, dim), F32), sds((low, 3 * dim), F32)]
        n_peers = n_f.bit_length() + blocks.bit_length() - 1
        scratch = [vmem(staged, BF16)] + scratch
        scratch += [
            vmem(x_all.shape, BF16),
            vmem((blocks, 2, n_f, low, 3 * width), BF16),
            vmem((low, columns + hidden_half), F32),
            vmem((blocks, low, 3 * width), BF16),
            vmem((n_peers, 16, dim), F32),
            dma((2 * n_f + 1,)),
            dma((2 * n_f + 1,)),
            dma((blocks,)),
            dma((blocks,)),
            dma((n_peers,)),
            dma((n_peers,)),
        ]
        cut = (n_f - 1) * (hidden_half // n_f)
        for cols in (cut, columns - cut, 3 * width, hidden_half):
            halved = cols == hidden_half
            scratch += [
                vmem((2, 1 if halved else n_f // 2, blocks, low, cols), BF16),
                vmem((2, 1, 1, 16, 128) if halved else (2, n_f - 1, blocks, low, cols), BF16),
                vmem((2, blocks - 1, low, cols), BF16),
                dma((2, n_f // 2)),
                dma((2, n_f - 1)),
                dma((2, n_f - 1)),
                dma((2, blocks - 1)),
                dma((2, blocks - 1)),
            ]
    else:
        out_shape += [sds(staged, BF16)]
    return pl.pallas_call(
        partial(
            back_kernel, blocks=blocks, heads=heads, n_f=n_f, reduce=reduce, q_rows=256, steps_per=2
        ),
        out_shape=out_shape,
        in_specs=[in_vmem] * inner + [anywhere] * (len(operands) - inner),
        out_specs=[in_vmem] * len(out_shape),
        scratch_shapes=scratch,
        compiler_params=pltpu.CompilerParams(
            vmem_limit_bytes=VMEM_MIDDLE, collective_id=2, has_side_effects=True
        ),
        cost_estimate=pl.CostEstimate(
            flops=40 * length * length * width, bytes_accessed=30 << 20,
            transcendentals=heads * length * length,
        ),
        name="back",
    )(*operands)


def on_device(x_in, w_qkv, w_out, w_in, w_back, vectors, bias_in, cot, *, n_ctx, n_f):
    ctx, fs = lax.axis_index("ctx"), lax.axis_index("fsdp")
    core, zed = ctx % 2, ctx // 2
    n_z = n_ctx // 2
    x_own = x_in[0]
    grad_out = cot[0]
    rows, width = x_own.shape
    hidden = w_back.shape[0]
    half_heads = HEADS // 2
    heads = half_heads // n_z
    wide = heads * HEAD

    def swap(v):
        return lax.ppermute(v, "ctx", [(i, i ^ 1) for i in range(n_ctx)])

    def over_z(v, m):
        return lax.ppermute(v, "ctx", [(i, i ^ (2 * m)) for i in range(n_ctx)])

    def over_f(v, m):
        return lax.ppermute(v, "fsdp", [(i, i ^ m) for i in range(n_f)])

    bits = [1 << b for b in range(n_f.bit_length() - 1)]

    def place(pieces, index, axis):
        count = len(pieces)
        for bit in range(count.bit_length() - 1):
            flag = (index >> bit) & 1
            pieces = [jnp.where(flag, pieces[m ^ (1 << bit)], pieces[m]) for m in range(count)]
        return jnp.concatenate(pieces, axis=axis)

    half_in = width // 2
    first = (core * half_heads + zed * heads) * HEAD
    span = 3 * wide
    bias_qkv = jnp.concatenate(
        [
            lax.dynamic_slice_in_dim(vectors[0], first, wide, 0),
            jnp.zeros((wide,), F32),
            lax.dynamic_slice_in_dim(vectors[1], first, wide, 0),
        ]
    )[None]
    ff_part = w_in.shape[1] // 2
    w_back4 = w_back.reshape(n_f, 2, ff_part, w_back.shape[1])
    qkv, x_all, w_local, wo_half, wi_got, wb_got = front(
        x_own, w_qkv, w_out, w_in, w_back4, bias_qkv, n_f, n_z, heads
    )

    att, att_full, lse, wi_half, wb_got2 = attend(qkv, w_in, wi_got, w_back4, heads, n_f)
    bias_half = lax.dynamic_index_in_dim(
        bias_in.reshape(n_f, 2, ff_part), core, 1, False
    ).reshape(-1)
    low = width // (n_ctx * n_f)
    in_kernel = low % 16 == 0 and wide % 128 == 0 and hidden == n_f * width and min(n_z, n_f) >= 4
    layer_out, grad_one, g_att, sums_mid, bias_sum, mid_grads, *back_sums = middle(
        att, x_own, grad_out, vectors, bias_half, wo_half, wi_half, w_back4, wb_got, wb_got2, n_f, n_z, in_kernel
    )
    layer_out = layer_out[None]


    def over_fsdp(partial_grad):
        cols = partial_grad.shape[1]
        view = partial_grad.reshape((n_z, 2) + (2,) * len(bits) + (low, cols))
        done = []
        for side in range(2):
            now = view[:, side]
            order = bits if side == 0 else bits[1:] + bits[:1]
            left = list(reversed(bits))
            for bit in order:
                axis = 1 + left.index(bit)
                left.remove(bit)
                flag = (fs // bit) % 2
                stay = lax.dynamic_index_in_dim(now, flag, axis, False)
                go = lax.dynamic_index_in_dim(now, 1 - flag, axis, False)
                now = (stay.astype(F32) + over_f(go, bit).astype(F32)).astype(BF16)
            done.append(now)
        return jnp.stack(done, axis=1)

    def over_ctx(both):
        total = lax.dynamic_index_in_dim(both, zed, 0, False).astype(F32)
        for m in range(1, n_z):
            part = lax.dynamic_index_in_dim(both, zed ^ m, 0, False)
            total = total + over_z(part, m).astype(F32)
        stay = lax.dynamic_index_in_dim(total, core, 0, False)
        go = lax.dynamic_index_in_dim(total, 1 - core, 0, False)
        return stay, swap(go.astype(BF16)).astype(F32)

    def halves(stay, came, parts):
        low = stay.shape[0]
        first = jnp.where(core == 0, stay, came).reshape(low, parts, 1, -1)
        second = jnp.where(core == 0, came, stay).reshape(low, parts, 1, -1)
        return jnp.concatenate([first, second], axis=2).reshape(low, -1)

    def reduced(partial_grad):
        return over_ctx(over_fsdp(partial_grad))

    if in_kernel:
        grad_in, table, in_weight_grad, back_turned, out_weight_grad, qkv_weight_grad = back(
            qkv, g_att, att_full, lse, grad_one, w_local, x_all,
            mid_grads.reshape(n_z, 2, n_f, low, -1), heads, n_f, True, back_sums[0], sums_mid, bias_sum,
        )
        mine_at = (ctx * n_f + fs) * low
        vector_grad = lax.dynamic_slice_in_dim(table[:8], mine_at, low, 1)
        share = hidden // (n_ctx * n_f)
        in_bias_grad = lax.dynamic_slice_in_dim(table[8 : 8 + n_f].reshape(-1), mine_at // low * share, share, 0)
        return (
            layer_out,
            grad_in[None],
            qkv_weight_grad,
            out_weight_grad,
            in_weight_grad,
            back_turned.T,
            vector_grad,
            in_bias_grad,
        )
    stay, came = reduced(mid_grads)
    grad_in, sums, g_local = back(
        qkv, g_att, att_full, lse, grad_one, w_local, None, None, heads, n_f, False
    )
    attn_grad = dot(x_all.reshape(-1, width), g_local.reshape(-1, span), TN).astype(BF16)
    both = over_fsdp(attn_grad)
    mine, others = [], []
    for m in range(n_z):
        part = lax.dynamic_index_in_dim(both, zed ^ m, 0, False)
        part = part if m == 0 else over_z(part, m)
        mine.append(lax.dynamic_index_in_dim(part, core, 0, False))
        others.append(lax.dynamic_index_in_dim(part, 1 - core, 0, False))
    others = swap(jnp.stack(others))
    others = [others[m] for m in range(n_z)]
    n_half = hidden // 2
    in_weight_grad = halves(stay[:, :n_half], came[:, :n_half], n_f)
    back_weight_grad = halves(stay[:, n_half : 2 * n_half], came[:, n_half : 2 * n_half], n_f).T
    out_weight_grad = halves(stay[:, 2 * n_half :], came[:, 2 * n_half :], 1)

    def heads_order(parts):
        parts = [p.reshape(low, 3, wide) for p in parts]
        return place(parts, zed, 2).astype(F32).reshape(low, -1)

    qkv_weight_grad = halves(heads_order(mine), heads_order(others), 3)

    def spread(half_row, parts):
        piece = half_row.reshape(parts, 1, -1)
        empty = jnp.zeros_like(piece)
        both = jnp.where(core == 0, jnp.concatenate([piece, empty], 1), jnp.concatenate([empty, piece], 1))
        return both.reshape(-1)

    def halve(now):
        left = list(reversed(bits))
        for bit in bits:
            axis = left.index(bit)
            left.remove(bit)
            flag = (fs // bit) % 2
            stay = lax.dynamic_index_in_dim(now, flag, axis, False)
            now = stay + over_f(lax.dynamic_index_in_dim(now, 1 - flag, axis, False), bit)
        return now

    sums = sums[0]
    sums = jnp.stack([sums[:wide].reshape(n_f, -1), sums[2 * wide :].reshape(n_f, -1)], axis=1)
    late = halve(sums.reshape((2,) * len(bits) + (-1,)))
    turn = [(2 * z + c, n_z * c + z) for z in range(n_z) for c in range(2)]
    late = lax.ppermute(late, "ctx", turn).reshape(2, -1)
    ratio = hidden // width
    early = sums_mid[:6].T
    bias_terms = spread(bias_sum[0], n_f).reshape(width, ratio)
    table = jnp.concatenate([early, bias_terms], axis=1)
    kinds = table.shape[1]
    now = jnp.swapaxes(table.reshape(n_z * 2, n_f, low, kinds), -1, -2)
    now = jnp.swapaxes(now, 0, 1).reshape((2,) * len(bits) + (n_z, 2, kinds * low))
    now = halve(now)
    total = lax.dynamic_index_in_dim(now, zed, 0, False)
    for m in range(1, n_z):
        total = total + over_z(lax.dynamic_index_in_dim(now, zed ^ m, 0, False), m)
    stay = lax.dynamic_index_in_dim(total, core, 0, False)
    table = stay + swap(lax.dynamic_index_in_dim(total, 1 - core, 0, False))
    table = table.reshape(kinds, low)
    vector_grad = jnp.concatenate([late, table[:6]], axis=0)
    in_bias_grad = table[6:].T.reshape(-1)
    return (
        layer_out,
        grad_in[None],
        qkv_weight_grad,
        out_weight_grad,
        in_weight_grad,
        back_weight_grad,
        vector_grad,
        in_bias_grad,
    )


def solution(mesh):
    tokens = P("fsdp", "ctx", None)
    cols = P(None, "fsdp")
    shared = P(("ctx", "fsdp"), None)
    return jax.shard_map(
        partial(on_device, n_ctx=mesh.shape["ctx"], n_f=mesh.shape["fsdp"]),
        mesh=mesh,
        in_specs=(tokens, cols, cols, cols, cols, P(), P(), tokens),
        out_specs=(
            tokens,
            tokens,
            shared,
            shared,
            shared,
            P(None, ("ctx", "fsdp")),
            P(None, ("ctx", "fsdp")),
            P(("ctx", "fsdp")),
        ),
        check_vma=False,
    )
```

```python
from functools import partial
import math

import jax
import jax.numpy as jnp
from jax import lax
from jax.experimental import pallas as pl
from jax.experimental.pallas import tpu as pltpu
from jax.sharding import PartitionSpec as P

HEADS = 16
HEAD = 64
EPS = 1e-12
F32 = jnp.float32
BF16 = jnp.bfloat16
NN = (((1,), (0,)), ((), ()))
NT = (((1,), (1,)), ((), ()))
TN = (((0,), (0,)), ((), ()))
VMEM_LIMIT = 50 * 1024 * 1024
VMEM_MIDDLE = 56 * 1024 * 1024
MESH = pl.DeviceIdType.MESH


def dot(left, right, dims):
    return lax.dot_general(left, right, dims, preferred_element_type=F32)


def front_kernel(
    x_ref, wq_ref, wo_ref, wi_ref, wb_ref, bias_ref, qkv_ref, xf_out, wl_out, wo_out, wi_out, wb_out, *scratch, n_z, n_f, heads
):
    xf, wfull, wloc = scratch[:3]
    own_sem, x_send, x_recv, xs_send, xs_recv, w_send, w_recv, ws_send, ws_recv, o_send, o_recv, i_send, i_recv, b_send, b_recv, out_sem = scratch[3:]
    ctx, fs = lax.axis_index("ctx"), lax.axis_index("fsdp")
    core, zed = ctx % 2, ctx // 2
    bits = [1 << b for b in range(n_f.bit_length() - 1)]
    orders = (bits, bits[1:] + bits[:1])
    rows, width = x_ref.shape
    half = width // 2
    quarter = half // 2
    wide = heads * HEAD
    partner = {"ctx": zed * 2 + (1 - core)}

    barrier = pltpu.get_barrier_semaphore()

    def greet(device):
        pl.semaphore_signal(barrier, inc=1, device_id=device, device_id_type=MESH)

    greet(partner)
    for bit in bits:
        greet({"fsdp": fs ^ bit})

    @pl.when(zed > 0)
    def _():
        greet({"ctx": ctx - 2})

    @pl.when(zed < n_z - 1)
    def _():
        greet({"ctx": ctx + 2})

    edges = (zed == 0).astype(jnp.int32) + (zed == n_z - 1).astype(jnp.int32)
    pl.semaphore_wait(barrier, 3 + len(bits) - edges)

    def remote(src, dst, send, recv, device):
        return pltpu.make_async_remote_copy(
            src_ref=src, dst_ref=dst, send_sem=send, recv_sem=recv, device_id=device, device_id_type=MESH
        )

    def x_move(away, step, first):
        block = zed - step * away
        src = x_ref if first else xf.at[block ^ zed, 0]
        index = (step + 1) // 2
        return remote(
            src, xf.at[block ^ (zed + step), 0], x_send.at[index, away], x_recv.at[block ^ (zed + step)],
            {"ctx": ctx + 2 * step},
        )

    def x_swap(m, first=False):
        src = x_ref if first else xf.at[m, 0]
        return remote(src, xf.at[m, 1], xs_send.at[m], xs_recv.at[m], partner)

    def has(step):
        return zed < n_z - 1 if step == 1 else zed > 0

    def came(away, step):
        return zed - away >= 0 if step == 1 else zed + away <= n_z - 1

    for step in (1, -1):

        @pl.when(has(step))
        def _(step=step):
            x_move(0, step, True).start()

    x_swap(0, True).start()
    own_x = pltpu.make_async_copy(x_ref, xf.at[0, 0], own_sem.at[0])
    own_x.start()

    def x_step(away):
        for step in (1, -1):

            @pl.when(came(away, step))
            def _(step=step):
                block = zed - step * away
                remote(
                    xf.at[block ^ zed, 0], xf.at[block ^ zed, 0], x_send.at[0, 0], x_recv.at[block ^ zed], partner
                ).wait_recv()

                @pl.when(has(step))
                def _():
                    x_move(away, step, False).start()

                x_swap(block ^ zed).start()

    def wq_place(side, origin, which):
        cols = wq_ref.shape[1]
        return wfull.at[
            pl.ds(pl.multiple_of(which * half + side * quarter, quarter), quarter),
            pl.ds(pl.multiple_of(origin * cols, 128), cols),
        ]

    def wq_own(side):
        return wq_ref.at[pl.ds(pl.multiple_of(core * half + side * quarter, quarter), quarter), :]

    def wo_place(side, origin):
        cols = wo_ref.shape[1]
        return wo_out.at[pl.ds(side * quarter, quarter), pl.ds(pl.multiple_of(origin * cols, 128), cols)]

    def wo_own(side):
        return wo_ref.at[pl.ds(pl.multiple_of(core * half + side * quarter, quarter), quarter), :]

    def wq_hop(side, m, bit):
        src = wq_own(side) if m == 0 else wq_place(side, fs ^ m, core)
        return remote(src, wq_place(side, fs ^ m, core), w_send.at[side, m ^ bit], w_recv.at[side, m ^ bit], {"fsdp": fs ^ bit})

    def wo_hop(side, m, bit):
        src = wo_own(side) if m == 0 else wo_place(side, fs ^ m)
        return remote(src, wo_place(side, fs ^ m), o_send.at[side, m ^ bit], o_recv.at[side, m ^ bit], {"fsdp": fs ^ bit})

    def wq_swap(side, m):
        src = wq_own(side) if m == 0 else wq_place(side, fs ^ m, core)
        return remote(src, wq_place(side, fs ^ m, core), ws_send.at[side, m], ws_recv.at[side, m], partner)

    own_w = []
    for side in range(2):
        wq_hop(side, 0, orders[side][0]).start()
        wq_swap(side, 0).start()
        own_w.append(pltpu.make_async_copy(wq_own(side), wq_place(side, fs, core), own_sem.at[1 + side]))
        own_w.append(pltpu.make_async_copy(wo_own(side), wo_place(side, fs), own_sem.at[3 + side]))
    for copy in own_w:
        copy.start()

    part = wi_ref.shape[1] // 2

    def wi_hop(side):
        src = wi_ref.at[pl.ds(side * half, half), pl.ds(pl.multiple_of(core * part, 128), part)]
        return remote(src, wi_out.at[side], i_send.at[side], i_recv.at[side], {"fsdp": fs ^ orders[side][0]})

    def wb_hop(seg):
        return remote(
            wb_ref.at[seg, core], wb_out.at[seg], b_send.at[seg], b_recv.at[seg],
            {"fsdp": fs ^ orders[seg * 2 // n_f][0]},
        )

    def doubling(hop, level, after=None):
        for side in range(2):
            known = [0]
            for bit in orders[side][:level]:
                known = known + [m ^ bit for m in known]
            bit = orders[side][level]
            for m in known:
                hop(side, m, bit).wait_recv()
                if after is not None:
                    after(side, m ^ bit).start()
            if level + 1 < len(bits):
                for m in known + [m ^ bit for m in known]:
                    hop(side, m, orders[side][level + 1]).start()

    doubling(wq_hop, 0, wq_swap)
    for side in range(2):
        wo_hop(side, 0, orders[side][0]).start()
    x_step(1)
    for level in range(1, len(bits)):
        doubling(wq_hop, level, wq_swap)
    for side in range(2):
        wi_hop(side).start()
    doubling(wo_hop, 0)
    for seg in range(n_f):
        wb_hop(seg).start()
    for away in range(2, n_z - 1):
        x_step(away)
    for copy in own_w:
        copy.wait()
    for side in range(2):
        for m in range(n_f):
            wq_swap_in = remote(
                wq_place(side, fs ^ m, 1 - core), wq_place(side, fs ^ m, 1 - core),
                ws_send.at[side, m], ws_recv.at[side, m], partner,
            )
            wq_swap_in.wait_recv()
    outs = []
    for j in range(3):
        cols = pl.ds(pl.multiple_of(j * width + core * half, 128), half)
        outs.append(pltpu.make_async_copy(wfull.at[:, cols], wl_out.at[:, pl.ds(j * half, half)], out_sem.at[j]))
    for copy in outs:
        copy.start()
    for j in range(3):
        base = j * width + core * half + zed * wide
        if wide % 128 == 0:
            piece = wfull[:, pl.ds(pl.multiple_of(base, 128), wide)]
        else:
            block = wfull[:, pl.ds(pl.multiple_of(base // 128 * 128, 128), 128)].astype(F32)
            piece = jnp.where(zed % 2 == 1, block[:, wide:], block[:, :wide]).astype(BF16)
        wloc[:, j * wide : (j + 1) * wide] = piece

    def x_ready(m, side):
        remote(xf.at[m, side], xf.at[m, side], xs_send.at[m], xs_recv.at[m], partner).wait_recv()

    def project(m):
        def run(side, carry):
            result = dot(xf[m, side], wloc[...], NN) + bias_ref[...]
            where = pl.ds(pl.multiple_of(side * rows, rows), rows)
            qkv_ref[m, where, :] = result.astype(BF16)
            return carry

        lax.fori_loop(0, 2, run, 0)

    own_x.wait()
    x_ready(0, 1)
    project(0)

    def finish(away):
        def run(i, carry):
            block = zed - (1 - 2 * i) * away

            @pl.when((block >= 0) & (block <= n_z - 1))
            def _():
                x_ready(block ^ zed, 1)
                project(block ^ zed)

            return carry

        lax.fori_loop(0, 2, run, 0)

    for away in range(1, n_z - 1):
        finish(away)
    for level in range(1, len(bits)):
        doubling(wo_hop, level)
    if n_z > 2:
        x_step(n_z - 1)
    finish(n_z - 1)
    x_out = pltpu.make_async_copy(xf, xf_out, own_sem.at[5])
    x_out.start()

    for step in (1, -1):

        @pl.when(has(step))
        def _(step=step):
            x_move(0, step, True).wait_send()
            for away in range(1, n_z):

                @pl.when(came(away, step))
                def _(away=away):
                    x_move(away, step, False).wait_send()

    x_swap(0, True).wait_send()
    for m in range(1, n_z):
        x_swap(m).wait_send()
    for side in range(2):
        known = [0]
        for bit in orders[side]:
            for m in known:
                wq_hop(side, m, bit).wait_send()
                wo_hop(side, m, bit).wait_send()
            known = known + [m ^ bit for m in known]
        for m in range(n_f):
            wq_swap(side, m).wait_send()
        wi_hop(side).wait()
    for seg in range(n_f):
        wb_hop(seg).wait()
    for copy in outs:
        copy.wait()
    x_out.wait()


def front(x_own, w_qkv, w_out, w_in, w_back4, bias, n_f, n_z, heads):
    rows, width = x_own.shape
    wide = heads * HEAD
    sds = jax.ShapeDtypeStruct
    in_vmem, anywhere = pl.BlockSpec(memory_space=pltpu.VMEM), pl.BlockSpec(memory_space=pl.ANY)
    part = w_in.shape[1] // 2
    dma = pltpu.SemaphoreType.DMA
    return pl.pallas_call(
        partial(front_kernel, n_z=n_z, n_f=n_f, heads=heads),
        out_shape=[
            sds((n_z, 2 * rows, 3 * wide), BF16),
            sds((n_z, 2, rows, width), BF16),
            sds((width, 3 * width // 2), BF16),
            sds((width // 2, width), BF16),
            sds((2, width // 2, part), BF16),
            sds((n_f,) + w_back4.shape[2:], BF16),
        ],
        in_specs=[anywhere] * 5 + [in_vmem],
        out_specs=[in_vmem] + [anywhere] * 5,
        scratch_shapes=[
            pltpu.VMEM((n_z, 2, rows, width), BF16),
            pltpu.VMEM((width, 3 * width), BF16),
            pltpu.VMEM((width, 3 * wide), BF16),
            dma((6,)),
            dma((2, n_z)),
            dma((n_z,)),
            dma((n_z,)),
            dma((n_z,)),
            dma((2, n_f)),
            dma((2, n_f)),
            dma((2, n_f)),
            dma((2, n_f)),
            dma((2, n_f)),
            dma((2, n_f)),
            dma((2,)),
            dma((2,)),
            dma((n_f,)),
            dma((n_f,)),
            dma((3,)),
        ],
        compiler_params=pltpu.CompilerParams(
            vmem_limit_bytes=VMEM_LIMIT, collective_id=1, has_side_effects=True
        ),
        cost_estimate=pl.CostEstimate(
            flops=4 * n_z * rows * width * 3 * wide, bytes_accessed=30 << 20, transcendentals=0
        ),
        name="front",
    )(x_own, w_qkv, w_out, w_in, w_back4, bias)


def one_head(block, head, heads):
    if heads == 1:
        return block
    lane = lax.broadcasted_iota(jnp.int32, block.shape, 1)
    return jnp.where(lane // HEAD == head, block, jnp.zeros_like(block))


def merge_heads(parts):
    if len(parts) == 1:
        return parts[0]
    lane = lax.broadcasted_iota(jnp.int32, parts[0].shape, 1)
    result = parts[0]
    for head in range(1, len(parts)):
        result = jnp.where(lane // HEAD == head, parts[head], result)
    return result


def remote(src, dst, send, recv, device):
    return pltpu.make_async_remote_copy(
        src_ref=src, dst_ref=dst, send_sem=send, recv_sem=recv, device_id=device, device_id_type=MESH
    )


def greet(barrier, devices):
    for device in devices:
        pl.semaphore_signal(barrier, inc=1, device_id=device, device_id_type=MESH)
    pl.semaphore_wait(barrier, len(devices))


def fsdp_orders(n_f):
    bits = [1 << b for b in range(n_f.bit_length() - 1)]
    return bits, (bits, bits[1:] + bits[:1])


def known_at(order, level):
    known = [0]
    for bit in order[:level]:
        known = known + [m ^ bit for m in known]
    return known


def attend_kernel(*refs, blocks, heads, n_f, q_rows, k_rows):
    qkv_ref, wi_ref, got_ref, wb_ref = refs[:4]
    att_ref, full_ref, lse_ref, wi_out, wb_out = refs[4:9]
    key_s, value_s, send_s, a_send, a_recv, i_send, i_recv, b_send, b_recv, own_sem = refs[9:]
    ins = [qkv_ref.at[b] for b in range(blocks)]
    rows = ins[0].shape[0]
    width = heads * HEAD
    length = rows * blocks
    ctx, fs = lax.axis_index("ctx"), lax.axis_index("fsdp")
    core, zed = ctx % 2, ctx // 2
    bits, orders = fsdp_orders(n_f)
    greet(
        pltpu.get_barrier_semaphore(),
        [{"fsdp": fs ^ bit} for bit in bits] + [{"ctx": (zed ^ m) * 2 + core} for m in range(1, blocks)],
    )

    half, part = got_ref.shape[1:]

    def wi_place(side, m):
        return wi_out.at[pl.ds(side * half, half), pl.ds(pl.multiple_of((fs ^ m) * part, 128), part)]

    def wi_source(side, m):
        if m == 0:
            return wi_ref.at[pl.ds(side * half, half), pl.ds(pl.multiple_of(core * part, 128), part)]
        return got_ref.at[side] if m == orders[side][0] else wi_place(side, m)

    def wi_hop(side, m, bit):
        return remote(
            wi_source(side, m), wi_place(side, m), i_send.at[side, m ^ bit], i_recv.at[side, m ^ bit], {"fsdp": fs ^ bit}
        )

    def wb_hop(seg):
        return remote(
            wb_ref.at[seg, core], wb_out.at[seg], b_send.at[seg], b_recv.at[seg],
            {"fsdp": fs ^ orders[seg * 2 // n_f][1]},
        )

    def level(number, act):
        for side in range(2):
            for m in known_at(orders[side], number):
                act(wi_hop(side, m, orders[side][number]))

    locals_ = []
    for side in range(2):
        for i, m in enumerate((0, orders[side][0])):
            locals_.append(pltpu.make_async_copy(wi_source(side, m), wi_place(side, m), own_sem.at[2 * side + i]))
    for copy in locals_:
        copy.start()
    level(1, lambda hop: hop.start())
    for seg in range(n_f):
        wb_hop(seg).start()

    def att_hop(b):
        return remote(send_s.at[b - 1], att_ref.at[b], a_send.at[b], a_recv.at[b], {"ctx": (zed ^ b) * 2 + core})

    for b in range(blocks):
        here = slice(b * rows, (b + 1) * rows)
        key_s[here, :] = ins[b][:, width : 2 * width]
        value_s[here, :] = ins[b][:, 2 * width : 3 * width]
    for turn, b in enumerate(list(range(blocks - 1, 0, -1)) + [0]):

        def step(i, carry, b=b):
            local = pl.ds(pl.multiple_of(i * q_rows, q_rows), q_rows)
            where = pl.ds(pl.multiple_of(b * rows + i * q_rows, q_rows), q_rows)
            query = ins[b][local, 0:width] * BF16(HEAD**-0.5)
            outputs, sums = [], []
            for head in range(heads):
                masked = one_head(query, head, heads)
                scores = [
                    dot(masked, key_s[j : j + k_rows, :], NT) for j in range(0, length, k_rows)
                ]
                top = None
                for part in scores:
                    part_top = jnp.max(part, axis=1, keepdims=True)
                    top = part_top if top is None else jnp.maximum(top, part_top)
                total = acc = None
                for j, part in enumerate(scores):
                    probs = jnp.exp(part - top)
                    part_total = jnp.sum(probs, axis=1, keepdims=True)
                    value = value_s[j * k_rows : (j + 1) * k_rows, :]
                    part_acc = dot(probs.astype(BF16), value, NN)
                    total = part_total if total is None else total + part_total
                    acc = part_acc if acc is None else acc + part_acc
                outputs.append(acc / total)
                sums.append(jnp.broadcast_to(top + jnp.log(total), (q_rows, width)))
            result = merge_heads(outputs)
            full_ref[where, :] = result
            if b == 0:
                att_ref[0, local, :] = result.astype(BF16)
            else:
                send_s[b - 1, local, :] = result.astype(BF16)
            lse_ref[where, :] = merge_heads(sums)
            return carry

        lax.fori_loop(0, rows // q_rows, step, 0)
        if b > 0:
            att_hop(b).start()
        if 0 < turn < len(bits) - 1:
            level(turn, lambda hop: hop.wait_recv())
            level(turn + 1, lambda hop: hop.start())
    level(len(bits) - 1, lambda hop: hop.wait_recv())
    for number in range(1, len(bits)):
        level(number, lambda hop: hop.wait_send())
    for seg in range(n_f):
        wb_hop(seg).wait()
    for b in range(1, blocks):
        att_hop(b).wait()
    for copy in locals_:
        copy.wait()


def attend(qkv, w_in, wi_got, w_back4, heads, n_f):
    blocks, rows, _ = qkv.shape
    width = heads * HEAD
    length = rows * blocks
    _, half, part = wi_got.shape
    _, _, seg_rows, seg_cols = w_back4.shape
    sds = jax.ShapeDtypeStruct
    in_vmem, anywhere = pl.BlockSpec(memory_space=pltpu.VMEM), pl.BlockSpec(memory_space=pl.ANY)
    dma = pltpu.SemaphoreType.DMA
    return pl.pallas_call(
        partial(attend_kernel, blocks=blocks, heads=heads, n_f=n_f, q_rows=256, k_rows=512),
        out_shape=[
            sds((blocks, rows, width), BF16),
            sds((length, width), F32),
            sds((length, width), F32),
            sds((2 * half, n_f * part), BF16),
            sds((n_f, seg_rows, seg_cols), BF16),
        ],
        in_specs=[in_vmem] + [anywhere] * 3,
        out_specs=[in_vmem] * 3 + [anywhere] * 2,
        scratch_shapes=[pltpu.VMEM((length, width), BF16)] * 2
        + [
            pltpu.VMEM((blocks - 1, rows, width), BF16),
            dma((blocks,)),
            dma((blocks,)),
            dma((2, n_f)),
            dma((2, n_f)),
            dma((n_f,)),
            dma((n_f,)),
            dma((4,)),
        ],
        compiler_params=pltpu.CompilerParams(
            vmem_limit_bytes=VMEM_LIMIT, collective_id=3, has_side_effects=True
        ),
        cost_estimate=pl.CostEstimate(
            flops=16 * length * length * width, bytes_accessed=10 * length * width,
            transcendentals=heads * length * length,
        ),
        name="attend",
    )(qkv, w_in, wi_got, w_back4)


def gelu_both(pre):
    slope = math.sqrt(2.0 / math.pi)
    square = pre * pre
    th = jnp.tanh(slope * (pre + 0.044715 * pre * square))
    half = 0.5 * (1.0 + th)
    grad = half + 0.5 * pre * (1.0 - th * th) * (slope * (1.0 + 3 * 0.044715 * square))
    return pre * half, grad


class Reduction:
    def __init__(self, src, cols, acc, got, far, sems, n_f, n_z, begin=0, summed=True):
        self.begin, self.summed = begin, summed
        self.z_bits = [1 << i for i in range(n_z.bit_length() - 1)]
        self.src, self.cols, self.acc, self.got, self.far = src, cols, acc, got, far
        self.load_sem, self.f_send, self.f_recv, self.z_send, self.z_recv = sems
        self.n_z = n_z
        ctx, self.fs = lax.axis_index("ctx"), lax.axis_index("fsdp")
        self.core, self.zed = ctx % 2, ctx // 2
        self.bits, self.orders = fsdp_orders(n_f)
        self.last = len(self.bits) - 1

    def targets(self, side, level):
        found = [0]
        for bit in reversed(self.orders[side][level + 1 :]):
            found = found + [d ^ bit for d in found]
        return found

    def part(self, side, target):
        return self.src.at[:, side, target, :, self.cols]

    def load(self, side, i):
        d = self.targets(side, 0)[i]
        return pltpu.make_async_copy(self.part(side, self.fs ^ d), self.acc.at[side, i], self.load_sem.at[side, i])

    def hop(self, side, level, i):
        bit = self.orders[side][level]
        first = sum(len(self.targets(side, l)) for l in range(level))
        if level == 0:
            src = self.part(side, self.fs ^ bit ^ self.targets(side, 0)[i])
        else:
            src = self.acc.at[side, len(self.targets(side, level)) + i]
        return remote(
            src, self.got.at[side, first + i], self.f_send.at[side, first + i], self.f_recv.at[side, first + i],
            {"fsdp": self.fs ^ bit},
        )

    def every(self, level, act):
        for side in range(2):
            for i in range(len(self.targets(side, level))):
                act(self.hop(side, level, i))

    def loads(self, act):
        for side in range(2):
            for i in range(len(self.targets(side, 0))):
                act(self.load(side, i))

    def start(self):
        self.every(0, lambda hop: hop.start())
        self.loads(lambda copy: copy.start())

    def level(self, level):
        if level == 0:
            self.loads(lambda copy: copy.wait())
        self.every(level, lambda hop: hop.wait_recv())
        first = sum(len(self.targets(0, l)) for l in range(level))
        count = len(self.targets(0, level))

        def add(n, carry):
            side, rest = n // (count * self.n_z), n % (count * self.n_z)
            i, z = rest // self.n_z, rest % self.n_z
            total = self.acc[side, i, z].astype(F32) + self.got[side, first + i, z].astype(F32)
            self.acc[side, i, z] = total.astype(BF16)
            return carry

        lax.fori_loop(0, 2 * count * self.n_z, add, 0)
        if level < self.last:
            self.every(level + 1, lambda hop: hop.start())
        elif self.far is not None:
            self.z_start()

    def z_targets(self, level):
        found = [0]
        for bit in reversed(self.z_bits[level + 1 :]):
            found = found + [d ^ bit for d in found]
        return found

    def z_hops(self, level):
        hops = []
        if self.summed:
            bit = self.z_bits[level]
            first = sum(len(self.z_targets(l)) for l in range(level))
            moves = [(bit ^ d, bit, first + i) for i, d in enumerate(self.z_targets(level))]
        else:
            moves = [(m, m, m - 1) for m in range(self.n_z - 1, 0, -1)]
        for block, away, slot in moves:
            for side in range(2):
                hops.append(
                    remote(
                        self.acc.at[side, 0, self.zed ^ block], self.far.at[side, slot], self.z_send.at[side, slot],
                        self.z_recv.at[side, slot], {"ctx": (self.zed ^ away) * 2 + self.core},
                    )
                )
        return hops

    def z_start(self, level=0):
        for hop in self.z_hops(level):
            hop.start()

    def z_level(self, level):
        for hop in self.z_hops(level):
            hop.wait_recv()
        if level == len(self.z_bits) - 1:
            return
        first = sum(len(self.z_targets(l)) for l in range(level))
        for i, d in enumerate(self.z_targets(level)):
            for side in range(2):
                total = self.acc[side, 0, self.zed ^ d].astype(F32) + self.far[side, first + i].astype(F32)
                self.acc[side, 0, self.zed ^ d] = total.astype(BF16)
        self.z_start(level + 1)

    def arrived(self):
        for hop in self.z_hops(0):
            hop.wait_recv()

    def total(self, side):
        return self.acc[side, 0, self.zed].astype(F32) + self.far[side, self.n_z - 2].astype(F32)

    def sent(self):
        for level in range(self.begin, self.last + 1):
            self.every(level, lambda hop: hop.wait_send())
        if self.far is not None:
            for level in range(len(self.z_bits) if self.summed else 1):
                for hop in self.z_hops(level):
                    hop.wait_send()


def row_stats(value):
    return jnp.mean(value, axis=1, keepdims=True)


def mid_kernel(*refs, n_f, n_z, reduce, cfg):
    refs = list(refs)
    red_refs = [refs.pop() for _ in range(6)][::-1] if reduce else None
    sum_out = refs.pop(16) if reduce else None
    att_in, x_ref, cot_ref, vec_ref, bias_ref, wo_ref, wi_ref, wb_ref, got_ref, got2_ref = refs[:10]
    layer_ref, grad_one_ref, ga_ref, sums_ref, bias_sum_ref, grads_out = refs[10:16]
    att_ref, att2_s, h_ref, act_ref, g2_ref, gp_ref, g1_ref, ga_s, turned_s, og_s = refs[16:26]
    wo_s, wi_s, wb_s, slope_s, normed_s, unit_s, acc_s, send_s, recv_s, rstd_s = refs[26:36]
    w_sem, send_sem, recv_sem, b_send, b_recv, a_send, a_recv, g_sem = refs[36:]
    ctx, fs = lax.axis_index("ctx"), lax.axis_index("fsdp")
    core, zed = ctx % 2, ctx // 2
    partner = {"ctx": zed * 2 + (1 - core)}
    rows, width = x_ref.shape
    own, other = slice(0, rows), slice(rows, 2 * rows)
    wide = att_in.shape[2]
    half_in = n_z * wide
    ff_half = wi_s.shape[1]
    step = cfg["step"]
    chunk = cfg["rows"]
    bits, orders = fsdp_orders(n_f)
    _, _, seg_rows, seg_cols = wb_ref.shape

    def wb_place(seg, m):
        return wb_s.at[
            pl.ds(seg * seg_rows, seg_rows), pl.ds(pl.multiple_of((fs ^ m) * seg_cols, 128), seg_cols)
        ]

    def wb_order(seg):
        return orders[seg * 2 // n_f]

    def wb_source(seg, m):
        if m == 0:
            return wb_ref.at[seg, core]
        if m == wb_order(seg)[1]:
            return got2_ref.at[seg]
        return got_ref.at[seg] if m == wb_order(seg)[0] else wb_place(seg, m)

    def wb_hop(seg, m, bit):
        return remote(
            wb_source(seg, m), wb_place(seg, m), b_send.at[seg, m ^ bit], b_recv.at[seg, m ^ bit], {"fsdp": fs ^ bit}
        )

    def wb_level(number, act):
        for seg in range(n_f):
            for m in known_at(wb_order(seg), number)[1 if number == 1 else 0 :]:
                act(wb_hop(seg, m, wb_order(seg)[number]))

    copies = [
        [pltpu.make_async_copy(wo_ref, wo_s, w_sem.at[0])],
        [pltpu.make_async_copy(wi_ref, wi_s, w_sem.at[1])],
        [],
    ]
    for seg in range(n_f):
        for i, m in enumerate((0, wb_order(seg)[0], wb_order(seg)[1])):
            copies[2].append(pltpu.make_async_copy(wb_source(seg, m), wb_place(seg, m), w_sem.at[2 + 3 * seg + i]))
    for copy in copies[0] + copies[1]:
        copy.start()
    greet(
        pltpu.get_barrier_semaphore(),
        [partner] + [{"fsdp": fs ^ bit} for bit in bits] + [{"ctx": (zed ^ m) * 2 + core} for m in range(1, n_z)],
    )
    wb_level(1, lambda hop: hop.start())
    for copy in copies[2]:
        copy.start()

    def exchange(n, src, dst):
        return remote(src, dst, send_sem.at[n], recv_sem.at[n], partner)

    def over_cols(total, body):
        def run(i, carry):
            body(pl.ds(pl.multiple_of(i * step, step), step))
            return carry

        lax.fori_loop(0, total // step, run, 0)

    def over_rows(body):
        def run(i, carry):
            return body(pl.ds(pl.multiple_of(i * chunk, chunk), chunk), carry)

        zero = jnp.zeros((1, width), F32)
        return lax.fori_loop(0, rows // chunk, run, (zero, zero, zero))

    if wide % 128 == 0:
        for m in range(n_z):
            att_ref[:, pl.ds(pl.multiple_of((zed ^ m) * wide, wide), wide)] = att_in[m]
    else:
        for m in range(0, n_z, 2):
            one, two = att_in[m].astype(F32), att_in[m + 1].astype(F32)
            odd = zed % 2 == 1
            block = jnp.concatenate([jnp.where(odd, two, one), jnp.where(odd, one, two)], axis=1)
            at = pl.ds(pl.multiple_of((zed // 2 ^ (m // 2)) * 2 * wide, 2 * wide), 2 * wide)
            att_ref[:, at] = block.astype(BF16)

    def wait_all(group):
        for copy in group:
            copy.wait()

    att_move = exchange(6, att_ref, att2_s)
    att_move.start()

    wait_all(copies[0])

    def out_other(cols):
        send_s[:, cols] = dot(att_ref[other, :], wo_s[:, cols], NN)

    over_cols(width, out_other)
    move = exchange(0, send_s, recv_s)
    move.start()

    def out_own(cols):
        part = dot(att_ref[own, :], wo_s[:, cols], NN)
        acc_s[:, cols] = part + x_ref[:, cols].astype(F32) + vec_ref[2:3, cols]

    over_cols(width, out_own)
    move.wait()

    def norm_one(r, carry):
        resid = acc_s[r, :] + recv_s[r, :]
        centre = resid - row_stats(resid)
        rstd = lax.rsqrt(row_stats(centre * centre) + EPS)
        unit = centre * rstd
        normed = unit * vec_ref[3:4, :] + vec_ref[4:5, :]
        unit_s[r, :] = unit
        rstd_s[r, :] = jnp.broadcast_to(rstd, (chunk, 128))
        normed_s[r, :] = normed
        h_ref[r, :] = normed.astype(BF16)
        return carry

    over_rows(norm_one)
    move = exchange(1, h_ref.at[own], h_ref.at[other])
    move.start()

    wait_all(copies[1])

    def up(where):
        def body(cols):
            pre = dot(h_ref[where, :], wi_s[:, cols], NN) + bias_ref[0:1, cols]
            act, slope = gelu_both(pre)
            act_ref[where, cols] = act.astype(BF16)
            slope_s[where, cols] = slope

        over_cols(ff_half, body)

    up(own)
    move.wait()
    up(other)
    for number in range(1, len(bits)):
        wb_level(number, lambda hop: hop.wait_recv())
        if number + 1 < len(bits):
            wb_level(number + 1, lambda hop: hop.start())
    wait_all(copies[2])

    def down_other(cols):
        send_s[:, cols] = dot(act_ref[other, :], wb_s[:, cols], NN)

    over_cols(width, down_other)
    move = exchange(2, send_s, recv_s)
    move.start()

    def down_own(cols):
        part = dot(act_ref[own, :], wb_s[:, cols], NN)
        acc_s[:, cols] = part + normed_s[:, cols] + vec_ref[5:6, cols]

    over_cols(width, down_own)
    move.wait()

    def norm_two(r, carry):
        resid = acc_s[r, :] + recv_s[r, :]
        centre = resid - row_stats(resid)
        rstd = lax.rsqrt(row_stats(centre * centre) + EPS)
        unit = centre * rstd
        gain = vec_ref[6:7, :]
        layer_ref[r, :] = (unit * gain + vec_ref[7:8, :]).astype(BF16)
        grad = cot_ref[r, :]
        scaled = grad * gain
        back = rstd * (scaled - row_stats(scaled) - unit * row_stats(scaled * unit))
        acc_s[r, :] = back
        g2_ref[r, :] = back.astype(BF16)
        sums = (back, grad * unit, grad)
        return tuple(c + jnp.sum(s, axis=0, keepdims=True) for c, s in zip(carry, sums))

    shift_two = over_rows(norm_two)
    move = exchange(3, g2_ref.at[own], g2_ref.at[other])
    move.start()
    for i, total in enumerate(shift_two):
        sums_ref[3 + i : 4 + i, :] = total

    def back_act(where, first):
        def body(cols):
            grad = dot(g2_ref[where, :], wb_s[cols, :], NT) * slope_s[where, cols]
            gp_ref[where, cols] = grad.astype(BF16)
            total = jnp.sum(grad, axis=0, keepdims=True)
            bias_sum_ref[0:1, cols] = total if first else bias_sum_ref[0:1, cols] + total

        over_cols(ff_half, body)

    back_act(own, True)
    move.wait()
    n_out = ff_half // step
    d_rows = width // n_z

    def product(left, right, store):
        for i in range(0, width, 256):
            turned_s[i : i + 256, :] = left[:, i : i + 256].T

        def cols_of(i, carry):
            cols = pl.ds(pl.multiple_of(i * step, step), step)
            store(i, cols, dot(turned_s[...], right[:, cols], NN).astype(BF16))
            return carry

        lax.fori_loop(0, n_out, cols_of, 0)

    if reduce:
        gb_s, acc_r, got_r, load_sem, f_send, f_recv = red_refs
        sums = Reduction(gb_s, pl.ds(0, ff_half), acc_r, got_r, None, (load_sem, f_send, f_recv, None, None), n_f, n_z)
        low = gb_s.shape[3]

        def store_back(i, cols, value):
            gb_s[:, :, :, :, cols] = value.reshape(n_z, 2, n_f, low, step)

        product(g2_ref, act_ref, store_back)
        sums.start()
    back_act(other, False)

    def back_other(cols):
        send_s[:, cols] = dot(gp_ref[other, :], wi_s[cols, :], NT)

    over_cols(width, back_other)
    move = exchange(4, send_s, recv_s)
    move.start()

    def back_own(cols):
        acc_s[:, cols] += dot(gp_ref[own, :], wi_s[cols, :], NT)

    over_cols(width, back_own)
    move.wait()

    def back_one(r, carry):
        grad = acc_s[r, :] + recv_s[r, :]
        unit = unit_s[r, :]
        rstd = rstd_s[r, 0:1]
        scaled = grad * vec_ref[3:4, :]
        back = rstd * (scaled - row_stats(scaled) - unit * row_stats(scaled * unit))
        grad_one_ref[r, :] = back
        g1_ref[r, :] = back.astype(BF16)
        sums = (back, grad * unit, grad)
        return tuple(c + jnp.sum(s, axis=0, keepdims=True) for c, s in zip(carry, sums))

    shift_one = over_rows(back_one)
    move = exchange(5, g1_ref.at[own], g1_ref.at[other])
    move.start()
    for i, total in enumerate(shift_one):
        sums_ref[i : 1 + i, :] = total
    sums_ref[6:8, :] = jnp.zeros((2, width), F32)

    def att_hop(m):
        return remote(ga_s.at[m - 1], ga_ref.at[m], a_send.at[m], a_recv.at[m], {"ctx": (zed ^ m) * 2 + core})

    move.wait()
    for m in list(range(n_z - 1, 0, -1)) + [0]:
        at = pl.ds(pl.multiple_of((zed ^ m) * wide, wide), wide)
        block = dot(g1_ref[...], wo_s[at, :], NT).astype(BF16)
        if m == 0:
            ga_ref[0] = block
        else:
            ga_s[m - 1] = block
            att_hop(m).start()

    if reduce:
        sums.level(0)

    def out_grad(i, which):
        cols = pl.ds(pl.multiple_of(i * step, step), step)
        there = pl.ds(pl.multiple_of(which * ff_half + i * step, step), step)
        return pltpu.make_async_copy(wi_s.at[:, cols], grads_out.at[:, there], g_sem.at[which * n_out + i])

    def store_staged(which):
        def store(i, cols, value):
            if which == 1:
                out_grad(i, 0).wait()
            wi_s[:, cols] = value
            out_grad(i, which).start()

        return store

    product(h_ref, gp_ref, store_staged(0))
    wide_out = ff_half
    if not reduce:
        product(g2_ref, act_ref, store_staged(1))
        wide_out = 2 * ff_half
    att_move.wait()
    half = width // 2
    cols = pl.ds(pl.multiple_of(core * half, 128), half)
    for i in range(0, half_in, 256):
        at = pl.ds(pl.multiple_of(core * half + i, 128), 256)
        og_s[at, :] = dot(att_ref[:, i : i + 256].T, g1_ref[:, cols], NN).astype(BF16)
        at = pl.ds(pl.multiple_of((1 - core) * half + i, 128), 256)
        turned = att2_s[:, i : i + 256].T
        og_s[at, :] = (
            dot(turned[:, :rows], g1_ref[rows:, cols], NN) + dot(turned[:, rows:], g1_ref[:rows, cols], NN)
        ).astype(BF16)
    out_move = pltpu.make_async_copy(og_s, grads_out.at[:, pl.ds(wide_out, half)], g_sem.at[2 * n_out])
    out_move.start()
    for number in range(1, len(bits)):
        wb_level(number, lambda hop: hop.wait_send())
    for m in range(1, n_z):
        att_hop(m).wait()
    for i in range(n_out):
        out_grad(i, 0 if reduce else 1).wait()
    out_move.wait()
    if reduce:
        for level in range(1, len(bits)):
            sums.level(level)
        final = pltpu.make_async_copy(acc_r.at[:, pl.ds(0, 1)], sum_out, load_sem.at[0, 0])
        final.start()
        sums.sent()
        final.wait()


def middle(att, x_own, cot, vectors, bias_half, wo, wi, wb4, got, got2, n_f, n_z, reduce):
    rows, width = x_own.shape
    wide = att.shape[2]
    ff_half = bias_half.shape[0]
    half_in = n_z * wide
    sds = jax.ShapeDtypeStruct
    vmem, dma = pltpu.VMEM, pltpu.SemaphoreType.DMA
    in_vmem, anywhere = pl.BlockSpec(memory_space=pltpu.VMEM), pl.BlockSpec(memory_space=pl.ANY)
    cfg = {"step": 512, "rows": 128}
    low = width // (2 * n_z * n_f)
    extra_out, extra = [], []
    if reduce:
        extra_out = [sds((2, 1, n_z, low, ff_half), BF16)]
        extra = [
            vmem((n_z, 2, n_f, low, ff_half), BF16),
            vmem((2, n_f // 2, n_z, low, ff_half), BF16),
            vmem((2, n_f - 1, n_z, low, ff_half), BF16),
            dma((2, n_f // 2)),
            dma((2, n_f - 1)),
            dma((2, n_f - 1)),
        ]
    return pl.pallas_call(
        partial(mid_kernel, n_f=n_f, n_z=n_z, reduce=reduce, cfg=cfg),
        out_shape=[
            sds((rows, width), BF16),
            sds((rows, width), F32),
            sds((n_z, 2 * rows, wide), BF16),
            sds((8, width), F32),
            sds((1, ff_half), F32),
            sds((width, (1 if reduce else 2) * ff_half + width // 2), BF16),
        ]
        + extra_out,
        in_specs=[in_vmem] * 5 + [anywhere] * 5,
        out_specs=[in_vmem] * 5 + [anywhere] * (1 + len(extra_out)),
        scratch_shapes=[
            vmem((2 * rows, half_in), BF16),
            vmem((2 * rows, half_in), BF16),
            vmem((2 * rows, width), BF16),
            vmem((2 * rows, ff_half), BF16),
            vmem((2 * rows, width), BF16),
            vmem((2 * rows, ff_half), BF16),
            vmem((2 * rows, width), BF16),
            vmem((n_z - 1, 2 * rows, wide), BF16),
            vmem((width, 2 * rows), BF16),
            vmem((width, width // 2), BF16),
            vmem((half_in, width), BF16),
            vmem((width, ff_half), BF16),
            vmem((ff_half, width), BF16),
            vmem((2 * rows, ff_half), F32),
            vmem((rows, width), F32),
            vmem((rows, width), F32),
            vmem((rows, width), F32),
            vmem((rows, width), F32),
            vmem((rows, width), F32),
            vmem((rows, 128), F32),
            dma((2 + 3 * n_f,)),
            dma((7,)),
            dma((7,)),
            dma((n_f, n_f)),
            dma((n_f, n_f)),
            dma((n_z,)),
            dma((n_z,)),
            dma((2 * (ff_half // cfg["step"]) + 1,)),
        ]
        + extra,
        compiler_params=pltpu.CompilerParams(
            vmem_limit_bytes=VMEM_MIDDLE, collective_id=0, has_side_effects=True
        ),
        cost_estimate=pl.CostEstimate(
            flops=2 * 2 * rows * width * (3 * half_in + 6 * ff_half),
            bytes_accessed=40 << 20, transcendentals=2 * rows * ff_half,
        ),
        name="middle",
    )(att, x_own, cot, vectors, bias_half[None], wo, wi, wb4, got, got2)


def back_kernel(*refs, blocks, heads, n_f, reduce, q_rows, steps_per):
    refs = list(refs)

    def take(count):
        taken = refs[:count]
        del refs[:count]
        return taken

    qkv_ref, ga_ref, full_ref, lse_ref, grad_one_ref = take(5)
    if reduce:
        mid_ref, bias_ref = take(2)
    (wl_hbm,) = take(1)
    if reduce:
        x_hbm, g_hbm, back_hbm = take(3)
    out_ref, sums_ref = take(2)
    if reduce:
        in_ref, back_ref, og_ref, qg_ref = take(4)
    (stage,) = take(1)
    lse_t, delta_t, gq_t, key_t, gin, wl_s, cat, send_s, recv_s = take(9)
    kv_send, kv_recv, q_send, q_recv, t_send, t_recv, own_sem = take(7)
    if reduce:
        x_s, gq_src, give_s, others, table_r, c_send, c_recv, o_send, o_recv, s_send, s_recv = take(11)
        bufs = [take(8) for _ in range(4)]
    ctx, fs = lax.axis_index("ctx"), lax.axis_index("fsdp")
    core, zed = ctx % 2, ctx // 2
    partner = {"ctx": zed * 2 + (1 - core)}
    bits, orders = fsdp_orders(n_f)
    rows = qkv_ref.shape[1]
    width = heads * HEAD
    scale = HEAD**-0.5
    chunk = 256
    half = wl_s.shape[1] // 3
    greeted = [partner] + [{"ctx": (zed ^ m) * 2 + core} for m in range(1, blocks)]
    if reduce:
        greeted += [{"fsdp": fs ^ bit} for bit in bits]
    greet(pltpu.get_barrier_semaphore(), greeted)
    wl_copy = pltpu.make_async_copy(wl_hbm, wl_s, own_sem.at[0])
    wl_copy.start()
    if reduce:
        cut = bufs[0][0].shape[-1]
        early, late, attn, lone = [
            Reduction(
                src, pl.ds(first, buf[0].shape[-1]), buf[0], buf[1], buf[2], buf[3:], n_f, blocks, begin, summed
            )
            for buf, src, first, begin, summed in zip(
                bufs, (g_hbm, g_hbm, gq_src, None), (0, cut, 0, 0), (0, 0, 0, len(bits)), (True, True, False, True)
            )
        ]
        lone_copy = pltpu.make_async_copy(back_hbm, lone.acc, own_sem.at[2])
        lone_copy.start()
        lone_copy.wait()
        lone.z_start()
        early.start()
        x_copy = pltpu.make_async_copy(x_hbm, x_s, own_sem.at[1])
        x_copy.start()

    for b in range(blocks):
        for i in range(0, rows, chunk):
            local = slice(i, i + chunk)
            where = slice(b * rows + i, b * rows + i + chunk)
            logs = lse_ref[where, :].T
            terms = (ga_ref[b, local, :].astype(F32) * full_ref[where, :]).T
            for head in range(heads):
                first = head * HEAD
                lse_t[head : head + 1, where] = logs[first : first + 1]
                delta_t[head : head + 1, where] = jnp.sum(
                    terms[first : first + HEAD], axis=0, keepdims=True
                )
        key_t[:, b * rows : (b + 1) * rows] = qkv_ref[b, :, width : 2 * width].T
    gq_t[...] = jnp.zeros_like(gq_t)

    split = width % 128 == 0

    def kv_hop(m, piece):
        at = pl.ds(pl.multiple_of(piece * (rows // steps_per), 128), rows // steps_per)
        cols = pl.ds(width, 2 * width)
        return remote(
            stage.at[m, at, cols], gin.at[m, at, cols], kv_send.at[m, piece], kv_recv.at[m, piece],
            {"ctx": (zed ^ m) * 2 + core},
        )

    def q_hop(m):
        cols = pl.ds(0, width if split else 3 * width)
        return remote(
            stage.at[m, :, cols], gin.at[m, :, cols], q_send.at[m], q_recv.at[m], {"ctx": (zed ^ m) * 2 + core}
        )

    k_rows = rows // steps_per

    def step(n, carry):
        b = blocks - 1 - n // steps_per
        start = n % steps_per * k_rows
        local = pl.ds(pl.multiple_of(start, 128), k_rows)
        where = pl.ds(pl.multiple_of(b * rows + start, 128), k_rows)
        key = qkv_ref[b, local, width : 2 * width]
        value = qkv_ref[b, local, 2 * width : 3 * width]
        key_grads, value_grads = [], []
        for head in range(heads):
            feats = slice(head * HEAD, (head + 1) * HEAD)
            key_h = one_head(key, head, heads) * BF16(scale)
            value_h = one_head(value, head, heads)
            key_grad = value_grad = None
            for other in range(blocks):
                for i in range(0, rows, q_rows):
                    here = slice(i, i + q_rows)
                    there = slice(other * rows + i, other * rows + i + q_rows)
                    query = qkv_ref[other, here, 0:width]
                    grad = ga_ref[other, here, :]
                    scores = dot(key_h, query, NT)
                    probs = jnp.exp(scores - lse_t[head : head + 1, there])
                    grad_probs = dot(value_h, grad, NT)
                    grad_scores = probs * (grad_probs - delta_t[head : head + 1, there])
                    grad_scores = grad_scores.astype(BF16)
                    term = dot(probs.astype(BF16), grad, NN)
                    value_grad = term if value_grad is None else value_grad + term
                    term = dot(grad_scores, query, NN)
                    key_grad = term if key_grad is None else key_grad + term
                    gq_t[feats, there] += dot(key_t[feats, where], grad_scores, NN)
            key_grads.append(key_grad)
            value_grads.append(value_grad)
        stage[b, local, width : 2 * width] = (merge_heads(key_grads) * scale).astype(BF16)
        stage[b, local, 2 * width : 3 * width] = merge_heads(value_grads).astype(BF16)
        if split:

            @pl.when(b > 0)
            def _():
                kv_hop(b, n % steps_per).start()

        if reduce:

            @pl.when(n == 1)
            def _():
                early.level(0)

            @pl.when(n == 2)
            def _():
                late.start()

            @pl.when(n == 3)
            def _():
                for level in range(1, len(bits)):
                    early.level(level)
                lone.z_level(0)

            @pl.when(n == 4)
            def _():
                late.level(0)

            @pl.when(n == 5)
            def _():
                early.z_level(0)
                for level in range(1, len(bits)):
                    late.level(level)

        return carry

    lax.fori_loop(0, blocks * steps_per, step, 0)
    for b in range(blocks - 1, -1, -1):
        for i in range(0, rows, chunk):
            there = slice(b * rows + i, b * rows + i + chunk)
            stage[b, i : i + chunk, 0:width] = (gq_t[:, there].T * scale).astype(BF16)
        if b > 0:
            q_hop(b).start()
    gin[0] = stage[0]
    sums = jnp.zeros((1, 3 * width), F32)
    for b in range(blocks):
        sums = sums + jnp.sum(stage[b].astype(F32), axis=0, keepdims=True)
    if reduce:
        dim = out_ref.shape[1]
        hidden_half = bias_ref.shape[1] // n_f
        sums_ref[...] = jnp.zeros_like(sums_ref)
        first = pl.ds(pl.multiple_of(core * half + zed * width, 128), width)
        sums_ref[0:1, first] = sums[:, 0:width]
        sums_ref[1:2, first] = sums[:, 2 * width :]
        sums_ref[2:8, :] = mid_ref[0:6, :]
        for f in range(n_f):
            at = pl.ds(pl.multiple_of(core * hidden_half, 128), hidden_half)
            sums_ref[8 + f : 9 + f, at] = bias_ref[:, f * hidden_half : (f + 1) * hidden_half]
        peers = [{"fsdp": fs ^ bit} for bit in bits]
        peers += [{"ctx": (zed ^ (1 << i)) * 2 + core} for i in range(blocks.bit_length() - 1)] + [partner]

        def table_hop(k):
            return remote(sums_ref, table_r.at[k], s_send.at[k], s_recv.at[k], peers[k])

        def table_step(k):
            if k < len(peers):
                table_hop(k).wait()
                sums_ref[...] += table_r[k]
                if k + 1 < len(peers):
                    table_hop(k + 1).start()

        table_hop(0).start()
    else:
        sums_ref[...] = sums

    if reduce:
        x_copy.wait()
        d_rows = x_s.shape[-1] // blocks
        low = gq_src.shape[3]
        for b in range(blocks):
            cat[0 : 3 * width, b * rows : (b + 1) * rows] = stage[b].T
        for z in range(blocks):
            cols = slice(z * d_rows, (z + 1) * d_rows)
            total = None
            for b in range(blocks):
                x_block = x_s[b, :, :, cols].reshape(rows, d_rows)
                term = dot(cat[0 : 3 * width, b * rows : (b + 1) * rows], x_block, NN)
                total = term if total is None else total + term
            gq_src[z] = total.T.astype(BF16).reshape(2, n_f, low, 3 * width)
        attn.start()
        table_step(0)
        late.z_level(0)

    tokens, dim = out_ref.shape
    pieces = dim // 256

    def collect(j):
        part = slice(j * width, (j + 1) * width)
        if split:
            for m in range(blocks):
                at = pl.ds(pl.multiple_of(j * half + (zed ^ m) * width, 128), width)
                cat[0:rows, at] = gin[m, :, part]
        else:
            for m in range(0, blocks, 2):
                one, two = gin[m, :, part].astype(F32), gin[m + 1, :, part].astype(F32)
                odd = zed % 2 == 1
                block = jnp.concatenate([jnp.where(odd, two, one), jnp.where(odd, one, two)], axis=1)
                at = j * half + (zed // 2 ^ (m // 2)) * 2 * width
                cat[0:rows, pl.ds(pl.multiple_of(at, 128), 2 * width)] = block.astype(BF16)

    def swap_hop(i):
        cols = slice(i * 256, (i + 1) * 256)
        return remote(send_s.at[:, cols], recv_s.at[:, cols], t_send.at[i], t_recv.at[i], partner)

    for m in range(blocks - 1, 0, -1):
        if split:
            for piece in range(steps_per):
                kv_hop(m, piece).wait()
        else:
            q_hop(m).wait()
    wl_copy.wait()
    collect(1)
    collect(2)
    keys = slice(half, 3 * half)
    for i in range(pieces):
        cols = slice(i * 256, (i + 1) * 256)
        send_s[:, cols] = dot(cat[tokens:rows, keys], wl_s[cols, keys], NT)
        out_ref[:, cols] = dot(cat[0:tokens, keys], wl_s[cols, keys], NT) + grad_one_ref[:, cols]
    if reduce:
        hops = []

        def settle(which, offset, places):
            count = which.acc.shape[-1]
            give_s[:, offset : offset + count] = which.total(1 - core)
            kept = which.total(core)
            start = 0
            for target, at, size in places:
                cols = pl.ds(pl.multiple_of(at, 128), size)
                hop = remote(
                    give_s.at[:, pl.ds(offset + start, size)], target.at[:, cols], c_send.at[len(hops)],
                    c_recv.at[len(hops)], partner,
                )
                hop.start()
                hops.append(hop)
                target[:, cols] = kept[:, start : start + size]
                start += size

        def units(target):
            return [(target, (2 * f + core) * hidden_half, hidden_half) for f in range(n_f)]

        for level in range(len(bits)):
            attn.level(level)
            table_step(1 + level)
        for level in range(1, len(lone.z_bits)):
            lone.z_level(level)
        settle(lone, 0, units(back_ref))
    if split:
        for m in range(blocks - 1, 0, -1):
            q_hop(m).wait()
    collect(0)
    for i in range(pieces):
        cols = slice(i * 256, (i + 1) * 256)
        send_s[:, cols] += dot(cat[tokens:rows, 0:half], wl_s[cols, 0:half], NT)
        swap_hop(i).start()
    for i in range(pieces):
        cols = slice(i * 256, (i + 1) * 256)
        out_ref[:, cols] += dot(cat[0:tokens, 0:half], wl_s[cols, 0:half], NT)
    if reduce:
        for k in range(1 + len(bits), len(peers)):
            table_step(k)
    for i in range(pieces):
        cols = slice(i * 256, (i + 1) * 256)
        swap_hop(i).wait_recv()
        out_ref[:, cols] += recv_s[:, cols]
    for i in range(pieces):
        swap_hop(i).wait_send()

    if reduce:
        attn.arrived()

        def other_hop(m):
            src = attn.acc.at[1 - core, 0, zed] if m == 0 else attn.far.at[1 - core, m - 1]
            return remote(src, others.at[m], o_send.at[m], o_recv.at[m], partner)

        def put_heads(m, value, which):
            for j in range(3):
                at = pl.ds(pl.multiple_of(j * dim + which * half + (zed ^ m) * width, 128), width)
                qg_ref[:, at] = value[:, j * width : (j + 1) * width].astype(F32)

        for m in range(blocks):
            other_hop(m).start()
        for m in range(blocks):
            put_heads(m, attn.acc[core, 0, zed] if m == 0 else attn.far[core, m - 1], core)

        places = units(in_ref) + [(og_ref, core * half, half)]
        offset = lone.acc.shape[-1]
        for which, some in ((early, places[: n_f - 1]), (late, places[n_f - 1 :])):
            for level in range(1, len(which.z_bits)):
                which.z_level(level)
            settle(which, offset, some)
            offset += cut
        for m in range(blocks):
            other_hop(m).wait()
            put_heads(m, others[m], 1 - core)
        for which in (early, late, attn, lone):
            which.sent()
        for hop in hops:
            hop.wait()


def back(qkv, grads, full, lse, grad_one, w_local, x_all, mid_grads, heads, n_f, reduce, back_sums=None, sums_mid=None, bias_sum=None):
    blocks, rows, _ = qkv.shape
    width = heads * HEAD
    length = rows * blocks
    tokens, dim = grad_one.shape
    sds = jax.ShapeDtypeStruct
    vmem, dma = pltpu.VMEM, pltpu.SemaphoreType.DMA
    in_vmem, anywhere = pl.BlockSpec(memory_space=pltpu.VMEM), pl.BlockSpec(memory_space=pl.ANY)
    operands = [qkv, grads, full, lse, grad_one]
    if reduce:
        operands += [sums_mid, bias_sum]
    inner = len(operands)
    operands += [w_local]
    out_shape = [sds((tokens, dim), F32), sds((16, dim) if reduce else (1, 3 * width), F32)]
    staged = (blocks, rows, 3 * width)
    scratch = [
        vmem((8, length), F32),
        vmem((8, length), F32),
        vmem((width, length), F32),
        vmem((width, length), BF16),
        vmem(staged, BF16),
        vmem(w_local.shape, BF16),
        vmem((rows, max(length, w_local.shape[1])), BF16),
        vmem((tokens, dim), F32),
        vmem((tokens, dim), F32),
        dma((blocks, 2)),
        dma((blocks, 2)),
        dma((blocks,)),
        dma((blocks,)),
        dma((dim // 256,)),
        dma((dim // 256,)),
        dma((3,)),
    ]
    if reduce:
        _, _, _, low, columns = mid_grads.shape
        operands += [x_all, mid_grads, back_sums]
        hidden_half = back_sums.shape[-1]
        out_shape += [sds((low, 2 * hidden_half), F32)] * 2 + [sds((low, dim), F32), sds((low, 3 * dim), F32)]
        n_peers = n_f.bit_length() + blocks.bit_length() - 1
        scratch = [vmem(staged, BF16)] + scratch
        scratch += [
            vmem(x_all.shape, BF16),
            vmem((blocks, 2, n_f, low, 3 * width), BF16),
            vmem((low, columns + hidden_half), F32),
            vmem((blocks, low, 3 * width), BF16),
            vmem((n_peers, 16, dim), F32),
            dma((2 * n_f + 1,)),
            dma((2 * n_f + 1,)),
            dma((blocks,)),
            dma((blocks,)),
            dma((n_peers,)),
            dma((n_peers,)),
        ]
        cut = (n_f - 1) * (hidden_half // n_f)
        for cols in (cut, columns - cut, 3 * width, hidden_half):
            halved = cols == hidden_half
            scratch += [
                vmem((2, 1 if halved else n_f // 2, blocks, low, cols), BF16),
                vmem((2, 1, 1, 16, 128) if halved else (2, n_f - 1, blocks, low, cols), BF16),
                vmem((2, blocks - 1, low, cols), BF16),
                dma((2, n_f // 2)),
                dma((2, n_f - 1)),
                dma((2, n_f - 1)),
                dma((2, blocks - 1)),
                dma((2, blocks - 1)),
            ]
    else:
        out_shape += [sds(staged, BF16)]
    return pl.pallas_call(
        partial(
            back_kernel, blocks=blocks, heads=heads, n_f=n_f, reduce=reduce, q_rows=256, steps_per=2
        ),
        out_shape=out_shape,
        in_specs=[in_vmem] * inner + [anywhere] * (len(operands) - inner),
        out_specs=[in_vmem] * len(out_shape),
        scratch_shapes=scratch,
        compiler_params=pltpu.CompilerParams(
            vmem_limit_bytes=VMEM_MIDDLE, collective_id=2, has_side_effects=True
        ),
        cost_estimate=pl.CostEstimate(
            flops=40 * length * length * width, bytes_accessed=30 << 20,
            transcendentals=heads * length * length,
        ),
        name="back",
    )(*operands)


def on_device(x_in, w_qkv, w_out, w_in, w_back, vectors, bias_in, cot, *, n_ctx, n_f):
    ctx, fs = lax.axis_index("ctx"), lax.axis_index("fsdp")
    core, zed = ctx % 2, ctx // 2
    n_z = n_ctx // 2
    x_own = x_in[0]
    grad_out = cot[0]
    rows, width = x_own.shape
    hidden = w_back.shape[0]
    half_heads = HEADS // 2
    heads = half_heads // n_z
    wide = heads * HEAD

    def swap(v):
        return lax.ppermute(v, "ctx", [(i, i ^ 1) for i in range(n_ctx)])

    def over_z(v, m):
        return lax.ppermute(v, "ctx", [(i, i ^ (2 * m)) for i in range(n_ctx)])

    def over_f(v, m):
        return lax.ppermute(v, "fsdp", [(i, i ^ m) for i in range(n_f)])

    bits = [1 << b for b in range(n_f.bit_length() - 1)]

    def place(pieces, index, axis):
        count = len(pieces)
        for bit in range(count.bit_length() - 1):
            flag = (index >> bit) & 1
            pieces = [jnp.where(flag, pieces[m ^ (1 << bit)], pieces[m]) for m in range(count)]
        return jnp.concatenate(pieces, axis=axis)

    half_in = width // 2
    first = (core * half_heads + zed * heads) * HEAD
    span = 3 * wide
    bias_qkv = jnp.concatenate(
        [
            lax.dynamic_slice_in_dim(vectors[0], first, wide, 0),
            jnp.zeros((wide,), F32),
            lax.dynamic_slice_in_dim(vectors[1], first, wide, 0),
        ]
    )[None]
    ff_part = w_in.shape[1] // 2
    w_back4 = w_back.reshape(n_f, 2, ff_part, w_back.shape[1])
    qkv, x_all, w_local, wo_half, wi_got, wb_got = front(
        x_own, w_qkv, w_out, w_in, w_back4, bias_qkv, n_f, n_z, heads
    )

    att, att_full, lse, wi_half, wb_got2 = attend(qkv, w_in, wi_got, w_back4, heads, n_f)
    bias_half = lax.dynamic_index_in_dim(
        bias_in.reshape(n_f, 2, ff_part), core, 1, False
    ).reshape(-1)
    low = width // (n_ctx * n_f)
    in_kernel = low % 16 == 0 and wide % 128 == 0 and hidden == n_f * width and min(n_z, n_f) >= 4
    layer_out, grad_one, g_att, sums_mid, bias_sum, mid_grads, *back_sums = middle(
        att, x_own, grad_out, vectors, bias_half, wo_half, wi_half, w_back4, wb_got, wb_got2, n_f, n_z, in_kernel
    )
    layer_out = layer_out[None]


    def over_fsdp(partial_grad):
        cols = partial_grad.shape[1]
        view = partial_grad.reshape((n_z, 2) + (2,) * len(bits) + (low, cols))
        done = []
        for side in range(2):
            now = view[:, side]
            order = bits if side == 0 else bits[1:] + bits[:1]
            left = list(reversed(bits))
            for bit in order:
                axis = 1 + left.index(bit)
                left.remove(bit)
                flag = (fs // bit) % 2
                stay = lax.dynamic_index_in_dim(now, flag, axis, False)
                go = lax.dynamic_index_in_dim(now, 1 - flag, axis, False)
                now = (stay.astype(F32) + over_f(go, bit).astype(F32)).astype(BF16)
            done.append(now)
        return jnp.stack(done, axis=1)

    def over_ctx(both):
        total = lax.dynamic_index_in_dim(both, zed, 0, False).astype(F32)
        for m in range(1, n_z):
            part = lax.dynamic_index_in_dim(both, zed ^ m, 0, False)
            total = total + over_z(part, m).astype(F32)
        stay = lax.dynamic_index_in_dim(total, core, 0, False)
        go = lax.dynamic_index_in_dim(total, 1 - core, 0, False)
        return stay, swap(go.astype(BF16)).astype(F32)

    def halves(stay, came, parts):
        low = stay.shape[0]
        first = jnp.where(core == 0, stay, came).reshape(low, parts, 1, -1)
        second = jnp.where(core == 0, came, stay).reshape(low, parts, 1, -1)
        return jnp.concatenate([first, second], axis=2).reshape(low, -1)

    def reduced(partial_grad):
        return over_ctx(over_fsdp(partial_grad))

    if in_kernel:
        grad_in, table, in_weight_grad, back_turned, out_weight_grad, qkv_weight_grad = back(
            qkv, g_att, att_full, lse, grad_one, w_local, x_all,
            mid_grads.reshape(n_z, 2, n_f, low, -1), heads, n_f, True, back_sums[0], sums_mid, bias_sum,
        )
        mine_at = (ctx * n_f + fs) * low
        vector_grad = lax.dynamic_slice_in_dim(table[:8], mine_at, low, 1)
        share = hidden // (n_ctx * n_f)
        in_bias_grad = lax.dynamic_slice_in_dim(table[8 : 8 + n_f].reshape(-1), mine_at // low * share, share, 0)
        return (
            layer_out,
            grad_in[None],
            qkv_weight_grad,
            out_weight_grad,
            in_weight_grad,
            back_turned.T,
            vector_grad,
            in_bias_grad,
        )
    stay, came = reduced(mid_grads)
    grad_in, sums, g_local = back(
        qkv, g_att, att_full, lse, grad_one, w_local, None, None, heads, n_f, False
    )
    attn_grad = dot(x_all.reshape(-1, width), g_local.reshape(-1, span), TN).astype(BF16)
    both = over_fsdp(attn_grad)
    mine, others = [], []
    for m in range(n_z):
        part = lax.dynamic_index_in_dim(both, zed ^ m, 0, False)
        part = part if m == 0 else over_z(part, m)
        mine.append(lax.dynamic_index_in_dim(part, core, 0, False))
        others.append(lax.dynamic_index_in_dim(part, 1 - core, 0, False))
    others = swap(jnp.stack(others))
    others = [others[m] for m in range(n_z)]
    n_half = hidden // 2
    in_weight_grad = halves(stay[:, :n_half], came[:, :n_half], n_f)
    back_weight_grad = halves(stay[:, n_half : 2 * n_half], came[:, n_half : 2 * n_half], n_f).T
    out_weight_grad = halves(stay[:, 2 * n_half :], came[:, 2 * n_half :], 1)

    def heads_order(parts):
        parts = [p.reshape(low, 3, wide) for p in parts]
        return place(parts, zed, 2).astype(F32).reshape(low, -1)

    qkv_weight_grad = halves(heads_order(mine), heads_order(others), 3)

    def spread(half_row, parts):
        piece = half_row.reshape(parts, 1, -1)
        empty = jnp.zeros_like(piece)
        both = jnp.where(core == 0, jnp.concatenate([piece, empty], 1), jnp.concatenate([empty, piece], 1))
        return both.reshape(-1)

    def halve(now):
        left = list(reversed(bits))
        for bit in bits:
            axis = left.index(bit)
            left.remove(bit)
            flag = (fs // bit) % 2
            stay = lax.dynamic_index_in_dim(now, flag, axis, False)
            now = stay + over_f(lax.dynamic_index_in_dim(now, 1 - flag, axis, False), bit)
        return now

    sums = sums[0]
    sums = jnp.stack([sums[:wide].reshape(n_f, -1), sums[2 * wide :].reshape(n_f, -1)], axis=1)
    late = halve(sums.reshape((2,) * len(bits) + (-1,)))
    turn = [(2 * z + c, n_z * c + z) for z in range(n_z) for c in range(2)]
    late = lax.ppermute(late, "ctx", turn).reshape(2, -1)
    ratio = hidden // width
    early = sums_mid[:6].T
    bias_terms = spread(bias_sum[0], n_f).reshape(width, ratio)
    table = jnp.concatenate([early, bias_terms], axis=1)
    kinds = table.shape[1]
    now = jnp.swapaxes(table.reshape(n_z * 2, n_f, low, kinds), -1, -2)
    now = jnp.swapaxes(now, 0, 1).reshape((2,) * len(bits) + (n_z, 2, kinds * low))
    now = halve(now)
    total = lax.dynamic_index_in_dim(now, zed, 0, False)
    for m in range(1, n_z):
        total = total + over_z(lax.dynamic_index_in_dim(now, zed ^ m, 0, False), m)
    stay = lax.dynamic_index_in_dim(total, core, 0, False)
    table = stay + swap(lax.dynamic_index_in_dim(total, 1 - core, 0, False))
    table = table.reshape(kinds, low)
    vector_grad = jnp.concatenate([late, table[:6]], axis=0)
    in_bias_grad = table[6:].T.reshape(-1)
    return (
        layer_out,
        grad_in[None],
        qkv_weight_grad,
        out_weight_grad,
        in_weight_grad,
        back_weight_grad,
        vector_grad,
        in_bias_grad,
    )


def solution(mesh):
    tokens = P("fsdp", "ctx", None)
    cols = P(None, "fsdp")
    shared = P(("ctx", "fsdp"), None)
    return jax.shard_map(
        partial(on_device, n_ctx=mesh.shape["ctx"], n_f=mesh.shape["fsdp"]),
        mesh=mesh,
        in_specs=(tokens, cols, cols, cols, cols, P(), P(), tokens),
        out_specs=(
            tokens,
            tokens,
            shared,
            shared,
            shared,
            P(None, ("ctx", "fsdp")),
            P(None, ("ctx", "fsdp")),
            P(("ctx", "fsdp")),
        ),
        check_vma=False,
    )
```

```python
from functools import partial
import math

import jax
import jax.numpy as jnp
from jax import lax
from jax.experimental import pallas as pl
from jax.experimental.pallas import tpu as pltpu
from jax.sharding import PartitionSpec as P

HEADS = 16
HEAD = 64
EPS = 1e-12
F32 = jnp.float32
BF16 = jnp.bfloat16
NN = (((1,), (0,)), ((), ()))
NT = (((1,), (1,)), ((), ()))
TN = (((0,), (0,)), ((), ()))
VMEM_LIMIT = 50 * 1024 * 1024
VMEM_MIDDLE = 56 * 1024 * 1024
MESH = pl.DeviceIdType.MESH


def dot(left, right, dims):
    return lax.dot_general(left, right, dims, preferred_element_type=F32)


def front_kernel(
    x_ref, wq_ref, wo_ref, wi_ref, wb_ref, bias_ref, qkv_ref, xf_out, wl_out, wo_out, wi_out, wb_out, *scratch, n_z, n_f, heads
):
    xf, wfull, wloc = scratch[:3]
    own_sem, x_send, x_recv, xs_send, xs_recv, w_send, w_recv, ws_send, ws_recv, o_send, o_recv, i_send, i_recv, b_send, b_recv, out_sem = scratch[3:]
    ctx, fs = lax.axis_index("ctx"), lax.axis_index("fsdp")
    core, zed = ctx % 2, ctx // 2
    bits = [1 << b for b in range(n_f.bit_length() - 1)]
    orders = (bits, bits[1:] + bits[:1])
    rows, width = x_ref.shape
    half = width // 2
    quarter = half // 2
    wide = heads * HEAD
    partner = {"ctx": zed * 2 + (1 - core)}

    barrier = pltpu.get_barrier_semaphore()

    def greet(device):
        pl.semaphore_signal(barrier, inc=1, device_id=device, device_id_type=MESH)

    greet(partner)
    for bit in bits:
        greet({"fsdp": fs ^ bit})

    @pl.when(zed > 0)
    def _():
        greet({"ctx": ctx - 2})

    @pl.when(zed < n_z - 1)
    def _():
        greet({"ctx": ctx + 2})

    edges = (zed == 0).astype(jnp.int32) + (zed == n_z - 1).astype(jnp.int32)
    pl.semaphore_wait(barrier, 3 + len(bits) - edges)

    def remote(src, dst, send, recv, device):
        return pltpu.make_async_remote_copy(
            src_ref=src, dst_ref=dst, send_sem=send, recv_sem=recv, device_id=device, device_id_type=MESH
        )

    def x_move(away, step, first):
        block = zed - step * away
        src = x_ref if first else xf.at[block ^ zed, 0]
        index = (step + 1) // 2
        return remote(
            src, xf.at[block ^ (zed + step), 0], x_send.at[index, away], x_recv.at[block ^ (zed + step)],
            {"ctx": ctx + 2 * step},
        )

    def x_swap(m, first=False):
        src = x_ref if first else xf.at[m, 0]
        return remote(src, xf.at[m, 1], xs_send.at[m], xs_recv.at[m], partner)

    def has(step):
        return zed < n_z - 1 if step == 1 else zed > 0

    def came(away, step):
        return zed - away >= 0 if step == 1 else zed + away <= n_z - 1

    for step in (1, -1):

        @pl.when(has(step))
        def _(step=step):
            x_move(0, step, True).start()

    x_swap(0, True).start()
    own_x = pltpu.make_async_copy(x_ref, xf.at[0, 0], own_sem.at[0])
    own_x.start()

    def x_step(away):
        for step in (1, -1):

            @pl.when(came(away, step))
            def _(step=step):
                block = zed - step * away
                remote(
                    xf.at[block ^ zed, 0], xf.at[block ^ zed, 0], x_send.at[0, 0], x_recv.at[block ^ zed], partner
                ).wait_recv()

                @pl.when(has(step))
                def _():
                    x_move(away, step, False).start()

                x_swap(block ^ zed).start()

    def wq_place(side, origin, which):
        cols = wq_ref.shape[1]
        return wfull.at[
            pl.ds(pl.multiple_of(which * half + side * quarter, quarter), quarter),
            pl.ds(pl.multiple_of(origin * cols, 128), cols),
        ]

    def wq_own(side):
        return wq_ref.at[pl.ds(pl.multiple_of(core * half + side * quarter, quarter), quarter), :]

    def wo_place(side, origin):
        cols = wo_ref.shape[1]
        return wo_out.at[pl.ds(side * quarter, quarter), pl.ds(pl.multiple_of(origin * cols, 128), cols)]

    def wo_own(side):
        return wo_ref.at[pl.ds(pl.multiple_of(core * half + side * quarter, quarter), quarter), :]

    def wq_hop(side, m, bit):
        src = wq_own(side) if m == 0 else wq_place(side, fs ^ m, core)
        return remote(src, wq_place(side, fs ^ m, core), w_send.at[side, m ^ bit], w_recv.at[side, m ^ bit], {"fsdp": fs ^ bit})

    def wo_hop(side, m, bit):
        src = wo_own(side) if m == 0 else wo_place(side, fs ^ m)
        return remote(src, wo_place(side, fs ^ m), o_send.at[side, m ^ bit], o_recv.at[side, m ^ bit], {"fsdp": fs ^ bit})

    def wq_swap(side, m):
        src = wq_own(side) if m == 0 else wq_place(side, fs ^ m, core)
        return remote(src, wq_place(side, fs ^ m, core), ws_send.at[side, m], ws_recv.at[side, m], partner)

    own_w = []
    for side in range(2):
        wq_hop(side, 0, orders[side][0]).start()
        wq_swap(side, 0).start()
        own_w.append(pltpu.make_async_copy(wq_own(side), wq_place(side, fs, core), own_sem.at[1 + side]))
        own_w.append(pltpu.make_async_copy(wo_own(side), wo_place(side, fs), own_sem.at[3 + side]))
    for copy in own_w:
        copy.start()

    part = wi_ref.shape[1] // 2

    def wi_hop(side):
        src = wi_ref.at[pl.ds(side * half, half), pl.ds(pl.multiple_of(core * part, 128), part)]
        return remote(src, wi_out.at[side], i_send.at[side], i_recv.at[side], {"fsdp": fs ^ orders[side][0]})

    def wb_hop(seg):
        return remote(
            wb_ref.at[seg, core], wb_out.at[seg], b_send.at[seg], b_recv.at[seg],
            {"fsdp": fs ^ orders[seg * 2 // n_f][0]},
        )

    def doubling(hop, level, after=None):
        for side in range(2):
            known = [0]
            for bit in orders[side][:level]:
                known = known + [m ^ bit for m in known]
            bit = orders[side][level]
            for m in known:
                hop(side, m, bit).wait_recv()
                if after is not None:
                    after(side, m ^ bit).start()
            if level + 1 < len(bits):
                for m in known + [m ^ bit for m in known]:
                    hop(side, m, orders[side][level + 1]).start()

    doubling(wq_hop, 0, wq_swap)
    for side in range(2):
        wo_hop(side, 0, orders[side][0]).start()
    x_step(1)
    for level in range(1, len(bits)):
        doubling(wq_hop, level, wq_swap)
    for side in range(2):
        wi_hop(side).start()
    doubling(wo_hop, 0)
    for seg in range(n_f):
        wb_hop(seg).start()
    for away in range(2, n_z - 1):
        x_step(away)
    for copy in own_w:
        copy.wait()
    for side in range(2):
        for m in range(n_f):
            wq_swap_in = remote(
                wq_place(side, fs ^ m, 1 - core), wq_place(side, fs ^ m, 1 - core),
                ws_send.at[side, m], ws_recv.at[side, m], partner,
            )
            wq_swap_in.wait_recv()
    outs = []
    for j in range(3):
        cols = pl.ds(pl.multiple_of(j * width + core * half, 128), half)
        outs.append(pltpu.make_async_copy(wfull.at[:, cols], wl_out.at[:, pl.ds(j * half, half)], out_sem.at[j]))
    for copy in outs:
        copy.start()
    for j in range(3):
        base = j * width + core * half + zed * wide
        if wide % 128 == 0:
            piece = wfull[:, pl.ds(pl.multiple_of(base, 128), wide)]
        else:
            block = wfull[:, pl.ds(pl.multiple_of(base // 128 * 128, 128), 128)].astype(F32)
            piece = jnp.where(zed % 2 == 1, block[:, wide:], block[:, :wide]).astype(BF16)
        wloc[:, j * wide : (j + 1) * wide] = piece

    def x_ready(m, side):
        remote(xf.at[m, side], xf.at[m, side], xs_send.at[m], xs_recv.at[m], partner).wait_recv()

    def project(m):
        def run(side, carry):
            result = dot(xf[m, side], wloc[...], NN) + bias_ref[...]
            where = pl.ds(pl.multiple_of(side * rows, rows), rows)
            qkv_ref[m, where, :] = result.astype(BF16)
            return carry

        lax.fori_loop(0, 2, run, 0)

    own_x.wait()
    x_ready(0, 1)
    project(0)

    def finish(away):
        def run(i, carry):
            block = zed - (1 - 2 * i) * away

            @pl.when((block >= 0) & (block <= n_z - 1))
            def _():
                x_ready(block ^ zed, 1)
                project(block ^ zed)

            return carry

        lax.fori_loop(0, 2, run, 0)

    for away in range(1, n_z - 1):
        finish(away)
    for level in range(1, len(bits)):
        doubling(wo_hop, level)
    if n_z > 2:
        x_step(n_z - 1)
    finish(n_z - 1)
    x_out = pltpu.make_async_copy(xf, xf_out, own_sem.at[5])
    x_out.start()

    for step in (1, -1):

        @pl.when(has(step))
        def _(step=step):
            x_move(0, step, True).wait_send()
            for away in range(1, n_z):

                @pl.when(came(away, step))
                def _(away=away):
                    x_move(away, step, False).wait_send()

    x_swap(0, True).wait_send()
    for m in range(1, n_z):
        x_swap(m).wait_send()
    for side in range(2):
        known = [0]
        for bit in orders[side]:
            for m in known:
                wq_hop(side, m, bit).wait_send()
                wo_hop(side, m, bit).wait_send()
            known = known + [m ^ bit for m in known]
        for m in range(n_f):
            wq_swap(side, m).wait_send()
        wi_hop(side).wait()
    for seg in range(n_f):
        wb_hop(seg).wait()
    for copy in outs:
        copy.wait()
    x_out.wait()


def front(x_own, w_qkv, w_out, w_in, w_back4, bias, n_f, n_z, heads):
    rows, width = x_own.shape
    wide = heads * HEAD
    sds = jax.ShapeDtypeStruct
    in_vmem, anywhere = pl.BlockSpec(memory_space=pltpu.VMEM), pl.BlockSpec(memory_space=pl.ANY)
    part = w_in.shape[1] // 2
    dma = pltpu.SemaphoreType.DMA
    return pl.pallas_call(
        partial(front_kernel, n_z=n_z, n_f=n_f, heads=heads),
        out_shape=[
            sds((n_z, 2 * rows, 3 * wide), BF16),
            sds((n_z, 2, rows, width), BF16),
            sds((width, 3 * width // 2), BF16),
            sds((width // 2, width), BF16),
            sds((2, width // 2, part), BF16),
            sds((n_f,) + w_back4.shape[2:], BF16),
        ],
        in_specs=[anywhere] * 5 + [in_vmem],
        out_specs=[in_vmem] + [anywhere] * 5,
        scratch_shapes=[
            pltpu.VMEM((n_z, 2, rows, width), BF16),
            pltpu.VMEM((width, 3 * width), BF16),
            pltpu.VMEM((width, 3 * wide), BF16),
            dma((6,)),
            dma((2, n_z)),
            dma((n_z,)),
            dma((n_z,)),
            dma((n_z,)),
            dma((2, n_f)),
            dma((2, n_f)),
            dma((2, n_f)),
            dma((2, n_f)),
            dma((2, n_f)),
            dma((2, n_f)),
            dma((2,)),
            dma((2,)),
            dma((n_f,)),
            dma((n_f,)),
            dma((3,)),
        ],
        compiler_params=pltpu.CompilerParams(
            vmem_limit_bytes=VMEM_LIMIT, collective_id=1, has_side_effects=True
        ),
        cost_estimate=pl.CostEstimate(
            flops=4 * n_z * rows * width * 3 * wide, bytes_accessed=30 << 20, transcendentals=0
        ),
        name="front",
    )(x_own, w_qkv, w_out, w_in, w_back4, bias)


def one_head(block, head, heads):
    if heads == 1:
        return block
    lane = lax.broadcasted_iota(jnp.int32, block.shape, 1)
    return jnp.where(lane // HEAD == head, block, jnp.zeros_like(block))


def merge_heads(parts):
    if len(parts) == 1:
        return parts[0]
    lane = lax.broadcasted_iota(jnp.int32, parts[0].shape, 1)
    result = parts[0]
    for head in range(1, len(parts)):
        result = jnp.where(lane // HEAD == head, parts[head], result)
    return result


def remote(src, dst, send, recv, device):
    return pltpu.make_async_remote_copy(
        src_ref=src, dst_ref=dst, send_sem=send, recv_sem=recv, device_id=device, device_id_type=MESH
    )


def greet(barrier, devices):
    for device in devices:
        pl.semaphore_signal(barrier, inc=1, device_id=device, device_id_type=MESH)
    pl.semaphore_wait(barrier, len(devices))


def fsdp_orders(n_f):
    bits = [1 << b for b in range(n_f.bit_length() - 1)]
    return bits, (bits, bits[1:] + bits[:1])


def known_at(order, level):
    known = [0]
    for bit in order[:level]:
        known = known + [m ^ bit for m in known]
    return known


def attend_kernel(*refs, blocks, heads, n_f, q_rows, k_rows):
    qkv_ref, wi_ref, got_ref, wb_ref = refs[:4]
    att_ref, full_ref, lse_ref, wi_out, wb_out = refs[4:9]
    key_s, value_s, send_s, a_send, a_recv, i_send, i_recv, b_send, b_recv, own_sem = refs[9:]
    ins = [qkv_ref.at[b] for b in range(blocks)]
    rows = ins[0].shape[0]
    width = heads * HEAD
    length = rows * blocks
    ctx, fs = lax.axis_index("ctx"), lax.axis_index("fsdp")
    core, zed = ctx % 2, ctx // 2
    bits, orders = fsdp_orders(n_f)
    greet(
        pltpu.get_barrier_semaphore(),
        [{"fsdp": fs ^ bit} for bit in bits] + [{"ctx": (zed ^ m) * 2 + core} for m in range(1, blocks)],
    )

    half, part = got_ref.shape[1:]

    def wi_place(side, m):
        return wi_out.at[pl.ds(side * half, half), pl.ds(pl.multiple_of((fs ^ m) * part, 128), part)]

    def wi_source(side, m):
        if m == 0:
            return wi_ref.at[pl.ds(side * half, half), pl.ds(pl.multiple_of(core * part, 128), part)]
        return got_ref.at[side] if m == orders[side][0] else wi_place(side, m)

    def wi_hop(side, m, bit):
        return remote(
            wi_source(side, m), wi_place(side, m), i_send.at[side, m ^ bit], i_recv.at[side, m ^ bit], {"fsdp": fs ^ bit}
        )

    def wb_hop(seg):
        return remote(
            wb_ref.at[seg, core], wb_out.at[seg], b_send.at[seg], b_recv.at[seg],
            {"fsdp": fs ^ orders[seg * 2 // n_f][1]},
        )

    def level(number, act):
        for side in range(2):
            for m in known_at(orders[side], number):
                act(wi_hop(side, m, orders[side][number]))

    locals_ = []
    for side in range(2):
        for i, m in enumerate((0, orders[side][0])):
            locals_.append(pltpu.make_async_copy(wi_source(side, m), wi_place(side, m), own_sem.at[2 * side + i]))
    for copy in locals_:
        copy.start()
    level(1, lambda hop: hop.start())
    for seg in range(n_f):
        wb_hop(seg).start()

    def att_hop(b):
        return remote(send_s.at[b - 1], att_ref.at[b], a_send.at[b], a_recv.at[b], {"ctx": (zed ^ b) * 2 + core})

    for b in range(blocks):
        here = slice(b * rows, (b + 1) * rows)
        key_s[here, :] = ins[b][:, width : 2 * width]
        value_s[here, :] = ins[b][:, 2 * width : 3 * width]
    for turn, b in enumerate(list(range(blocks - 1, 0, -1)) + [0]):

        def step(i, carry, b=b):
            local = pl.ds(pl.multiple_of(i * q_rows, q_rows), q_rows)
            where = pl.ds(pl.multiple_of(b * rows + i * q_rows, q_rows), q_rows)
            query = ins[b][local, 0:width] * BF16(HEAD**-0.5)
            outputs, sums = [], []
            for head in range(heads):
                masked = one_head(query, head, heads)
                scores = [
                    dot(masked, key_s[j : j + k_rows, :], NT) for j in range(0, length, k_rows)
                ]
                top = None
                for part in scores:
                    part_top = jnp.max(part, axis=1, keepdims=True)
                    top = part_top if top is None else jnp.maximum(top, part_top)
                total = acc = None
                for j, part in enumerate(scores):
                    probs = jnp.exp(part - top)
                    part_total = jnp.sum(probs, axis=1, keepdims=True)
                    value = value_s[j * k_rows : (j + 1) * k_rows, :]
                    part_acc = dot(probs.astype(BF16), value, NN)
                    total = part_total if total is None else total + part_total
                    acc = part_acc if acc is None else acc + part_acc
                outputs.append(acc / total)
                sums.append(jnp.broadcast_to(top + jnp.log(total), (q_rows, width)))
            result = merge_heads(outputs)
            full_ref[where, :] = result
            if b == 0:
                att_ref[0, local, :] = result.astype(BF16)
            else:
                send_s[b - 1, local, :] = result.astype(BF16)
            lse_ref[where, :] = merge_heads(sums)
            return carry

        lax.fori_loop(0, rows // q_rows, step, 0)
        if b > 0:
            att_hop(b).start()
        if 0 < turn < len(bits) - 1:
            level(turn, lambda hop: hop.wait_recv())
            level(turn + 1, lambda hop: hop.start())
    level(len(bits) - 1, lambda hop: hop.wait_recv())
    for number in range(1, len(bits)):
        level(number, lambda hop: hop.wait_send())
    for seg in range(n_f):
        wb_hop(seg).wait()
    for b in range(1, blocks):
        att_hop(b).wait()
    for copy in locals_:
        copy.wait()


def attend(qkv, w_in, wi_got, w_back4, heads, n_f):
    blocks, rows, _ = qkv.shape
    width = heads * HEAD
    length = rows * blocks
    _, half, part = wi_got.shape
    _, _, seg_rows, seg_cols = w_back4.shape
    sds = jax.ShapeDtypeStruct
    in_vmem, anywhere = pl.BlockSpec(memory_space=pltpu.VMEM), pl.BlockSpec(memory_space=pl.ANY)
    dma = pltpu.SemaphoreType.DMA
    return pl.pallas_call(
        partial(attend_kernel, blocks=blocks, heads=heads, n_f=n_f, q_rows=256, k_rows=512),
        out_shape=[
            sds((blocks, rows, width), BF16),
            sds((length, width), F32),
            sds((length, width), F32),
            sds((2 * half, n_f * part), BF16),
            sds((n_f, seg_rows, seg_cols), BF16),
        ],
        in_specs=[in_vmem] + [anywhere] * 3,
        out_specs=[in_vmem] * 3 + [anywhere] * 2,
        scratch_shapes=[pltpu.VMEM((length, width), BF16)] * 2
        + [
            pltpu.VMEM((blocks - 1, rows, width), BF16),
            dma((blocks,)),
            dma((blocks,)),
            dma((2, n_f)),
            dma((2, n_f)),
            dma((n_f,)),
            dma((n_f,)),
            dma((4,)),
        ],
        compiler_params=pltpu.CompilerParams(
            vmem_limit_bytes=VMEM_LIMIT, collective_id=3, has_side_effects=True
        ),
        cost_estimate=pl.CostEstimate(
            flops=16 * length * length * width, bytes_accessed=10 * length * width,
            transcendentals=heads * length * length,
        ),
        name="attend",
    )(qkv, w_in, wi_got, w_back4)


def gelu_both(pre):
    slope = math.sqrt(2.0 / math.pi)
    square = pre * pre
    th = jnp.tanh(slope * (pre + 0.044715 * pre * square))
    half = 0.5 * (1.0 + th)
    grad = half + 0.5 * pre * (1.0 - th * th) * (slope * (1.0 + 3 * 0.044715 * square))
    return pre * half, grad


class Reduction:
    def __init__(self, src, cols, acc, got, far, sems, n_f, n_z, begin=0, summed=True):
        self.begin, self.summed = begin, summed
        self.z_bits = [1 << i for i in range(n_z.bit_length() - 1)]
        self.src, self.cols, self.acc, self.got, self.far = src, cols, acc, got, far
        self.load_sem, self.f_send, self.f_recv, self.z_send, self.z_recv = sems
        self.n_z = n_z
        ctx, self.fs = lax.axis_index("ctx"), lax.axis_index("fsdp")
        self.core, self.zed = ctx % 2, ctx // 2
        self.bits, self.orders = fsdp_orders(n_f)
        self.last = len(self.bits) - 1

    def targets(self, side, level):
        found = [0]
        for bit in reversed(self.orders[side][level + 1 :]):
            found = found + [d ^ bit for d in found]
        return found

    def part(self, side, target):
        return self.src.at[:, side, target, :, self.cols]

    def load(self, side, i):
        d = self.targets(side, 0)[i]
        return pltpu.make_async_copy(self.part(side, self.fs ^ d), self.acc.at[side, i], self.load_sem.at[side, i])

    def hop(self, side, level, i):
        bit = self.orders[side][level]
        first = sum(len(self.targets(side, l)) for l in range(level))
        if level == 0:
            src = self.part(side, self.fs ^ bit ^ self.targets(side, 0)[i])
        else:
            src = self.acc.at[side, len(self.targets(side, level)) + i]
        return remote(
            src, self.got.at[side, first + i], self.f_send.at[side, first + i], self.f_recv.at[side, first + i],
            {"fsdp": self.fs ^ bit},
        )

    def every(self, level, act):
        for side in range(2):
            for i in range(len(self.targets(side, level))):
                act(self.hop(side, level, i))

    def loads(self, act):
        for side in range(2):
            for i in range(len(self.targets(side, 0))):
                act(self.load(side, i))

    def start(self):
        self.every(0, lambda hop: hop.start())
        self.loads(lambda copy: copy.start())

    def level(self, level):
        if level == 0:
            self.loads(lambda copy: copy.wait())
        self.every(level, lambda hop: hop.wait_recv())
        first = sum(len(self.targets(0, l)) for l in range(level))
        count = len(self.targets(0, level))

        def add(n, carry):
            side, rest = n // (count * self.n_z), n % (count * self.n_z)
            i, z = rest // self.n_z, rest % self.n_z
            total = self.acc[side, i, z].astype(F32) + self.got[side, first + i, z].astype(F32)
            self.acc[side, i, z] = total.astype(BF16)
            return carry

        lax.fori_loop(0, 2 * count * self.n_z, add, 0)
        if level < self.last:
            self.every(level + 1, lambda hop: hop.start())
        elif self.far is not None:
            self.z_start()

    def z_targets(self, level):
        found = [0]
        for bit in reversed(self.z_bits[level + 1 :]):
            found = found + [d ^ bit for d in found]
        return found

    def z_hops(self, level):
        hops = []
        if self.summed:
            bit = self.z_bits[level]
            first = sum(len(self.z_targets(l)) for l in range(level))
            moves = [(bit ^ d, bit, first + i) for i, d in enumerate(self.z_targets(level))]
        else:
            moves = [(m, m, m - 1) for m in range(self.n_z - 1, 0, -1)]
        for block, away, slot in moves:
            for side in range(2):
                hops.append(
                    remote(
                        self.acc.at[side, 0, self.zed ^ block], self.far.at[side, slot], self.z_send.at[side, slot],
                        self.z_recv.at[side, slot], {"ctx": (self.zed ^ away) * 2 + self.core},
                    )
                )
        return hops

    def z_start(self, level=0):
        for hop in self.z_hops(level):
            hop.start()

    def z_level(self, level):
        for hop in self.z_hops(level):
            hop.wait_recv()
        if level == len(self.z_bits) - 1:
            return
        first = sum(len(self.z_targets(l)) for l in range(level))
        for i, d in enumerate(self.z_targets(level)):
            for side in range(2):
                total = self.acc[side, 0, self.zed ^ d].astype(F32) + self.far[side, first + i].astype(F32)
                self.acc[side, 0, self.zed ^ d] = total.astype(BF16)
        self.z_start(level + 1)

    def arrived(self):
        for hop in self.z_hops(0):
            hop.wait_recv()

    def total(self, side):
        return self.acc[side, 0, self.zed].astype(F32) + self.far[side, self.n_z - 2].astype(F32)

    def sent(self):
        for level in range(self.begin, self.last + 1):
            self.every(level, lambda hop: hop.wait_send())
        if self.far is not None:
            for level in range(len(self.z_bits) if self.summed else 1):
                for hop in self.z_hops(level):
                    hop.wait_send()


def row_stats(value):
    return jnp.mean(value, axis=1, keepdims=True)


def mid_kernel(*refs, n_f, n_z, reduce, cfg):
    refs = list(refs)
    red_refs = [refs.pop() for _ in range(6)][::-1] if reduce else None
    sum_out = refs.pop(16) if reduce else None
    att_in, x_ref, cot_ref, vec_ref, bias_ref, wo_ref, wi_ref, wb_ref, got_ref, got2_ref = refs[:10]
    layer_ref, grad_one_ref, ga_ref, sums_ref, bias_sum_ref, grads_out = refs[10:16]
    att_ref, att2_s, h_ref, act_ref, g2_ref, gp_ref, g1_ref, ga_s, turned_s, og_s = refs[16:26]
    wo_s, wi_s, wb_s, slope_s, normed_s, unit_s, acc_s, send_s, recv_s, rstd_s = refs[26:36]
    w_sem, send_sem, recv_sem, b_send, b_recv, a_send, a_recv, g_sem = refs[36:]
    ctx, fs = lax.axis_index("ctx"), lax.axis_index("fsdp")
    core, zed = ctx % 2, ctx // 2
    partner = {"ctx": zed * 2 + (1 - core)}
    rows, width = x_ref.shape
    own, other = slice(0, rows), slice(rows, 2 * rows)
    wide = att_in.shape[2]
    half_in = n_z * wide
    ff_half = wi_s.shape[1]
    step = cfg["step"]
    chunk = cfg["rows"]
    bits, orders = fsdp_orders(n_f)
    _, _, seg_rows, seg_cols = wb_ref.shape

    def wb_place(seg, m):
        return wb_s.at[
            pl.ds(seg * seg_rows, seg_rows), pl.ds(pl.multiple_of((fs ^ m) * seg_cols, 128), seg_cols)
        ]

    def wb_order(seg):
        return orders[seg * 2 // n_f]

    def wb_source(seg, m):
        if m == 0:
            return wb_ref.at[seg, core]
        if m == wb_order(seg)[1]:
            return got2_ref.at[seg]
        return got_ref.at[seg] if m == wb_order(seg)[0] else wb_place(seg, m)

    def wb_hop(seg, m, bit):
        return remote(
            wb_source(seg, m), wb_place(seg, m), b_send.at[seg, m ^ bit], b_recv.at[seg, m ^ bit], {"fsdp": fs ^ bit}
        )

    def wb_level(number, act):
        for seg in range(n_f):
            for m in known_at(wb_order(seg), number)[1 if number == 1 else 0 :]:
                act(wb_hop(seg, m, wb_order(seg)[number]))

    copies = [
        [pltpu.make_async_copy(wo_ref, wo_s, w_sem.at[0])],
        [pltpu.make_async_copy(wi_ref, wi_s, w_sem.at[1])],
        [],
    ]
    for seg in range(n_f):
        for i, m in enumerate((0, wb_order(seg)[0], wb_order(seg)[1])):
            copies[2].append(pltpu.make_async_copy(wb_source(seg, m), wb_place(seg, m), w_sem.at[2 + 3 * seg + i]))
    for copy in copies[0] + copies[1]:
        copy.start()
    greet(
        pltpu.get_barrier_semaphore(),
        [partner] + [{"fsdp": fs ^ bit} for bit in bits] + [{"ctx": (zed ^ m) * 2 + core} for m in range(1, n_z)],
    )
    wb_level(1, lambda hop: hop.start())
    for copy in copies[2]:
        copy.start()

    def exchange(n, src, dst):
        return remote(src, dst, send_sem.at[n], recv_sem.at[n], partner)

    def over_cols(total, body):
        def run(i, carry):
            body(pl.ds(pl.multiple_of(i * step, step), step))
            return carry

        lax.fori_loop(0, total // step, run, 0)

    def over_rows(body):
        def run(i, carry):
            return body(pl.ds(pl.multiple_of(i * chunk, chunk), chunk), carry)

        zero = jnp.zeros((1, width), F32)
        return lax.fori_loop(0, rows // chunk, run, (zero, zero, zero))

    if wide % 128 == 0:
        for m in range(n_z):
            att_ref[:, pl.ds(pl.multiple_of((zed ^ m) * wide, wide), wide)] = att_in[m]
    else:
        for m in range(0, n_z, 2):
            one, two = att_in[m].astype(F32), att_in[m + 1].astype(F32)
            odd = zed % 2 == 1
            block = jnp.concatenate([jnp.where(odd, two, one), jnp.where(odd, one, two)], axis=1)
            at = pl.ds(pl.multiple_of((zed // 2 ^ (m // 2)) * 2 * wide, 2 * wide), 2 * wide)
            att_ref[:, at] = block.astype(BF16)

    def wait_all(group):
        for copy in group:
            copy.wait()

    att_move = exchange(6, att_ref, att2_s)
    att_move.start()

    wait_all(copies[0])

    def out_other(cols):
        send_s[:, cols] = dot(att_ref[other, :], wo_s[:, cols], NN)

    over_cols(width, out_other)
    move = exchange(0, send_s, recv_s)
    move.start()

    def out_own(cols):
        part = dot(att_ref[own, :], wo_s[:, cols], NN)
        acc_s[:, cols] = part + x_ref[:, cols].astype(F32) + vec_ref[2:3, cols]

    over_cols(width, out_own)
    move.wait()

    def norm_one(r, carry):
        resid = acc_s[r, :] + recv_s[r, :]
        centre = resid - row_stats(resid)
        rstd = lax.rsqrt(row_stats(centre * centre) + EPS)
        unit = centre * rstd
        normed = unit * vec_ref[3:4, :] + vec_ref[4:5, :]
        unit_s[r, :] = unit
        rstd_s[r, :] = jnp.broadcast_to(rstd, (chunk, 128))
        normed_s[r, :] = normed
        h_ref[r, :] = normed.astype(BF16)
        return carry

    over_rows(norm_one)
    move = exchange(1, h_ref.at[own], h_ref.at[other])
    move.start()

    wait_all(copies[1])

    def up(where):
        def body(cols):
            pre = dot(h_ref[where, :], wi_s[:, cols], NN) + bias_ref[0:1, cols]
            act, slope = gelu_both(pre)
            act_ref[where, cols] = act.astype(BF16)
            slope_s[where, cols] = slope

        over_cols(ff_half, body)

    up(own)
    move.wait()
    up(other)
    for number in range(1, len(bits)):
        wb_level(number, lambda hop: hop.wait_recv())
        if number + 1 < len(bits):
            wb_level(number + 1, lambda hop: hop.start())
    wait_all(copies[2])

    def down_other(cols):
        send_s[:, cols] = dot(act_ref[other, :], wb_s[:, cols], NN)

    over_cols(width, down_other)
    move = exchange(2, send_s, recv_s)
    move.start()

    def down_own(cols):
        part = dot(act_ref[own, :], wb_s[:, cols], NN)
        acc_s[:, cols] = part + normed_s[:, cols] + vec_ref[5:6, cols]

    over_cols(width, down_own)
    move.wait()

    def norm_two(r, carry):
        resid = acc_s[r, :] + recv_s[r, :]
        centre = resid - row_stats(resid)
        rstd = lax.rsqrt(row_stats(centre * centre) + EPS)
        unit = centre * rstd
        gain = vec_ref[6:7, :]
        layer_ref[r, :] = (unit * gain + vec_ref[7:8, :]).astype(BF16)
        grad = cot_ref[r, :]
        scaled = grad * gain
        back = rstd * (scaled - row_stats(scaled) - unit * row_stats(scaled * unit))
        acc_s[r, :] = back
        g2_ref[r, :] = back.astype(BF16)
        sums = (back, grad * unit, grad)
        return tuple(c + jnp.sum(s, axis=0, keepdims=True) for c, s in zip(carry, sums))

    shift_two = over_rows(norm_two)
    move = exchange(3, g2_ref.at[own], g2_ref.at[other])
    move.start()
    for i, total in enumerate(shift_two):
        sums_ref[3 + i : 4 + i, :] = total

    def back_act(where, first):
        def body(cols):
            grad = dot(g2_ref[where, :], wb_s[cols, :], NT) * slope_s[where, cols]
            gp_ref[where, cols] = grad.astype(BF16)
            total = jnp.sum(grad, axis=0, keepdims=True)
            bias_sum_ref[0:1, cols] = total if first else bias_sum_ref[0:1, cols] + total

        over_cols(ff_half, body)

    back_act(own, True)
    move.wait()
    n_out = ff_half // step
    d_rows = width // n_z

    def product(left, right, store):
        for i in range(0, width, 256):
            turned_s[i : i + 256, :] = left[:, i : i + 256].T

        def cols_of(i, carry):
            cols = pl.ds(pl.multiple_of(i * step, step), step)
            store(i, cols, dot(turned_s[...], right[:, cols], NN).astype(BF16))
            return carry

        lax.fori_loop(0, n_out, cols_of, 0)

    if reduce:
        gb_s, acc_r, got_r, load_sem, f_send, f_recv = red_refs
        sums = Reduction(gb_s, pl.ds(0, ff_half), acc_r, got_r, None, (load_sem, f_send, f_recv, None, None), n_f, n_z)
        low = gb_s.shape[3]

        def store_back(i, cols, value):
            gb_s[:, :, :, :, cols] = value.reshape(n_z, 2, n_f, low, step)

        product(g2_ref, act_ref, store_back)
        sums.start()
    back_act(other, False)

    def back_other(cols):
        send_s[:, cols] = dot(gp_ref[other, :], wi_s[cols, :], NT)

    over_cols(width, back_other)
    move = exchange(4, send_s, recv_s)
    move.start()

    def back_own(cols):
        acc_s[:, cols] += dot(gp_ref[own, :], wi_s[cols, :], NT)

    over_cols(width, back_own)
    move.wait()

    def back_one(r, carry):
        grad = acc_s[r, :] + recv_s[r, :]
        unit = unit_s[r, :]
        rstd = rstd_s[r, 0:1]
        scaled = grad * vec_ref[3:4, :]
        back = rstd * (scaled - row_stats(scaled) - unit * row_stats(scaled * unit))
        grad_one_ref[r, :] = back
        g1_ref[r, :] = back.astype(BF16)
        sums = (back, grad * unit, grad)
        return tuple(c + jnp.sum(s, axis=0, keepdims=True) for c, s in zip(carry, sums))

    shift_one = over_rows(back_one)
    move = exchange(5, g1_ref.at[own], g1_ref.at[other])
    move.start()
    for i, total in enumerate(shift_one):
        sums_ref[i : 1 + i, :] = total
    sums_ref[6:8, :] = jnp.zeros((2, width), F32)

    def att_hop(m):
        return remote(ga_s.at[m - 1], ga_ref.at[m], a_send.at[m], a_recv.at[m], {"ctx": (zed ^ m) * 2 + core})

    move.wait()
    for m in list(range(n_z - 1, 0, -1)) + [0]:
        at = pl.ds(pl.multiple_of((zed ^ m) * wide, wide), wide)
        block = dot(g1_ref[...], wo_s[at, :], NT).astype(BF16)
        if m == 0:
            ga_ref[0] = block
        else:
            ga_s[m - 1] = block
            att_hop(m).start()

    if reduce:
        sums.level(0)

    def out_grad(i, which):
        cols = pl.ds(pl.multiple_of(i * step, step), step)
        there = pl.ds(pl.multiple_of(which * ff_half + i * step, step), step)
        return pltpu.make_async_copy(wi_s.at[:, cols], grads_out.at[:, there], g_sem.at[which * n_out + i])

    def store_staged(which):
        def store(i, cols, value):
            if which == 1:
                out_grad(i, 0).wait()
            wi_s[:, cols] = value
            out_grad(i, which).start()

        return store

    product(h_ref, gp_ref, store_staged(0))
    wide_out = ff_half
    if not reduce:
        product(g2_ref, act_ref, store_staged(1))
        wide_out = 2 * ff_half
    att_move.wait()
    half = width // 2
    cols = pl.ds(pl.multiple_of(core * half, 128), half)
    for i in range(0, half_in, 256):
        at = pl.ds(pl.multiple_of(core * half + i, 128), 256)
        og_s[at, :] = dot(att_ref[:, i : i + 256].T, g1_ref[:, cols], NN).astype(BF16)
        at = pl.ds(pl.multiple_of((1 - core) * half + i, 128), 256)
        turned = att2_s[:, i : i + 256].T
        og_s[at, :] = (
            dot(turned[:, :rows], g1_ref[rows:, cols], NN) + dot(turned[:, rows:], g1_ref[:rows, cols], NN)
        ).astype(BF16)
    out_move = pltpu.make_async_copy(og_s, grads_out.at[:, pl.ds(wide_out, half)], g_sem.at[2 * n_out])
    out_move.start()
    for number in range(1, len(bits)):
        wb_level(number, lambda hop: hop.wait_send())
    for m in range(1, n_z):
        att_hop(m).wait()
    for i in range(n_out):
        out_grad(i, 0 if reduce else 1).wait()
    out_move.wait()
    if reduce:
        for level in range(1, len(bits)):
            sums.level(level)
        final = pltpu.make_async_copy(acc_r.at[:, pl.ds(0, 1)], sum_out, load_sem.at[0, 0])
        final.start()
        sums.sent()
        final.wait()


def middle(att, x_own, cot, vectors, bias_half, wo, wi, wb4, got, got2, n_f, n_z, reduce):
    rows, width = x_own.shape
    wide = att.shape[2]
    ff_half = bias_half.shape[0]
    half_in = n_z * wide
    sds = jax.ShapeDtypeStruct
    vmem, dma = pltpu.VMEM, pltpu.SemaphoreType.DMA
    in_vmem, anywhere = pl.BlockSpec(memory_space=pltpu.VMEM), pl.BlockSpec(memory_space=pl.ANY)
    cfg = {"step": 512, "rows": 128}
    low = width // (2 * n_z * n_f)
    extra_out, extra = [], []
    if reduce:
        extra_out = [sds((2, 1, n_z, low, ff_half), BF16)]
        extra = [
            vmem((n_z, 2, n_f, low, ff_half), BF16),
            vmem((2, n_f // 2, n_z, low, ff_half), BF16),
            vmem((2, n_f - 1, n_z, low, ff_half), BF16),
            dma((2, n_f // 2)),
            dma((2, n_f - 1)),
            dma((2, n_f - 1)),
        ]
    return pl.pallas_call(
        partial(mid_kernel, n_f=n_f, n_z=n_z, reduce=reduce, cfg=cfg),
        out_shape=[
            sds((rows, width), BF16),
            sds((rows, width), F32),
            sds((n_z, 2 * rows, wide), BF16),
            sds((8, width), F32),
            sds((1, ff_half), F32),
            sds((width, (1 if reduce else 2) * ff_half + width // 2), BF16),
        ]
        + extra_out,
        in_specs=[in_vmem] * 5 + [anywhere] * 5,
        out_specs=[in_vmem] * 5 + [anywhere] * (1 + len(extra_out)),
        scratch_shapes=[
            vmem((2 * rows, half_in), BF16),
            vmem((2 * rows, half_in), BF16),
            vmem((2 * rows, width), BF16),
            vmem((2 * rows, ff_half), BF16),
            vmem((2 * rows, width), BF16),
            vmem((2 * rows, ff_half), BF16),
            vmem((2 * rows, width), BF16),
            vmem((n_z - 1, 2 * rows, wide), BF16),
            vmem((width, 2 * rows), BF16),
            vmem((width, width // 2), BF16),
            vmem((half_in, width), BF16),
            vmem((width, ff_half), BF16),
            vmem((ff_half, width), BF16),
            vmem((2 * rows, ff_half), F32),
            vmem((rows, width), F32),
            vmem((rows, width), F32),
            vmem((rows, width), F32),
            vmem((rows, width), F32),
            vmem((rows, width), F32),
            vmem((rows, 128), F32),
            dma((2 + 3 * n_f,)),
            dma((7,)),
            dma((7,)),
            dma((n_f, n_f)),
            dma((n_f, n_f)),
            dma((n_z,)),
            dma((n_z,)),
            dma((2 * (ff_half // cfg["step"]) + 1,)),
        ]
        + extra,
        compiler_params=pltpu.CompilerParams(
            vmem_limit_bytes=VMEM_MIDDLE, collective_id=0, has_side_effects=True
        ),
        cost_estimate=pl.CostEstimate(
            flops=2 * 2 * rows * width * (3 * half_in + 6 * ff_half),
            bytes_accessed=40 << 20, transcendentals=2 * rows * ff_half,
        ),
        name="middle",
    )(att, x_own, cot, vectors, bias_half[None], wo, wi, wb4, got, got2)


def back_kernel(*refs, blocks, heads, n_f, reduce, q_rows, steps_per):
    refs = list(refs)

    def take(count):
        taken = refs[:count]
        del refs[:count]
        return taken

    qkv_ref, ga_ref, full_ref, lse_ref, grad_one_ref = take(5)
    if reduce:
        mid_ref, bias_ref = take(2)
    (wl_hbm,) = take(1)
    if reduce:
        x_hbm, g_hbm, back_hbm = take(3)
    out_ref, sums_ref = take(2)
    if reduce:
        in_ref, back_ref, og_ref, qg_ref = take(4)
    (stage,) = take(1)
    lse_t, delta_t, gq_t, key_t, gin, wl_s, cat, send_s, recv_s = take(9)
    kv_send, kv_recv, q_send, q_recv, t_send, t_recv, own_sem = take(7)
    if reduce:
        x_s, gq_src, give_s, others, table_r, c_send, c_recv, o_send, o_recv, s_send, s_recv = take(11)
        bufs = [take(8) for _ in range(4)]
    ctx, fs = lax.axis_index("ctx"), lax.axis_index("fsdp")
    core, zed = ctx % 2, ctx // 2
    partner = {"ctx": zed * 2 + (1 - core)}
    bits, orders = fsdp_orders(n_f)
    rows = qkv_ref.shape[1]
    width = heads * HEAD
    scale = HEAD**-0.5
    chunk = 256
    half = wl_s.shape[1] // 3
    greeted = [partner] + [{"ctx": (zed ^ m) * 2 + core} for m in range(1, blocks)]
    if reduce:
        greeted += [{"fsdp": fs ^ bit} for bit in bits]
    greet(pltpu.get_barrier_semaphore(), greeted)
    wl_copy = pltpu.make_async_copy(wl_hbm, wl_s, own_sem.at[0])
    wl_copy.start()
    if reduce:
        cut = bufs[0][0].shape[-1]
        early, late, attn, lone = [
            Reduction(
                src, pl.ds(first, buf[0].shape[-1]), buf[0], buf[1], buf[2], buf[3:], n_f, blocks, begin, summed
            )
            for buf, src, first, begin, summed in zip(
                bufs, (g_hbm, g_hbm, gq_src, None), (0, cut, 0, 0), (0, 0, 0, len(bits)), (True, True, False, True)
            )
        ]
        lone_copy = pltpu.make_async_copy(back_hbm, lone.acc, own_sem.at[2])
        lone_copy.start()
        lone_copy.wait()
        lone.z_start()
        early.start()
        x_copy = pltpu.make_async_copy(x_hbm, x_s, own_sem.at[1])
        x_copy.start()

    for b in range(blocks):
        for i in range(0, rows, chunk):
            local = slice(i, i + chunk)
            where = slice(b * rows + i, b * rows + i + chunk)
            logs = lse_ref[where, :].T
            terms = (ga_ref[b, local, :].astype(F32) * full_ref[where, :]).T
            for head in range(heads):
                first = head * HEAD
                lse_t[head : head + 1, where] = logs[first : first + 1]
                delta_t[head : head + 1, where] = jnp.sum(
                    terms[first : first + HEAD], axis=0, keepdims=True
                )
        key_t[:, b * rows : (b + 1) * rows] = qkv_ref[b, :, width : 2 * width].T
    gq_t[...] = jnp.zeros_like(gq_t)

    split = width % 128 == 0

    def kv_hop(m, piece):
        at = pl.ds(pl.multiple_of(piece * (rows // steps_per), 128), rows // steps_per)
        cols = pl.ds(width, 2 * width)
        return remote(
            stage.at[m, at, cols], gin.at[m, at, cols], kv_send.at[m, piece], kv_recv.at[m, piece],
            {"ctx": (zed ^ m) * 2 + core},
        )

    def q_hop(m):
        cols = pl.ds(0, width if split else 3 * width)
        return remote(
            stage.at[m, :, cols], gin.at[m, :, cols], q_send.at[m], q_recv.at[m], {"ctx": (zed ^ m) * 2 + core}
        )

    k_rows = rows // steps_per

    def step(n, carry):
        b = blocks - 1 - n // steps_per
        start = n % steps_per * k_rows
        local = pl.ds(pl.multiple_of(start, 128), k_rows)
        where = pl.ds(pl.multiple_of(b * rows + start, 128), k_rows)
        key = qkv_ref[b, local, width : 2 * width]
        value = qkv_ref[b, local, 2 * width : 3 * width]
        key_grads, value_grads = [], []
        for head in range(heads):
            feats = slice(head * HEAD, (head + 1) * HEAD)
            key_h = one_head(key, head, heads) * BF16(scale)
            value_h = one_head(value, head, heads)
            key_grad = value_grad = None
            for other in range(blocks):
                for i in range(0, rows, q_rows):
                    here = slice(i, i + q_rows)
                    there = slice(other * rows + i, other * rows + i + q_rows)
                    query = qkv_ref[other, here, 0:width]
                    grad = ga_ref[other, here, :]
                    scores = dot(key_h, query, NT)
                    probs = jnp.exp(scores - lse_t[head : head + 1, there])
                    grad_probs = dot(value_h, grad, NT)
                    grad_scores = probs * (grad_probs - delta_t[head : head + 1, there])
                    grad_scores = grad_scores.astype(BF16)
                    term = dot(probs.astype(BF16), grad, NN)
                    value_grad = term if value_grad is None else value_grad + term
                    term = dot(grad_scores, query, NN)
                    key_grad = term if key_grad is None else key_grad + term
                    gq_t[feats, there] += dot(key_t[feats, where], grad_scores, NN)
            key_grads.append(key_grad)
            value_grads.append(value_grad)
        stage[b, local, width : 2 * width] = (merge_heads(key_grads) * scale).astype(BF16)
        stage[b, local, 2 * width : 3 * width] = merge_heads(value_grads).astype(BF16)
        if split:

            @pl.when(b > 0)
            def _():
                kv_hop(b, n % steps_per).start()

        if reduce:

            @pl.when(n == 1)
            def _():
                early.level(0)

            @pl.when(n == 2)
            def _():
                late.start()

            @pl.when(n == 3)
            def _():
                for level in range(1, len(bits)):
                    early.level(level)
                lone.z_level(0)

            @pl.when(n == 4)
            def _():
                late.level(0)

            @pl.when(n == 5)
            def _():
                early.z_level(0)

            @pl.when(n == 6)
            def _():
                for level in range(1, len(bits)):
                    late.level(level)

        return carry

    lax.fori_loop(0, blocks * steps_per, step, 0)
    for b in range(blocks - 1, -1, -1):
        for i in range(0, rows, chunk):
            there = slice(b * rows + i, b * rows + i + chunk)
            stage[b, i : i + chunk, 0:width] = (gq_t[:, there].T * scale).astype(BF16)
        if b > 0:
            q_hop(b).start()
    gin[0] = stage[0]
    sums = jnp.zeros((1, 3 * width), F32)
    for b in range(blocks):
        sums = sums + jnp.sum(stage[b].astype(F32), axis=0, keepdims=True)
    if reduce:
        dim = out_ref.shape[1]
        hidden_half = bias_ref.shape[1] // n_f
        sums_ref[...] = jnp.zeros_like(sums_ref)
        first = pl.ds(pl.multiple_of(core * half + zed * width, 128), width)
        sums_ref[0:1, first] = sums[:, 0:width]
        sums_ref[1:2, first] = sums[:, 2 * width :]
        sums_ref[2:8, :] = mid_ref[0:6, :]
        for f in range(n_f):
            at = pl.ds(pl.multiple_of(core * hidden_half, 128), hidden_half)
            sums_ref[8 + f : 9 + f, at] = bias_ref[:, f * hidden_half : (f + 1) * hidden_half]
        peers = [{"fsdp": fs ^ bit} for bit in bits]
        peers += [{"ctx": (zed ^ (1 << i)) * 2 + core} for i in range(blocks.bit_length() - 1)] + [partner]

        def table_hop(k):
            return remote(sums_ref, table_r.at[k], s_send.at[k], s_recv.at[k], peers[k])

        def table_step(k):
            if k < len(peers):
                table_hop(k).wait()
                sums_ref[...] += table_r[k]
                if k + 1 < len(peers):
                    table_hop(k + 1).start()

        table_hop(0).start()
    else:
        sums_ref[...] = sums

    if reduce:
        x_copy.wait()
        d_rows = x_s.shape[-1] // blocks
        low = gq_src.shape[3]
        for b in range(blocks):
            cat[0 : 3 * width, b * rows : (b + 1) * rows] = stage[b].T
        for z in range(blocks):
            cols = slice(z * d_rows, (z + 1) * d_rows)
            total = None
            for b in range(blocks):
                x_block = x_s[b, :, :, cols].reshape(rows, d_rows)
                term = dot(cat[0 : 3 * width, b * rows : (b + 1) * rows], x_block, NN)
                total = term if total is None else total + term
            gq_src[z] = total.T.astype(BF16).reshape(2, n_f, low, 3 * width)
        attn.start()
        table_step(0)
        late.z_level(0)

    tokens, dim = out_ref.shape
    pieces = dim // 256

    def collect(j):
        part = slice(j * width, (j + 1) * width)
        if split:
            for m in range(blocks):
                at = pl.ds(pl.multiple_of(j * half + (zed ^ m) * width, 128), width)
                cat[0:rows, at] = gin[m, :, part]
        else:
            for m in range(0, blocks, 2):
                one, two = gin[m, :, part].astype(F32), gin[m + 1, :, part].astype(F32)
                odd = zed % 2 == 1
                block = jnp.concatenate([jnp.where(odd, two, one), jnp.where(odd, one, two)], axis=1)
                at = j * half + (zed // 2 ^ (m // 2)) * 2 * width
                cat[0:rows, pl.ds(pl.multiple_of(at, 128), 2 * width)] = block.astype(BF16)

    def swap_hop(i):
        cols = slice(i * 256, (i + 1) * 256)
        return remote(send_s.at[:, cols], recv_s.at[:, cols], t_send.at[i], t_recv.at[i], partner)

    for m in range(blocks - 1, 0, -1):
        if split:
            for piece in range(steps_per):
                kv_hop(m, piece).wait()
        else:
            q_hop(m).wait()
    wl_copy.wait()
    collect(1)
    collect(2)
    keys = slice(half, 3 * half)
    for i in range(pieces):
        cols = slice(i * 256, (i + 1) * 256)
        send_s[:, cols] = dot(cat[tokens:rows, keys], wl_s[cols, keys], NT)
        out_ref[:, cols] = dot(cat[0:tokens, keys], wl_s[cols, keys], NT) + grad_one_ref[:, cols]
    if reduce:
        hops = []

        def settle(which, offset, places):
            count = which.acc.shape[-1]
            give_s[:, offset : offset + count] = which.total(1 - core)
            kept = which.total(core)
            start = 0
            for target, at, size in places:
                cols = pl.ds(pl.multiple_of(at, 128), size)
                hop = remote(
                    give_s.at[:, pl.ds(offset + start, size)], target.at[:, cols], c_send.at[len(hops)],
                    c_recv.at[len(hops)], partner,
                )
                hop.start()
                hops.append(hop)
                target[:, cols] = kept[:, start : start + size]
                start += size

        def units(target):
            return [(target, (2 * f + core) * hidden_half, hidden_half) for f in range(n_f)]

        for level in range(len(bits)):
            attn.level(level)
            table_step(1 + level)
        for level in range(1, len(lone.z_bits)):
            lone.z_level(level)
        settle(lone, 0, units(back_ref))
    if split:
        for m in range(blocks - 1, 0, -1):
            q_hop(m).wait()
    collect(0)
    for i in range(pieces):
        cols = slice(i * 256, (i + 1) * 256)
        send_s[:, cols] += dot(cat[tokens:rows, 0:half], wl_s[cols, 0:half], NT)
        swap_hop(i).start()
    for i in range(pieces):
        cols = slice(i * 256, (i + 1) * 256)
        out_ref[:, cols] += dot(cat[0:tokens, 0:half], wl_s[cols, 0:half], NT)
    if reduce:
        for k in range(1 + len(bits), len(peers)):
            table_step(k)
    for i in range(pieces):
        cols = slice(i * 256, (i + 1) * 256)
        swap_hop(i).wait_recv()
        out_ref[:, cols] += recv_s[:, cols]
    for i in range(pieces):
        swap_hop(i).wait_send()

    if reduce:
        attn.arrived()

        def other_hop(m):
            src = attn.acc.at[1 - core, 0, zed] if m == 0 else attn.far.at[1 - core, m - 1]
            return remote(src, others.at[m], o_send.at[m], o_recv.at[m], partner)

        def put_heads(m, value, which):
            for j in range(3):
                at = pl.ds(pl.multiple_of(j * dim + which * half + (zed ^ m) * width, 128), width)
                qg_ref[:, at] = value[:, j * width : (j + 1) * width].astype(F32)

        for m in range(blocks):
            other_hop(m).start()
        for m in range(blocks):
            put_heads(m, attn.acc[core, 0, zed] if m == 0 else attn.far[core, m - 1], core)

        places = units(in_ref) + [(og_ref, core * half, half)]
        offset = lone.acc.shape[-1]
        for which, some in ((early, places[: n_f - 1]), (late, places[n_f - 1 :])):
            for level in range(1, len(which.z_bits)):
                which.z_level(level)
            settle(which, offset, some)
            offset += cut
        for m in range(blocks):
            other_hop(m).wait()
            put_heads(m, others[m], 1 - core)
        for which in (early, late, attn, lone):
            which.sent()
        for hop in hops:
            hop.wait()


def back(qkv, grads, full, lse, grad_one, w_local, x_all, mid_grads, heads, n_f, reduce, back_sums=None, sums_mid=None, bias_sum=None):
    blocks, rows, _ = qkv.shape
    width = heads * HEAD
    length = rows * blocks
    tokens, dim = grad_one.shape
    sds = jax.ShapeDtypeStruct
    vmem, dma = pltpu.VMEM, pltpu.SemaphoreType.DMA
    in_vmem, anywhere = pl.BlockSpec(memory_space=pltpu.VMEM), pl.BlockSpec(memory_space=pl.ANY)
    operands = [qkv, grads, full, lse, grad_one]
    if reduce:
        operands += [sums_mid, bias_sum]
    inner = len(operands)
    operands += [w_local]
    out_shape = [sds((tokens, dim), F32), sds((16, dim) if reduce else (1, 3 * width), F32)]
    staged = (blocks, rows, 3 * width)
    scratch = [
        vmem((8, length), F32),
        vmem((8, length), F32),
        vmem((width, length), F32),
        vmem((width, length), BF16),
        vmem(staged, BF16),
        vmem(w_local.shape, BF16),
        vmem((rows, max(length, w_local.shape[1])), BF16),
        vmem((tokens, dim), F32),
        vmem((tokens, dim), F32),
        dma((blocks, 2)),
        dma((blocks, 2)),
        dma((blocks,)),
        dma((blocks,)),
        dma((dim // 256,)),
        dma((dim // 256,)),
        dma((3,)),
    ]
    if reduce:
        _, _, _, low, columns = mid_grads.shape
        operands += [x_all, mid_grads, back_sums]
        hidden_half = back_sums.shape[-1]
        out_shape += [sds((low, 2 * hidden_half), F32)] * 2 + [sds((low, dim), F32), sds((low, 3 * dim), F32)]
        n_peers = n_f.bit_length() + blocks.bit_length() - 1
        scratch = [vmem(staged, BF16)] + scratch
        scratch += [
            vmem(x_all.shape, BF16),
            vmem((blocks, 2, n_f, low, 3 * width), BF16),
            vmem((low, columns + hidden_half), F32),
            vmem((blocks, low, 3 * width), BF16),
            vmem((n_peers, 16, dim), F32),
            dma((2 * n_f + 1,)),
            dma((2 * n_f + 1,)),
            dma((blocks,)),
            dma((blocks,)),
            dma((n_peers,)),
            dma((n_peers,)),
        ]
        cut = (n_f - 1) * (hidden_half // n_f)
        for cols in (cut, columns - cut, 3 * width, hidden_half):
            halved = cols == hidden_half
            scratch += [
                vmem((2, 1 if halved else n_f // 2, blocks, low, cols), BF16),
                vmem((2, 1, 1, 16, 128) if halved else (2, n_f - 1, blocks, low, cols), BF16),
                vmem((2, blocks - 1, low, cols), BF16),
                dma((2, n_f // 2)),
                dma((2, n_f - 1)),
                dma((2, n_f - 1)),
                dma((2, blocks - 1)),
                dma((2, blocks - 1)),
            ]
    else:
        out_shape += [sds(staged, BF16)]
    return pl.pallas_call(
        partial(
            back_kernel, blocks=blocks, heads=heads, n_f=n_f, reduce=reduce, q_rows=256, steps_per=2
        ),
        out_shape=out_shape,
        in_specs=[in_vmem] * inner + [anywhere] * (len(operands) - inner),
        out_specs=[in_vmem] * len(out_shape),
        scratch_shapes=scratch,
        compiler_params=pltpu.CompilerParams(
            vmem_limit_bytes=VMEM_MIDDLE, collective_id=2, has_side_effects=True
        ),
        cost_estimate=pl.CostEstimate(
            flops=40 * length * length * width, bytes_accessed=30 << 20,
            transcendentals=heads * length * length,
        ),
        name="back",
    )(*operands)


def on_device(x_in, w_qkv, w_out, w_in, w_back, vectors, bias_in, cot, *, n_ctx, n_f):
    ctx, fs = lax.axis_index("ctx"), lax.axis_index("fsdp")
    core, zed = ctx % 2, ctx // 2
    n_z = n_ctx // 2
    x_own = x_in[0]
    grad_out = cot[0]
    rows, width = x_own.shape
    hidden = w_back.shape[0]
    half_heads = HEADS // 2
    heads = half_heads // n_z
    wide = heads * HEAD

    def swap(v):
        return lax.ppermute(v, "ctx", [(i, i ^ 1) for i in range(n_ctx)])

    def over_z(v, m):
        return lax.ppermute(v, "ctx", [(i, i ^ (2 * m)) for i in range(n_ctx)])

    def over_f(v, m):
        return lax.ppermute(v, "fsdp", [(i, i ^ m) for i in range(n_f)])

    bits = [1 << b for b in range(n_f.bit_length() - 1)]

    def place(pieces, index, axis):
        count = len(pieces)
        for bit in range(count.bit_length() - 1):
            flag = (index >> bit) & 1
            pieces = [jnp.where(flag, pieces[m ^ (1 << bit)], pieces[m]) for m in range(count)]
        return jnp.concatenate(pieces, axis=axis)

    half_in = width // 2
    first = (core * half_heads + zed * heads) * HEAD
    span = 3 * wide
    bias_qkv = jnp.concatenate(
        [
            lax.dynamic_slice_in_dim(vectors[0], first, wide, 0),
            jnp.zeros((wide,), F32),
            lax.dynamic_slice_in_dim(vectors[1], first, wide, 0),
        ]
    )[None]
    ff_part = w_in.shape[1] // 2
    w_back4 = w_back.reshape(n_f, 2, ff_part, w_back.shape[1])
    qkv, x_all, w_local, wo_half, wi_got, wb_got = front(
        x_own, w_qkv, w_out, w_in, w_back4, bias_qkv, n_f, n_z, heads
    )

    att, att_full, lse, wi_half, wb_got2 = attend(qkv, w_in, wi_got, w_back4, heads, n_f)
    bias_half = lax.dynamic_index_in_dim(
        bias_in.reshape(n_f, 2, ff_part), core, 1, False
    ).reshape(-1)
    low = width // (n_ctx * n_f)
    in_kernel = low % 16 == 0 and wide % 128 == 0 and hidden == n_f * width and min(n_z, n_f) >= 4
    layer_out, grad_one, g_att, sums_mid, bias_sum, mid_grads, *back_sums = middle(
        att, x_own, grad_out, vectors, bias_half, wo_half, wi_half, w_back4, wb_got, wb_got2, n_f, n_z, in_kernel
    )
    layer_out = layer_out[None]


    def over_fsdp(partial_grad):
        cols = partial_grad.shape[1]
        view = partial_grad.reshape((n_z, 2) + (2,) * len(bits) + (low, cols))
        done = []
        for side in range(2):
            now = view[:, side]
            order = bits if side == 0 else bits[1:] + bits[:1]
            left = list(reversed(bits))
            for bit in order:
                axis = 1 + left.index(bit)
                left.remove(bit)
                flag = (fs // bit) % 2
                stay = lax.dynamic_index_in_dim(now, flag, axis, False)
                go = lax.dynamic_index_in_dim(now, 1 - flag, axis, False)
                now = (stay.astype(F32) + over_f(go, bit).astype(F32)).astype(BF16)
            done.append(now)
        return jnp.stack(done, axis=1)

    def over_ctx(both):
        total = lax.dynamic_index_in_dim(both, zed, 0, False).astype(F32)
        for m in range(1, n_z):
            part = lax.dynamic_index_in_dim(both, zed ^ m, 0, False)
            total = total + over_z(part, m).astype(F32)
        stay = lax.dynamic_index_in_dim(total, core, 0, False)
        go = lax.dynamic_index_in_dim(total, 1 - core, 0, False)
        return stay, swap(go.astype(BF16)).astype(F32)

    def halves(stay, came, parts):
        low = stay.shape[0]
        first = jnp.where(core == 0, stay, came).reshape(low, parts, 1, -1)
        second = jnp.where(core == 0, came, stay).reshape(low, parts, 1, -1)
        return jnp.concatenate([first, second], axis=2).reshape(low, -1)

    def reduced(partial_grad):
        return over_ctx(over_fsdp(partial_grad))

    if in_kernel:
        grad_in, table, in_weight_grad, back_turned, out_weight_grad, qkv_weight_grad = back(
            qkv, g_att, att_full, lse, grad_one, w_local, x_all,
            mid_grads.reshape(n_z, 2, n_f, low, -1), heads, n_f, True, back_sums[0], sums_mid, bias_sum,
        )
        mine_at = (ctx * n_f + fs) * low
        vector_grad = lax.dynamic_slice_in_dim(table[:8], mine_at, low, 1)
        share = hidden // (n_ctx * n_f)
        in_bias_grad = lax.dynamic_slice_in_dim(table[8 : 8 + n_f].reshape(-1), mine_at // low * share, share, 0)
        return (
            layer_out,
            grad_in[None],
            qkv_weight_grad,
            out_weight_grad,
            in_weight_grad,
            back_turned.T,
            vector_grad,
            in_bias_grad,
        )
    stay, came = reduced(mid_grads)
    grad_in, sums, g_local = back(
        qkv, g_att, att_full, lse, grad_one, w_local, None, None, heads, n_f, False
    )
    attn_grad = dot(x_all.reshape(-1, width), g_local.reshape(-1, span), TN).astype(BF16)
    both = over_fsdp(attn_grad)
    mine, others = [], []
    for m in range(n_z):
        part = lax.dynamic_index_in_dim(both, zed ^ m, 0, False)
        part = part if m == 0 else over_z(part, m)
        mine.append(lax.dynamic_index_in_dim(part, core, 0, False))
        others.append(lax.dynamic_index_in_dim(part, 1 - core, 0, False))
    others = swap(jnp.stack(others))
    others = [others[m] for m in range(n_z)]
    n_half = hidden // 2
    in_weight_grad = halves(stay[:, :n_half], came[:, :n_half], n_f)
    back_weight_grad = halves(stay[:, n_half : 2 * n_half], came[:, n_half : 2 * n_half], n_f).T
    out_weight_grad = halves(stay[:, 2 * n_half :], came[:, 2 * n_half :], 1)

    def heads_order(parts):
        parts = [p.reshape(low, 3, wide) for p in parts]
        return place(parts, zed, 2).astype(F32).reshape(low, -1)

    qkv_weight_grad = halves(heads_order(mine), heads_order(others), 3)

    def spread(half_row, parts):
        piece = half_row.reshape(parts, 1, -1)
        empty = jnp.zeros_like(piece)
        both = jnp.where(core == 0, jnp.concatenate([piece, empty], 1), jnp.concatenate([empty, piece], 1))
        return both.reshape(-1)

    def halve(now):
        left = list(reversed(bits))
        for bit in bits:
            axis = left.index(bit)
            left.remove(bit)
            flag = (fs // bit) % 2
            stay = lax.dynamic_index_in_dim(now, flag, axis, False)
            now = stay + over_f(lax.dynamic_index_in_dim(now, 1 - flag, axis, False), bit)
        return now

    sums = sums[0]
    sums = jnp.stack([sums[:wide].reshape(n_f, -1), sums[2 * wide :].reshape(n_f, -1)], axis=1)
    late = halve(sums.reshape((2,) * len(bits) + (-1,)))
    turn = [(2 * z + c, n_z * c + z) for z in range(n_z) for c in range(2)]
    late = lax.ppermute(late, "ctx", turn).reshape(2, -1)
    ratio = hidden // width
    early = sums_mid[:6].T
    bias_terms = spread(bias_sum[0], n_f).reshape(width, ratio)
    table = jnp.concatenate([early, bias_terms], axis=1)
    kinds = table.shape[1]
    now = jnp.swapaxes(table.reshape(n_z * 2, n_f, low, kinds), -1, -2)
    now = jnp.swapaxes(now, 0, 1).reshape((2,) * len(bits) + (n_z, 2, kinds * low))
    now = halve(now)
    total = lax.dynamic_index_in_dim(now, zed, 0, False)
    for m in range(1, n_z):
        total = total + over_z(lax.dynamic_index_in_dim(now, zed ^ m, 0, False), m)
    stay = lax.dynamic_index_in_dim(total, core, 0, False)
    table = stay + swap(lax.dynamic_index_in_dim(total, 1 - core, 0, False))
    table = table.reshape(kinds, low)
    vector_grad = jnp.concatenate([late, table[:6]], axis=0)
    in_bias_grad = table[6:].T.reshape(-1)
    return (
        layer_out,
        grad_in[None],
        qkv_weight_grad,
        out_weight_grad,
        in_weight_grad,
        back_weight_grad,
        vector_grad,
        in_bias_grad,
    )


def solution(mesh):
    tokens = P("fsdp", "ctx", None)
    cols = P(None, "fsdp")
    shared = P(("ctx", "fsdp"), None)
    return jax.shard_map(
        partial(on_device, n_ctx=mesh.shape["ctx"], n_f=mesh.shape["fsdp"]),
        mesh=mesh,
        in_specs=(tokens, cols, cols, cols, cols, P(), P(), tokens),
        out_specs=(
            tokens,
            tokens,
            shared,
            shared,
            shared,
            P(None, ("ctx", "fsdp")),
            P(None, ("ctx", "fsdp")),
            P(("ctx", "fsdp")),
        ),
        check_vma=False,
    )
```
